32 devices in a mesh: ra: 16 (over z, x, core), band: 2 (over y).
Axes of the slice: x: 2, y: 2, z: 4, core: 2. Of those that a mesh axis runs over, the one named last changes fastest.
Arguments:
- tiles: bfloat16 [1024, 64, 128], P(('ra', 'band')), may hold values from -6 to 6
- tile_patch: int32 [1024], P(('ra', 'band')), may hold values from 0 to 15, as said below
- tile_offset: int32 [1024], P(('ra', 'band')), may hold values from 0 to 128
- tile_weight: bfloat16 [1024], P(('ra', 'band')), may hold values from 0.25 to 4
- visit_band: int32 [128], P(('ra', 'band')), may hold values from 0 to 5
- coeff_index: int32 [1024], P(('ra', 'band')), may hold values from 0 to 63
- coeff_table: float32 [64, 21], replicated, may hold values from -1.3 to 1.3
- row_kernels: bfloat16 [21, 21], replicated, may hold values from -1.25 to 1.25
- column_kernels: bfloat16 [21, 21], replicated, may hold values from -1.25 to 1.25
- band_weight: float32 [6], replicated, may hold values from 0.3 to 1.5
Outputs:
- band_coadds: float32 [6, 64, 4096], P(None, 'band', 'ra')
- detection: float32 [64, 4096], P('band', 'ra')
The draws below stay inside these ranges and needn't reach their ends.
Inputs may be any that keep to these rules, and one draw needn't show every extreme that they name: `tile_patch`: tile j is owned by RA index o = j // 64 and by group g = (j // 32) % 2 of visit owners; its patch lies within 2 patches of o around the cycle of 16 patches. Among the tiles of one device at most 16 fall on one patch, and in every draw, for each group g, one patch receives exactly 16 tiles from each of the 5 devices of group g within reach.
All inputs are finite; a program needn't handle non-finite values.
Results may differ from the reference program's by a relative error of at most 0.005.
Values may be sent and summed in bfloat16 or wider, within the bound.
No kernel may reach another device: no remote copies, remote signals or barrier semaphores. Data moves between devices by JAX's collectives and lax.ppermute only.
A program may use at most 64 MiB of HBM per device.

```python
import math
import jax
import jax.numpy as jnp
from jax import lax

ROWS = 64
TW = 128
PW = 256
TAPS = 21
BASIS = 21
BANDS = 6
NTAB = 64
REACH = 2
TILES_VISIT = 8
TILES_DEV = 32
CAP = 16
PATCHES = 16
GROUPS = 2
TILES = 1024
VISITS = 128


def draw_tile_patch(key, part):
    base = jax.random.fold_in(key, 7)
    key_hot, key_heavy, key_other, key_order = jax.random.split(base, 4)
    hot_patch = jax.random.randint(key_hot, (GROUPS,), 0, PATCHES)
    owner_ra = jnp.arange(PATCHES, dtype=jnp.int32)[:, None]
    distance = (hot_patch[None, :] - owner_ra + PATCHES // 2) % PATCHES - PATCHES // 2
    random_heavy = jax.random.randint(key_heavy, (PATCHES, GROUPS), -REACH, REACH + 1)
    heavy = jnp.where(jnp.abs(distance) <= REACH, distance, random_heavy)
    candidate = jax.random.randint(key_other, (PATCHES, GROUPS, TILES_DEV), 0, 2 * REACH) - REACH
    other = jnp.where(candidate >= heavy[:, :, None], candidate + 1, candidate)
    scores = jax.random.randint(key_order, (PATCHES, GROUPS, TILES_DEV), 0, 1 << 20) * TILES_DEV + jnp.arange(TILES_DEV, dtype=jnp.int32)
    order_rank = jnp.argsort(jnp.argsort(scores, axis=-1), axis=-1)
    offsets = jnp.where(order_rank < CAP, heavy[:, :, None], other)
    return ((owner_ra[:, :, None] + offsets) % PATCHES).reshape(-1).astype(jnp.int32)


def touch_ends(entries, stream_key, least, high):
    dims = entries.shape
    spot = [jax.random.randint(jax.random.fold_in(stream_key, axis), (), 0, dims[axis]) for axis in range(len(dims))]
    entries = entries.at[tuple(spot)].set(least)
    longest = dims.index(max(dims))
    spot[longest] = (spot[longest] + 1) % dims[longest]
    return entries.at[tuple(spot)].set(high)


def levels(key, shape, cuts, least, top_value):
    level, own = 1.0, jax.random.fold_in(key, 6)
    for dim, blocks in cuts:
        steps = jnp.exp(jax.random.uniform(jax.random.fold_in(own, dim), (blocks,), jnp.float32, least / len(cuts), top_value / len(cuts)))
        level = level * jnp.repeat(steps, shape[dim] // blocks).reshape([-1 if axis == dim else 1 for axis in range(len(shape))])
    return level


def scatter_about(rng, dims, width, bound, pieces=(), held_as=jnp.bfloat16):
    factor_of = levels(rng, dims, pieces, -0.22, 0.18) if pieces else 1.0
    entries = jax.random.normal(rng, dims, jnp.float32) * width * factor_of
    return jnp.minimum(jnp.maximum(entries, -bound), bound).astype(held_as)


def setup_inputs(seed: int = 0) -> dict:
    splits = jax.random.split(jax.random.key(seed), 11)
    return {
        "tiles": scatter_about(splits[0], (TILES, ROWS, TW), 1.0, 6.0, ((0, 32),)),
        "tile_patch": draw_tile_patch(jax.random.fold_in(splits[10], 71), 0),
        "tile_offset": touch_ends(jax.random.randint(splits[2], (TILES,), 0, PW - TW + 1), jax.random.fold_in(splits[2], 1), 0, PW - TW).astype(jnp.int32),
        "tile_weight": jnp.clip(jnp.exp(math.log(4.0) - 2.7725887 * jax.random.uniform(splits[3], (TILES,), jnp.float32) ** levels(splits[3], (TILES,), ((0, 32),), -0.2, 0.2)), 0.25, 4.0).astype(jnp.bfloat16),
        "visit_band": touch_ends(jax.random.randint(splits[4], (VISITS,), 0, BANDS), jax.random.fold_in(splits[4], 1), 0, BANDS - 1).astype(jnp.int32),
        "coeff_index": touch_ends(jax.random.randint(splits[5], (TILES,), 0, NTAB), jax.random.fold_in(splits[5], 1), 0, NTAB - 1).astype(jnp.int32),
        "coeff_table": scatter_about(splits[6], (NTAB, BASIS), 0.22, 1.3, (), jnp.float32),
        "row_kernels": scatter_about(splits[7], (BASIS, TAPS), TAPS ** -0.5, 1.25),
        "column_kernels": scatter_about(splits[8], (BASIS, TAPS), TAPS ** -0.5, 1.25),
        "band_weight": jnp.clip(jnp.exp(jax.random.uniform(splits[9], (BANDS,), jnp.float32, math.log(0.3), math.log(1.5))), 0.3, 1.5),
    }


HIGHEST_PRECISION = lax.Precision.HIGHEST


def band_matrices(kernels, extent):
    tap_count = kernels.shape[1]
    tap_of = jnp.arange(extent)[None, :] - jnp.arange(extent)[:, None] + tap_count // 2
    tap_hits = (tap_of[None, :, :] == jnp.arange(tap_count)[:, None, None]).astype(jnp.float32)
    return jnp.einsum("kl,lab->kab", kernels.astype(jnp.float32), tap_hits, precision=HIGHEST_PRECISION)


def reference(tiles, tile_patch, tile_offset, tile_weight, visit_band, coeff_index, coeff_table, row_kernels, column_kernels, band_weight):
    rowmats = band_matrices(row_kernels, ROWS)
    colmats = band_matrices(column_kernels, TW)
    tile_band = jnp.repeat(visit_band, TILES_VISIT).astype(jnp.int32)
    coeffs = jnp.take(coeff_table, coeff_index, axis=0)
    group_size = 16
    groups_total = TILES // group_size
    blocks = (tiles.reshape(groups_total, group_size, ROWS, TW),
              coeffs.reshape(groups_total, group_size, BASIS),
              tile_patch.astype(jnp.int32).reshape(groups_total, group_size),
              tile_offset.astype(jnp.int32).reshape(groups_total, group_size),
              tile_weight.reshape(groups_total, group_size),
              tile_band.reshape(groups_total, group_size))
    zero_index = jnp.zeros((), jnp.int32)

    def one_block(carry, block_in):
        tiles_in, coeff_in, patch_in, offset_in, weight_in, band_in = block_in
        column_pass = jnp.einsum("jic,kdc->jkid", tiles_in.astype(jnp.float32), colmats, precision=HIGHEST_PRECISION).astype(jnp.bfloat16)
        scaled = (coeff_in[:, :, None, None] * rowmats[None]).astype(jnp.bfloat16)
        matched = jnp.einsum("jkab,jkbd->jad", scaled.astype(jnp.float32), column_pass.astype(jnp.float32), precision=HIGHEST_PRECISION).astype(jnp.bfloat16)

        def add_one(position, state):
            numerator, weight_sum = state
            patch_at = patch_in[position]
            band_at = band_in[position]
            offset_at = offset_in[position]
            weight_at = weight_in[position].astype(jnp.float32)
            current = lax.dynamic_slice(numerator, (patch_at, band_at, zero_index, offset_at), (1, 1, ROWS, TW))
            numerator = lax.dynamic_update_slice(numerator, current + weight_at * matched[position].astype(jnp.float32)[None, None], (patch_at, band_at, zero_index, offset_at))
            current_weight = lax.dynamic_slice(weight_sum, (patch_at, band_at, offset_at), (1, 1, TW))
            weight_sum = lax.dynamic_update_slice(weight_sum, current_weight + weight_at, (patch_at, band_at, offset_at))
            return numerator, weight_sum

        return lax.fori_loop(0, group_size, add_one, carry), None

    start_state = (jnp.zeros((PATCHES, BANDS, ROWS, PW), jnp.float32), jnp.zeros((PATCHES, BANDS, PW), jnp.float32))
    (numerator, weight_sum), unused = lax.scan(one_block, start_state, blocks)
    coadds = numerator / jnp.maximum(weight_sum, 1.0)[:, :, None, :]
    band_coadds = jnp.transpose(coadds, (1, 2, 0, 3)).reshape(BANDS, ROWS, PATCHES * PW)
    detection = jnp.einsum("b,brq->rq", band_weight, band_coadds, precision=HIGHEST_PRECISION)
    return band_coadds, detection
```

```python
import functools

import jax
import jax.numpy as jnp
from jax import lax
from jax.experimental import pallas as pl
from jax.experimental.pallas import tpu as pltpu
from jax.sharding import PartitionSpec as P

PW = 256
BANDS = 6
REACH = 2
SPREAD = 2 * REACH + 1
EXTRA = 16


def slot_rows(row_share):
    return max(row_share, 16)


def match_kernel(
    patches,
    groups,
    patch_ref,
    offset_ref,
    index_ref,
    band_ref,
    table_ref,
    weight_ref,
    rowk_ref,
    colk_ref,
    tiles_ref,
    *rest,
):
    messages = rest[: SPREAD * groups]
    rowmat, colmat, scaled, sums, extra = rest[SPREAD * groups :]
    visit = pl.program_id(0)
    visits = pl.num_programs(0)
    per_visit, rows, width = tiles_ref.shape
    basis, taps = rowk_ref.shape
    half = taps // 2
    row_share = rows // groups
    slot = slot_rows(row_share)
    owner = lax.axis_index("ra")
    group = lax.axis_index("band")

    @pl.when(visit == 0)
    def build():
        tap = lax.broadcasted_iota(jnp.int32, (taps, width), 0)
        lane = lax.broadcasted_iota(jnp.int32, (taps, width), 1)
        back = half // 8 * 8
        shifted = lax.rem(lane + half - back, width)
        forward = (shifted == tap).astype(jnp.bfloat16)
        backward = (shifted == taps - 1 - tap).astype(jnp.bfloat16)
        row_taps = jnp.dot(rowk_ref[...], forward, preferred_element_type=jnp.float32)
        col_taps = jnp.dot(colk_ref[...], backward, preferred_element_type=jnp.float32)
        apart = lax.broadcasted_iota(jnp.int32, (width, width), 0) - lax.broadcasted_iota(
            jnp.int32, (width, width), 1
        )
        near = jnp.abs(apart) <= half
        for k in range(basis):
            spread = jnp.broadcast_to(row_taps[k : k + 1], (rows, width))
            turned = pltpu.roll(spread, width - back, 1, stride=1, stride_axis=0)
            rowmat[k * rows : (k + 1) * rows, :] = turned[:, :rows].astype(jnp.bfloat16)
            spread = jnp.broadcast_to(col_taps[k : k + 1], (width, width))
            turned = pltpu.roll(spread, width - back, 1, stride=1, stride_axis=0)
            colmat[k * width : (k + 1) * width, :] = jnp.where(near, turned, 0.0).astype(
                jnp.bfloat16
            )
        extra[...] = jnp.zeros_like(extra)

    sums[...] = jnp.zeros_like(sums)
    first = visit * per_visit
    for pair in range(per_visit // 2):
        both = jnp.concatenate([tiles_ref[2 * pair], tiles_ref[2 * pair + 1]], axis=1)
        passed = jnp.dot(rowmat[...], both, preferred_element_type=jnp.float32)
        for side in range(2):
            place = 2 * pair + side
            table_row = index_ref[first + place]
            for k in range(basis):
                block = passed[k * rows : (k + 1) * rows, side * width : (side + 1) * width]
                scaled[place * rows : (place + 1) * rows, k * width : (k + 1) * width] = (
                    block * table_ref[table_row, k]
                ).astype(jnp.bfloat16)
    matched = jnp.dot(scaled[...], colmat[...], preferred_element_type=jnp.float32)

    lane = lax.broadcasted_iota(jnp.int32, (rows, width), 1)
    column = lax.broadcasted_iota(jnp.int32, (1, PW), 1)
    tile_lane = lax.broadcasted_iota(jnp.int32, weight_ref.shape, 1)
    weights = weight_ref[...].astype(jnp.float32)
    for place in range(per_visit):
        tile = first + place
        offset = offset_ref[tile]
        bucket = lax.rem(patch_ref[tile] - owner + REACH + patches, patches)
        weight = jnp.sum(jnp.where(tile_lane == tile, weights, 0.0), axis=1, keepdims=True)
        turned = pltpu.roll(
            matched[place * rows : (place + 1) * rows] * weight, lax.rem(offset, width), 1
        )
        sums[bucket, :, :width] += jnp.where(lane >= offset, turned, 0.0)
        sums[bucket, :, width:] += jnp.where(lane < offset, turned, 0.0)
        covered = (column >= offset) & (column < offset + width)
        extra[bucket, pl.ds(visit, 1), :] += jnp.where(covered, weight, 0.0)

    for bucket in range(SPREAD):
        extra[bucket, pl.ds(2 * visits + visit, 1), :] = jnp.full(
            (1, PW), band_ref[visit], jnp.int32
        ).astype(jnp.float32)
        for turn in range(groups):
            part = lax.rem(group + turn, groups)
            own = sums[bucket, pl.ds(pl.multiple_of(part * row_share, row_share), row_share), :]
            if slot > row_share:
                own = jnp.concatenate(
                    [own, jnp.zeros((slot - row_share, PW), jnp.float32)], axis=0
                )
            messages[bucket * groups + turn][
                pl.ds(pl.multiple_of(visit * slot, slot), slot), :
            ] = own.astype(jnp.bfloat16)

    @pl.when(visit == visits - 1)
    def finish():
        row = lax.broadcasted_iota(jnp.int32, (EXTRA, PW), 0)
        count = extra.shape[1] // 4
        for bucket in range(SPREAD):
            held = extra[bucket]
            high = held.astype(jnp.bfloat16).astype(jnp.float32)
            low = jnp.concatenate([held[-count:], (held - high)[:-count]], axis=0)
            mixed = jnp.where((row >= count) & (row < 2 * count), low, high).astype(jnp.bfloat16)
            for turn in range(groups):
                messages[bucket * groups + turn][slot * count :, :] = mixed


def combine_kernel(count, weight_ref, *refs):
    messages = refs[:-2]
    coadd_ref, detection_ref = refs[-2:]
    row_share = coadd_ref.shape[1]
    slot = slot_rows(row_share)
    totals = [jnp.zeros((row_share, PW), jnp.float32) for _ in range(BANDS)]
    weight_totals = [jnp.zeros((1, PW), jnp.float32) for _ in range(BANDS)]
    for message in messages:
        extra = message[slot * count :, :].astype(jnp.float32)
        for visit in range(count):
            band = extra[2 * count + visit : 2 * count + visit + 1]
            weight = extra[visit : visit + 1] + extra[count + visit : count + visit + 1]
            part = message[slot * visit : slot * (visit + 1), :].astype(jnp.float32)[:row_share]
            for b in range(BANDS):
                here = band == float(b)
                totals[b] += jnp.where(here, part, 0.0)
                weight_totals[b] += jnp.where(here, weight, 0.0)
    detection = jnp.zeros((row_share, PW), jnp.float32)
    for b in range(BANDS):
        coadd = totals[b] / jnp.maximum(weight_totals[b], 1.0)
        coadd_ref[b] = coadd
        detection += weight_ref[b] * coadd
    detection_ref[...] = detection


def local(
    tiles,
    tile_patch,
    tile_offset,
    tile_weight,
    visit_band,
    coeff_index,
    coeff_table,
    row_kernels,
    column_kernels,
    band_weight,
):
    tile_count, rows, width = tiles.shape
    visits = visit_band.shape[0]
    per_visit = tile_count // visits
    basis, taps = row_kernels.shape
    patches = lax.axis_size("ra")
    groups = lax.axis_size("band")
    row_share = rows // groups
    slot = slot_rows(row_share)
    length = visits * slot + EXTRA
    smem = pl.BlockSpec(memory_space=pltpu.SMEM)

    def whole(shape):
        return pl.BlockSpec(shape, lambda v: (0,) * len(shape))

    messages = pl.pallas_call(
        functools.partial(match_kernel, patches, groups),
        grid=(visits,),
        in_specs=[smem] * 5
        + [
            whole((1, tile_count)),
            whole((basis, taps)),
            whole((basis, taps)),
            pl.BlockSpec((per_visit, rows, width), lambda v: (v, 0, 0)),
        ],
        out_specs=[whole((length, PW))] * (SPREAD * groups),
        out_shape=[jax.ShapeDtypeStruct((length, PW), jnp.bfloat16)] * (SPREAD * groups),
        scratch_shapes=[
            pltpu.VMEM((basis * rows, rows), jnp.bfloat16),
            pltpu.VMEM((basis * width, width), jnp.bfloat16),
            pltpu.VMEM((per_visit * rows, basis * width), jnp.bfloat16),
            pltpu.VMEM((SPREAD, rows, PW), jnp.float32),
            pltpu.VMEM((SPREAD, EXTRA, PW), jnp.float32),
        ],
        compiler_params=pltpu.CompilerParams(vmem_limit_bytes=40 * 1024 * 1024),
        name="match_and_sum",
    )(
        tile_patch,
        tile_offset,
        coeff_index,
        visit_band,
        coeff_table,
        tile_weight.reshape(1, tile_count),
        row_kernels,
        column_kernels,
        tiles,
    )

    arrived = []
    for bucket in range(SPREAD):
        for turn in range(groups):
            message = messages[bucket * groups + turn]
            distance = bucket - REACH
            if distance != 0 or turn != 0:
                route = [
                    (o * groups + g, (o + distance) % patches * groups + (g + turn) % groups)
                    for o in range(patches)
                    for g in range(groups)
                ]
                message = lax.ppermute(message, ("ra", "band"), route)
            arrived.append(message)

    vmem = pl.BlockSpec(memory_space=pltpu.VMEM)
    return pl.pallas_call(
        functools.partial(combine_kernel, visits),
        in_specs=[smem] + [vmem] * len(arrived),
        out_specs=(vmem, vmem),
        out_shape=(
            jax.ShapeDtypeStruct((BANDS, row_share, PW), jnp.float32),
            jax.ShapeDtypeStruct((row_share, PW), jnp.float32),
        ),
        compiler_params=pltpu.CompilerParams(vmem_limit_bytes=40 * 1024 * 1024),
        name="combine",
    )(band_weight, *arrived)


def solution(mesh):
    return jax.shard_map(
        local,
        mesh=mesh,
        in_specs=(
            P(("ra", "band"), None, None),
            P(("ra", "band")),
            P(("ra", "band")),
            P(("ra", "band")),
            P(("ra", "band")),
            P(("ra", "band")),
            P(),
            P(),
            P(),
            P(),
        ),
        out_specs=(P(None, "band", "ra"), P("band", "ra")),
        check_vma=False,
    )
```

```python
import functools

import jax
import jax.numpy as jnp
from jax import lax
from jax.experimental import pallas as pl
from jax.experimental.pallas import tpu as pltpu
from jax.sharding import PartitionSpec as P

PW = 256
BANDS = 6
REACH = 2
SPREAD = 2 * REACH + 1
EXTRA = 16


def slot_rows(row_share):
    return max(row_share, 16)


def match_kernel(
    patches,
    groups,
    patch_ref,
    offset_ref,
    index_ref,
    band_ref,
    table_ref,
    weight_ref,
    rowk_ref,
    colk_ref,
    tiles_hbm,
    *rest,
):
    messages = rest[: SPREAD * groups]
    tiles_ref, kernels, weights, toeplitz, sums, extra, arrival = rest[SPREAD * groups :]
    visits = band_ref.shape[0]
    tile_count, rows, width = tiles_ref.shape
    per_visit = tile_count // visits
    basis, taps = rowk_ref.shape
    half = taps // 2
    back = half // 8 * 8
    lead = half - back
    deep = kernels.shape[1]
    row_share = rows // groups
    slot = slot_rows(row_share)
    owner = lax.axis_index("ra")
    group = lax.axis_index("band")

    def fetch(visit):
        held = pl.ds(visit * per_visit, per_visit)
        return pltpu.make_async_copy(tiles_hbm.at[held], tiles_ref.at[held], arrival.at[visit])

    for visit in range(visits):
        fetch(visit).start()

    def iota(shape, axis):
        return lax.broadcasted_iota(jnp.int32, shape, axis)

    def across(left, right, **options):
        return lax.dot_general(
            left,
            right,
            (((1,), (1,)), ((), ())),
            preferred_element_type=jnp.float32,
            **options,
        )

    eye = (iota((tile_count, tile_count), 0) == iota((tile_count, tile_count), 1)).astype(
        jnp.bfloat16
    )
    weights[...] = across(eye, jnp.broadcast_to(weight_ref[...], (width, tile_count)))
    entry = iota((1, table_ref.shape[1]), 1)
    chosen = jnp.concatenate(
        [(entry == index_ref[j]).astype(jnp.float32) for j in range(tile_count)], axis=0
    )
    coeffs = across(chosen, table_ref[...], precision=lax.Precision.HIGHEST)
    tap_rows = (iota((deep, taps), 0) == iota((deep, taps), 1)).astype(jnp.bfloat16)
    col_taps = across(tap_rows, colk_ref[...])
    tap = iota((taps, 2 * width), 0)
    lane = iota((taps, 2 * width), 1)
    spot = jnp.where(
        lane < width, lax.rem(lane + lead, width), lane - width - rows + lead
    )
    row_taps = jnp.dot(
        rowk_ref[...], (spot == tap).astype(jnp.bfloat16), preferred_element_type=jnp.float32
    ).astype(jnp.bfloat16)
    for pair in range(tile_count // 2):
        parts = []
        for side in range(2):
            mix = col_taps * coeffs[2 * pair + side : 2 * pair + side + 1]
            high = mix.astype(jnp.bfloat16)
            low = (mix - high.astype(jnp.float32)).astype(jnp.bfloat16)
            place = row_taps[:, side * width : (side + 1) * width]
            parts.append(
                jnp.dot(high, place, preferred_element_type=jnp.float32)
                + jnp.dot(low, place, preferred_element_type=jnp.float32)
            )
        kernels[pair] = parts[0] + parts[1]
    extra[...] = jnp.zeros_like(extra)

    lane = iota((rows, width), 1)
    near = jnp.abs(lax.rem(lane, rows) - iota((rows, width), 0)) <= half
    edge = 2 * half // 8 * 8
    column = iota((1, width), 1)
    empty = jnp.zeros((rows, width), jnp.bfloat16)

    def one_visit(visit, unused):
        fetch(visit).wait()
        sums[...] = jnp.zeros_like(sums)
        first = visit * per_visit
        for pair in range(per_visit // 2):
            for m in range(taps):
                spread = jnp.broadcast_to(
                    kernels[visit * (per_visit // 2) + pair, pl.ds(m, 1), :], (rows, width)
                )
                turned = pltpu.roll(spread, width - back, 1, stride=1, stride_axis=0)
                turned = jnp.concatenate(
                    [
                        jnp.where(near[:edge], turned[:edge], 0.0),
                        turned[edge : rows - edge],
                        jnp.where(near[rows - edge :], turned[rows - edge :], 0.0),
                    ],
                    axis=0,
                )
                toeplitz[pair, m * rows : (m + 1) * rows, :] = turned.astype(jnp.bfloat16)
            both = jnp.concatenate(
                [
                    jnp.concatenate([tiles_ref[first + 2 * pair], empty], axis=1),
                    jnp.concatenate([empty, tiles_ref[first + 2 * pair + 1]], axis=1),
                ],
                axis=0,
            )
            passed = jnp.dot(toeplitz[pair], both, preferred_element_type=jnp.float32)
            for side in range(2):
                matched = jnp.zeros((rows, width), jnp.float32)
                for m in range(taps):
                    block = passed[m * rows : (m + 1) * rows, side * width : (side + 1) * width]
                    if m != half:
                        turned = pltpu.roll(block, (half - m) % width, 1)
                        inside = (lane + (m - half) >= 0) & (lane + (m - half) < width)
                        block = jnp.where(inside, turned, 0.0)
                    matched += block
                tile = first + 2 * pair + side
                offset = offset_ref[tile]
                bucket = lax.rem(patch_ref[tile] - owner + REACH + patches, patches)
                weight = weights[pl.ds(tile, 1), :]
                turned = pltpu.roll(matched * weight, lax.rem(offset, width), 1)
                sums[bucket, :, :width] += jnp.where(lane >= offset, turned, 0.0)
                sums[bucket, :, width:] += jnp.where(lane < offset, turned, 0.0)
                extra[bucket, pl.ds(visit, 1), :] += jnp.concatenate(
                    [
                        jnp.where(column >= offset, weight, 0.0),
                        jnp.where(column < offset, weight, 0.0),
                    ],
                    axis=1,
                )

        for bucket in range(SPREAD):
            extra[bucket, pl.ds(2 * visits + visit, 1), :] = jnp.full(
                (1, PW), band_ref[visit], jnp.int32
            ).astype(jnp.float32)
            for turn in range(groups):
                part = lax.rem(group + turn, groups)
                own = sums[bucket, pl.ds(pl.multiple_of(part * row_share, row_share), row_share), :]
                if slot > row_share:
                    own = jnp.concatenate(
                        [own, jnp.zeros((slot - row_share, PW), jnp.float32)], axis=0
                    )
                messages[bucket * groups + turn][
                    pl.ds(pl.multiple_of(visit * slot, slot), slot), :
                ] = own.astype(jnp.bfloat16)
        return unused

    lax.fori_loop(0, visits, one_visit, 0)

    row = iota((EXTRA, PW), 0)
    for bucket in range(SPREAD):
        held = extra[bucket]
        high = held.astype(jnp.bfloat16).astype(jnp.float32)
        low = jnp.concatenate([held[-visits:], (held - high)[:-visits]], axis=0)
        mixed = jnp.where((row >= visits) & (row < 2 * visits), low, high).astype(jnp.bfloat16)
        for turn in range(groups):
            messages[bucket * groups + turn][slot * visits :, :] = mixed


def combine_kernel(count, weight_ref, *refs):
    messages = refs[:-2]
    coadd_ref, detection_ref = refs[-2:]
    row_share = coadd_ref.shape[1]
    slot = slot_rows(row_share)
    totals = [jnp.zeros((row_share, PW), jnp.float32) for _ in range(BANDS)]
    weight_totals = [jnp.zeros((1, PW), jnp.float32) for _ in range(BANDS)]
    for message in messages:
        extra = message[slot * count :, :].astype(jnp.float32)
        for visit in range(count):
            band = extra[2 * count + visit : 2 * count + visit + 1]
            weight = extra[visit : visit + 1] + extra[count + visit : count + visit + 1]
            part = message[slot * visit : slot * (visit + 1), :].astype(jnp.float32)[:row_share]
            for b in range(BANDS):
                here = band == float(b)
                totals[b] += jnp.where(here, part, 0.0)
                weight_totals[b] += jnp.where(here, weight, 0.0)
    detection = jnp.zeros((row_share, PW), jnp.float32)
    for b in range(BANDS):
        coadd = totals[b] / jnp.maximum(weight_totals[b], 1.0)
        coadd_ref[b] = coadd
        detection += weight_ref[b] * coadd
    detection_ref[...] = detection


def local(
    tiles,
    tile_patch,
    tile_offset,
    tile_weight,
    visit_band,
    coeff_index,
    coeff_table,
    row_kernels,
    column_kernels,
    band_weight,
):
    tile_count, rows, width = tiles.shape
    visits = visit_band.shape[0]
    per_visit = tile_count // visits
    basis, taps = row_kernels.shape
    patches = lax.axis_size("ra")
    groups = lax.axis_size("band")
    row_share = rows // groups
    slot = slot_rows(row_share)
    length = visits * slot + EXTRA
    smem = pl.BlockSpec(memory_space=pltpu.SMEM)

    vmem = pl.BlockSpec(memory_space=pltpu.VMEM)
    deep = (taps + 7) // 8 * 8
    messages = pl.pallas_call(
        functools.partial(match_kernel, patches, groups),
        in_specs=[smem] * 4 + [vmem] * 4 + [pl.BlockSpec(memory_space=pltpu.HBM)],
        out_specs=[vmem] * (SPREAD * groups),
        out_shape=[jax.ShapeDtypeStruct((length, PW), jnp.bfloat16)] * (SPREAD * groups),
        scratch_shapes=[
            pltpu.VMEM((tile_count, rows, width), jnp.bfloat16),
            pltpu.VMEM((tile_count // 2, deep, width), jnp.float32),
            pltpu.VMEM((tile_count, width), jnp.float32),
            pltpu.VMEM((per_visit // 2, taps * rows, width), jnp.bfloat16),
            pltpu.VMEM((SPREAD, rows, PW), jnp.float32),
            pltpu.VMEM((SPREAD, EXTRA, PW), jnp.float32),
            pltpu.SemaphoreType.DMA((visits,)),
        ],
        compiler_params=pltpu.CompilerParams(vmem_limit_bytes=40 * 1024 * 1024),
        name="match_and_sum",
    )(
        tile_patch,
        tile_offset,
        coeff_index,
        visit_band,
        coeff_table.T,
        tile_weight.reshape(1, tile_count),
        row_kernels,
        column_kernels,
        tiles,
    )

    arrived = []
    for bucket in range(SPREAD):
        for turn in range(groups):
            message = messages[bucket * groups + turn]
            distance = bucket - REACH
            if distance != 0 or turn != 0:
                route = [
                    (o * groups + g, (o + distance) % patches * groups + (g + turn) % groups)
                    for o in range(patches)
                    for g in range(groups)
                ]
                message = lax.ppermute(message, ("ra", "band"), route)
            arrived.append(message)

    return pl.pallas_call(
        functools.partial(combine_kernel, visits),
        in_specs=[smem] + [vmem] * len(arrived),
        out_specs=(vmem, vmem),
        out_shape=(
            jax.ShapeDtypeStruct((BANDS, row_share, PW), jnp.float32),
            jax.ShapeDtypeStruct((row_share, PW), jnp.float32),
        ),
        compiler_params=pltpu.CompilerParams(vmem_limit_bytes=40 * 1024 * 1024),
        name="combine",
    )(band_weight, *arrived)


def solution(mesh):
    return jax.shard_map(
        local,
        mesh=mesh,
        in_specs=(
            P(("ra", "band"), None, None),
            P(("ra", "band")),
            P(("ra", "band")),
            P(("ra", "band")),
            P(("ra", "band")),
            P(("ra", "band")),
            P(),
            P(),
            P(),
            P(),
        ),
        out_specs=(P(None, "band", "ra"), P("band", "ra")),
        check_vma=False,
    )
```

```python
import functools

import jax
import jax.numpy as jnp
from jax import lax
from jax.experimental import pallas as pl
from jax.experimental.pallas import tpu as pltpu
from jax.sharding import PartitionSpec as P

PW = 256
BANDS = 6
REACH = 2
SPREAD = 2 * REACH + 1
EXTRA = 16
BLOCK = 32
COARSE = 3
VECTORS = 16
FINE_ROWS = 64
LEAD = 6


def slot_rows(row_share):
    return max(row_share, 16)


def match_kernel(
    patches,
    groups,
    patch_ref,
    offset_ref,
    index_ref,
    band_ref,
    table_hbm,
    weight_hbm,
    rowk_hbm,
    colk_hbm,
    tiles_hbm,
    *rest,
):
    messages = rest[: SPREAD * groups]
    (
        table_ref,
        weight_ref,
        rowk_ref,
        colk_ref,
        tiles_ref,
        kernels,
        weights,
        shifted,
        toeplitz,
        sums,
        extra,
        arrival,
        ready,
    ) = rest[SPREAD * groups :]
    visits = band_ref.shape[0]
    tile_count, rows, width = tiles_ref.shape
    per_visit = tile_count // visits
    basis, taps = rowk_ref.shape
    half = taps // 2
    row_share = rows // groups
    slot = slot_rows(row_share)
    owner = lax.axis_index("ra")
    group = lax.axis_index("band")

    small = [
        pltpu.make_async_copy(source, target, ready.at[place])
        for place, (source, target) in enumerate(
            (
                (table_hbm, table_ref),
                (weight_hbm, weight_ref),
                (rowk_hbm, rowk_ref),
                (colk_hbm, colk_ref),
            )
        )
    ]
    for copy in small:
        copy.start()

    def fetch(visit):
        held = pl.ds(visit * per_visit, per_visit)
        return pltpu.make_async_copy(tiles_hbm.at[held], tiles_ref.at[held], arrival.at[visit])

    for visit in range(visits):
        fetch(visit).start()

    def iota(shape, axis):
        return lax.broadcasted_iota(jnp.int32, shape, axis)

    def across(left, right, **options):
        return lax.dot_general(
            left,
            right,
            (((1,), (1,)), ((), ())),
            preferred_element_type=jnp.float32,
            **options,
        )

    extra[...] = jnp.zeros_like(extra)
    shifted[...] = jnp.zeros_like(shifted)
    eye = (iota((tile_count, tile_count), 0) == iota((tile_count, tile_count), 1)).astype(
        jnp.bfloat16
    )
    entry = iota((1, table_ref.shape[1]), 1)
    chosen = jnp.concatenate(
        [(entry == index_ref[j]).astype(jnp.float32) for j in range(tile_count)], axis=0
    )
    for copy in small:
        copy.wait()
    weights[...] = across(eye, jnp.broadcast_to(weight_ref[...], (width, tile_count)))
    coeffs = across(chosen, table_ref[...], precision=lax.Precision.HIGHEST)

    line = iota((2 * VECTORS, taps), 0)
    column = iota((2 * VECTORS, taps), 1)
    block = lax.rem(line, VECTORS) // 2
    step = 4 * lax.rem(block, COARSE) + 2 * lax.rem(line, 2) + line // VECTORS
    wanted = jnp.where(block < COARSE, half + step, half - 1 - step)
    wanted = jnp.where(lax.rem(line, VECTORS) < 4 * COARSE, wanted, -1)
    col_taps = across((wanted == column).astype(jnp.bfloat16), colk_ref[...])
    tap = iota((taps, width), 0)
    lane = iota((taps, width), 1)
    total = None
    for side in range(2):
        place = (lane == tap + LEAD + side * FINE_ROWS).astype(jnp.bfloat16)
        row_taps = jnp.dot(
            rowk_ref[...], place, preferred_element_type=jnp.float32
        ).astype(jnp.bfloat16)
        part = col_taps[side * VECTORS : (side + 1) * VECTORS]
        mix = jnp.concatenate([part * coeffs[j : j + 1] for j in range(tile_count)], axis=0)
        high = mix.astype(jnp.bfloat16)
        low = (mix - high.astype(jnp.float32)).astype(jnp.bfloat16)
        term = jnp.dot(high, row_taps, preferred_element_type=jnp.float32) + jnp.dot(
            low, row_taps, preferred_element_type=jnp.float32
        )
        total = term if total is None else total + term
    kernels[...] = total

    lane = iota((rows, width), 1)
    column = iota((1, width), 1)

    def moved(value, distance):
        if distance == 0:
            return value
        turned = pltpu.roll(value, -distance % width, 1)
        here = lane[: value.shape[0]] + distance
        return jnp.where((here >= 0) & (here < width), turned, jnp.zeros_like(turned))

    def one_visit(visit, unused):
        fetch(visit).wait()
        sums[...] = jnp.zeros_like(sums)
        first = visit * per_visit
        for place in range(per_visit):
            tile = first + place
            pixels = tiles_ref[tile].astype(jnp.float32)
            for side in range(2):
                for fine in range(4):
                    part = moved(pixels, -1 - fine if side else fine).astype(jnp.bfloat16)
                    top = fine * FINE_ROWS
                    shifted[place, side, top + 16 : top + 64, :width] = part[:48]
                    shifted[place, side, top : top + 48, width:] = part[16:]
                for coarse in range(COARSE):
                    for pair in range(2):
                        vector = pl.ds(
                            tile * VECTORS + (side * COARSE + coarse) * 2 + pair, 1
                        )
                        spread = jnp.broadcast_to(kernels[vector, :], (BLOCK, width))
                        turned = pltpu.roll(spread, 0, 1, stride=1, stride_axis=0)
                        toeplitz[
                            place,
                            side,
                            coarse * BLOCK : (coarse + 1) * BLOCK,
                            pair * width : (pair + 1) * width,
                        ] = turned.astype(jnp.bfloat16)
            matched = [jnp.zeros((BLOCK, width), jnp.float32) for _ in range(2)]
            for side in range(2):
                passed = jnp.dot(
                    toeplitz[place, side],
                    shifted[place, side],
                    preferred_element_type=jnp.float32,
                )
                for part in range(2):
                    for coarse in range(COARSE):
                        matched[part] += moved(
                            passed[
                                coarse * BLOCK : (coarse + 1) * BLOCK,
                                part * width : (part + 1) * width,
                            ],
                            -4 * coarse if side else 4 * coarse,
                        )
            offset = offset_ref[tile]
            bucket = lax.rem(patch_ref[tile] - owner + REACH + patches, patches)
            weight = weights[pl.ds(tile, 1), :]
            turned = pltpu.roll(
                jnp.concatenate(matched, axis=0) * weight, lax.rem(offset, width), 1
            )
            sums[bucket, :, :width] += jnp.where(lane >= offset, turned, 0.0)
            sums[bucket, :, width:] += jnp.where(lane < offset, turned, 0.0)
            extra[bucket, pl.ds(visit, 1), :] += jnp.concatenate(
                [
                    jnp.where(column >= offset, weight, 0.0),
                    jnp.where(column < offset, weight, 0.0),
                ],
                axis=1,
            )

        for bucket in range(SPREAD):
            extra[bucket, pl.ds(2 * visits + visit, 1), :] = jnp.full(
                (1, PW), band_ref[visit], jnp.int32
            ).astype(jnp.float32)
            for turn in range(groups):
                part = lax.rem(group + turn, groups)
                own = sums[bucket, pl.ds(pl.multiple_of(part * row_share, row_share), row_share), :]
                if slot > row_share:
                    own = jnp.concatenate(
                        [own, jnp.zeros((slot - row_share, PW), jnp.float32)], axis=0
                    )
                messages[bucket * groups + turn][
                    pl.ds(pl.multiple_of(visit * slot, slot), slot), :
                ] = own.astype(jnp.bfloat16)
        return unused

    lax.fori_loop(0, visits, one_visit, 0)

    row = iota((EXTRA, PW), 0)
    for bucket in range(SPREAD):
        held = extra[bucket]
        high = held.astype(jnp.bfloat16).astype(jnp.float32)
        low = jnp.concatenate([held[-visits:], (held - high)[:-visits]], axis=0)
        mixed = jnp.where((row >= visits) & (row < 2 * visits), low, high).astype(jnp.bfloat16)
        for turn in range(groups):
            messages[bucket * groups + turn][slot * visits :, :] = mixed


def combine_kernel(count, weight_ref, *refs):
    messages = refs[:-2]
    coadd_ref, detection_ref = refs[-2:]
    row_share = coadd_ref.shape[1]
    slot = slot_rows(row_share)
    totals = [jnp.zeros((row_share, PW), jnp.float32) for _ in range(BANDS)]
    weight_totals = [jnp.zeros((1, PW), jnp.float32) for _ in range(BANDS)]
    for message in messages:
        extra = message[slot * count :, :].astype(jnp.float32)
        for visit in range(count):
            band = extra[2 * count + visit : 2 * count + visit + 1]
            weight = extra[visit : visit + 1] + extra[count + visit : count + visit + 1]
            part = message[slot * visit : slot * (visit + 1), :].astype(jnp.float32)[:row_share]
            for b in range(BANDS):
                here = band == float(b)
                totals[b] += jnp.where(here, part, 0.0)
                weight_totals[b] += jnp.where(here, weight, 0.0)
    detection = jnp.zeros((row_share, PW), jnp.float32)
    for b in range(BANDS):
        coadd = totals[b] / jnp.maximum(weight_totals[b], 1.0)
        coadd_ref[b] = coadd
        detection += weight_ref[b] * coadd
    detection_ref[...] = detection


def local(
    tiles,
    tile_patch,
    tile_offset,
    tile_weight,
    visit_band,
    coeff_index,
    coeff_table,
    row_kernels,
    column_kernels,
    band_weight,
):
    tile_count, rows, width = tiles.shape
    visits = visit_band.shape[0]
    per_visit = tile_count // visits
    basis, taps = row_kernels.shape
    patches = lax.axis_size("ra")
    groups = lax.axis_size("band")
    row_share = rows // groups
    slot = slot_rows(row_share)
    length = visits * slot + EXTRA
    smem = pl.BlockSpec(memory_space=pltpu.SMEM)

    vmem = pl.BlockSpec(memory_space=pltpu.VMEM)
    anywhere = pl.BlockSpec(memory_space=pl.ANY)
    messages = pl.pallas_call(
        functools.partial(match_kernel, patches, groups),
        in_specs=[smem] * 4 + [anywhere] * 5,
        out_specs=[vmem] * (SPREAD * groups),
        out_shape=[jax.ShapeDtypeStruct((length, PW), jnp.bfloat16)] * (SPREAD * groups),
        scratch_shapes=[
            pltpu.VMEM(coeff_table.shape[::-1], jnp.float32),
            pltpu.VMEM((1, tile_count), jnp.bfloat16),
            pltpu.VMEM((basis, taps), jnp.bfloat16),
            pltpu.VMEM((basis, taps), jnp.bfloat16),
            pltpu.VMEM((tile_count, rows, width), jnp.bfloat16),
            pltpu.VMEM((tile_count * VECTORS, width), jnp.float32),
            pltpu.VMEM((tile_count, width), jnp.float32),
            pltpu.VMEM((per_visit, 2, 4 * FINE_ROWS, 2 * width), jnp.bfloat16),
            pltpu.VMEM((per_visit, 2, COARSE * BLOCK, 2 * width), jnp.bfloat16),
            pltpu.VMEM((SPREAD, rows, PW), jnp.float32),
            pltpu.VMEM((SPREAD, EXTRA, PW), jnp.float32),
            pltpu.SemaphoreType.DMA((visits,)),
            pltpu.SemaphoreType.DMA((4,)),
        ],
        compiler_params=pltpu.CompilerParams(vmem_limit_bytes=62 * 1024 * 1024),
        name="match_and_sum",
    )(
        tile_patch,
        tile_offset,
        coeff_index,
        visit_band,
        coeff_table.T,
        tile_weight.reshape(1, tile_count),
        row_kernels,
        column_kernels,
        tiles,
    )

    arrived = []
    for bucket in range(SPREAD):
        for turn in range(groups):
            message = messages[bucket * groups + turn]
            distance = bucket - REACH
            if distance != 0 or turn != 0:
                route = [
                    (o * groups + g, (o + distance) % patches * groups + (g + turn) % groups)
                    for o in range(patches)
                    for g in range(groups)
                ]
                message = lax.ppermute(message, ("ra", "band"), route)
            arrived.append(message)

    return pl.pallas_call(
        functools.partial(combine_kernel, visits),
        in_specs=[smem] + [vmem] * len(arrived),
        out_specs=(vmem, vmem),
        out_shape=(
            jax.ShapeDtypeStruct((BANDS, row_share, PW), jnp.float32),
            jax.ShapeDtypeStruct((row_share, PW), jnp.float32),
        ),
        compiler_params=pltpu.CompilerParams(vmem_limit_bytes=40 * 1024 * 1024),
        name="combine",
    )(band_weight, *arrived)


def solution(mesh):
    return jax.shard_map(
        local,
        mesh=mesh,
        in_specs=(
            P(("ra", "band"), None, None),
            P(("ra", "band")),
            P(("ra", "band")),
            P(("ra", "band")),
            P(("ra", "band")),
            P(("ra", "band")),
            P(),
            P(),
            P(),
            P(),
        ),
        out_specs=(P(None, "band", "ra"), P("band", "ra")),
        check_vma=False,
    )
```

```python
import functools

import jax
import jax.numpy as jnp
from jax import lax
from jax.experimental import pallas as pl
from jax.experimental.pallas import tpu as pltpu
from jax.sharding import PartitionSpec as P

PW = 256
BANDS = 6
REACH = 2
SPREAD = 2 * REACH + 1
EXTRA = 16
BLOCK = 32
COARSE = 3
VECTORS = 16
FINE_ROWS = 64
LEAD = 6


def slot_rows(row_share):
    return max(row_share, 16)


def match_kernel(
    patches,
    groups,
    patch_ref,
    offset_ref,
    index_ref,
    band_ref,
    table_hbm,
    weight_hbm,
    rowk_hbm,
    colk_hbm,
    tiles_hbm,
    *rest,
):
    messages = rest[: SPREAD * groups]
    (
        table_ref,
        weight_ref,
        rowk_ref,
        colk_ref,
        tiles_ref,
        kernels,
        weights,
        shifted,
        toeplitz,
        matches,
        sums,
        extra,
        arrival,
        ready,
    ) = rest[SPREAD * groups :]
    visits = band_ref.shape[0]
    tile_count, rows, width = tiles_ref.shape
    per_visit = tile_count // visits
    basis, taps = rowk_ref.shape
    half = taps // 2
    row_share = rows // groups
    slot = slot_rows(row_share)
    owner = lax.axis_index("ra")
    group = lax.axis_index("band")

    small = [
        pltpu.make_async_copy(source, target, ready.at[place])
        for place, (source, target) in enumerate(
            (
                (table_hbm, table_ref),
                (weight_hbm, weight_ref),
                (rowk_hbm, rowk_ref),
                (colk_hbm, colk_ref),
            )
        )
    ]
    for copy in small:
        copy.start()

    def fetch(visit):
        held = pl.ds(visit * per_visit, per_visit)
        return pltpu.make_async_copy(tiles_hbm.at[held], tiles_ref.at[held], arrival.at[visit])

    for visit in range(visits):
        fetch(visit).start()

    def iota(shape, axis):
        return lax.broadcasted_iota(jnp.int32, shape, axis)

    def across(left, right, **options):
        return lax.dot_general(
            left,
            right,
            (((1,), (1,)), ((), ())),
            preferred_element_type=jnp.float32,
            **options,
        )

    extra[...] = jnp.zeros_like(extra)
    shifted[...] = jnp.zeros_like(shifted)
    eye = (iota((tile_count, tile_count), 0) == iota((tile_count, tile_count), 1)).astype(
        jnp.bfloat16
    )
    entry = iota((1, table_ref.shape[1]), 1)
    chosen = jnp.concatenate(
        [(entry == index_ref[j]).astype(jnp.float32) for j in range(tile_count)], axis=0
    )
    for copy in small:
        copy.wait()
    weights[...] = across(eye, jnp.broadcast_to(weight_ref[...], (width, tile_count)))
    coeffs = across(chosen, table_ref[...], precision=lax.Precision.HIGHEST)

    line = iota((2 * VECTORS, taps), 0)
    column = iota((2 * VECTORS, taps), 1)
    block = lax.rem(line, VECTORS) // 2
    step = 4 * lax.rem(block, COARSE) + 2 * lax.rem(line, 2) + line // VECTORS
    wanted = jnp.where(block < COARSE, half + step, half - 1 - step)
    wanted = jnp.where(lax.rem(line, VECTORS) < 4 * COARSE, wanted, -1)
    col_taps = across((wanted == column).astype(jnp.bfloat16), colk_ref[...])
    tap = iota((taps, width), 0)
    lane = iota((taps, width), 1)
    total = None
    for side in range(2):
        place = (lane == tap + LEAD + side * FINE_ROWS).astype(jnp.bfloat16)
        row_taps = jnp.dot(
            rowk_ref[...], place, preferred_element_type=jnp.float32
        ).astype(jnp.bfloat16)
        part = col_taps[side * VECTORS : (side + 1) * VECTORS]
        mix = jnp.concatenate([part * coeffs[j : j + 1] for j in range(tile_count)], axis=0)
        high = mix.astype(jnp.bfloat16)
        low = (mix - high.astype(jnp.float32)).astype(jnp.bfloat16)
        term = jnp.dot(high, row_taps, preferred_element_type=jnp.float32) + jnp.dot(
            low, row_taps, preferred_element_type=jnp.float32
        )
        total = term if total is None else total + term
    kernels[...] = total

    lane = iota((rows, width), 1)
    column = iota((1, width), 1)

    def moved(value, distance):
        if distance == 0:
            return value
        turned = pltpu.roll(value, -distance % width, 1)
        here = lane[: value.shape[0]] + distance
        return jnp.where((here >= 0) & (here < width), turned, jnp.zeros_like(turned))

    def one_visit(visit, unused):
        fetch(visit).wait()
        sums[...] = jnp.zeros_like(sums)
        first = visit * per_visit
        for place in range(per_visit):
            tile = first + place
            pixels = tiles_ref[tile]
            for side in range(2):
                for fine in range(4):
                    part = moved(pixels, -1 - fine if side else fine)
                    top = fine * FINE_ROWS
                    shifted[place, side, top + 16 : top + 64, :width] = part[:48]
                    shifted[place, side, top : top + 48, width:] = part[16:]
                for coarse in range(COARSE):
                    for pair in range(2):
                        vector = pl.ds(
                            tile * VECTORS + (side * COARSE + coarse) * 2 + pair, 1
                        )
                        spread = jnp.broadcast_to(kernels[vector, :], (BLOCK, width))
                        turned = pltpu.roll(spread, 0, 1, stride=1, stride_axis=0)
                        toeplitz[
                            place,
                            side,
                            coarse * BLOCK : (coarse + 1) * BLOCK,
                            pair * width : (pair + 1) * width,
                        ] = turned.astype(jnp.bfloat16)
        for place in range(per_visit):
            matched = [jnp.zeros((BLOCK, width), jnp.float32) for _ in range(2)]
            for side in range(2):
                passed = jnp.dot(
                    toeplitz[place, side],
                    shifted[place, side],
                    preferred_element_type=jnp.float32,
                )
                for part in range(2):
                    for coarse in range(COARSE):
                        matched[part] += moved(
                            passed[
                                coarse * BLOCK : (coarse + 1) * BLOCK,
                                part * width : (part + 1) * width,
                            ],
                            -4 * coarse if side else 4 * coarse,
                        )
            matches[place] = jnp.concatenate(matched, axis=0)
        for place in range(per_visit):
            tile = first + place
            offset = offset_ref[tile]
            bucket = lax.rem(patch_ref[tile] - owner + REACH + patches, patches)
            weight = weights[pl.ds(tile, 1), :]
            turned = pltpu.roll(
                matches[place] * weight, lax.rem(offset, width), 1
            )
            sums[bucket, :, :width] += jnp.where(lane >= offset, turned, 0.0)
            sums[bucket, :, width:] += jnp.where(lane < offset, turned, 0.0)
            extra[bucket, pl.ds(visit, 1), :] += jnp.concatenate(
                [
                    jnp.where(column >= offset, weight, 0.0),
                    jnp.where(column < offset, weight, 0.0),
                ],
                axis=1,
            )

        for bucket in range(SPREAD):
            extra[bucket, pl.ds(2 * visits + visit, 1), :] = jnp.full(
                (1, PW), band_ref[visit], jnp.int32
            ).astype(jnp.float32)
            for turn in range(groups):
                part = lax.rem(group + turn, groups)
                own = sums[bucket, pl.ds(pl.multiple_of(part * row_share, row_share), row_share), :]
                if slot > row_share:
                    own = jnp.concatenate(
                        [own, jnp.zeros((slot - row_share, PW), jnp.float32)], axis=0
                    )
                messages[bucket * groups + turn][
                    pl.ds(pl.multiple_of(visit * slot, slot), slot), :
                ] = own.astype(jnp.bfloat16)
        return unused

    lax.fori_loop(0, visits, one_visit, 0)

    row = iota((EXTRA, PW), 0)
    for bucket in range(SPREAD):
        held = extra[bucket]
        high = held.astype(jnp.bfloat16).astype(jnp.float32)
        low = jnp.concatenate([held[-visits:], (held - high)[:-visits]], axis=0)
        mixed = jnp.where((row >= visits) & (row < 2 * visits), low, high).astype(jnp.bfloat16)
        for turn in range(groups):
            messages[bucket * groups + turn][slot * visits :, :] = mixed


def combine_kernel(count, weight_ref, *refs):
    messages = refs[:-2]
    coadd_ref, detection_ref = refs[-2:]
    row_share = coadd_ref.shape[1]
    slot = slot_rows(row_share)
    totals = [jnp.zeros((row_share, PW), jnp.float32) for _ in range(BANDS)]
    weight_totals = [jnp.zeros((1, PW), jnp.float32) for _ in range(BANDS)]
    for message in messages:
        extra = message[slot * count :, :].astype(jnp.float32)
        for visit in range(count):
            band = extra[2 * count + visit : 2 * count + visit + 1]
            weight = extra[visit : visit + 1] + extra[count + visit : count + visit + 1]
            part = message[slot * visit : slot * (visit + 1), :].astype(jnp.float32)[:row_share]
            for b in range(BANDS):
                here = band == float(b)
                totals[b] += jnp.where(here, part, 0.0)
                weight_totals[b] += jnp.where(here, weight, 0.0)
    detection = jnp.zeros((row_share, PW), jnp.float32)
    for b in range(BANDS):
        coadd = totals[b] / jnp.maximum(weight_totals[b], 1.0)
        coadd_ref[b] = coadd
        detection += weight_ref[b] * coadd
    detection_ref[...] = detection


def local(
    tiles,
    tile_patch,
    tile_offset,
    tile_weight,
    visit_band,
    coeff_index,
    coeff_table,
    row_kernels,
    column_kernels,
    band_weight,
):
    tile_count, rows, width = tiles.shape
    visits = visit_band.shape[0]
    per_visit = tile_count // visits
    basis, taps = row_kernels.shape
    patches = lax.axis_size("ra")
    groups = lax.axis_size("band")
    row_share = rows // groups
    slot = slot_rows(row_share)
    length = visits * slot + EXTRA
    smem = pl.BlockSpec(memory_space=pltpu.SMEM)

    vmem = pl.BlockSpec(memory_space=pltpu.VMEM)
    anywhere = pl.BlockSpec(memory_space=pl.ANY)
    messages = pl.pallas_call(
        functools.partial(match_kernel, patches, groups),
        in_specs=[smem] * 4 + [anywhere] * 5,
        out_specs=[vmem] * (SPREAD * groups),
        out_shape=[jax.ShapeDtypeStruct((length, PW), jnp.bfloat16)] * (SPREAD * groups),
        scratch_shapes=[
            pltpu.VMEM(coeff_table.shape[::-1], jnp.float32),
            pltpu.VMEM((1, tile_count), jnp.bfloat16),
            pltpu.VMEM((basis, taps), jnp.bfloat16),
            pltpu.VMEM((basis, taps), jnp.bfloat16),
            pltpu.VMEM((tile_count, rows, width), jnp.bfloat16),
            pltpu.VMEM((tile_count * VECTORS, width), jnp.float32),
            pltpu.VMEM((tile_count, width), jnp.float32),
            pltpu.VMEM((per_visit, 2, 4 * FINE_ROWS, 2 * width), jnp.bfloat16),
            pltpu.VMEM((per_visit, 2, COARSE * BLOCK, 2 * width), jnp.bfloat16),
            pltpu.VMEM((per_visit, rows, width), jnp.float32),
            pltpu.VMEM((SPREAD, rows, PW), jnp.float32),
            pltpu.VMEM((SPREAD, EXTRA, PW), jnp.float32),
            pltpu.SemaphoreType.DMA((visits,)),
            pltpu.SemaphoreType.DMA((4,)),
        ],
        compiler_params=pltpu.CompilerParams(vmem_limit_bytes=62 * 1024 * 1024),
        name="match_and_sum",
    )(
        tile_patch,
        tile_offset,
        coeff_index,
        visit_band,
        coeff_table.T,
        tile_weight.reshape(1, tile_count),
        row_kernels,
        column_kernels,
        tiles,
    )

    arrived = []
    for bucket in range(SPREAD):
        for turn in range(groups):
            message = messages[bucket * groups + turn]
            distance = bucket - REACH
            if distance != 0 or turn != 0:
                route = [
                    (o * groups + g, (o + distance) % patches * groups + (g + turn) % groups)
                    for o in range(patches)
                    for g in range(groups)
                ]
                message = lax.ppermute(message, ("ra", "band"), route)
            arrived.append(message)

    return pl.pallas_call(
        functools.partial(combine_kernel, visits),
        in_specs=[smem] + [vmem] * len(arrived),
        out_specs=(vmem, vmem),
        out_shape=(
            jax.ShapeDtypeStruct((BANDS, row_share, PW), jnp.float32),
            jax.ShapeDtypeStruct((row_share, PW), jnp.float32),
        ),
        compiler_params=pltpu.CompilerParams(vmem_limit_bytes=40 * 1024 * 1024),
        name="combine",
    )(band_weight, *arrived)


def solution(mesh):
    return jax.shard_map(
        local,
        mesh=mesh,
        in_specs=(
            P(("ra", "band"), None, None),
            P(("ra", "band")),
            P(("ra", "band")),
            P(("ra", "band")),
            P(("ra", "band")),
            P(("ra", "band")),
            P(),
            P(),
            P(),
            P(),
        ),
        out_specs=(P(None, "band", "ra"), P("band", "ra")),
        check_vma=False,
    )
```

```python
import functools

import jax
import jax.numpy as jnp
from jax import lax
from jax.experimental import pallas as pl
from jax.experimental.pallas import tpu as pltpu
from jax.sharding import PartitionSpec as P

PW = 256
BANDS = 6
REACH = 2
SPREAD = 2 * REACH + 1
EXTRA = 16
BLOCK = 32
COARSE = 3
VECTORS = 16
FINE_ROWS = 64
LEAD = 6


def slot_rows(row_share):
    return max(row_share, 16)


def match_kernel(
    patches,
    groups,
    patch_ref,
    offset_ref,
    index_ref,
    band_ref,
    table_hbm,
    weight_hbm,
    rowk_hbm,
    colk_hbm,
    tiles_hbm,
    *rest,
):
    messages = rest[: SPREAD * groups]
    (
        table_ref,
        weight_ref,
        rowk_ref,
        colk_ref,
        tiles_ref,
        kernels,
        weights,
        shifted,
        toeplitz,
        matches,
        sums,
        extra,
        arrival,
        ready,
    ) = rest[SPREAD * groups :]
    visits = band_ref.shape[0]
    tile_count, rows, width = tiles_ref.shape
    per_visit = tile_count // visits
    basis, taps = rowk_ref.shape
    half = taps // 2
    row_share = rows // groups
    slot = slot_rows(row_share)
    owner = lax.axis_index("ra")
    group = lax.axis_index("band")

    small = [
        pltpu.make_async_copy(source, target, ready.at[place])
        for place, (source, target) in enumerate(
            (
                (table_hbm, table_ref),
                (weight_hbm, weight_ref),
                (rowk_hbm, rowk_ref),
                (colk_hbm, colk_ref),
            )
        )
    ]
    for copy in small:
        copy.start()

    def fetch(visit):
        held = pl.ds(visit * per_visit, per_visit)
        return pltpu.make_async_copy(tiles_hbm.at[held], tiles_ref.at[held], arrival.at[visit])

    for visit in range(visits):
        fetch(visit).start()

    def iota(shape, axis):
        return lax.broadcasted_iota(jnp.int32, shape, axis)

    def across(left, right, **options):
        return lax.dot_general(
            left,
            right,
            (((1,), (1,)), ((), ())),
            preferred_element_type=jnp.float32,
            **options,
        )

    extra[...] = jnp.zeros_like(extra)
    shifted[...] = jnp.zeros_like(shifted)
    eye = (iota((tile_count, tile_count), 0) == iota((tile_count, tile_count), 1)).astype(
        jnp.bfloat16
    )
    entry = iota((1, table_ref.shape[1]), 1)
    chosen = jnp.concatenate(
        [(entry == index_ref[j]).astype(jnp.float32) for j in range(tile_count)], axis=0
    )
    for copy in small:
        copy.wait()
    weights[...] = across(eye, jnp.broadcast_to(weight_ref[...], (width, tile_count)))
    coeffs = across(chosen, table_ref[...], precision=lax.Precision.HIGHEST)

    line = iota((2 * VECTORS, taps), 0)
    column = iota((2 * VECTORS, taps), 1)
    block = lax.rem(line, VECTORS) // 2
    step = 4 * lax.rem(block, COARSE) + 2 * lax.rem(line, 2) + line // VECTORS
    wanted = jnp.where(block < COARSE, half + step, half - 1 - step)
    wanted = jnp.where(lax.rem(line, VECTORS) < 4 * COARSE, wanted, -1)
    col_taps = across((wanted == column).astype(jnp.bfloat16), colk_ref[...])
    tap = iota((taps, width), 0)
    lane = iota((taps, width), 1)
    total = None
    for side in range(2):
        place = (lane == tap + LEAD + side * FINE_ROWS).astype(jnp.bfloat16)
        row_taps = jnp.dot(
            rowk_ref[...], place, preferred_element_type=jnp.float32
        ).astype(jnp.bfloat16)
        part = col_taps[side * VECTORS : (side + 1) * VECTORS]
        mix = jnp.concatenate([part * coeffs[j : j + 1] for j in range(tile_count)], axis=0)
        high = mix.astype(jnp.bfloat16)
        low = (mix - high.astype(jnp.float32)).astype(jnp.bfloat16)
        term = jnp.dot(high, row_taps, preferred_element_type=jnp.float32) + jnp.dot(
            low, row_taps, preferred_element_type=jnp.float32
        )
        total = term if total is None else total + term
    kernels[...] = total

    lane = iota((rows, width), 1)
    column = iota((1, width), 1)

    def moved(value, distance):
        if distance == 0:
            return value
        turned = pltpu.roll(value, -distance % width, 1)
        here = lane[: value.shape[0]] + distance
        return jnp.where((here >= 0) & (here < width), turned, jnp.zeros_like(turned))

    def one_visit(visit, unused):
        fetch(visit).wait()
        sums[...] = jnp.zeros_like(sums)
        first = visit * per_visit
        for place in range(per_visit):
            tile = first + place
            pixels = tiles_ref[tile]
            for side in range(2):
                for fine in range(4):
                    part = moved(pixels, -1 - fine if side else fine)
                    top = fine * FINE_ROWS
                    shifted[place, side, top + 16 : top + 64, :width] = part[:48]
                    shifted[place, side, top : top + 48, width:] = part[16:]
                for coarse in range(COARSE):
                    for pair in range(2):
                        vector = pl.ds(
                            tile * VECTORS + (side * COARSE + coarse) * 2 + pair, 1
                        )
                        spread = jnp.broadcast_to(kernels[vector, :], (BLOCK, width))
                        turned = pltpu.roll(spread, 0, 1, stride=1, stride_axis=0)
                        toeplitz[
                            place,
                            side,
                            coarse * BLOCK : (coarse + 1) * BLOCK,
                            pair * width : (pair + 1) * width,
                        ] = turned.astype(jnp.bfloat16)
        for place in range(per_visit):
            matched = [jnp.zeros((BLOCK, width), jnp.float32) for _ in range(2)]
            for side in range(2):
                passed = jnp.dot(
                    toeplitz[place, side],
                    shifted[place, side],
                    preferred_element_type=jnp.float32,
                )
                for part in range(2):
                    for coarse in range(COARSE):
                        matched[part] += moved(
                            passed[
                                coarse * BLOCK : (coarse + 1) * BLOCK,
                                part * width : (part + 1) * width,
                            ],
                            -4 * coarse if side else 4 * coarse,
                        )
            matches[place] = jnp.concatenate(matched, axis=0)
        for place in range(per_visit):
            tile = first + place
            offset = offset_ref[tile]
            bucket = lax.rem(patch_ref[tile] - owner + REACH + patches, patches)
            weight = weights[pl.ds(tile, 1), :]
            turned = pltpu.roll(
                matches[place] * weight, lax.rem(offset, width), 1
            )
            sums[bucket, :, :width] += jnp.where(lane >= offset, turned, 0.0)
            sums[bucket, :, width:] += jnp.where(lane < offset, turned, 0.0)
            extra[bucket, pl.ds(visit, 1), :] += jnp.concatenate(
                [
                    jnp.where(column >= offset, weight, 0.0),
                    jnp.where(column < offset, weight, 0.0),
                ],
                axis=1,
            )

        for bucket in range(SPREAD):
            for turn in range(groups):
                part = lax.rem(group + turn, groups)
                own = sums[bucket, pl.ds(pl.multiple_of(part * row_share, row_share), row_share), :]
                if slot > row_share:
                    own = jnp.concatenate(
                        [own, jnp.zeros((slot - row_share, PW), jnp.float32)], axis=0
                    )
                messages[bucket * groups + turn][
                    pl.ds(pl.multiple_of(visit * slot, slot), slot), :
                ] = own.astype(jnp.bfloat16)
        return unused

    lax.fori_loop(0, visits, one_visit, 0)

    row = iota((EXTRA, PW), 0)
    lane = iota((1, PW), 1)
    by_row = jnp.zeros((1, PW), jnp.float32)
    by_weight = jnp.full((1, PW), -1.0, jnp.float32)
    for visit in range(visits):
        band = band_ref[visit].astype(jnp.float32)
        by_row = jnp.where(lane // slot == visit, band, by_row)
        by_weight = jnp.where(
            (lane < 2 * visits) & (lax.rem(lane, visits) == visit), band, by_weight
        )
    for bucket in range(SPREAD):
        held = extra[bucket]
        high = held.astype(jnp.bfloat16).astype(jnp.float32)
        low = jnp.concatenate([held[-visits:], (held - high)[:-visits]], axis=0)
        mixed = jnp.where((row >= visits) & (row < 2 * visits), low, high)
        mixed = jnp.where(row == 2 * visits, by_row, mixed)
        mixed = jnp.where(row == 2 * visits + 1, by_weight, mixed).astype(jnp.bfloat16)
        for turn in range(groups):
            messages[bucket * groups + turn][slot * visits :, :] = mixed


def combine_kernel(count, weight_ref, own_hbm, *refs):
    coadd_ref, detection_ref, own_ref, arrival = refs[-4:]
    row_share = coadd_ref.shape[1]
    slot = slot_rows(row_share)
    depth = slot * count
    fetch = pltpu.make_async_copy(own_hbm, own_ref, arrival)
    fetch.start()
    line = lax.broadcasted_iota(jnp.int32, (row_share, depth), 0)
    lane = lax.broadcasted_iota(jnp.int32, (row_share, depth), 1)
    same = (lax.rem(lane, slot) == line).astype(jnp.float32)
    band_line = lax.broadcasted_iota(jnp.int32, (8, EXTRA), 0).astype(jnp.float32)
    totals = jnp.zeros((BANDS * row_share, PW), jnp.float32)
    weight_totals = jnp.zeros((8, PW), jnp.float32)
    for message in refs[:-4] + (own_ref,):
        if message is own_ref:
            fetch.wait()
        extra = message[depth:, :]
        bands = extra[2 * count : 2 * count + 2].astype(jnp.float32)
        pick = jnp.concatenate(
            [jnp.where(bands[:1, :depth] == float(b), same, 0.0) for b in range(BANDS)], axis=0
        ).astype(jnp.bfloat16)
        totals += jnp.dot(pick, message[:depth, :], preferred_element_type=jnp.float32)
        pick = (bands[1:, :EXTRA] == band_line).astype(jnp.bfloat16)
        weight_totals += jnp.dot(pick, extra, preferred_element_type=jnp.float32)
    detection = jnp.zeros((row_share, PW), jnp.float32)
    for b in range(BANDS):
        coadd = totals[b * row_share : (b + 1) * row_share] / jnp.maximum(
            weight_totals[b : b + 1], 1.0
        )
        coadd_ref[b] = coadd
        detection += weight_ref[b] * coadd
    detection_ref[...] = detection


def local(
    tiles,
    tile_patch,
    tile_offset,
    tile_weight,
    visit_band,
    coeff_index,
    coeff_table,
    row_kernels,
    column_kernels,
    band_weight,
):
    tile_count, rows, width = tiles.shape
    visits = visit_band.shape[0]
    per_visit = tile_count // visits
    basis, taps = row_kernels.shape
    patches = lax.axis_size("ra")
    groups = lax.axis_size("band")
    row_share = rows // groups
    slot = slot_rows(row_share)
    length = visits * slot + EXTRA
    smem = pl.BlockSpec(memory_space=pltpu.SMEM)

    vmem = pl.BlockSpec(memory_space=pltpu.VMEM)
    anywhere = pl.BlockSpec(memory_space=pl.ANY)
    messages = pl.pallas_call(
        functools.partial(match_kernel, patches, groups),
        in_specs=[smem] * 4 + [anywhere] * 5,
        out_specs=[vmem] * (SPREAD * groups),
        out_shape=[jax.ShapeDtypeStruct((length, PW), jnp.bfloat16)] * (SPREAD * groups),
        scratch_shapes=[
            pltpu.VMEM(coeff_table.shape[::-1], jnp.float32),
            pltpu.VMEM((1, tile_count), jnp.bfloat16),
            pltpu.VMEM((basis, taps), jnp.bfloat16),
            pltpu.VMEM((basis, taps), jnp.bfloat16),
            pltpu.VMEM((tile_count, rows, width), jnp.bfloat16),
            pltpu.VMEM((tile_count * VECTORS, width), jnp.float32),
            pltpu.VMEM((tile_count, width), jnp.float32),
            pltpu.VMEM((per_visit, 2, 4 * FINE_ROWS, 2 * width), jnp.bfloat16),
            pltpu.VMEM((per_visit, 2, COARSE * BLOCK, 2 * width), jnp.bfloat16),
            pltpu.VMEM((per_visit, rows, width), jnp.float32),
            pltpu.VMEM((SPREAD, rows, PW), jnp.float32),
            pltpu.VMEM((SPREAD, EXTRA, PW), jnp.float32),
            pltpu.SemaphoreType.DMA((visits,)),
            pltpu.SemaphoreType.DMA((4,)),
        ],
        compiler_params=pltpu.CompilerParams(vmem_limit_bytes=62 * 1024 * 1024),
        name="match_and_sum",
    )(
        tile_patch,
        tile_offset,
        coeff_index,
        visit_band,
        coeff_table.T,
        tile_weight.reshape(1, tile_count),
        row_kernels,
        column_kernels,
        tiles,
    )

    arrived = []
    for distance, turn in sorted(
        ((d, t) for d in range(-REACH, REACH + 1) for t in range(groups)),
        key=lambda way: (abs(way[0]), way[1], way[0]),
    ):
        message = messages[(distance + REACH) * groups + turn]
        if distance != 0 or turn != 0:
            route = [
                (o * groups + g, (o + distance) % patches * groups + (g + turn) % groups)
                for o in range(patches)
                for g in range(groups)
            ]
            message = lax.ppermute(message, ("ra", "band"), route)
        arrived.append(message)

    return pl.pallas_call(
        functools.partial(combine_kernel, visits),
        in_specs=[smem, anywhere] + [vmem] * (len(arrived) - 1),
        out_specs=(vmem, vmem),
        out_shape=(
            jax.ShapeDtypeStruct((BANDS, row_share, PW), jnp.float32),
            jax.ShapeDtypeStruct((row_share, PW), jnp.float32),
        ),
        scratch_shapes=[pltpu.VMEM((length, PW), jnp.bfloat16), pltpu.SemaphoreType.DMA],
        compiler_params=pltpu.CompilerParams(vmem_limit_bytes=40 * 1024 * 1024),
        name="combine",
    )(band_weight, *arrived)


def solution(mesh):
    return jax.shard_map(
        local,
        mesh=mesh,
        in_specs=(
            P(("ra", "band"), None, None),
            P(("ra", "band")),
            P(("ra", "band")),
            P(("ra", "band")),
            P(("ra", "band")),
            P(("ra", "band")),
            P(),
            P(),
            P(),
            P(),
        ),
        out_specs=(P(None, "band", "ra"), P("band", "ra")),
        check_vma=False,
    )
```

```python
import functools

import jax
import jax.numpy as jnp
from jax import lax
from jax.experimental import pallas as pl
from jax.experimental.pallas import tpu as pltpu
from jax.sharding import PartitionSpec as P

PW = 256
BANDS = 6
REACH = 2
SPREAD = 2 * REACH + 1
EXTRA = 16
BLOCK = 32
COARSE = 3
VECTORS = 16
FINE_ROWS = 64
LEAD = 6


def slot_rows(row_share):
    return max(row_share, 16)


def match_kernel(
    patches,
    groups,
    patch_ref,
    offset_ref,
    index_ref,
    band_ref,
    table_hbm,
    weight_hbm,
    rowk_hbm,
    colk_hbm,
    tiles_hbm,
    *rest,
):
    messages = rest[: SPREAD * groups]
    (
        table_ref,
        weight_ref,
        rowk_ref,
        colk_ref,
        tiles_ref,
        kernels,
        weights,
        shifted,
        toeplitz,
        matches,
        sums,
        extra,
        arrival,
        ready,
    ) = rest[SPREAD * groups :]
    visits = band_ref.shape[0]
    tile_count, rows, width = tiles_ref.shape
    per_visit = tile_count // visits
    basis, taps = rowk_ref.shape
    half = taps // 2
    row_share = rows // groups
    slot = slot_rows(row_share)
    owner = lax.axis_index("ra")
    group = lax.axis_index("band")

    small = [
        pltpu.make_async_copy(source, target, ready.at[place])
        for place, (source, target) in enumerate(
            (
                (table_hbm, table_ref),
                (weight_hbm, weight_ref),
                (rowk_hbm, rowk_ref),
                (colk_hbm, colk_ref),
            )
        )
    ]
    for copy in small:
        copy.start()

    def fetch(visit):
        held = pl.ds(visit * per_visit, per_visit)
        return pltpu.make_async_copy(tiles_hbm.at[held], tiles_ref.at[held], arrival.at[visit])

    for visit in range(visits):
        fetch(visit).start()

    def iota(shape, axis):
        return lax.broadcasted_iota(jnp.int32, shape, axis)

    def across(left, right, **options):
        return lax.dot_general(
            left,
            right,
            (((1,), (1,)), ((), ())),
            preferred_element_type=jnp.float32,
            **options,
        )

    extra[...] = jnp.zeros_like(extra)
    shifted[...] = jnp.zeros_like(shifted)
    eye = (iota((tile_count, tile_count), 0) == iota((tile_count, tile_count), 1)).astype(
        jnp.bfloat16
    )
    entry = iota((1, table_ref.shape[1]), 1)
    chosen = jnp.concatenate(
        [(entry == index_ref[j]).astype(jnp.float32) for j in range(tile_count)], axis=0
    )
    for copy in small:
        copy.wait()
    weights[...] = across(eye, jnp.broadcast_to(weight_ref[...], (width, tile_count)))
    coeffs = across(chosen, table_ref[...], precision=lax.Precision.HIGHEST)

    line = iota((2 * VECTORS, taps), 0)
    column = iota((2 * VECTORS, taps), 1)
    block = lax.rem(line, VECTORS) // 2
    step = 4 * lax.rem(block, COARSE) + 2 * lax.rem(line, 2) + line // VECTORS
    wanted = jnp.where(block < COARSE, half + step, half - 1 - step)
    wanted = jnp.where(lax.rem(line, VECTORS) < 4 * COARSE, wanted, -1)
    col_taps = across((wanted == column).astype(jnp.bfloat16), colk_ref[...])
    tap = iota((taps, width), 0)
    lane = iota((taps, width), 1)
    total = None
    for side in range(2):
        place = (lane == tap + LEAD + side * FINE_ROWS).astype(jnp.bfloat16)
        row_taps = jnp.dot(
            rowk_ref[...], place, preferred_element_type=jnp.float32
        ).astype(jnp.bfloat16)
        part = col_taps[side * VECTORS : (side + 1) * VECTORS]
        mix = jnp.concatenate([part * coeffs[j : j + 1] for j in range(tile_count)], axis=0)
        high = mix.astype(jnp.bfloat16)
        low = (mix - high.astype(jnp.float32)).astype(jnp.bfloat16)
        term = jnp.dot(high, row_taps, preferred_element_type=jnp.float32) + jnp.dot(
            low, row_taps, preferred_element_type=jnp.float32
        )
        total = term if total is None else total + term
    kernels[...] = total

    lane = iota((rows, width), 1)
    column = iota((1, width), 1)

    def moved(value, distance):
        if distance == 0:
            return value
        turned = pltpu.roll(value, -distance % width, 1)
        here = lane[: value.shape[0]] + distance
        return jnp.where((here >= 0) & (here < width), turned, jnp.zeros_like(turned))

    def one_visit(visit, unused):
        fetch(visit).wait()
        sums[...] = jnp.zeros_like(sums)
        first = visit * per_visit
        for place in range(per_visit):
            tile = first + place
            pixels = tiles_ref[tile]
            for side in range(2):
                for fine in range(4):
                    part = moved(pixels, -1 - fine if side else fine)
                    top = fine * FINE_ROWS
                    shifted[place, side, top + 16 : top + 64, :width] = part[:48]
                    shifted[place, side, top : top + 48, width:] = part[16:]
                for coarse in range(COARSE):
                    for pair in range(2):
                        vector = pl.ds(
                            tile * VECTORS + (side * COARSE + coarse) * 2 + pair, 1
                        )
                        spread = jnp.broadcast_to(kernels[vector, :], (BLOCK, width))
                        turned = pltpu.roll(spread, 0, 1, stride=1, stride_axis=0)
                        toeplitz[
                            place,
                            side,
                            coarse * BLOCK : (coarse + 1) * BLOCK,
                            pair * width : (pair + 1) * width,
                        ] = turned.astype(jnp.bfloat16)
        for place in range(per_visit):
            matched = [jnp.zeros((BLOCK, width), jnp.float32) for _ in range(2)]
            for side in range(2):
                passed = jnp.dot(
                    toeplitz[place, side],
                    shifted[place, side],
                    preferred_element_type=jnp.float32,
                )
                for part in range(2):
                    for coarse in range(COARSE):
                        matched[part] += moved(
                            passed[
                                coarse * BLOCK : (coarse + 1) * BLOCK,
                                part * width : (part + 1) * width,
                            ],
                            -4 * coarse if side else 4 * coarse,
                        )
            matches[place] = jnp.concatenate(matched, axis=0)
        for place in range(per_visit):
            tile = first + place
            offset = offset_ref[tile]
            bucket = lax.rem(patch_ref[tile] - owner + REACH + patches, patches)
            weight = weights[pl.ds(tile, 1), :]
            turned = pltpu.roll(
                matches[place] * weight, lax.rem(offset, width), 1
            )
            sums[bucket, :, :width] += jnp.where(lane >= offset, turned, 0.0)
            sums[bucket, :, width:] += jnp.where(lane < offset, turned, 0.0)
            extra[bucket, pl.ds(visit, 1), :] += jnp.concatenate(
                [
                    jnp.where(column >= offset, weight, 0.0),
                    jnp.where(column < offset, weight, 0.0),
                ],
                axis=1,
            )

        for bucket in range(SPREAD):
            for turn in range(groups):
                part = lax.rem(group + turn, groups)
                own = sums[bucket, pl.ds(pl.multiple_of(part * row_share, row_share), row_share), :]
                if slot > row_share:
                    own = jnp.concatenate(
                        [own, jnp.zeros((slot - row_share, PW), jnp.float32)], axis=0
                    )
                messages[bucket * groups + turn][
                    pl.ds(pl.multiple_of(visit * slot, slot), slot), :
                ] = own.astype(jnp.bfloat16)
        return unused

    lax.fori_loop(0, visits, one_visit, 0)

    row = iota((EXTRA, PW), 0)
    lane = iota((1, PW), 1)
    by_row = jnp.zeros((1, PW), jnp.float32)
    by_weight = jnp.full((1, PW), -1.0, jnp.float32)
    for visit in range(visits):
        band = band_ref[visit].astype(jnp.float32)
        by_row = jnp.where(lane // slot == visit, band, by_row)
        by_weight = jnp.where(
            (lane < 2 * visits) & (lax.rem(lane, visits) == visit), band, by_weight
        )
    for bucket in range(SPREAD):
        held = extra[bucket]
        high = held.astype(jnp.bfloat16).astype(jnp.float32)
        low = jnp.concatenate([held[-visits:], (held - high)[:-visits]], axis=0)
        mixed = jnp.where((row >= visits) & (row < 2 * visits), low, high)
        mixed = jnp.where(row == 2 * visits, by_row, mixed)
        mixed = jnp.where(row == 2 * visits + 1, by_weight, mixed).astype(jnp.bfloat16)
        for turn in range(groups):
            messages[bucket * groups + turn][slot * visits :, :] = mixed


def add_messages(count, row_share, messages):
    slot = slot_rows(row_share)
    depth = slot * count
    line = lax.broadcasted_iota(jnp.int32, (row_share, depth), 0)
    lane = lax.broadcasted_iota(jnp.int32, (row_share, depth), 1)
    same = (lax.rem(lane, slot) == line).astype(jnp.float32)
    band_line = lax.broadcasted_iota(jnp.int32, (8, EXTRA), 0).astype(jnp.float32)
    totals = jnp.zeros((BANDS * row_share, PW), jnp.float32)
    weight_totals = jnp.zeros((8, PW), jnp.float32)
    for message in messages:
        extra = message[depth:, :]
        bands = extra[2 * count : 2 * count + 2].astype(jnp.float32)
        pick = jnp.concatenate(
            [jnp.where(bands[:1, :depth] == float(b), same, 0.0) for b in range(BANDS)], axis=0
        ).astype(jnp.bfloat16)
        totals += jnp.dot(pick, message[:depth, :], preferred_element_type=jnp.float32)
        pick = (bands[1:, :EXTRA] == band_line).astype(jnp.bfloat16)
        weight_totals += jnp.dot(pick, extra, preferred_element_type=jnp.float32)
    return totals, weight_totals


def early_kernel(count, row_share, *refs):
    totals_ref, weight_totals_ref = refs[-2:]
    totals_ref[...], weight_totals_ref[...] = add_messages(count, row_share, refs[:-2])


def combine_kernel(count, weight_ref, totals_ref, weight_totals_ref, *refs):
    coadd_ref, detection_ref = refs[-2:]
    row_share = coadd_ref.shape[1]
    totals, weight_totals = add_messages(count, row_share, refs[:-2])
    weight_totals = jnp.maximum(weight_totals + weight_totals_ref[...], 1.0)
    detection = jnp.zeros((row_share, PW), jnp.float32)
    for b in range(BANDS):
        held = pl.ds(b * row_share, row_share)
        coadd = (totals[b * row_share : (b + 1) * row_share] + totals_ref[held, :]) / (
            weight_totals[b : b + 1]
        )
        coadd_ref[b] = coadd
        detection += weight_ref[b] * coadd
    detection_ref[...] = detection


def local(
    tiles,
    tile_patch,
    tile_offset,
    tile_weight,
    visit_band,
    coeff_index,
    coeff_table,
    row_kernels,
    column_kernels,
    band_weight,
):
    tile_count, rows, width = tiles.shape
    visits = visit_band.shape[0]
    per_visit = tile_count // visits
    basis, taps = row_kernels.shape
    patches = lax.axis_size("ra")
    groups = lax.axis_size("band")
    row_share = rows // groups
    slot = slot_rows(row_share)
    length = visits * slot + EXTRA
    smem = pl.BlockSpec(memory_space=pltpu.SMEM)

    vmem = pl.BlockSpec(memory_space=pltpu.VMEM)
    anywhere = pl.BlockSpec(memory_space=pl.ANY)
    messages = pl.pallas_call(
        functools.partial(match_kernel, patches, groups),
        in_specs=[smem] * 4 + [anywhere] * 5,
        out_specs=[vmem] * (SPREAD * groups),
        out_shape=[jax.ShapeDtypeStruct((length, PW), jnp.bfloat16)] * (SPREAD * groups),
        scratch_shapes=[
            pltpu.VMEM(coeff_table.shape[::-1], jnp.float32),
            pltpu.VMEM((1, tile_count), jnp.bfloat16),
            pltpu.VMEM((basis, taps), jnp.bfloat16),
            pltpu.VMEM((basis, taps), jnp.bfloat16),
            pltpu.VMEM((tile_count, rows, width), jnp.bfloat16),
            pltpu.VMEM((tile_count * VECTORS, width), jnp.float32),
            pltpu.VMEM((tile_count, width), jnp.float32),
            pltpu.VMEM((per_visit, 2, 4 * FINE_ROWS, 2 * width), jnp.bfloat16),
            pltpu.VMEM((per_visit, 2, COARSE * BLOCK, 2 * width), jnp.bfloat16),
            pltpu.VMEM((per_visit, rows, width), jnp.float32),
            pltpu.VMEM((SPREAD, rows, PW), jnp.float32),
            pltpu.VMEM((SPREAD, EXTRA, PW), jnp.float32),
            pltpu.SemaphoreType.DMA((visits,)),
            pltpu.SemaphoreType.DMA((4,)),
        ],
        compiler_params=pltpu.CompilerParams(vmem_limit_bytes=62 * 1024 * 1024),
        name="match_and_sum",
    )(
        tile_patch,
        tile_offset,
        coeff_index,
        visit_band,
        coeff_table.T,
        tile_weight.reshape(1, tile_count),
        row_kernels,
        column_kernels,
        tiles,
    )

    order = [(d, t) for d in range(-1, -REACH - 1, -1) for t in range(groups)]
    order += [(0, t) for t in range(1, groups)]
    early = len(order)
    order += [(d, t) for d in range(REACH, 0, -1) for t in range(groups)]
    arrived = []
    for distance, turn in order:
        route = [
            (o * groups + g, (o + distance) % patches * groups + (g + turn) % groups)
            for o in range(patches)
            for g in range(groups)
        ]
        arrived.append(
            lax.ppermute(messages[(distance + REACH) * groups + turn], ("ra", "band"), route)
        )

    params = pltpu.CompilerParams(vmem_limit_bytes=40 * 1024 * 1024)
    first = [messages[REACH * groups]] + arrived[:early]
    totals = pl.pallas_call(
        functools.partial(early_kernel, visits, row_share),
        in_specs=[vmem] * len(first),
        out_specs=(vmem, vmem),
        out_shape=(
            jax.ShapeDtypeStruct((BANDS * row_share, PW), jnp.float32),
            jax.ShapeDtypeStruct((8, PW), jnp.float32),
        ),
        compiler_params=params,
        name="combine_early",
    )(*first)
    return pl.pallas_call(
        functools.partial(combine_kernel, visits),
        in_specs=[smem] + [vmem] * (len(arrived) - early + 2),
        out_specs=(vmem, vmem),
        out_shape=(
            jax.ShapeDtypeStruct((BANDS, row_share, PW), jnp.float32),
            jax.ShapeDtypeStruct((row_share, PW), jnp.float32),
        ),
        compiler_params=params,
        name="combine",
    )(band_weight, *totals, *arrived[early:])


def solution(mesh):
    return jax.shard_map(
        local,
        mesh=mesh,
        in_specs=(
            P(("ra", "band"), None, None),
            P(("ra", "band")),
            P(("ra", "band")),
            P(("ra", "band")),
            P(("ra", "band")),
            P(("ra", "band")),
            P(),
            P(),
            P(),
            P(),
        ),
        out_specs=(P(None, "band", "ra"), P("band", "ra")),
        check_vma=False,
    )
```

```python
import functools

import jax
import jax.numpy as jnp
from jax import lax
from jax.experimental import pallas as pl
from jax.experimental.pallas import tpu as pltpu
from jax.sharding import PartitionSpec as P

PW = 256
BANDS = 6
REACH = 2
SPREAD = 2 * REACH + 1
EXTRA = 16
BLOCK = 32
COARSE = 3
VECTORS = 16
FINE_ROWS = 64
LEAD = 6


def slot_rows(row_share):
    return max(row_share, 16)


def match_kernel(
    patches,
    groups,
    patch_ref,
    offset_ref,
    index_ref,
    band_ref,
    table_hbm,
    weight_hbm,
    rowk_hbm,
    colk_hbm,
    tiles_hbm,
    *rest,
):
    messages = rest[: SPREAD * groups]
    (
        table_ref,
        weight_ref,
        rowk_ref,
        colk_ref,
        tiles_ref,
        kernels,
        weights,
        shifted,
        toeplitz,
        matches,
        sums,
        extra,
        arrival,
        ready,
    ) = rest[SPREAD * groups :]
    visits = band_ref.shape[0]
    tile_count, rows, width = tiles_ref.shape
    per_visit = tile_count // visits
    basis, taps = rowk_ref.shape
    half = taps // 2
    row_share = rows // groups
    slot = slot_rows(row_share)
    owner = lax.axis_index("ra")
    group = lax.axis_index("band")

    small = [
        pltpu.make_async_copy(source, target, ready.at[place])
        for place, (source, target) in enumerate(
            (
                (table_hbm, table_ref),
                (weight_hbm, weight_ref),
                (rowk_hbm, rowk_ref),
                (colk_hbm, colk_ref),
            )
        )
    ]
    for copy in small:
        copy.start()

    def fetch(visit):
        held = pl.ds(visit * per_visit, per_visit)
        return pltpu.make_async_copy(tiles_hbm.at[held], tiles_ref.at[held], arrival.at[visit])

    for visit in range(visits):
        fetch(visit).start()

    def iota(shape, axis):
        return lax.broadcasted_iota(jnp.int32, shape, axis)

    def across(left, right, **options):
        return lax.dot_general(
            left,
            right,
            (((1,), (1,)), ((), ())),
            preferred_element_type=jnp.float32,
            **options,
        )

    extra[...] = jnp.zeros_like(extra)
    shifted[...] = jnp.zeros_like(shifted)
    eye = (iota((tile_count, tile_count), 0) == iota((tile_count, tile_count), 1)).astype(
        jnp.bfloat16
    )
    entry = iota((1, table_ref.shape[1]), 1)
    chosen = jnp.concatenate(
        [(entry == index_ref[j]).astype(jnp.float32) for j in range(tile_count)], axis=0
    )
    for copy in small:
        copy.wait()
    weights[...] = across(eye, jnp.broadcast_to(weight_ref[...], (width, tile_count)))
    coeffs = across(chosen, table_ref[...], precision=lax.Precision.HIGHEST)

    line = iota((2 * VECTORS, taps), 0)
    column = iota((2 * VECTORS, taps), 1)
    block = lax.rem(line, VECTORS) // 2
    step = 4 * lax.rem(block, COARSE) + 2 * lax.rem(line, 2) + line // VECTORS
    wanted = jnp.where(block < COARSE, half + step, half - 1 - step)
    wanted = jnp.where(lax.rem(line, VECTORS) < 4 * COARSE, wanted, -1)
    col_taps = across((wanted == column).astype(jnp.bfloat16), colk_ref[...])
    tap = iota((taps, width), 0)
    lane = iota((taps, width), 1)
    total = None
    for side in range(2):
        place = (lane == tap + LEAD + side * FINE_ROWS).astype(jnp.bfloat16)
        row_taps = jnp.dot(
            rowk_ref[...], place, preferred_element_type=jnp.float32
        ).astype(jnp.bfloat16)
        part = col_taps[side * VECTORS : (side + 1) * VECTORS]
        mix = jnp.concatenate([part * coeffs[j : j + 1] for j in range(tile_count)], axis=0)
        high = mix.astype(jnp.bfloat16)
        low = (mix - high.astype(jnp.float32)).astype(jnp.bfloat16)
        term = jnp.dot(high, row_taps, preferred_element_type=jnp.float32) + jnp.dot(
            low, row_taps, preferred_element_type=jnp.float32
        )
        total = term if total is None else total + term
    kernels[...] = total

    lane = iota((rows, width), 1)
    column = iota((1, width), 1)

    def moved(value, distance):
        if distance == 0:
            return value
        turned = pltpu.roll(value, -distance % width, 1)
        here = lane[: value.shape[0]] + distance
        return jnp.where((here >= 0) & (here < width), turned, jnp.zeros_like(turned))

    def one_visit(visit, unused):
        fetch(visit).wait()
        sums[...] = jnp.zeros_like(sums)
        first = visit * per_visit
        for place in range(per_visit):
            tile = first + place
            pixels = tiles_ref[tile]
            for side in range(2):
                for fine in range(4):
                    part = moved(pixels, -1 - fine if side else fine)
                    top = fine * FINE_ROWS
                    shifted[place, side, top + 16 : top + 64, :width] = part[:48]
                    shifted[place, side, top : top + 48, width:] = part[16:]
                for coarse in range(COARSE):
                    for pair in range(2):
                        vector = pl.ds(
                            tile * VECTORS + (side * COARSE + coarse) * 2 + pair, 1
                        )
                        spread = jnp.broadcast_to(kernels[vector, :], (BLOCK, width))
                        turned = pltpu.roll(spread, 0, 1, stride=1, stride_axis=0)
                        toeplitz[
                            place,
                            side,
                            coarse * BLOCK : (coarse + 1) * BLOCK,
                            pair * width : (pair + 1) * width,
                        ] = turned.astype(jnp.bfloat16)
        for place in range(per_visit):
            matched = [jnp.zeros((BLOCK, width), jnp.float32) for _ in range(2)]
            for side in range(2):
                passed = jnp.dot(
                    toeplitz[place, side],
                    shifted[place, side],
                    preferred_element_type=jnp.float32,
                )
                for part in range(2):
                    for coarse in range(COARSE):
                        matched[part] += moved(
                            passed[
                                coarse * BLOCK : (coarse + 1) * BLOCK,
                                part * width : (part + 1) * width,
                            ],
                            -4 * coarse if side else 4 * coarse,
                        )
            matches[place] = jnp.concatenate(matched, axis=0)
        for place in range(per_visit):
            tile = first + place
            offset = offset_ref[tile]
            bucket = lax.rem(patch_ref[tile] - owner + REACH + patches, patches)
            weight = weights[pl.ds(tile, 1), :]
            turned = pltpu.roll(
                matches[place] * weight, lax.rem(offset, width), 1
            )
            sums[bucket, :, :width] += jnp.where(lane >= offset, turned, 0.0)
            sums[bucket, :, width:] += jnp.where(lane < offset, turned, 0.0)
            extra[bucket, pl.ds(visit, 1), :] += jnp.concatenate(
                [
                    jnp.where(column >= offset, weight, 0.0),
                    jnp.where(column < offset, weight, 0.0),
                ],
                axis=1,
            )

        for bucket in range(SPREAD):
            for turn in range(groups):
                part = lax.rem(group + turn, groups)
                own = sums[bucket, pl.ds(pl.multiple_of(part * row_share, row_share), row_share), :]
                if slot > row_share:
                    own = jnp.concatenate(
                        [own, jnp.zeros((slot - row_share, PW), jnp.float32)], axis=0
                    )
                messages[bucket * groups + turn][
                    pl.ds(pl.multiple_of(visit * slot, slot), slot), :
                ] = own.astype(jnp.bfloat16)
        return unused

    lax.fori_loop(0, visits, one_visit, 0)

    row = iota((EXTRA, PW), 0)
    lane = iota((1, PW), 1)
    by_row = jnp.zeros((1, PW), jnp.float32)
    by_weight = jnp.full((1, PW), -1.0, jnp.float32)
    for visit in range(visits):
        band = band_ref[visit].astype(jnp.float32)
        by_row = jnp.where(lane // slot == visit, band, by_row)
        by_weight = jnp.where(
            (lane < 2 * visits) & (lax.rem(lane, visits) == visit), band, by_weight
        )
    for bucket in range(SPREAD):
        held = extra[bucket]
        high = held.astype(jnp.bfloat16).astype(jnp.float32)
        low = jnp.concatenate([held[-visits:], (held - high)[:-visits]], axis=0)
        mixed = jnp.where((row >= visits) & (row < 2 * visits), low, high)
        mixed = jnp.where(row == 2 * visits, by_row, mixed)
        mixed = jnp.where(row == 2 * visits + 1, by_weight, mixed).astype(jnp.bfloat16)
        for turn in range(groups):
            messages[bucket * groups + turn][slot * visits :, :] = mixed


def add_messages(count, row_share, messages):
    slot = slot_rows(row_share)
    depth = slot * count
    line = lax.broadcasted_iota(jnp.int32, (row_share, depth), 0)
    lane = lax.broadcasted_iota(jnp.int32, (row_share, depth), 1)
    same = (lax.rem(lane, slot) == line).astype(jnp.float32)
    band_line = lax.broadcasted_iota(jnp.int32, (8, EXTRA), 0).astype(jnp.float32)
    totals = jnp.zeros((BANDS * row_share, PW), jnp.float32)
    weight_totals = jnp.zeros((8, PW), jnp.float32)
    for message in messages:
        extra = message[depth:, :]
        bands = extra[2 * count : 2 * count + 2].astype(jnp.float32)
        pick = jnp.concatenate(
            [jnp.where(bands[:1, :depth] == float(b), same, 0.0) for b in range(BANDS)], axis=0
        ).astype(jnp.bfloat16)
        totals += jnp.dot(pick, message[:depth, :], preferred_element_type=jnp.float32)
        pick = (bands[1:, :EXTRA] == band_line).astype(jnp.bfloat16)
        weight_totals += jnp.dot(pick, extra, preferred_element_type=jnp.float32)
    return totals, weight_totals


def early_kernel(count, row_share, weight_ref, *refs):
    totals_ref, rows_ref = refs[-2:]
    totals_ref[...], rows_ref[:8] = add_messages(count, row_share, refs[:-2])
    line = lax.broadcasted_iota(jnp.int32, (8, PW), 0)
    band_weights = jnp.zeros((8, PW), jnp.float32)
    for b in range(BANDS):
        band_weights = jnp.where(line == b, weight_ref[b], band_weights)
    rows_ref[8:] = band_weights


def combine_kernel(count, totals_ref, rows_ref, *refs):
    coadd_ref, detection_ref = refs[-2:]
    row_share = coadd_ref.shape[1]
    totals, weight_totals = add_messages(count, row_share, refs[:-2])
    weight_totals = jnp.maximum(weight_totals + rows_ref[:8], 1.0)
    detection = jnp.zeros((row_share, PW), jnp.float32)
    for b in range(BANDS):
        held = pl.ds(b * row_share, row_share)
        coadd = (totals[b * row_share : (b + 1) * row_share] + totals_ref[held, :]) / (
            weight_totals[b : b + 1]
        )
        coadd_ref[b] = coadd
        detection += rows_ref[8 + b : 9 + b] * coadd
    detection_ref[...] = detection


def local(
    tiles,
    tile_patch,
    tile_offset,
    tile_weight,
    visit_band,
    coeff_index,
    coeff_table,
    row_kernels,
    column_kernels,
    band_weight,
):
    tile_count, rows, width = tiles.shape
    visits = visit_band.shape[0]
    per_visit = tile_count // visits
    basis, taps = row_kernels.shape
    patches = lax.axis_size("ra")
    groups = lax.axis_size("band")
    row_share = rows // groups
    slot = slot_rows(row_share)
    length = visits * slot + EXTRA
    smem = pl.BlockSpec(memory_space=pltpu.SMEM)

    vmem = pl.BlockSpec(memory_space=pltpu.VMEM)
    anywhere = pl.BlockSpec(memory_space=pl.ANY)
    messages = pl.pallas_call(
        functools.partial(match_kernel, patches, groups),
        in_specs=[smem] * 4 + [anywhere] * 5,
        out_specs=[vmem] * (SPREAD * groups),
        out_shape=[jax.ShapeDtypeStruct((length, PW), jnp.bfloat16)] * (SPREAD * groups),
        scratch_shapes=[
            pltpu.VMEM(coeff_table.shape[::-1], jnp.float32),
            pltpu.VMEM((1, tile_count), jnp.bfloat16),
            pltpu.VMEM((basis, taps), jnp.bfloat16),
            pltpu.VMEM((basis, taps), jnp.bfloat16),
            pltpu.VMEM((tile_count, rows, width), jnp.bfloat16),
            pltpu.VMEM((tile_count * VECTORS, width), jnp.float32),
            pltpu.VMEM((tile_count, width), jnp.float32),
            pltpu.VMEM((per_visit, 2, 4 * FINE_ROWS, 2 * width), jnp.bfloat16),
            pltpu.VMEM((per_visit, 2, COARSE * BLOCK, 2 * width), jnp.bfloat16),
            pltpu.VMEM((per_visit, rows, width), jnp.float32),
            pltpu.VMEM((SPREAD, rows, PW), jnp.float32),
            pltpu.VMEM((SPREAD, EXTRA, PW), jnp.float32),
            pltpu.SemaphoreType.DMA((visits,)),
            pltpu.SemaphoreType.DMA((4,)),
        ],
        compiler_params=pltpu.CompilerParams(vmem_limit_bytes=62 * 1024 * 1024),
        name="match_and_sum",
    )(
        tile_patch,
        tile_offset,
        coeff_index,
        visit_band,
        coeff_table.T,
        tile_weight.reshape(1, tile_count),
        row_kernels,
        column_kernels,
        tiles,
    )

    order = [(d, t) for d in range(1, REACH + 1) for t in range(groups)]
    order += [(0, t) for t in range(1, groups)]
    early = len(order)
    order += [(d, t) for d in range(-REACH, 0) for t in range(groups)]
    arrived = []
    for distance, turn in order:
        route = [
            (o * groups + g, (o + distance) % patches * groups + (g + turn) % groups)
            for o in range(patches)
            for g in range(groups)
        ]
        arrived.append(
            lax.ppermute(messages[(distance + REACH) * groups + turn], ("ra", "band"), route)
        )

    params = pltpu.CompilerParams(vmem_limit_bytes=40 * 1024 * 1024)
    first = [messages[REACH * groups]] + arrived[:early]
    totals = pl.pallas_call(
        functools.partial(early_kernel, visits, row_share),
        in_specs=[smem] + [vmem] * len(first),
        out_specs=(vmem, vmem),
        out_shape=(
            jax.ShapeDtypeStruct((BANDS * row_share, PW), jnp.float32),
            jax.ShapeDtypeStruct((16, PW), jnp.float32),
        ),
        compiler_params=params,
        name="combine_early",
    )(band_weight, *first)
    return pl.pallas_call(
        functools.partial(combine_kernel, visits),
        in_specs=[vmem] * (len(arrived) - early + 2),
        out_specs=(vmem, vmem),
        out_shape=(
            jax.ShapeDtypeStruct((BANDS, row_share, PW), jnp.float32),
            jax.ShapeDtypeStruct((row_share, PW), jnp.float32),
        ),
        compiler_params=params,
        name="combine",
    )(*totals, *arrived[early:])


def solution(mesh):
    return jax.shard_map(
        local,
        mesh=mesh,
        in_specs=(
            P(("ra", "band"), None, None),
            P(("ra", "band")),
            P(("ra", "band")),
            P(("ra", "band")),
            P(("ra", "band")),
            P(("ra", "band")),
            P(),
            P(),
            P(),
            P(),
        ),
        out_specs=(P(None, "band", "ra"), P("band", "ra")),
        check_vma=False,
    )
```

```python
import functools

import jax
import jax.numpy as jnp
from jax import lax
from jax.experimental import pallas as pl
from jax.experimental.pallas import tpu as pltpu
from jax.sharding import PartitionSpec as P

PW = 256
BANDS = 6
REACH = 2
SPREAD = 2 * REACH + 1
EXTRA = 16
BLOCK = 32
COARSE = 3
VECTORS = 16
FINE_ROWS = 64
LEAD = 6


def slot_rows(row_share):
    return max(row_share, 16)


def match_kernel(
    patches,
    groups,
    patch_ref,
    offset_ref,
    index_ref,
    band_ref,
    table_hbm,
    weight_hbm,
    rowk_hbm,
    colk_hbm,
    tiles_hbm,
    *rest,
):
    far = rest[:groups]
    cross, kept = rest[groups : groups + 2]
    (
        table_ref,
        weight_ref,
        rowk_ref,
        colk_ref,
        tiles_ref,
        kernels,
        weights,
        shifted,
        toeplitz,
        matches,
        sums,
        extra,
        arrival,
        ready,
    ) = rest[groups + 2 :]
    visits = band_ref.shape[0]
    tile_count, rows, width = tiles_ref.shape
    per_visit = tile_count // visits
    basis, taps = rowk_ref.shape
    half = taps // 2
    row_share = rows // groups
    slot = slot_rows(row_share)
    owner = lax.axis_index("ra")
    group = lax.axis_index("band")
    way = 2 * lax.rem(owner, 2) - 1

    small = [
        pltpu.make_async_copy(source, target, ready.at[place])
        for place, (source, target) in enumerate(
            (
                (table_hbm, table_ref),
                (weight_hbm, weight_ref),
                (rowk_hbm, rowk_ref),
                (colk_hbm, colk_ref),
            )
        )
    ]
    for copy in small:
        copy.start()

    def fetch(visit):
        held = pl.ds(visit * per_visit, per_visit)
        return pltpu.make_async_copy(tiles_hbm.at[held], tiles_ref.at[held], arrival.at[visit])

    for visit in range(visits):
        fetch(visit).start()

    def iota(shape, axis):
        return lax.broadcasted_iota(jnp.int32, shape, axis)

    def across(left, right, **options):
        return lax.dot_general(
            left,
            right,
            (((1,), (1,)), ((), ())),
            preferred_element_type=jnp.float32,
            **options,
        )

    extra[...] = jnp.zeros_like(extra)
    shifted[...] = jnp.zeros_like(shifted)
    eye = (iota((tile_count, tile_count), 0) == iota((tile_count, tile_count), 1)).astype(
        jnp.bfloat16
    )
    entry = iota((1, table_ref.shape[1]), 1)
    chosen = jnp.concatenate(
        [(entry == index_ref[j]).astype(jnp.float32) for j in range(tile_count)], axis=0
    )
    for copy in small:
        copy.wait()
    weights[...] = across(eye, jnp.broadcast_to(weight_ref[...], (width, tile_count)))
    coeffs = across(chosen, table_ref[...], precision=lax.Precision.HIGHEST)

    line = iota((2 * VECTORS, taps), 0)
    column = iota((2 * VECTORS, taps), 1)
    block = lax.rem(line, VECTORS) // 2
    step = 4 * lax.rem(block, COARSE) + 2 * lax.rem(line, 2) + line // VECTORS
    wanted = jnp.where(block < COARSE, half + step, half - 1 - step)
    wanted = jnp.where(lax.rem(line, VECTORS) < 4 * COARSE, wanted, -1)
    col_taps = across((wanted == column).astype(jnp.bfloat16), colk_ref[...])
    tap = iota((taps, width), 0)
    lane = iota((taps, width), 1)
    total = None
    for side in range(2):
        place = (lane == tap + LEAD + side * FINE_ROWS).astype(jnp.bfloat16)
        row_taps = jnp.dot(
            rowk_ref[...], place, preferred_element_type=jnp.float32
        ).astype(jnp.bfloat16)
        part = col_taps[side * VECTORS : (side + 1) * VECTORS]
        mix = jnp.concatenate([part * coeffs[j : j + 1] for j in range(tile_count)], axis=0)
        high = mix.astype(jnp.bfloat16)
        low = (mix - high.astype(jnp.float32)).astype(jnp.bfloat16)
        term = jnp.dot(high, row_taps, preferred_element_type=jnp.float32) + jnp.dot(
            low, row_taps, preferred_element_type=jnp.float32
        )
        total = term if total is None else total + term
    kernels[...] = total

    lane = iota((rows, width), 1)
    column = iota((1, width), 1)

    def moved(value, distance):
        if distance == 0:
            return value
        turned = pltpu.roll(value, -distance % width, 1)
        here = lane[: value.shape[0]] + distance
        return jnp.where((here >= 0) & (here < width), turned, jnp.zeros_like(turned))

    def one_visit(visit, unused):
        fetch(visit).wait()
        sums[...] = jnp.zeros_like(sums)
        first = visit * per_visit
        for place in range(per_visit):
            tile = first + place
            pixels = tiles_ref[tile]
            for side in range(2):
                for fine in range(4):
                    part = moved(pixels, -1 - fine if side else fine)
                    top = fine * FINE_ROWS
                    shifted[place, side, top + 16 : top + 64, :width] = part[:48]
                    shifted[place, side, top : top + 48, width:] = part[16:]
                for coarse in range(COARSE):
                    for pair in range(2):
                        vector = pl.ds(
                            tile * VECTORS + (side * COARSE + coarse) * 2 + pair, 1
                        )
                        spread = jnp.broadcast_to(kernels[vector, :], (BLOCK, width))
                        turned = pltpu.roll(spread, 0, 1, stride=1, stride_axis=0)
                        toeplitz[
                            place,
                            side,
                            coarse * BLOCK : (coarse + 1) * BLOCK,
                            pair * width : (pair + 1) * width,
                        ] = turned.astype(jnp.bfloat16)
        for place in range(per_visit):
            matched = [jnp.zeros((BLOCK, width), jnp.float32) for _ in range(2)]
            for side in range(2):
                passed = jnp.dot(
                    toeplitz[place, side],
                    shifted[place, side],
                    preferred_element_type=jnp.float32,
                )
                for part in range(2):
                    for coarse in range(COARSE):
                        matched[part] += moved(
                            passed[
                                coarse * BLOCK : (coarse + 1) * BLOCK,
                                part * width : (part + 1) * width,
                            ],
                            -4 * coarse if side else 4 * coarse,
                        )
            matches[place] = jnp.concatenate(matched, axis=0)
        for place in range(per_visit):
            tile = first + place
            offset = offset_ref[tile]
            bucket = lax.rem(patch_ref[tile] - owner + REACH + patches, patches)
            weight = weights[pl.ds(tile, 1), :]
            turned = pltpu.roll(
                matches[place] * weight, lax.rem(offset, width), 1
            )
            sums[bucket, :, :width] += jnp.where(lane >= offset, turned, 0.0)
            sums[bucket, :, width:] += jnp.where(lane < offset, turned, 0.0)
            extra[bucket, pl.ds(visit, 1), :] += jnp.concatenate(
                [
                    jnp.where(column >= offset, weight, 0.0),
                    jnp.where(column < offset, weight, 0.0),
                ],
                axis=1,
            )

        for turn in range(groups):
            part = lax.rem(group + turn, groups)
            own = sums[
                REACH + 2 * way, pl.ds(pl.multiple_of(part * row_share, row_share), row_share), :
            ]
            if slot > row_share:
                own = jnp.concatenate(
                    [own, jnp.zeros((slot - row_share, PW), jnp.float32)], axis=0
                )
            far[turn][pl.ds(pl.multiple_of(visit * slot, slot), slot), :] = own.astype(
                jnp.bfloat16
            )
        held = pl.ds(pl.multiple_of(visit * rows, rows), rows)
        cross[0, held, :] = sums[REACH - 2 * way].astype(jnp.bfloat16)
        cross[1, held, :] = sums[REACH - way].astype(jnp.bfloat16)
        kept[0, held, :] = sums[REACH + way].astype(jnp.bfloat16)
        kept[1, held, :] = sums[REACH].astype(jnp.bfloat16)
        return unused

    lax.fori_loop(0, visits, one_visit, 0)

    row = iota((EXTRA, PW), 0)
    lane = iota((1, PW), 1)

    def spread_bands(visit_of, limit):
        line = jnp.full((1, PW), -1.0, jnp.float32)
        for visit in range(visits):
            line = jnp.where(
                (lane < limit) & (visit_of == visit), band_ref[visit].astype(jnp.float32), line
            )
        return line

    by_slot = spread_bands(lane // slot, visits * slot)
    by_rows = spread_bands(lane // rows, visits * rows)
    by_weight = spread_bands(lax.rem(lane, visits), 2 * visits)

    def footer(bucket, by_row):
        held = extra[bucket]
        high = held.astype(jnp.bfloat16).astype(jnp.float32)
        low = jnp.concatenate([held[-visits:], (held - high)[:-visits]], axis=0)
        mixed = jnp.where((row >= visits) & (row < 2 * visits), low, high)
        mixed = jnp.where(row == 2 * visits, by_row, mixed)
        return jnp.where(row == 2 * visits + 1, by_weight, mixed).astype(jnp.bfloat16)

    for turn in range(groups):
        far[turn][slot * visits :, :] = footer(REACH + 2 * way, by_slot)
    cross[0, rows * visits :, :] = footer(REACH - 2 * way, by_rows)
    cross[1, rows * visits :, :] = footer(REACH - way, by_rows)
    kept[0, rows * visits :, :] = footer(REACH + way, by_rows)
    kept[1, rows * visits :, :] = footer(REACH, by_rows)


def add_messages(count, span, row_share, parts, messages):
    depth = span * count
    line = lax.broadcasted_iota(jnp.int32, (row_share, depth), 0)
    lane = lax.rem(lax.broadcasted_iota(jnp.int32, (row_share, depth), 1), span)
    same = [(lane == line + part * row_share).astype(jnp.float32) for part in range(parts)]
    band_line = lax.broadcasted_iota(jnp.int32, (8, EXTRA), 0).astype(jnp.float32)
    totals = jnp.zeros((parts * BANDS * row_share, PW), jnp.float32)
    weight_totals = jnp.zeros((8, PW), jnp.float32)
    for message in messages:
        extra = message[depth:, :]
        bands = extra[2 * count : 2 * count + 2].astype(jnp.float32)
        pick = jnp.concatenate(
            [
                jnp.where(bands[:1, :depth] == float(b), same[part], 0.0)
                for part in range(parts)
                for b in range(BANDS)
            ],
            axis=0,
        ).astype(jnp.bfloat16)
        totals += jnp.dot(pick, message[:depth, :], preferred_element_type=jnp.float32)
        pick = (bands[1:, :EXTRA] == band_line).astype(jnp.bfloat16)
        weight_totals += jnp.dot(pick, extra, preferred_element_type=jnp.float32)
    return totals, weight_totals


def keep_kernel(count, groups, kept_ref, totals_ref, weights_ref):
    span = (kept_ref.shape[1] - EXTRA) // count
    for place in range(2):
        totals_ref[place], weights_ref[place] = add_messages(
            count, span, span // groups, groups, (kept_ref.at[place],)
        )


def merge_kernel(count, groups, totals_ref, weights_ref, cross_ref, *refs):
    near = refs[:groups]
    home = refs[groups : 2 * groups - 1]
    own_ref, own_weight_ref, held = refs[2 * groups - 1 :]
    span = (cross_ref.shape[1] - EXTRA) // count
    row_share = span // groups
    depth = BANDS * row_share
    group = lax.axis_index("band")
    for place, messages in enumerate((near, home)):
        totals, weight_totals = add_messages(
            count, span, row_share, groups, (cross_ref.at[place],)
        )
        held[place] = totals + totals_ref[place]
        weight_totals += weights_ref[place]
        high = weight_totals.astype(jnp.bfloat16).astype(jnp.float32)
        footer = jnp.concatenate([high, weight_totals - high], axis=0).astype(jnp.bfloat16)
        for turn, message in enumerate(messages, groups - len(messages)):
            part = lax.rem(group + turn, groups)
            message[:depth, :] = held[
                place, pl.ds(pl.multiple_of(part * depth, depth), depth), :
            ].astype(jnp.bfloat16)
            message[depth:, :] = footer
    own_ref[...] = held[1, pl.ds(pl.multiple_of(group * depth, depth), depth), :]
    own_weight_ref[...] = weight_totals


def early_kernel(weight_ref, own_ref, own_weight_ref, *refs):
    messages = refs[:-2]
    totals_ref, rows_ref = refs[-2:]
    depth = own_ref.shape[0]
    totals = own_ref[...]
    weight_totals = own_weight_ref[...]
    for message in messages:
        totals += message[:depth, :].astype(jnp.float32)
        footer = message[depth:, :].astype(jnp.float32)
        weight_totals += footer[:8] + footer[8:]
    totals_ref[...] = totals
    rows_ref[:8] = weight_totals
    line = lax.broadcasted_iota(jnp.int32, (8, PW), 0)
    band_weights = jnp.zeros((8, PW), jnp.float32)
    for b in range(BANDS):
        band_weights = jnp.where(line == b, weight_ref[b], band_weights)
    rows_ref[8:] = band_weights


def combine_kernel(count, totals_ref, rows_ref, *refs):
    coadd_ref, detection_ref = refs[-2:]
    row_share = coadd_ref.shape[1]
    totals, weight_totals = add_messages(count, slot_rows(row_share), row_share, 1, refs[:-2])
    weight_totals = jnp.maximum(weight_totals + rows_ref[:8], 1.0)
    detection = jnp.zeros((row_share, PW), jnp.float32)
    for b in range(BANDS):
        held = slice(b * row_share, (b + 1) * row_share)
        coadd = (totals[held] + totals_ref[held, :]) / weight_totals[b : b + 1]
        coadd_ref[b] = coadd
        detection += rows_ref[8 + b : 9 + b] * coadd
    detection_ref[...] = detection


def local(
    tiles,
    tile_patch,
    tile_offset,
    tile_weight,
    visit_band,
    coeff_index,
    coeff_table,
    row_kernels,
    column_kernels,
    band_weight,
):
    tile_count, rows, width = tiles.shape
    visits = visit_band.shape[0]
    per_visit = tile_count // visits
    basis, taps = row_kernels.shape
    patches = lax.axis_size("ra")
    groups = lax.axis_size("band")
    row_share = rows // groups
    slot = slot_rows(row_share)
    far_shape = jax.ShapeDtypeStruct((visits * slot + EXTRA, PW), jnp.bfloat16)
    pair_shape = jax.ShapeDtypeStruct((2, visits * rows + EXTRA, PW), jnp.bfloat16)
    band_shape = jax.ShapeDtypeStruct((BANDS * row_share + EXTRA, PW), jnp.bfloat16)
    total_shape = jax.ShapeDtypeStruct((BANDS * row_share, PW), jnp.float32)
    smem = pl.BlockSpec(memory_space=pltpu.SMEM)

    vmem = pl.BlockSpec(memory_space=pltpu.VMEM)
    anywhere = pl.BlockSpec(memory_space=pl.ANY)
    *far, cross, kept = pl.pallas_call(
        functools.partial(match_kernel, patches, groups),
        in_specs=[smem] * 4 + [anywhere] * 5,
        out_specs=[vmem] * (groups + 2),
        out_shape=[far_shape] * groups + [pair_shape] * 2,
        scratch_shapes=[
            pltpu.VMEM(coeff_table.shape[::-1], jnp.float32),
            pltpu.VMEM((1, tile_count), jnp.bfloat16),
            pltpu.VMEM((basis, taps), jnp.bfloat16),
            pltpu.VMEM((basis, taps), jnp.bfloat16),
            pltpu.VMEM((tile_count, rows, width), jnp.bfloat16),
            pltpu.VMEM((tile_count * VECTORS, width), jnp.float32),
            pltpu.VMEM((tile_count, width), jnp.float32),
            pltpu.VMEM((per_visit, 2, 4 * FINE_ROWS, 2 * width), jnp.bfloat16),
            pltpu.VMEM((per_visit, 2, COARSE * BLOCK, 2 * width), jnp.bfloat16),
            pltpu.VMEM((per_visit, rows, width), jnp.float32),
            pltpu.VMEM((SPREAD, rows, PW), jnp.float32),
            pltpu.VMEM((SPREAD, EXTRA, PW), jnp.float32),
            pltpu.SemaphoreType.DMA((visits,)),
            pltpu.SemaphoreType.DMA((4,)),
        ],
        compiler_params=pltpu.CompilerParams(vmem_limit_bytes=62 * 1024 * 1024),
        name="match_and_sum",
    )(
        tile_patch,
        tile_offset,
        coeff_index,
        visit_band,
        coeff_table.T,
        tile_weight.reshape(1, tile_count),
        row_kernels,
        column_kernels,
        tiles,
    )

    def send(message, goal, turn):
        route = [
            (o * groups + g, goal(o) % patches * groups + (g + turn) % groups)
            for o in range(patches)
            for g in range(groups)
        ]
        return lax.ppermute(message, ("ra", "band"), route)

    def onward(distance):
        return lambda o: o + distance if o % 2 else o - distance

    params = pltpu.CompilerParams(vmem_limit_bytes=40 * 1024 * 1024)
    cross = send(cross, onward(-1), 0)
    far = [send(far[turn], onward(2), turn) for turn in range(groups)]
    kept = pl.pallas_call(
        functools.partial(keep_kernel, visits, groups),
        in_specs=[vmem],
        out_specs=(vmem, vmem),
        out_shape=(
            jax.ShapeDtypeStruct((2, BANDS * rows, PW), jnp.float32),
            jax.ShapeDtypeStruct((2, 8, PW), jnp.float32),
        ),
        compiler_params=params,
        name="keep",
    )(kept)
    *merged, own, own_weight = pl.pallas_call(
        functools.partial(merge_kernel, visits, groups),
        in_specs=[vmem] * 3,
        out_specs=[vmem] * (2 * groups + 1),
        out_shape=[band_shape] * (2 * groups - 1)
        + [total_shape, jax.ShapeDtypeStruct((8, PW), jnp.float32)],
        scratch_shapes=[pltpu.VMEM((2, BANDS * rows, PW), jnp.float32)],
        compiler_params=params,
        name="merge",
    )(*kept, cross)
    near = [send(merged[turn], onward(1), turn) for turn in range(groups)]
    home = [send(merged[groups - 1 + turn], onward(0), turn) for turn in range(1, groups)]
    totals = pl.pallas_call(
        early_kernel,
        in_specs=[smem] + [vmem] * (2 * groups + 1),
        out_specs=(vmem, vmem),
        out_shape=(total_shape, jax.ShapeDtypeStruct((16, PW), jnp.float32)),
        compiler_params=params,
        name="combine_early",
    )(band_weight, own, own_weight, *near, *home)
    return pl.pallas_call(
        functools.partial(combine_kernel, visits),
        in_specs=[vmem] * (groups + 2),
        out_specs=(vmem, vmem),
        out_shape=(
            jax.ShapeDtypeStruct((BANDS, row_share, PW), jnp.float32),
            jax.ShapeDtypeStruct((row_share, PW), jnp.float32),
        ),
        compiler_params=params,
        name="combine",
    )(*totals, *far)


def solution(mesh):
    return jax.shard_map(
        local,
        mesh=mesh,
        in_specs=(
            P(("ra", "band"), None, None),
            P(("ra", "band")),
            P(("ra", "band")),
            P(("ra", "band")),
            P(("ra", "band")),
            P(("ra", "band")),
            P(),
            P(),
            P(),
            P(),
        ),
        out_specs=(P(None, "band", "ra"), P("band", "ra")),
        check_vma=False,
    )
```

```python
import functools

import jax
import jax.numpy as jnp
from jax import lax
from jax.experimental import pallas as pl
from jax.experimental.pallas import tpu as pltpu
from jax.sharding import PartitionSpec as P

PW = 256
BANDS = 6
REACH = 2
SPREAD = 2 * REACH + 1
EXTRA = 16
DETECT = 10
BLOCK = 32
COARSE = 3
VECTORS = 16
FINE_ROWS = 64
LEAD = 6


def match_kernel(
    patches,
    patch_ref,
    offset_ref,
    index_ref,
    band_ref,
    detect_ref,
    table_hbm,
    weight_hbm,
    rowk_hbm,
    colk_hbm,
    tiles_hbm,
    far,
    cross,
    kept,
    table_ref,
    weight_ref,
    rowk_ref,
    colk_ref,
    tiles_ref,
    kernels,
    weights,
    shifted,
    toeplitz,
    matches,
    sums,
    extra,
    arrival,
    ready,
    ):
    visits = band_ref.shape[0]
    tile_count, rows, width = tiles_ref.shape
    per_visit = tile_count // visits
    basis, taps = rowk_ref.shape
    half = taps // 2
    owner = lax.axis_index("ra")
    way = 2 * lax.rem(owner, 2) - 1

    small = [
        pltpu.make_async_copy(source, target, ready.at[place])
        for place, (source, target) in enumerate(
            (
                (table_hbm, table_ref),
                (weight_hbm, weight_ref),
                (rowk_hbm, rowk_ref),
                (colk_hbm, colk_ref),
            )
        )
    ]
    for copy in small:
        copy.start()

    def fetch(visit):
        held = pl.ds(visit * per_visit, per_visit)
        return pltpu.make_async_copy(tiles_hbm.at[held], tiles_ref.at[held], arrival.at[visit])

    for visit in range(visits):
        fetch(visit).start()

    def iota(shape, axis):
        return lax.broadcasted_iota(jnp.int32, shape, axis)

    def across(left, right, **options):
        return lax.dot_general(
            left,
            right,
            (((1,), (1,)), ((), ())),
            preferred_element_type=jnp.float32,
            **options,
        )

    extra[...] = jnp.zeros_like(extra)
    shifted[...] = jnp.zeros_like(shifted)
    eye = (iota((tile_count, tile_count), 0) == iota((tile_count, tile_count), 1)).astype(
        jnp.bfloat16
    )
    entry = iota((1, table_ref.shape[1]), 1)
    chosen = jnp.concatenate(
        [(entry == index_ref[j]).astype(jnp.float32) for j in range(tile_count)], axis=0
    )
    for copy in small:
        copy.wait()
    weights[...] = across(eye, jnp.broadcast_to(weight_ref[...], (width, tile_count)))
    coeffs = across(chosen, table_ref[...], precision=lax.Precision.HIGHEST)

    line = iota((2 * VECTORS, taps), 0)
    column = iota((2 * VECTORS, taps), 1)
    block = lax.rem(line, VECTORS) // 2
    step = 4 * lax.rem(block, COARSE) + 2 * lax.rem(line, 2) + line // VECTORS
    wanted = jnp.where(block < COARSE, half + step, half - 1 - step)
    wanted = jnp.where(lax.rem(line, VECTORS) < 4 * COARSE, wanted, -1)
    col_taps = across((wanted == column).astype(jnp.bfloat16), colk_ref[...])
    tap = iota((taps, width), 0)
    lane = iota((taps, width), 1)
    total = None
    for side in range(2):
        place = (lane == tap + LEAD + side * FINE_ROWS).astype(jnp.bfloat16)
        row_taps = jnp.dot(
            rowk_ref[...], place, preferred_element_type=jnp.float32
        ).astype(jnp.bfloat16)
        part = col_taps[side * VECTORS : (side + 1) * VECTORS]
        mix = jnp.concatenate([part * coeffs[j : j + 1] for j in range(tile_count)], axis=0)
        high = mix.astype(jnp.bfloat16)
        low = (mix - high.astype(jnp.float32)).astype(jnp.bfloat16)
        term = jnp.dot(high, row_taps, preferred_element_type=jnp.float32) + jnp.dot(
            low, row_taps, preferred_element_type=jnp.float32
        )
        total = term if total is None else total + term
    kernels[...] = total

    lane = iota((rows, width), 1)
    column = iota((1, width), 1)

    def moved(value, distance):
        if distance == 0:
            return value
        turned = pltpu.roll(value, -distance % width, 1)
        here = lane[: value.shape[0]] + distance
        return jnp.where((here >= 0) & (here < width), turned, jnp.zeros_like(turned))

    def one_visit(visit, unused):
        fetch(visit).wait()
        sums[...] = jnp.zeros_like(sums)
        first = visit * per_visit
        for place in range(per_visit):
            tile = first + place
            pixels = tiles_ref[tile]
            for side in range(2):
                for fine in range(4):
                    part = moved(pixels, -1 - fine if side else fine)
                    top = fine * FINE_ROWS
                    shifted[place, side, top + 16 : top + 64, :width] = part[:48]
                    shifted[place, side, top : top + 48, width:] = part[16:]
                for coarse in range(COARSE):
                    for pair in range(2):
                        vector = pl.ds(
                            tile * VECTORS + (side * COARSE + coarse) * 2 + pair, 1
                        )
                        spread = jnp.broadcast_to(kernels[vector, :], (BLOCK, width))
                        turned = pltpu.roll(spread, 0, 1, stride=1, stride_axis=0)
                        toeplitz[
                            place,
                            side,
                            coarse * BLOCK : (coarse + 1) * BLOCK,
                            pair * width : (pair + 1) * width,
                        ] = turned.astype(jnp.bfloat16)
        for place in range(per_visit):
            matched = [jnp.zeros((BLOCK, width), jnp.float32) for _ in range(2)]
            for side in range(2):
                passed = jnp.dot(
                    toeplitz[place, side],
                    shifted[place, side],
                    preferred_element_type=jnp.float32,
                )
                for part in range(2):
                    for coarse in range(COARSE):
                        matched[part] += moved(
                            passed[
                                coarse * BLOCK : (coarse + 1) * BLOCK,
                                part * width : (part + 1) * width,
                            ],
                            -4 * coarse if side else 4 * coarse,
                        )
            matches[place] = jnp.concatenate(matched, axis=0)
        for place in range(per_visit):
            tile = first + place
            offset = offset_ref[tile]
            bucket = lax.rem(patch_ref[tile] - owner + REACH + patches, patches)
            weight = weights[pl.ds(tile, 1), :]
            turned = pltpu.roll(
                matches[place] * weight, lax.rem(offset, width), 1
            )
            sums[bucket, :, :width] += jnp.where(lane >= offset, turned, 0.0)
            sums[bucket, :, width:] += jnp.where(lane < offset, turned, 0.0)
            extra[bucket, pl.ds(visit, 1), :] += jnp.concatenate(
                [
                    jnp.where(column >= offset, weight, 0.0),
                    jnp.where(column < offset, weight, 0.0),
                ],
                axis=1,
            )

        held = pl.ds(pl.multiple_of(visit * rows, rows), rows)
        far[held, :] = sums[REACH + 2 * way].astype(jnp.bfloat16)
        cross[0, held, :] = sums[REACH - 2 * way].astype(jnp.bfloat16)
        cross[1, held, :] = sums[REACH - way].astype(jnp.bfloat16)
        kept[0, held, :] = sums[REACH + way].astype(jnp.bfloat16)
        kept[1, held, :] = sums[REACH].astype(jnp.bfloat16)
        return unused

    lax.fori_loop(0, visits, one_visit, 0)

    row = iota((EXTRA, PW), 0)
    lane = iota((1, PW), 1)

    def spread_bands(visit_of, limit):
        line = jnp.full((1, PW), -1.0, jnp.float32)
        for visit in range(visits):
            line = jnp.where(
                (lane < limit) & (visit_of == visit), band_ref[visit].astype(jnp.float32), line
            )
        return line

    by_row = spread_bands(lane // rows, visits * rows)
    by_weight = spread_bands(lax.rem(lane, visits), 2 * visits)
    detect = jnp.zeros((1, PW), jnp.float32)
    for b in range(BANDS):
        detect = jnp.where(lane == b, detect_ref[b], detect)

    def footer(bucket):
        held = extra[bucket]
        high = held.astype(jnp.bfloat16).astype(jnp.float32)
        low = jnp.concatenate([held[-visits:], (held - high)[:-visits]], axis=0)
        mixed = jnp.where((row >= visits) & (row < 2 * visits), low, high)
        mixed = jnp.where(row == 2 * visits, by_row, mixed)
        mixed = jnp.where(row == 2 * visits + 1, by_weight, mixed)
        rest = detect
        for place in range(DETECT, DETECT + 3):
            piece = rest.astype(jnp.bfloat16).astype(jnp.float32)
            rest = rest - piece
            mixed = jnp.where(row == place, piece, mixed)
        return mixed.astype(jnp.bfloat16)

    far[rows * visits :, :] = footer(REACH + 2 * way)
    cross[0, rows * visits :, :] = footer(REACH - 2 * way)
    cross[1, rows * visits :, :] = footer(REACH - way)
    kept[0, rows * visits :, :] = footer(REACH + way)
    kept[1, rows * visits :, :] = footer(REACH)


def add_message(count, groups, message):
    depth = message.shape[0] - EXTRA
    span = depth // count
    row_share = span // groups
    line = lax.broadcasted_iota(jnp.int32, (row_share, depth), 0)
    lane = lax.rem(lax.broadcasted_iota(jnp.int32, (row_share, depth), 1), span)
    band_line = lax.broadcasted_iota(jnp.int32, (8, EXTRA), 0).astype(jnp.float32)
    extra = message[depth:, :]
    bands = extra[2 * count : 2 * count + 2].astype(jnp.float32)
    pick = jnp.concatenate(
        [
            jnp.where(
                (lane == line + part * row_share) & (bands[:1, :depth] == float(b)), 1.0, 0.0
            )
            for part in range(groups)
            for b in range(BANDS)
        ],
        axis=0,
    ).astype(jnp.bfloat16)
    totals = jnp.dot(pick, message[:depth, :], preferred_element_type=jnp.float32)
    pick = (bands[1:, :EXTRA] == band_line).astype(jnp.bfloat16)
    return totals, jnp.dot(pick, extra, preferred_element_type=jnp.float32)


def add_banded(totals, weights, messages):
    depth = totals.shape[0]
    for message in messages:
        totals += message[:depth, :].astype(jnp.float32)
        footer = message[depth:, :].astype(jnp.float32)
        weights += footer[:8] + footer[8:]
    return totals, weights


def write_banded(message, totals, weights):
    depth = totals.shape[0]
    high = weights.astype(jnp.bfloat16).astype(jnp.float32)
    message[:depth, :] = totals.astype(jnp.bfloat16)
    message[depth:, :] = jnp.concatenate([high, weights - high], axis=0).astype(jnp.bfloat16)


def part_of(held, turn, groups):
    depth = held.shape[0] // groups
    part = lax.rem(lax.axis_index("band") + turn, groups)
    return held[pl.ds(pl.multiple_of(part * depth, depth), depth), :]


def keep_kernel(count, groups, kept_ref, totals_ref, weights_ref, detect_ref):
    for place in range(2):
        totals_ref[place], weights_ref[place] = add_message(count, groups, kept_ref.at[place])
    extra = kept_ref[0, kept_ref.shape[1] - EXTRA :, :].astype(jnp.float32)
    detect = extra[DETECT : DETECT + 1] + extra[DETECT + 1 : DETECT + 2]
    detect += extra[DETECT + 2 : DETECT + 3]
    line = lax.broadcasted_iota(jnp.int32, (8, PW), 0)
    lane = lax.broadcasted_iota(jnp.int32, (8, PW), 1)
    chosen = jnp.sum(jnp.where(line == lane, detect, 0.0), axis=1, keepdims=True)
    detect_ref[...] = jnp.broadcast_to(chosen, (8, PW))


def merge_kernel(count, groups, totals_ref, weights_ref, cross_ref, *refs):
    messages = refs[: groups - 1]
    near_ref, near_weight_ref, home_ref, home_weight_ref, held = refs[groups - 1 :]
    totals, weights = add_message(count, groups, cross_ref.at[0])
    held[...] = totals + totals_ref[0]
    weights += weights_ref[0]
    for turn, message in enumerate(messages, 1):
        write_banded(message, part_of(held, turn, groups), weights)
    near_ref[...] = part_of(held, 0, groups)
    near_weight_ref[...] = weights
    totals, weights = add_message(count, groups, cross_ref.at[1])
    home_ref[...] = totals + totals_ref[1]
    home_weight_ref[...] = weights + weights_ref[1]


def forward_kernel(
    count, groups, near_ref, near_weight_ref, home_ref, home_weight_ref, far_ref, *refs
):
    arrived = refs[: groups - 1]
    onward_ref = refs[groups - 1]
    messages = refs[groups : 2 * groups - 1]
    own_ref, own_weight_ref, held = refs[2 * groups - 1 :]
    totals, weights = add_banded(near_ref[...], near_weight_ref[...], arrived)
    write_banded(onward_ref, totals, weights)
    totals, weights = add_message(count, groups, far_ref)
    held[...] = totals + home_ref[...]
    weights += home_weight_ref[...]
    for turn, message in enumerate(messages, 1):
        write_banded(message, part_of(held, turn, groups), weights)
    own_ref[...] = part_of(held, 0, groups)
    own_weight_ref[...] = weights


def combine_kernel(detect_ref, own_ref, own_weight_ref, *refs):
    coadd_ref, detection_ref = refs[-2:]
    row_share = coadd_ref.shape[1]
    totals, weights = add_banded(own_ref[...], own_weight_ref[...], refs[:-2])
    weights = jnp.maximum(weights, 1.0)
    detection = jnp.zeros((row_share, PW), jnp.float32)
    for b in range(BANDS):
        coadd = totals[b * row_share : (b + 1) * row_share] / weights[b : b + 1]
        coadd_ref[b] = coadd
        detection += detect_ref[b : b + 1] * coadd
    detection_ref[...] = detection


def local(
    tiles,
    tile_patch,
    tile_offset,
    tile_weight,
    visit_band,
    coeff_index,
    coeff_table,
    row_kernels,
    column_kernels,
    band_weight,
):
    tile_count, rows, width = tiles.shape
    visits = visit_band.shape[0]
    per_visit = tile_count // visits
    basis, taps = row_kernels.shape
    patches = lax.axis_size("ra")
    groups = lax.axis_size("band")
    row_share = rows // groups
    length = visits * rows + EXTRA
    message_shape = jax.ShapeDtypeStruct((length, PW), jnp.bfloat16)
    pair_shape = jax.ShapeDtypeStruct((2, length, PW), jnp.bfloat16)
    band_shape = jax.ShapeDtypeStruct((BANDS * row_share + EXTRA, PW), jnp.bfloat16)
    part_shape = jax.ShapeDtypeStruct((BANDS * row_share, PW), jnp.float32)
    whole_shape = jax.ShapeDtypeStruct((BANDS * rows, PW), jnp.float32)
    weight_shape = jax.ShapeDtypeStruct((8, PW), jnp.float32)
    smem = pl.BlockSpec(memory_space=pltpu.SMEM)

    vmem = pl.BlockSpec(memory_space=pltpu.VMEM)
    anywhere = pl.BlockSpec(memory_space=pl.ANY)
    far, cross, kept = pl.pallas_call(
        functools.partial(match_kernel, patches),
        in_specs=[smem] * 5 + [anywhere] * 5,
        out_specs=[vmem] * 3,
        out_shape=[message_shape, pair_shape, pair_shape],
        scratch_shapes=[
            pltpu.VMEM(coeff_table.shape[::-1], jnp.float32),
            pltpu.VMEM((1, tile_count), jnp.bfloat16),
            pltpu.VMEM((basis, taps), jnp.bfloat16),
            pltpu.VMEM((basis, taps), jnp.bfloat16),
            pltpu.VMEM((tile_count, rows, width), jnp.bfloat16),
            pltpu.VMEM((tile_count * VECTORS, width), jnp.float32),
            pltpu.VMEM((tile_count, width), jnp.float32),
            pltpu.VMEM((per_visit, 2, 4 * FINE_ROWS, 2 * width), jnp.bfloat16),
            pltpu.VMEM((per_visit, 2, COARSE * BLOCK, 2 * width), jnp.bfloat16),
            pltpu.VMEM((per_visit, rows, width), jnp.float32),
            pltpu.VMEM((SPREAD, rows, PW), jnp.float32),
            pltpu.VMEM((SPREAD, EXTRA, PW), jnp.float32),
            pltpu.SemaphoreType.DMA((visits,)),
            pltpu.SemaphoreType.DMA((4,)),
        ],
        compiler_params=pltpu.CompilerParams(vmem_limit_bytes=62 * 1024 * 1024),
        name="match_and_sum",
    )(
        tile_patch,
        tile_offset,
        coeff_index,
        visit_band,
        band_weight,
        coeff_table.T,
        tile_weight.reshape(1, tile_count),
        row_kernels,
        column_kernels,
        tiles,
    )

    def send(message, goal, turn):
        route = [
            (o * groups + g, goal(o) % patches * groups + (g + turn) % groups)
            for o in range(patches)
            for g in range(groups)
        ]
        return lax.ppermute(message, ("ra", "band"), route)

    def onward(distance):
        return lambda o: o + distance if o % 2 else o - distance

    def local_call(kernel, name, out_shape, *operands, **options):
        return pl.pallas_call(
            kernel,
            in_specs=[vmem] * len(operands),
            out_specs=[vmem] * len(out_shape),
            out_shape=out_shape,
            compiler_params=pltpu.CompilerParams(vmem_limit_bytes=40 * 1024 * 1024),
            name=name,
            **options,
        )(*operands)

    held = [pltpu.VMEM(whole_shape.shape, jnp.float32)]
    cross = send(cross, onward(-1), 0)
    far = send(far, onward(2), 0)
    *kept, detect = local_call(
        functools.partial(keep_kernel, visits, groups),
        "keep",
        [
            jax.ShapeDtypeStruct((2,) + whole_shape.shape, jnp.float32),
            jax.ShapeDtypeStruct((2,) + weight_shape.shape, jnp.float32),
            weight_shape,
        ],
        kept,
    )
    *others, near, near_weight, home, home_weight = local_call(
        functools.partial(merge_kernel, visits, groups),
        "merge",
        [band_shape] * (groups - 1) + [part_shape, weight_shape, whole_shape, weight_shape],
        *kept,
        cross,
        scratch_shapes=held,
    )
    others = [send(others[turn - 1], onward(0), turn) for turn in range(1, groups)]
    near, *others, own, own_weight = local_call(
        functools.partial(forward_kernel, visits, groups),
        "forward",
        [band_shape] * groups + [part_shape, weight_shape],
        near,
        near_weight,
        home,
        home_weight,
        far,
        *others,
        scratch_shapes=held,
    )
    near = send(near, onward(1), 0)
    others = [send(others[turn - 1], onward(0), turn) for turn in range(1, groups)]
    return local_call(
        combine_kernel,
        "combine",
        (
            jax.ShapeDtypeStruct((BANDS, row_share, PW), jnp.float32),
            jax.ShapeDtypeStruct((row_share, PW), jnp.float32),
        ),
        detect,
        own,
        own_weight,
        near,
        *others,
    )


def solution(mesh):
    return jax.shard_map(
        local,
        mesh=mesh,
        in_specs=(
            P(("ra", "band"), None, None),
            P(("ra", "band")),
            P(("ra", "band")),
            P(("ra", "band")),
            P(("ra", "band")),
            P(("ra", "band")),
            P(),
            P(),
            P(),
            P(),
        ),
        out_specs=(P(None, "band", "ra"), P("band", "ra")),
        check_vma=False,
    )
```

```python
import functools

import jax
import jax.numpy as jnp
from jax import lax
from jax.experimental import pallas as pl
from jax.experimental.pallas import tpu as pltpu
from jax.sharding import PartitionSpec as P

PW = 256
BANDS = 6
REACH = 2
SPREAD = 2 * REACH + 1
EXTRA = 16
DETECT = 10
BLOCK = 32
COARSE = 3
VECTORS = 16
FINE_ROWS = 64
LEAD = 6


def match_kernel(
    patches,
    patch_ref,
    offset_ref,
    index_ref,
    band_ref,
    detect_ref,
    table_hbm,
    weight_hbm,
    rowk_hbm,
    colk_hbm,
    tiles_hbm,
    cross,
    kept,
    table_ref,
    weight_ref,
    rowk_ref,
    colk_ref,
    tiles_ref,
    kernels,
    weights,
    shifted,
    toeplitz,
    matches,
    sums,
    extra,
    arrival,
    ready,
):
    visits = band_ref.shape[0]
    tile_count, rows, width = tiles_ref.shape
    per_visit = tile_count // visits
    basis, taps = rowk_ref.shape
    half = taps // 2
    owner = lax.axis_index("ra")
    way = 2 * lax.rem(owner, 2) - 1

    small = [
        pltpu.make_async_copy(source, target, ready.at[place])
        for place, (source, target) in enumerate(
            (
                (table_hbm, table_ref),
                (weight_hbm, weight_ref),
                (rowk_hbm, rowk_ref),
                (colk_hbm, colk_ref),
            )
        )
    ]
    for copy in small:
        copy.start()

    def fetch(visit):
        held = pl.ds(visit * per_visit, per_visit)
        return pltpu.make_async_copy(tiles_hbm.at[held], tiles_ref.at[held], arrival.at[visit])

    for visit in range(visits):
        fetch(visit).start()

    def iota(shape, axis):
        return lax.broadcasted_iota(jnp.int32, shape, axis)

    def across(left, right, **options):
        return lax.dot_general(
            left,
            right,
            (((1,), (1,)), ((), ())),
            preferred_element_type=jnp.float32,
            **options,
        )

    extra[...] = jnp.zeros_like(extra)
    shifted[...] = jnp.zeros_like(shifted)
    eye = (iota((tile_count, tile_count), 0) == iota((tile_count, tile_count), 1)).astype(
        jnp.bfloat16
    )
    entry = iota((1, table_ref.shape[1]), 1)
    chosen = jnp.concatenate(
        [(entry == index_ref[j]).astype(jnp.float32) for j in range(tile_count)], axis=0
    )
    for copy in small:
        copy.wait()
    weights[...] = across(eye, jnp.broadcast_to(weight_ref[...], (width, tile_count)))
    coeffs = across(chosen, table_ref[...], precision=lax.Precision.HIGHEST)

    line = iota((2 * VECTORS, taps), 0)
    column = iota((2 * VECTORS, taps), 1)
    block = lax.rem(line, VECTORS) // 2
    step = 4 * lax.rem(block, COARSE) + 2 * lax.rem(line, 2) + line // VECTORS
    wanted = jnp.where(block < COARSE, half + step, half - 1 - step)
    wanted = jnp.where(lax.rem(line, VECTORS) < 4 * COARSE, wanted, -1)
    col_taps = across((wanted == column).astype(jnp.bfloat16), colk_ref[...])
    tap = iota((taps, width), 0)
    lane = iota((taps, width), 1)
    total = None
    for side in range(2):
        place = (lane == tap + LEAD + side * FINE_ROWS).astype(jnp.bfloat16)
        row_taps = jnp.dot(
            rowk_ref[...], place, preferred_element_type=jnp.float32
        ).astype(jnp.bfloat16)
        part = col_taps[side * VECTORS : (side + 1) * VECTORS]
        mix = jnp.concatenate([part * coeffs[j : j + 1] for j in range(tile_count)], axis=0)
        high = mix.astype(jnp.bfloat16)
        low = (mix - high.astype(jnp.float32)).astype(jnp.bfloat16)
        term = jnp.dot(high, row_taps, preferred_element_type=jnp.float32) + jnp.dot(
            low, row_taps, preferred_element_type=jnp.float32
        )
        total = term if total is None else total + term
    kernels[...] = total

    lane = iota((rows, width), 1)
    column = iota((1, width), 1)

    def moved(value, distance):
        if distance == 0:
            return value
        turned = pltpu.roll(value, -distance % width, 1)
        here = lane[: value.shape[0]] + distance
        return jnp.where((here >= 0) & (here < width), turned, jnp.zeros_like(turned))

    def one_visit(visit, unused):
        fetch(visit).wait()
        sums[...] = jnp.zeros_like(sums)
        first = visit * per_visit
        for place in range(per_visit):
            tile = first + place
            pixels = tiles_ref[tile]
            for side in range(2):
                for fine in range(4):
                    part = moved(pixels, -1 - fine if side else fine)
                    top = fine * FINE_ROWS
                    shifted[place, side, top + 16 : top + 64, :width] = part[:48]
                    shifted[place, side, top : top + 48, width:] = part[16:]
                for coarse in range(COARSE):
                    for pair in range(2):
                        vector = pl.ds(
                            tile * VECTORS + (side * COARSE + coarse) * 2 + pair, 1
                        )
                        spread = jnp.broadcast_to(kernels[vector, :], (BLOCK, width))
                        turned = pltpu.roll(spread, 0, 1, stride=1, stride_axis=0)
                        toeplitz[
                            place,
                            side,
                            coarse * BLOCK : (coarse + 1) * BLOCK,
                            pair * width : (pair + 1) * width,
                        ] = turned.astype(jnp.bfloat16)
        for place in range(per_visit):
            matched = [jnp.zeros((BLOCK, width), jnp.float32) for _ in range(2)]
            for side in range(2):
                passed = jnp.dot(
                    toeplitz[place, side],
                    shifted[place, side],
                    preferred_element_type=jnp.float32,
                )
                for part in range(2):
                    for coarse in range(COARSE):
                        matched[part] += moved(
                            passed[
                                coarse * BLOCK : (coarse + 1) * BLOCK,
                                part * width : (part + 1) * width,
                            ],
                            -4 * coarse if side else 4 * coarse,
                        )
            matches[place] = jnp.concatenate(matched, axis=0)
        for place in range(per_visit):
            tile = first + place
            offset = offset_ref[tile]
            bucket = lax.rem(patch_ref[tile] - owner + REACH + patches, patches)
            weight = weights[pl.ds(tile, 1), :]
            turned = pltpu.roll(
                matches[place] * weight, lax.rem(offset, width), 1
            )
            sums[bucket, :, :width] += jnp.where(lane >= offset, turned, 0.0)
            sums[bucket, :, width:] += jnp.where(lane < offset, turned, 0.0)
            extra[bucket, pl.ds(visit, 1), :] += jnp.concatenate(
                [
                    jnp.where(column >= offset, weight, 0.0),
                    jnp.where(column < offset, weight, 0.0),
                ],
                axis=1,
            )

        held = pl.ds(pl.multiple_of(visit * rows, rows), rows)
        kept[2, held, :] = sums[REACH + 2 * way].astype(jnp.bfloat16)
        cross[0, held, :] = sums[REACH - 2 * way].astype(jnp.bfloat16)
        cross[1, held, :] = sums[REACH - way].astype(jnp.bfloat16)
        kept[0, held, :] = sums[REACH + way].astype(jnp.bfloat16)
        kept[1, held, :] = sums[REACH].astype(jnp.bfloat16)
        return unused

    lax.fori_loop(0, visits, one_visit, 0)

    row = iota((EXTRA, PW), 0)
    lane = iota((1, PW), 1)

    def spread_bands(visit_of, limit):
        line = jnp.full((1, PW), -1.0, jnp.float32)
        for visit in range(visits):
            line = jnp.where(
                (lane < limit) & (visit_of == visit), band_ref[visit].astype(jnp.float32), line
            )
        return line

    by_row = spread_bands(lane // rows, visits * rows)
    by_weight = spread_bands(lax.rem(lane, visits), 2 * visits)
    detect = jnp.zeros((1, PW), jnp.float32)
    for b in range(BANDS):
        detect = jnp.where(lane == b, detect_ref[b], detect)

    def footer(bucket):
        held = extra[bucket]
        high = held.astype(jnp.bfloat16).astype(jnp.float32)
        low = jnp.concatenate([held[-visits:], (held - high)[:-visits]], axis=0)
        mixed = jnp.where((row >= visits) & (row < 2 * visits), low, high)
        mixed = jnp.where(row == 2 * visits, by_row, mixed)
        mixed = jnp.where(row == 2 * visits + 1, by_weight, mixed)
        rest = detect
        for place in range(DETECT, DETECT + 3):
            piece = rest.astype(jnp.bfloat16).astype(jnp.float32)
            rest = rest - piece
            mixed = jnp.where(row == place, piece, mixed)
        return mixed.astype(jnp.bfloat16)

    kept[2, rows * visits :, :] = footer(REACH + 2 * way)
    cross[0, rows * visits :, :] = footer(REACH - 2 * way)
    cross[1, rows * visits :, :] = footer(REACH - way)
    kept[0, rows * visits :, :] = footer(REACH + way)
    kept[1, rows * visits :, :] = footer(REACH)


def add_message(count, groups, message):
    depth = message.shape[0] - EXTRA
    span = depth // count
    row_share = span // groups
    line = lax.broadcasted_iota(jnp.int32, (row_share, depth), 0)
    lane = lax.rem(lax.broadcasted_iota(jnp.int32, (row_share, depth), 1), span)
    band_line = lax.broadcasted_iota(jnp.int32, (8, EXTRA), 0).astype(jnp.float32)
    extra = message[depth:, :]
    bands = extra[2 * count : 2 * count + 2].astype(jnp.float32)
    pick = jnp.concatenate(
        [
            jnp.where(
                (lane == line + part * row_share) & (bands[:1, :depth] == float(b)), 1.0, 0.0
            )
            for part in range(groups)
            for b in range(BANDS)
        ],
        axis=0,
    ).astype(jnp.bfloat16)
    totals = jnp.dot(pick, message[:depth, :], preferred_element_type=jnp.float32)
    pick = (bands[1:, :EXTRA] == band_line).astype(jnp.bfloat16)
    return totals, jnp.dot(pick, extra, preferred_element_type=jnp.float32)


def add_banded(totals, weights, messages):
    depth = totals.shape[0]
    for message in messages:
        totals += message[:depth, :].astype(jnp.float32)
        footer = message[depth:, :].astype(jnp.float32)
        weights += footer[:8] + footer[8:]
    return totals, weights


def write_banded(message, totals, weights):
    depth = totals.shape[0]
    high = weights.astype(jnp.bfloat16).astype(jnp.float32)
    message[:depth, :] = totals.astype(jnp.bfloat16)
    message[depth:, :] = jnp.concatenate([high, weights - high], axis=0).astype(jnp.bfloat16)


def part_of(held, turn, groups):
    depth = held.shape[0] // groups
    part = lax.rem(lax.axis_index("band") + turn, groups)
    return held[pl.ds(pl.multiple_of(part * depth, depth), depth), :]


def keep_kernel(count, groups, kept_ref, totals_ref, weights_ref, detect_ref, far_ref):
    far_ref[...] = kept_ref[2]
    for place in range(2):
        totals_ref[place], weights_ref[place] = add_message(count, groups, kept_ref.at[place])
    extra = kept_ref[0, kept_ref.shape[1] - EXTRA :, :].astype(jnp.float32)
    detect = extra[DETECT : DETECT + 1] + extra[DETECT + 1 : DETECT + 2]
    detect += extra[DETECT + 2 : DETECT + 3]
    line = lax.broadcasted_iota(jnp.int32, (8, PW), 0)
    lane = lax.broadcasted_iota(jnp.int32, (8, PW), 1)
    chosen = jnp.sum(jnp.where(line == lane, detect, 0.0), axis=1, keepdims=True)
    detect_ref[...] = jnp.broadcast_to(chosen, (8, PW))


def near_kernel(count, groups, totals_ref, weights_ref, cross_ref, *refs):
    messages = refs[: groups - 1]
    near_ref, near_weight_ref, held = refs[groups - 1 :]
    totals, weights = add_message(count, groups, cross_ref.at[0])
    held[...] = totals + totals_ref[0]
    weights += weights_ref[0]
    for turn, message in enumerate(messages, 1):
        write_banded(message, part_of(held, turn, groups), weights)
    near_ref[...] = part_of(held, 0, groups)
    near_weight_ref[...] = weights


def merge_kernel(
    count,
    groups,
    after_ref,
    totals_ref,
    weights_ref,
    far_in_ref,
    cross_ref,
    home_ref,
    home_weight_ref,
    far_ref,
    rest_ref,
):
    far_ref[...] = far_in_ref[: far_ref.shape[0]]
    rest_ref[...] = far_in_ref[far_ref.shape[0] :]
    totals, weights = add_message(count, groups, cross_ref.at[1])
    home_ref[...] = totals + totals_ref[1]
    home_weight_ref[...] = weights + weights_ref[1]


def forward_kernel(near_ref, near_weight_ref, *refs):
    totals, weights = add_banded(near_ref[...], near_weight_ref[...], refs[:-2])
    write_banded(refs[-2], totals, weights)
    refs[-1][...] = weights


def home_kernel(count, groups, after_ref, home_ref, home_weight_ref, top_ref, rest_ref, *refs):
    messages = refs[: groups - 1]
    own_ref, own_weight_ref, held, far_ref = refs[groups - 1 :]
    far_ref[: top_ref.shape[0]] = top_ref[...]
    far_ref[top_ref.shape[0] :] = rest_ref[...]
    totals, weights = add_message(count, groups, far_ref)
    held[...] = totals + home_ref[...]
    weights += home_weight_ref[...]
    for turn, message in enumerate(messages, 1):
        write_banded(message, part_of(held, turn, groups), weights)
    own_ref[...] = part_of(held, 0, groups)
    own_weight_ref[...] = weights


def combine_kernel(detect_ref, own_ref, own_weight_ref, *refs):
    coadd_ref, detection_ref = refs[-2:]
    row_share = coadd_ref.shape[1]
    totals, weights = add_banded(own_ref[...], own_weight_ref[...], refs[:-2])
    weights = jnp.maximum(weights, 1.0)
    detection = jnp.zeros((row_share, PW), jnp.float32)
    for b in range(BANDS):
        coadd = totals[b * row_share : (b + 1) * row_share] / weights[b : b + 1]
        coadd_ref[b] = coadd
        detection += detect_ref[b : b + 1] * coadd
    detection_ref[...] = detection


def local(
    tiles,
    tile_patch,
    tile_offset,
    tile_weight,
    visit_band,
    coeff_index,
    coeff_table,
    row_kernels,
    column_kernels,
    band_weight,
):
    tile_count, rows, width = tiles.shape
    visits = visit_band.shape[0]
    per_visit = tile_count // visits
    basis, taps = row_kernels.shape
    patches = lax.axis_size("ra")
    groups = lax.axis_size("band")
    row_share = rows // groups
    length = visits * rows + EXTRA
    message_shape = jax.ShapeDtypeStruct((length, PW), jnp.bfloat16)
    band_shape = jax.ShapeDtypeStruct((BANDS * row_share + EXTRA, PW), jnp.bfloat16)
    part_shape = jax.ShapeDtypeStruct((BANDS * row_share, PW), jnp.float32)
    whole_shape = jax.ShapeDtypeStruct((BANDS * rows, PW), jnp.float32)
    weight_shape = jax.ShapeDtypeStruct((8, PW), jnp.float32)
    smem = pl.BlockSpec(memory_space=pltpu.SMEM)

    vmem = pl.BlockSpec(memory_space=pltpu.VMEM)
    anywhere = pl.BlockSpec(memory_space=pl.ANY)
    cross, kept = pl.pallas_call(
        functools.partial(match_kernel, patches),
        in_specs=[smem] * 5 + [anywhere] * 5,
        out_specs=[vmem] * 2,
        out_shape=[
            jax.ShapeDtypeStruct((2,) + message_shape.shape, jnp.bfloat16),
            jax.ShapeDtypeStruct((3,) + message_shape.shape, jnp.bfloat16),
        ],
        scratch_shapes=[
            pltpu.VMEM(coeff_table.shape[::-1], jnp.float32),
            pltpu.VMEM((1, tile_count), jnp.bfloat16),
            pltpu.VMEM((basis, taps), jnp.bfloat16),
            pltpu.VMEM((basis, taps), jnp.bfloat16),
            pltpu.VMEM((tile_count, rows, width), jnp.bfloat16),
            pltpu.VMEM((tile_count * VECTORS, width), jnp.float32),
            pltpu.VMEM((tile_count, width), jnp.float32),
            pltpu.VMEM((per_visit, 2, 4 * FINE_ROWS, 2 * width), jnp.bfloat16),
            pltpu.VMEM((per_visit, 2, COARSE * BLOCK, 2 * width), jnp.bfloat16),
            pltpu.VMEM((per_visit, rows, width), jnp.float32),
            pltpu.VMEM((SPREAD, rows, PW), jnp.float32),
            pltpu.VMEM((SPREAD, EXTRA, PW), jnp.float32),
            pltpu.SemaphoreType.DMA((visits,)),
            pltpu.SemaphoreType.DMA((4,)),
        ],
        compiler_params=pltpu.CompilerParams(vmem_limit_bytes=62 * 1024 * 1024),
        name="match_and_sum",
    )(
        tile_patch,
        tile_offset,
        coeff_index,
        visit_band,
        band_weight,
        coeff_table.T,
        tile_weight.reshape(1, tile_count),
        row_kernels,
        column_kernels,
        tiles,
    )

    def send(message, goal, turn):
        route = [
            (o * groups + g, goal(o) % patches * groups + (g + turn) % groups)
            for o in range(patches)
            for g in range(groups)
        ]
        return lax.ppermute(message, ("ra", "band"), route)

    def onward(distance):
        return lambda o: o + distance if o % 2 else o - distance

    def local_call(kernel, name, out_shape, *operands, **options):
        return pl.pallas_call(
            kernel,
            in_specs=[vmem] * len(operands),
            out_specs=[vmem] * len(out_shape),
            out_shape=out_shape,
            compiler_params=pltpu.CompilerParams(vmem_limit_bytes=40 * 1024 * 1024),
            name=name,
            **options,
        )(*operands)

    held = [pltpu.VMEM(whole_shape.shape, jnp.float32)]
    cross = send(cross, onward(-1), 0)
    *kept, detect, far = local_call(
        functools.partial(keep_kernel, visits, groups),
        "keep",
        [
            jax.ShapeDtypeStruct((2,) + whole_shape.shape, jnp.float32),
            jax.ShapeDtypeStruct((2,) + weight_shape.shape, jnp.float32),
            weight_shape,
            message_shape,
        ],
        kept,
    )
    *others, near, near_weight = local_call(
        functools.partial(near_kernel, visits, groups),
        "near",
        [band_shape] * (groups - 1) + [part_shape, weight_shape],
        *kept,
        cross,
        scratch_shapes=held,
    )
    others = [send(others[turn - 1], onward(0), turn) for turn in range(1, groups)]
    home, home_weight, *far = local_call(
        functools.partial(merge_kernel, visits, groups),
        "merge",
        [
            whole_shape,
            weight_shape,
            jax.ShapeDtypeStruct((length // 32 * 16 + EXTRA, PW), jnp.bfloat16),
            jax.ShapeDtypeStruct((length - length // 32 * 16 - EXTRA, PW), jnp.bfloat16),
        ],
        near_weight,
        *kept,
        far,
        cross,
    )
    far = [send(piece, onward(2), 0) for piece in far]
    near, after = local_call(
        forward_kernel,
        "forward",
        [band_shape, weight_shape],
        near,
        near_weight,
        *others,
        cost_estimate=pl.CostEstimate(flops=0, bytes_accessed=1 << 26, transcendentals=0),
    )
    near = send(near, onward(1), 0)
    *others, own, own_weight = local_call(
        functools.partial(home_kernel, visits, groups),
        "home",
        [band_shape] * (groups - 1) + [part_shape, weight_shape],
        after,
        home,
        home_weight,
        *far,
        scratch_shapes=held + [pltpu.VMEM(message_shape.shape, jnp.bfloat16)],
    )
    others = [send(others[turn - 1], onward(0), turn) for turn in range(1, groups)]
    return local_call(
        combine_kernel,
        "combine",
        (
            jax.ShapeDtypeStruct((BANDS, row_share, PW), jnp.float32),
            jax.ShapeDtypeStruct((row_share, PW), jnp.float32),
        ),
        detect,
        own,
        own_weight,
        near,
        *others,
    )


def solution(mesh):
    return jax.shard_map(
        local,
        mesh=mesh,
        in_specs=(
            P(("ra", "band"), None, None),
            P(("ra", "band")),
            P(("ra", "band")),
            P(("ra", "band")),
            P(("ra", "band")),
            P(("ra", "band")),
            P(),
            P(),
            P(),
            P(),
        ),
        out_specs=(P(None, "band", "ra"), P("band", "ra")),
        check_vma=False,
    )
```

```python
import functools

import jax
import jax.numpy as jnp
from jax import lax
from jax.experimental import pallas as pl
from jax.experimental.pallas import tpu as pltpu
from jax.sharding import PartitionSpec as P

PW = 256
BANDS = 6
REACH = 2
SPREAD = 2 * REACH + 1
EXTRA = 16
BLOCK = 32
COARSE = 3
VECTORS = 16
FINE_ROWS = 64
LEAD = 6


def slot_rows(row_share):
    return max(row_share, 16)


def match_kernel(
    patches,
    groups,
    patch_ref,
    offset_ref,
    index_ref,
    band_ref,
    table_hbm,
    weight_hbm,
    rowk_hbm,
    colk_hbm,
    tiles_hbm,
    *rest,
):
    messages = rest[: SPREAD * groups]
    (
        table_ref,
        weight_ref,
        rowk_ref,
        colk_ref,
        tiles_ref,
        kernels,
        weights,
        shifted,
        toeplitz,
        matches,
        sums,
        extra,
        arrival,
        ready,
    ) = rest[SPREAD * groups :]
    visits = band_ref.shape[0]
    tile_count, rows, width = tiles_ref.shape
    per_visit = tile_count // visits
    basis, taps = rowk_ref.shape
    half = taps // 2
    row_share = rows // groups
    slot = slot_rows(row_share)
    owner = lax.axis_index("ra")
    group = lax.axis_index("band")

    small = [
        pltpu.make_async_copy(source, target, ready.at[place])
        for place, (source, target) in enumerate(
            (
                (table_hbm, table_ref),
                (weight_hbm, weight_ref),
                (rowk_hbm, rowk_ref),
                (colk_hbm, colk_ref),
            )
        )
    ]
    for copy in small:
        copy.start()

    fetch = pltpu.make_async_copy(tiles_hbm, tiles_ref, arrival)
    fetch.start()

    def iota(shape, axis):
        return lax.broadcasted_iota(jnp.int32, shape, axis)

    def across(left, right, **options):
        return lax.dot_general(
            left,
            right,
            (((1,), (1,)), ((), ())),
            preferred_element_type=jnp.float32,
            **options,
        )

    extra[...] = jnp.zeros_like(extra)
    shifted[...] = jnp.zeros_like(shifted)
    eye = (iota((8 * tile_count, tile_count), 0) // 8 == iota((8 * tile_count, tile_count), 1))
    entry = iota((1, table_ref.shape[1]), 1)
    chosen = jnp.concatenate(
        [(entry == index_ref[j]).astype(jnp.float32) for j in range(tile_count)], axis=0
    )
    for copy in small:
        copy.wait()
    fetch.wait()
    weights[...] = across(
        eye.astype(jnp.bfloat16), jnp.broadcast_to(weight_ref[...], (width, tile_count))
    ).reshape(weights.shape)
    coeffs = across(chosen, table_ref[...], precision=lax.Precision.HIGHEST)

    line = iota((2 * VECTORS, taps), 0)
    column = iota((2 * VECTORS, taps), 1)
    block = lax.rem(line, VECTORS) // 2
    step = 4 * lax.rem(block, COARSE) + 2 * lax.rem(line, 2) + line // VECTORS
    wanted = jnp.where(block < COARSE, half + step, half - 1 - step)
    wanted = jnp.where(lax.rem(line, VECTORS) < 4 * COARSE, wanted, -1)
    col_taps = across((wanted == column).astype(jnp.bfloat16), colk_ref[...])
    tap = iota((taps, width), 0)
    lane = iota((taps, width), 1)
    total = None
    for side in range(2):
        place = (lane == tap + LEAD + side * FINE_ROWS).astype(jnp.bfloat16)
        row_taps = jnp.dot(
            rowk_ref[...], place, preferred_element_type=jnp.float32
        ).astype(jnp.bfloat16)
        part = col_taps[side * VECTORS : (side + 1) * VECTORS]
        mix = jnp.concatenate([part * coeffs[j : j + 1] for j in range(tile_count)], axis=0)
        high = mix.astype(jnp.bfloat16)
        low = (mix - high.astype(jnp.float32)).astype(jnp.bfloat16)
        term = jnp.dot(high, row_taps, preferred_element_type=jnp.float32) + jnp.dot(
            low, row_taps, preferred_element_type=jnp.float32
        )
        total = term if total is None else total + term
    kernels[...] = total.reshape(kernels.shape)

    lane = iota((rows, width), 1)
    column = iota((1, width), 1)

    def moved(value, distance):
        if distance == 0:
            return value
        turned = pltpu.roll(value, -distance % width, 1)
        here = lane[: value.shape[0]] + distance
        return jnp.where((here >= 0) & (here < width), turned, jnp.zeros_like(turned))

    def build(visit, place, buffer):
        tile = visit * per_visit + place
        pixels = tiles_ref[tile]
        for side in range(2):
            for fine in range(4):
                part = moved(pixels, -1 - fine if side else fine)
                top = fine * FINE_ROWS
                shifted[buffer, place, side, top + 16 : top + 64, :width] = part[:48]
                shifted[buffer, place, side, top : top + 48, width:] = part[16:]
            for coarse in range(COARSE):
                for pair in range(2):
                    vector = (side * COARSE + coarse) * 2 + pair
                    spread = jnp.broadcast_to(
                        kernels[tile, vector : vector + 1, :], (BLOCK, width)
                    )
                    turned = pltpu.roll(spread, 0, 1, stride=1, stride_axis=0)
                    toeplitz[
                        buffer,
                        place,
                        side,
                        coarse * BLOCK : (coarse + 1) * BLOCK,
                        pair * width : (pair + 1) * width,
                    ] = turned.astype(jnp.bfloat16)

    def multiply(place, buffer):
        matched = [jnp.zeros((BLOCK, width), jnp.float32) for _ in range(2)]
        for side in range(2):
            passed = jnp.dot(
                toeplitz[buffer, place, side],
                shifted[buffer, place, side],
                preferred_element_type=jnp.float32,
            )
            for part in range(2):
                for coarse in range(COARSE):
                    matched[part] += moved(
                        passed[
                            coarse * BLOCK : (coarse + 1) * BLOCK,
                            part * width : (part + 1) * width,
                        ],
                        -4 * coarse if side else 4 * coarse,
                    )
        matches[buffer, place] = jnp.concatenate(matched, axis=0)

    def deliver(visit, buffer):
        sums[...] = jnp.zeros_like(sums)
        for place in range(per_visit):
            tile = visit * per_visit + place
            offset = offset_ref[tile]
            bucket = lax.rem(patch_ref[tile] - owner + REACH + patches, patches)
            weight = weights[tile]
            value = matches[buffer, place].reshape(rows // 8, 8, width) * weight[None]
            turned = pltpu.roll(value.reshape(rows, width), lax.rem(offset, width), 1)
            sums[bucket, :, :width] += jnp.where(lane >= offset, turned, 0.0)
            sums[bucket, :, width:] += jnp.where(lane < offset, turned, 0.0)
            extra[bucket, pl.ds(visit, 1), :] += jnp.concatenate(
                [
                    jnp.where(column >= offset, weight[:1], 0.0),
                    jnp.where(column < offset, weight[:1], 0.0),
                ],
                axis=1,
            )

        for bucket in range(SPREAD):
            for turn in range(groups):
                part = lax.rem(group + turn, groups)
                own = sums[bucket, pl.ds(pl.multiple_of(part * row_share, row_share), row_share), :]
                if slot > row_share:
                    own = jnp.concatenate(
                        [own, jnp.zeros((slot - row_share, PW), jnp.float32)], axis=0
                    )
                messages[bucket * groups + turn][
                    pl.ds(pl.multiple_of(visit * slot, slot), slot), :
                ] = own.astype(jnp.bfloat16)

    def two_visits(step, unused):
        for buffer in range(2):
            visit = 2 * step + buffer
            later = jnp.minimum(visit + 1, visits - 1)
            for place in range(per_visit):
                build(later, place, 1 - buffer)
                multiply(place, buffer)
            deliver(visit, buffer)
        return unused

    for place in range(per_visit):
        build(0, place, 0)
    lax.fori_loop(0, visits // 2, two_visits, 0)

    row = iota((EXTRA, PW), 0)
    lane = iota((1, PW), 1)
    by_row = jnp.zeros((1, PW), jnp.float32)
    by_weight = jnp.full((1, PW), -1.0, jnp.float32)
    for visit in range(visits):
        band = band_ref[visit].astype(jnp.float32)
        by_row = jnp.where(lane // slot == visit, band, by_row)
        by_weight = jnp.where(
            (lane < 2 * visits) & (lax.rem(lane, visits) == visit), band, by_weight
        )
    for bucket in range(SPREAD):
        held = extra[bucket]
        high = held.astype(jnp.bfloat16).astype(jnp.float32)
        low = jnp.concatenate([held[-visits:], (held - high)[:-visits]], axis=0)
        mixed = jnp.where((row >= visits) & (row < 2 * visits), low, high)
        mixed = jnp.where(row == 2 * visits, by_row, mixed)
        mixed = jnp.where(row == 2 * visits + 1, by_weight, mixed).astype(jnp.bfloat16)
        for turn in range(groups):
            messages[bucket * groups + turn][slot * visits :, :] = mixed


def add_messages(count, row_share, messages):
    slot = slot_rows(row_share)
    depth = slot * count
    line = lax.broadcasted_iota(jnp.int32, (row_share, depth), 0)
    lane = lax.broadcasted_iota(jnp.int32, (row_share, depth), 1)
    same = (lax.rem(lane, slot) == line).astype(jnp.float32)
    band_line = lax.broadcasted_iota(jnp.int32, (8, EXTRA), 0).astype(jnp.float32)
    totals = jnp.zeros((BANDS * row_share, PW), jnp.float32)
    weight_totals = jnp.zeros((8, PW), jnp.float32)
    for message in messages:
        extra = message[depth:, :]
        bands = extra[2 * count : 2 * count + 2].astype(jnp.float32)
        pick = jnp.concatenate(
            [jnp.where(bands[:1, :depth] == float(b), same, 0.0) for b in range(BANDS)], axis=0
        ).astype(jnp.bfloat16)
        totals += jnp.dot(pick, message[:depth, :], preferred_element_type=jnp.float32)
        pick = (bands[1:, :EXTRA] == band_line).astype(jnp.bfloat16)
        weight_totals += jnp.dot(pick, extra, preferred_element_type=jnp.float32)
    return totals, weight_totals


def early_kernel(count, row_share, weight_ref, *refs):
    totals_ref, rows_ref = refs[-2:]
    totals_ref[...], rows_ref[:8] = add_messages(count, row_share, refs[:-2])
    line = lax.broadcasted_iota(jnp.int32, (8, PW), 0)
    band_weights = jnp.zeros((8, PW), jnp.float32)
    for b in range(BANDS):
        band_weights = jnp.where(line == b, weight_ref[b], band_weights)
    rows_ref[8:] = band_weights


def combine_kernel(count, totals_ref, rows_ref, *refs):
    coadd_ref, detection_ref = refs[-2:]
    row_share = coadd_ref.shape[1]
    totals, weight_totals = add_messages(count, row_share, refs[:-2])
    weight_totals = jnp.maximum(weight_totals + rows_ref[:8], 1.0)
    detection = jnp.zeros((row_share, PW), jnp.float32)
    for b in range(BANDS):
        held = pl.ds(b * row_share, row_share)
        coadd = (totals[b * row_share : (b + 1) * row_share] + totals_ref[held, :]) / (
            weight_totals[b : b + 1]
        )
        coadd_ref[b] = coadd
        detection += rows_ref[8 + b : 9 + b] * coadd
    detection_ref[...] = detection


def local(
    tiles,
    tile_patch,
    tile_offset,
    tile_weight,
    visit_band,
    coeff_index,
    coeff_table,
    row_kernels,
    column_kernels,
    band_weight,
):
    tile_count, rows, width = tiles.shape
    visits = visit_band.shape[0]
    per_visit = tile_count // visits
    basis, taps = row_kernels.shape
    patches = lax.axis_size("ra")
    groups = lax.axis_size("band")
    row_share = rows // groups
    slot = slot_rows(row_share)
    length = visits * slot + EXTRA
    smem = pl.BlockSpec(memory_space=pltpu.SMEM)

    vmem = pl.BlockSpec(memory_space=pltpu.VMEM)
    anywhere = pl.BlockSpec(memory_space=pl.ANY)
    messages = pl.pallas_call(
        functools.partial(match_kernel, patches, groups),
        in_specs=[smem] * 4 + [anywhere] * 5,
        out_specs=[vmem] * (SPREAD * groups),
        out_shape=[jax.ShapeDtypeStruct((length, PW), jnp.bfloat16)] * (SPREAD * groups),
        scratch_shapes=[
            pltpu.VMEM(coeff_table.shape[::-1], jnp.float32),
            pltpu.VMEM((1, tile_count), jnp.bfloat16),
            pltpu.VMEM((basis, taps), jnp.bfloat16),
            pltpu.VMEM((basis, taps), jnp.bfloat16),
            pltpu.VMEM((tile_count, rows, width), jnp.bfloat16),
            pltpu.VMEM((tile_count, VECTORS, width), jnp.float32),
            pltpu.VMEM((tile_count, 8, width), jnp.float32),
            pltpu.VMEM((2, per_visit, 2, 4 * FINE_ROWS, 2 * width), jnp.bfloat16),
            pltpu.VMEM((2, per_visit, 2, COARSE * BLOCK, 2 * width), jnp.bfloat16),
            pltpu.VMEM((2, per_visit, rows, width), jnp.float32),
            pltpu.VMEM((SPREAD, rows, PW), jnp.float32),
            pltpu.VMEM((SPREAD, EXTRA, PW), jnp.float32),
            pltpu.SemaphoreType.DMA,
            pltpu.SemaphoreType.DMA((4,)),
        ],
        compiler_params=pltpu.CompilerParams(vmem_limit_bytes=62 * 1024 * 1024),
        name="match_and_sum",
    )(
        tile_patch,
        tile_offset,
        coeff_index,
        visit_band,
        coeff_table.T,
        tile_weight.reshape(1, tile_count),
        row_kernels,
        column_kernels,
        tiles,
    )

    order = [(d, t) for d in range(1, REACH + 1) for t in range(groups)]
    order += [(0, t) for t in range(1, groups)]
    early = len(order)
    order += [(d, t) for d in range(-REACH, 0) for t in range(groups)]
    arrived = []
    for distance, turn in order:
        route = [
            (o * groups + g, (o + distance) % patches * groups + (g + turn) % groups)
            for o in range(patches)
            for g in range(groups)
        ]
        arrived.append(
            lax.ppermute(messages[(distance + REACH) * groups + turn], ("ra", "band"), route)
        )

    params = pltpu.CompilerParams(vmem_limit_bytes=40 * 1024 * 1024)
    first = [messages[REACH * groups]] + arrived[:early]
    totals = pl.pallas_call(
        functools.partial(early_kernel, visits, row_share),
        in_specs=[smem] + [vmem] * len(first),
        out_specs=(vmem, vmem),
        out_shape=(
            jax.ShapeDtypeStruct((BANDS * row_share, PW), jnp.float32),
            jax.ShapeDtypeStruct((16, PW), jnp.float32),
        ),
        compiler_params=params,
        name="combine_early",
    )(band_weight, *first)
    return pl.pallas_call(
        functools.partial(combine_kernel, visits),
        in_specs=[vmem] * (len(arrived) - early + 2),
        out_specs=(vmem, vmem),
        out_shape=(
            jax.ShapeDtypeStruct((BANDS, row_share, PW), jnp.float32),
            jax.ShapeDtypeStruct((row_share, PW), jnp.float32),
        ),
        compiler_params=params,
        name="combine",
    )(*totals, *arrived[early:])


def solution(mesh):
    return jax.shard_map(
        local,
        mesh=mesh,
        in_specs=(
            P(("ra", "band"), None, None),
            P(("ra", "band")),
            P(("ra", "band")),
            P(("ra", "band")),
            P(("ra", "band")),
            P(("ra", "band")),
            P(),
            P(),
            P(),
            P(),
        ),
        out_specs=(P(None, "band", "ra"), P("band", "ra")),
        check_vma=False,
    )
```

```python
import functools

import jax
import jax.numpy as jnp
from jax import lax
from jax.experimental import pallas as pl
from jax.experimental.pallas import tpu as pltpu
from jax.sharding import PartitionSpec as P

PW = 256
BANDS = 6
REACH = 2
SPREAD = 2 * REACH + 1
EXTRA = 16
BLOCK = 32
COARSE = 3
VECTORS = 16
FINE_ROWS = 64
LEAD = 6


def slot_rows(row_share):
    return max(row_share, 16)


def match_kernel(
    patches,
    groups,
    patch_ref,
    offset_ref,
    index_ref,
    band_ref,
    table_hbm,
    weight_hbm,
    rowk_hbm,
    colk_hbm,
    tiles_hbm,
    *rest,
):
    messages = rest[: SPREAD * groups]
    (
        table_ref,
        weight_ref,
        rowk_ref,
        colk_ref,
        tiles_ref,
        kernels,
        weights,
        shifted_even,
        shifted_odd,
        toeplitz_even,
        toeplitz_odd,
        matches_even,
        matches_odd,
        sums,
        extra,
        arrival,
        ready,
    ) = rest[SPREAD * groups :]
    visits = band_ref.shape[0]
    tile_count, rows, width = tiles_ref.shape
    per_visit = tile_count // visits
    basis, taps = rowk_ref.shape
    half = taps // 2
    row_share = rows // groups
    slot = slot_rows(row_share)
    owner = lax.axis_index("ra")
    group = lax.axis_index("band")

    small = [
        pltpu.make_async_copy(source, target, ready.at[place])
        for place, (source, target) in enumerate(
            (
                (table_hbm, table_ref),
                (weight_hbm, weight_ref),
                (rowk_hbm, rowk_ref),
                (colk_hbm, colk_ref),
            )
        )
    ]
    for copy in small:
        copy.start()

    fetch = pltpu.make_async_copy(tiles_hbm, tiles_ref, arrival)
    fetch.start()

    def iota(shape, axis):
        return lax.broadcasted_iota(jnp.int32, shape, axis)

    def across(left, right, **options):
        return lax.dot_general(
            left,
            right,
            (((1,), (1,)), ((), ())),
            preferred_element_type=jnp.float32,
            **options,
        )

    extra[...] = jnp.zeros_like(extra)
    shifted = (shifted_even, shifted_odd)
    toeplitz = (toeplitz_even, toeplitz_odd)
    matches = (matches_even, matches_odd)
    for buffer in range(2):
        shifted[buffer][...] = jnp.zeros_like(shifted[buffer])
    eye = (iota((8 * tile_count, tile_count), 0) // 8 == iota((8 * tile_count, tile_count), 1))
    entry = iota((1, table_ref.shape[1]), 1)
    chosen = jnp.concatenate(
        [(entry == index_ref[j]).astype(jnp.float32) for j in range(tile_count)], axis=0
    )
    for copy in small:
        copy.wait()
    fetch.wait()
    weights[...] = across(
        eye.astype(jnp.bfloat16), jnp.broadcast_to(weight_ref[...], (width, tile_count))
    ).reshape(weights.shape)
    coeffs = across(chosen, table_ref[...], precision=lax.Precision.HIGHEST)

    line = iota((2 * VECTORS, taps), 0)
    column = iota((2 * VECTORS, taps), 1)
    block = lax.rem(line, VECTORS) // 2
    step = 4 * lax.rem(block, COARSE) + 2 * lax.rem(line, 2) + line // VECTORS
    wanted = jnp.where(block < COARSE, half + step, half - 1 - step)
    wanted = jnp.where(lax.rem(line, VECTORS) < 4 * COARSE, wanted, -1)
    col_taps = across((wanted == column).astype(jnp.bfloat16), colk_ref[...])
    tap = iota((taps, width), 0)
    lane = iota((taps, width), 1)
    total = None
    for side in range(2):
        place = (lane == tap + LEAD + side * FINE_ROWS).astype(jnp.bfloat16)
        row_taps = jnp.dot(
            rowk_ref[...], place, preferred_element_type=jnp.float32
        ).astype(jnp.bfloat16)
        part = col_taps[side * VECTORS : (side + 1) * VECTORS]
        mix = jnp.concatenate([part * coeffs[j : j + 1] for j in range(tile_count)], axis=0)
        high = mix.astype(jnp.bfloat16)
        low = (mix - high.astype(jnp.float32)).astype(jnp.bfloat16)
        term = jnp.dot(high, row_taps, preferred_element_type=jnp.float32) + jnp.dot(
            low, row_taps, preferred_element_type=jnp.float32
        )
        total = term if total is None else total + term
    kernels[...] = total.reshape(kernels.shape)

    lane = iota((rows, width), 1)
    column = iota((1, width), 1)

    def moved(value, distance):
        if distance == 0:
            return value
        turned = pltpu.roll(value, -distance % width, 1)
        here = lane[: value.shape[0]] + distance
        return jnp.where((here >= 0) & (here < width), turned, jnp.zeros_like(turned))

    def build(visit, place, buffer):
        tile = visit * per_visit + place
        pixels = tiles_ref[tile]
        for side in range(2):
            for fine in range(4):
                part = moved(pixels, -1 - fine if side else fine)
                top = fine * FINE_ROWS
                shifted[buffer][place, side, top + 16 : top + 64, :width] = part[:48]
                shifted[buffer][place, side, top : top + 48, width:] = part[16:]
            for coarse in range(COARSE):
                for pair in range(2):
                    vector = (side * COARSE + coarse) * 2 + pair
                    spread = jnp.broadcast_to(
                        kernels[tile, vector : vector + 1, :], (BLOCK, width)
                    )
                    turned = pltpu.roll(spread, 0, 1, stride=1, stride_axis=0)
                    toeplitz[buffer][
                        place,
                        side,
                        coarse * BLOCK : (coarse + 1) * BLOCK,
                        pair * width : (pair + 1) * width,
                    ] = turned.astype(jnp.bfloat16)

    def multiply(place, buffer):
        matched = [jnp.zeros((BLOCK, width), jnp.float32) for _ in range(2)]
        for side in range(2):
            passed = jnp.dot(
                toeplitz[buffer][place, side],
                shifted[buffer][place, side],
                preferred_element_type=jnp.float32,
            )
            for part in range(2):
                for coarse in range(COARSE):
                    matched[part] += moved(
                        passed[
                            coarse * BLOCK : (coarse + 1) * BLOCK,
                            part * width : (part + 1) * width,
                        ],
                        -4 * coarse if side else 4 * coarse,
                    )
        matches[buffer][place] = jnp.concatenate(matched, axis=0)

    def deliver(visit, buffer):
        sums[...] = jnp.zeros_like(sums)
        for place in range(per_visit):
            tile = visit * per_visit + place
            offset = offset_ref[tile]
            bucket = lax.rem(patch_ref[tile] - owner + REACH + patches, patches)
            weight = weights[tile]
            value = matches[buffer][place].reshape(rows // 8, 8, width) * weight[None]
            turned = pltpu.roll(value.reshape(rows, width), lax.rem(offset, width), 1)
            sums[bucket, :, :width] += jnp.where(lane >= offset, turned, 0.0)
            sums[bucket, :, width:] += jnp.where(lane < offset, turned, 0.0)
            extra[bucket, pl.ds(visit, 1), :] += jnp.concatenate(
                [
                    jnp.where(column >= offset, weight[:1], 0.0),
                    jnp.where(column < offset, weight[:1], 0.0),
                ],
                axis=1,
            )

        for bucket in range(SPREAD):
            for turn in range(groups):
                part = lax.rem(group + turn, groups)
                own = sums[bucket, pl.ds(pl.multiple_of(part * row_share, row_share), row_share), :]
                if slot > row_share:
                    own = jnp.concatenate(
                        [own, jnp.zeros((slot - row_share, PW), jnp.float32)], axis=0
                    )
                messages[bucket * groups + turn][
                    pl.ds(pl.multiple_of(visit * slot, slot), slot), :
                ] = own.astype(jnp.bfloat16)

    def two_visits(step, unused):
        for buffer in range(2):
            visit = 2 * step + buffer
            later = jnp.minimum(visit + 1, visits - 1)
            for place in range(per_visit):
                build(later, place, 1 - buffer)
                multiply(place, buffer)
            deliver(visit, buffer)
        return unused

    for place in range(per_visit):
        build(0, place, 0)
    lax.fori_loop(0, visits // 2, two_visits, 0)

    row = iota((EXTRA, PW), 0)
    lane = iota((1, PW), 1)
    by_row = jnp.zeros((1, PW), jnp.float32)
    by_weight = jnp.full((1, PW), -1.0, jnp.float32)
    for visit in range(visits):
        band = band_ref[visit].astype(jnp.float32)
        by_row = jnp.where(lane // slot == visit, band, by_row)
        by_weight = jnp.where(
            (lane < 2 * visits) & (lax.rem(lane, visits) == visit), band, by_weight
        )
    for bucket in range(SPREAD):
        held = extra[bucket]
        high = held.astype(jnp.bfloat16).astype(jnp.float32)
        low = jnp.concatenate([held[-visits:], (held - high)[:-visits]], axis=0)
        mixed = jnp.where((row >= visits) & (row < 2 * visits), low, high)
        mixed = jnp.where(row == 2 * visits, by_row, mixed)
        mixed = jnp.where(row == 2 * visits + 1, by_weight, mixed).astype(jnp.bfloat16)
        for turn in range(groups):
            messages[bucket * groups + turn][slot * visits :, :] = mixed


def add_messages(count, row_share, messages):
    slot = slot_rows(row_share)
    depth = slot * count
    line = lax.broadcasted_iota(jnp.int32, (row_share, depth), 0)
    lane = lax.broadcasted_iota(jnp.int32, (row_share, depth), 1)
    same = (lax.rem(lane, slot) == line).astype(jnp.float32)
    band_line = lax.broadcasted_iota(jnp.int32, (8, EXTRA), 0).astype(jnp.float32)
    totals = jnp.zeros((BANDS * row_share, PW), jnp.float32)
    weight_totals = jnp.zeros((8, PW), jnp.float32)
    for message in messages:
        extra = message[depth:, :]
        bands = extra[2 * count : 2 * count + 2].astype(jnp.float32)
        pick = jnp.concatenate(
            [jnp.where(bands[:1, :depth] == float(b), same, 0.0) for b in range(BANDS)], axis=0
        ).astype(jnp.bfloat16)
        totals += jnp.dot(pick, message[:depth, :], preferred_element_type=jnp.float32)
        pick = (bands[1:, :EXTRA] == band_line).astype(jnp.bfloat16)
        weight_totals += jnp.dot(pick, extra, preferred_element_type=jnp.float32)
    return totals, weight_totals


def early_kernel(count, row_share, weight_ref, *refs):
    totals_ref, rows_ref = refs[-2:]
    totals_ref[...], rows_ref[:8] = add_messages(count, row_share, refs[:-2])
    line = lax.broadcasted_iota(jnp.int32, (8, PW), 0)
    band_weights = jnp.zeros((8, PW), jnp.float32)
    for b in range(BANDS):
        band_weights = jnp.where(line == b, weight_ref[b], band_weights)
    rows_ref[8:] = band_weights


def combine_kernel(count, totals_ref, rows_ref, *refs):
    coadd_ref, detection_ref = refs[-2:]
    row_share = coadd_ref.shape[1]
    totals, weight_totals = add_messages(count, row_share, refs[:-2])
    weight_totals = jnp.maximum(weight_totals + rows_ref[:8], 1.0)
    detection = jnp.zeros((row_share, PW), jnp.float32)
    for b in range(BANDS):
        held = pl.ds(b * row_share, row_share)
        coadd = (totals[b * row_share : (b + 1) * row_share] + totals_ref[held, :]) / (
            weight_totals[b : b + 1]
        )
        coadd_ref[b] = coadd
        detection += rows_ref[8 + b : 9 + b] * coadd
    detection_ref[...] = detection


def local(
    tiles,
    tile_patch,
    tile_offset,
    tile_weight,
    visit_band,
    coeff_index,
    coeff_table,
    row_kernels,
    column_kernels,
    band_weight,
):
    tile_count, rows, width = tiles.shape
    visits = visit_band.shape[0]
    per_visit = tile_count // visits
    basis, taps = row_kernels.shape
    patches = lax.axis_size("ra")
    groups = lax.axis_size("band")
    row_share = rows // groups
    slot = slot_rows(row_share)
    length = visits * slot + EXTRA
    smem = pl.BlockSpec(memory_space=pltpu.SMEM)

    vmem = pl.BlockSpec(memory_space=pltpu.VMEM)
    anywhere = pl.BlockSpec(memory_space=pl.ANY)
    messages = pl.pallas_call(
        functools.partial(match_kernel, patches, groups),
        in_specs=[smem] * 4 + [anywhere] * 5,
        out_specs=[vmem] * (SPREAD * groups),
        out_shape=[jax.ShapeDtypeStruct((length, PW), jnp.bfloat16)] * (SPREAD * groups),
        scratch_shapes=[
            pltpu.VMEM(coeff_table.shape[::-1], jnp.float32),
            pltpu.VMEM((1, tile_count), jnp.bfloat16),
            pltpu.VMEM((basis, taps), jnp.bfloat16),
            pltpu.VMEM((basis, taps), jnp.bfloat16),
            pltpu.VMEM((tile_count, rows, width), jnp.bfloat16),
            pltpu.VMEM((tile_count, VECTORS, width), jnp.float32),
            pltpu.VMEM((tile_count, 8, width), jnp.float32),
        ]
        + [pltpu.VMEM((per_visit, 2, 4 * FINE_ROWS, 2 * width), jnp.bfloat16)] * 2
        + [pltpu.VMEM((per_visit, 2, COARSE * BLOCK, 2 * width), jnp.bfloat16)] * 2
        + [pltpu.VMEM((per_visit, rows, width), jnp.float32)] * 2
        + [
            pltpu.VMEM((SPREAD, rows, PW), jnp.float32),
            pltpu.VMEM((SPREAD, EXTRA, PW), jnp.float32),
            pltpu.SemaphoreType.DMA,
            pltpu.SemaphoreType.DMA((4,)),
        ],
        compiler_params=pltpu.CompilerParams(vmem_limit_bytes=62 * 1024 * 1024),
        name="match_and_sum",
    )(
        tile_patch,
        tile_offset,
        coeff_index,
        visit_band,
        coeff_table.T,
        tile_weight.reshape(1, tile_count),
        row_kernels,
        column_kernels,
        tiles,
    )

    order = [(d, t) for d in range(1, REACH + 1) for t in range(groups)]
    order += [(0, t) for t in range(1, groups)]
    early = len(order)
    order += [(d, t) for d in range(-REACH, 0) for t in range(groups)]
    arrived = []
    for distance, turn in order:
        route = [
            (o * groups + g, (o + distance) % patches * groups + (g + turn) % groups)
            for o in range(patches)
            for g in range(groups)
        ]
        arrived.append(
            lax.ppermute(messages[(distance + REACH) * groups + turn], ("ra", "band"), route)
        )

    params = pltpu.CompilerParams(vmem_limit_bytes=40 * 1024 * 1024)
    first = [messages[REACH * groups]] + arrived[:early]
    totals = pl.pallas_call(
        functools.partial(early_kernel, visits, row_share),
        in_specs=[smem] + [vmem] * len(first),
        out_specs=(vmem, vmem),
        out_shape=(
            jax.ShapeDtypeStruct((BANDS * row_share, PW), jnp.float32),
            jax.ShapeDtypeStruct((16, PW), jnp.float32),
        ),
        compiler_params=params,
        name="combine_early",
    )(band_weight, *first)
    return pl.pallas_call(
        functools.partial(combine_kernel, visits),
        in_specs=[vmem] * (len(arrived) - early + 2),
        out_specs=(vmem, vmem),
        out_shape=(
            jax.ShapeDtypeStruct((BANDS, row_share, PW), jnp.float32),
            jax.ShapeDtypeStruct((row_share, PW), jnp.float32),
        ),
        compiler_params=params,
        name="combine",
    )(*totals, *arrived[early:])


def solution(mesh):
    return jax.shard_map(
        local,
        mesh=mesh,
        in_specs=(
            P(("ra", "band"), None, None),
            P(("ra", "band")),
            P(("ra", "band")),
            P(("ra", "band")),
            P(("ra", "band")),
            P(("ra", "band")),
            P(),
            P(),
            P(),
            P(),
        ),
        out_specs=(P(None, "band", "ra"), P("band", "ra")),
        check_vma=False,
    )
```

```python
import functools

import jax
import jax.numpy as jnp
from jax import lax
from jax.experimental import pallas as pl
from jax.experimental.pallas import tpu as pltpu
from jax.sharding import PartitionSpec as P

PW = 256
BANDS = 6
REACH = 2
SPREAD = 2 * REACH + 1
EXTRA = 16
BLOCK = 32
COARSE = 3
VECTORS = 16
FINE_ROWS = 64
LEAD = 6


def slot_rows(row_share):
    return max(row_share, 16)


def match_kernel(
    patches,
    groups,
    patch_hbm,
    offset_hbm,
    index_hbm,
    band_hbm,
    table_hbm,
    weight_hbm,
    rowk_hbm,
    colk_hbm,
    tiles_hbm,
    *rest,
):
    messages = rest[: SPREAD * groups]
    (
        patch_ref,
        offset_ref,
        index_ref,
        band_ref,
        table_ref,
        weight_ref,
        rowk_ref,
        colk_ref,
        tiles_ref,
        kernels,
        weights,
        shifted,
        toeplitz,
        matches,
        sums,
        extra,
        arrival,
        ready,
    ) = rest[SPREAD * groups :]
    visits = band_ref.shape[0]
    tile_count, rows, width = tiles_ref.shape
    per_visit = tile_count // visits
    basis, taps = rowk_ref.shape
    half = taps // 2
    row_share = rows // groups
    slot = slot_rows(row_share)
    owner = lax.axis_index("ra")
    group = lax.axis_index("band")

    small = [
        pltpu.make_async_copy(source, target, ready.at[place])
        for place, (source, target) in enumerate(
            (
                (index_hbm, index_ref),
                (table_hbm, table_ref),
                (weight_hbm, weight_ref),
                (rowk_hbm, rowk_ref),
                (colk_hbm, colk_ref),
                (patch_hbm, patch_ref),
                (offset_hbm, offset_ref),
                (band_hbm, band_ref),
            )
        )
    ]
    for copy in small:
        copy.start()

    def fetch(visit):
        held = pl.ds(visit * per_visit, per_visit)
        return pltpu.make_async_copy(tiles_hbm.at[held], tiles_ref.at[held], arrival.at[visit])

    for visit in range(visits):
        fetch(visit).start()

    def iota(shape, axis):
        return lax.broadcasted_iota(jnp.int32, shape, axis)

    def across(left, right, **options):
        return lax.dot_general(
            left,
            right,
            (((1,), (1,)), ((), ())),
            preferred_element_type=jnp.float32,
            **options,
        )

    extra[...] = jnp.zeros_like(extra)
    for place in range(per_visit):
        for side in range(2):
            for fine in range(4):
                top = fine * FINE_ROWS
                shifted[place, side, top : top + 16, :width] = jnp.zeros(
                    (16, width), jnp.bfloat16
                )
                shifted[place, side, top + 48 : top + 64, width:] = jnp.zeros(
                    (16, width), jnp.bfloat16
                )
    eye = (iota((tile_count, tile_count), 0) == iota((tile_count, tile_count), 1)).astype(
        jnp.bfloat16
    )
    for copy in small:
        copy.wait()
    weights[...] = across(eye, jnp.broadcast_to(weight_ref[...], (width, tile_count)))
    entry = iota((1, table_ref.shape[1]), 1)
    chosen = jnp.concatenate(
        [(entry == index_ref[j]).astype(jnp.float32) for j in range(tile_count)], axis=0
    ).astype(jnp.bfloat16)
    rest_of = table_ref[...]
    coeffs = jnp.zeros((tile_count, basis), jnp.float32)
    for _ in range(3):
        piece = rest_of.astype(jnp.bfloat16)
        rest_of = rest_of - piece.astype(jnp.float32)
        coeffs += across(chosen, piece)

    line = iota((2 * VECTORS, taps), 0)
    column = iota((2 * VECTORS, taps), 1)
    block = lax.rem(line, VECTORS) // 2
    step = 4 * lax.rem(block, COARSE) + 2 * lax.rem(line, 2) + line // VECTORS
    wanted = jnp.where(block < COARSE, half + step, half - 1 - step)
    wanted = jnp.where(lax.rem(line, VECTORS) < 4 * COARSE, wanted, -1)
    col_taps = across((wanted == column).astype(jnp.bfloat16), colk_ref[...])
    tap = iota((taps, width), 0)
    lane = iota((taps, width), 1)
    total = None
    for side in range(2):
        place = (lane == tap + LEAD + side * FINE_ROWS).astype(jnp.bfloat16)
        row_taps = jnp.dot(
            rowk_ref[...], place, preferred_element_type=jnp.float32
        ).astype(jnp.bfloat16)
        part = col_taps[side * VECTORS : (side + 1) * VECTORS]
        mix = jnp.concatenate([part * coeffs[j : j + 1] for j in range(tile_count)], axis=0)
        high = mix.astype(jnp.bfloat16)
        low = (mix - high.astype(jnp.float32)).astype(jnp.bfloat16)
        term = jnp.dot(high, row_taps, preferred_element_type=jnp.float32) + jnp.dot(
            low, row_taps, preferred_element_type=jnp.float32
        )
        total = term if total is None else total + term
    kernels[...] = total

    lane = iota((rows, width), 1)
    column = iota((1, width), 1)

    def edge(distance):
        here = iota((16, width), 1) + distance
        return ((here >= 0) & (here < width)).astype(jnp.float32).astype(jnp.bfloat16)

    edges = {distance: edge(distance) for distance in range(-4, 4) if distance != 0}

    def moved_tile(value, distance):
        if distance == 0:
            return value
        turned = pltpu.roll(value, -distance % width, 1).reshape(rows // 16, 16, width)
        return (turned * edges[distance][None]).reshape(rows, width)

    def moved(value, distance):
        if distance == 0:
            return value
        turned = pltpu.roll(value, -distance % width, 1)
        here = lane[: value.shape[0]] + distance
        return jnp.where((here >= 0) & (here < width), turned, jnp.zeros_like(turned))

    def one_visit(visit, unused):
        fetch(visit).wait()
        sums[...] = jnp.zeros_like(sums)
        first = visit * per_visit
        for place in range(per_visit):
            tile = first + place
            pixels = tiles_ref[tile]
            for side in range(2):
                for fine in range(4):
                    part = moved_tile(pixels, -1 - fine if side else fine)
                    top = fine * FINE_ROWS
                    shifted[place, side, top + 16 : top + 64, :width] = part[:48]
                    shifted[place, side, top : top + 48, width:] = part[16:]
                for coarse in range(COARSE):
                    for pair in range(2):
                        vector = pl.ds(
                            tile * VECTORS + (side * COARSE + coarse) * 2 + pair, 1
                        )
                        spread = jnp.broadcast_to(kernels[vector, :], (BLOCK, width))
                        turned = pltpu.roll(spread, 0, 1, stride=1, stride_axis=0)
                        toeplitz[
                            place,
                            side,
                            coarse * BLOCK : (coarse + 1) * BLOCK,
                            pair * width : (pair + 1) * width,
                        ] = turned.astype(jnp.bfloat16)
        for place in range(per_visit):
            matched = [jnp.zeros((BLOCK, width), jnp.float32) for _ in range(2)]
            for side in range(2):
                passed = jnp.dot(
                    toeplitz[place, side],
                    shifted[place, side],
                    preferred_element_type=jnp.float32,
                )
                for part in range(2):
                    for coarse in range(COARSE):
                        matched[part] += moved(
                            passed[
                                coarse * BLOCK : (coarse + 1) * BLOCK,
                                part * width : (part + 1) * width,
                            ],
                            -4 * coarse if side else 4 * coarse,
                        )
            matches[place] = jnp.concatenate(matched, axis=0)
        for place in range(per_visit):
            tile = first + place
            offset = offset_ref[tile]
            bucket = lax.rem(patch_ref[tile] - owner + REACH + patches, patches)
            weight = weights[pl.ds(tile, 1), :]
            turned = pltpu.roll(
                matches[place] * weight, lax.rem(offset, width), 1
            )
            sums[bucket, :, :width] += jnp.where(lane >= offset, turned, 0.0)
            sums[bucket, :, width:] += jnp.where(lane < offset, turned, 0.0)
            extra[bucket, pl.ds(visit, 1), :] += jnp.concatenate(
                [
                    jnp.where(column >= offset, weight, 0.0),
                    jnp.where(column < offset, weight, 0.0),
                ],
                axis=1,
            )

        for bucket in range(SPREAD):
            for turn in range(groups):
                part = lax.rem(group + turn, groups)
                own = sums[bucket, pl.ds(pl.multiple_of(part * row_share, row_share), row_share), :]
                if slot > row_share:
                    own = jnp.concatenate(
                        [own, jnp.zeros((slot - row_share, PW), jnp.float32)], axis=0
                    )
                messages[bucket * groups + turn][
                    pl.ds(pl.multiple_of(visit * slot, slot), slot), :
                ] = own.astype(jnp.bfloat16)
        return unused

    lax.fori_loop(0, visits, one_visit, 0)

    row = iota((EXTRA, PW), 0)
    lane = iota((1, PW), 1)
    by_row = jnp.zeros((1, PW), jnp.float32)
    by_weight = jnp.full((1, PW), -1.0, jnp.float32)
    for visit in range(visits):
        band = band_ref[visit].astype(jnp.float32)
        by_row = jnp.where(lane // slot == visit, band, by_row)
        by_weight = jnp.where(
            (lane < 2 * visits) & (lax.rem(lane, visits) == visit), band, by_weight
        )
    for bucket in range(SPREAD):
        held = extra[bucket]
        high = held.astype(jnp.bfloat16).astype(jnp.float32)
        low = jnp.concatenate([held[-visits:], (held - high)[:-visits]], axis=0)
        mixed = jnp.where((row >= visits) & (row < 2 * visits), low, high)
        mixed = jnp.where(row == 2 * visits, by_row, mixed)
        mixed = jnp.where(row == 2 * visits + 1, by_weight, mixed).astype(jnp.bfloat16)
        for turn in range(groups):
            messages[bucket * groups + turn][slot * visits :, :] = mixed


def add_messages(count, row_share, messages):
    slot = slot_rows(row_share)
    depth = slot * count
    line = lax.broadcasted_iota(jnp.int32, (row_share, depth), 0)
    lane = lax.broadcasted_iota(jnp.int32, (row_share, depth), 1)
    same = (lax.rem(lane, slot) == line).astype(jnp.float32)
    band_line = lax.broadcasted_iota(jnp.int32, (8, EXTRA), 0).astype(jnp.float32)
    totals = jnp.zeros((BANDS * row_share, PW), jnp.float32)
    weight_totals = jnp.zeros((8, PW), jnp.float32)
    for message in messages:
        extra = message[depth:, :]
        bands = extra[2 * count : 2 * count + 2].astype(jnp.float32)
        pick = jnp.concatenate(
            [jnp.where(bands[:1, :depth] == float(b), same, 0.0) for b in range(BANDS)], axis=0
        ).astype(jnp.bfloat16)
        totals += jnp.dot(pick, message[:depth, :], preferred_element_type=jnp.float32)
        pick = (bands[1:, :EXTRA] == band_line).astype(jnp.bfloat16)
        weight_totals += jnp.dot(pick, extra, preferred_element_type=jnp.float32)
    return totals, weight_totals


def early_kernel(count, row_share, weight_ref, *refs):
    totals_ref, rows_ref = refs[-2:]
    totals_ref[...], rows_ref[:8] = add_messages(count, row_share, refs[:-2])
    line = lax.broadcasted_iota(jnp.int32, (8, PW), 0)
    band_weights = jnp.zeros((8, PW), jnp.float32)
    for b in range(BANDS):
        band_weights = jnp.where(line == b, weight_ref[b], band_weights)
    rows_ref[8:] = band_weights


def combine_kernel(count, totals_ref, rows_ref, *refs):
    coadd_ref, detection_ref = refs[-2:]
    row_share = coadd_ref.shape[1]
    totals, weight_totals = add_messages(count, row_share, refs[:-2])
    weight_totals = jnp.maximum(weight_totals + rows_ref[:8], 1.0)
    detection = jnp.zeros((row_share, PW), jnp.float32)
    for b in range(BANDS):
        held = pl.ds(b * row_share, row_share)
        coadd = (totals[b * row_share : (b + 1) * row_share] + totals_ref[held, :]) / (
            weight_totals[b : b + 1]
        )
        coadd_ref[b] = coadd
        detection += rows_ref[8 + b : 9 + b] * coadd
    detection_ref[...] = detection


def local(
    tiles,
    tile_patch,
    tile_offset,
    tile_weight,
    visit_band,
    coeff_index,
    coeff_table,
    row_kernels,
    column_kernels,
    band_weight,
):
    tile_count, rows, width = tiles.shape
    visits = visit_band.shape[0]
    per_visit = tile_count // visits
    basis, taps = row_kernels.shape
    patches = lax.axis_size("ra")
    groups = lax.axis_size("band")
    row_share = rows // groups
    slot = slot_rows(row_share)
    length = visits * slot + EXTRA
    smem = pl.BlockSpec(memory_space=pltpu.SMEM)

    vmem = pl.BlockSpec(memory_space=pltpu.VMEM)
    anywhere = pl.BlockSpec(memory_space=pl.ANY)
    messages = pl.pallas_call(
        functools.partial(match_kernel, patches, groups),
        in_specs=[anywhere] * 9,
        out_specs=[vmem] * (SPREAD * groups),
        out_shape=[jax.ShapeDtypeStruct((length, PW), jnp.bfloat16)] * (SPREAD * groups),
        scratch_shapes=[
            pltpu.SMEM((tile_count,), jnp.int32),
            pltpu.SMEM((tile_count,), jnp.int32),
            pltpu.SMEM((tile_count,), jnp.int32),
            pltpu.SMEM((visits,), jnp.int32),
            pltpu.VMEM(coeff_table.shape[::-1], jnp.float32),
            pltpu.VMEM((1, tile_count), jnp.bfloat16),
            pltpu.VMEM((basis, taps), jnp.bfloat16),
            pltpu.VMEM((basis, taps), jnp.bfloat16),
            pltpu.VMEM((tile_count, rows, width), jnp.bfloat16),
            pltpu.VMEM((tile_count * VECTORS, width), jnp.float32),
            pltpu.VMEM((tile_count, width), jnp.float32),
            pltpu.VMEM((per_visit, 2, 4 * FINE_ROWS, 2 * width), jnp.bfloat16),
            pltpu.VMEM((per_visit, 2, COARSE * BLOCK, 2 * width), jnp.bfloat16),
            pltpu.VMEM((per_visit, rows, width), jnp.float32),
            pltpu.VMEM((SPREAD, rows, PW), jnp.float32),
            pltpu.VMEM((SPREAD, EXTRA, PW), jnp.float32),
            pltpu.SemaphoreType.DMA((visits,)),
            pltpu.SemaphoreType.DMA((8,)),
        ],
        compiler_params=pltpu.CompilerParams(vmem_limit_bytes=62 * 1024 * 1024),
        name="match_and_sum",
    )(
        tile_patch,
        tile_offset,
        coeff_index,
        visit_band,
        coeff_table.T,
        tile_weight.reshape(1, tile_count),
        row_kernels,
        column_kernels,
        tiles,
    )

    order = [(d, t) for d in range(1, REACH + 1) for t in range(groups)]
    order += [(0, t) for t in range(1, groups)]
    early = len(order)
    order += [(d, t) for d in range(-REACH, 0) for t in range(groups)]
    arrived = []
    for distance, turn in order:
        route = [
            (o * groups + g, (o + distance) % patches * groups + (g + turn) % groups)
            for o in range(patches)
            for g in range(groups)
        ]
        arrived.append(
            lax.ppermute(messages[(distance + REACH) * groups + turn], ("ra", "band"), route)
        )

    params = pltpu.CompilerParams(vmem_limit_bytes=40 * 1024 * 1024)
    first = [messages[REACH * groups]] + arrived[:early]
    totals = pl.pallas_call(
        functools.partial(early_kernel, visits, row_share),
        in_specs=[smem] + [vmem] * len(first),
        out_specs=(vmem, vmem),
        out_shape=(
            jax.ShapeDtypeStruct((BANDS * row_share, PW), jnp.float32),
            jax.ShapeDtypeStruct((16, PW), jnp.float32),
        ),
        compiler_params=params,
        name="combine_early",
    )(band_weight, *first)
    return pl.pallas_call(
        functools.partial(combine_kernel, visits),
        in_specs=[vmem] * (len(arrived) - early + 2),
        out_specs=(vmem, vmem),
        out_shape=(
            jax.ShapeDtypeStruct((BANDS, row_share, PW), jnp.float32),
            jax.ShapeDtypeStruct((row_share, PW), jnp.float32),
        ),
        compiler_params=params,
        name="combine",
    )(*totals, *arrived[early:])


def solution(mesh):
    return jax.shard_map(
        local,
        mesh=mesh,
        in_specs=(
            P(("ra", "band"), None, None),
            P(("ra", "band")),
            P(("ra", "band")),
            P(("ra", "band")),
            P(("ra", "band")),
            P(("ra", "band")),
            P(),
            P(),
            P(),
            P(),
        ),
        out_specs=(P(None, "band", "ra"), P("band", "ra")),
        check_vma=False,
    )
```

```python
import functools

import jax
import jax.numpy as jnp
from jax import lax
from jax.experimental import pallas as pl
from jax.experimental.pallas import tpu as pltpu
from jax.sharding import PartitionSpec as P

PW = 256
BANDS = 6
REACH = 2
SPREAD = 2 * REACH + 1
EXTRA = 16
BLOCK = 32
COARSE = 3
VECTORS = 16
FINE_ROWS = 64
LEAD = 6


def slot_rows(row_share):
    return max(row_share, 16)


def match_kernel(
    patches,
    groups,
    patch_hbm,
    offset_hbm,
    index_hbm,
    band_hbm,
    table_hbm,
    weight_hbm,
    rowk_hbm,
    colk_hbm,
    tiles_hbm,
    *rest,
):
    messages = rest[: SPREAD * groups]
    (
        patch_ref,
        offset_ref,
        index_ref,
        band_ref,
        table_ref,
        weight_ref,
        rowk_ref,
        colk_ref,
        tiles_ref,
        kernels,
        weights,
        shifted,
        toeplitz,
        matches,
        sums,
        extra,
        arrival,
        ready,
    ) = rest[SPREAD * groups :]
    visits = band_ref.shape[0]
    tile_count, rows, width = tiles_ref.shape
    per_visit = tile_count // visits
    basis, taps = rowk_ref.shape
    half = taps // 2
    row_share = rows // groups
    slot = slot_rows(row_share)
    owner = lax.axis_index("ra")
    group = lax.axis_index("band")

    small = [
        pltpu.make_async_copy(source, target, ready.at[place])
        for place, (source, target) in enumerate(
            (
                (index_hbm, index_ref),
                (table_hbm, table_ref),
                (weight_hbm, weight_ref),
                (rowk_hbm, rowk_ref),
                (colk_hbm, colk_ref),
                (patch_hbm, patch_ref),
                (offset_hbm, offset_ref),
                (band_hbm, band_ref),
            )
        )
    ]
    for copy in small:
        copy.start()

    def fetch(visit):
        held = pl.ds(visit * per_visit, per_visit)
        return pltpu.make_async_copy(tiles_hbm.at[held], tiles_ref.at[held], arrival.at[visit])

    for visit in range(visits):
        fetch(visit).start()

    def iota(shape, axis):
        return lax.broadcasted_iota(jnp.int32, shape, axis)

    def across(left, right, **options):
        return lax.dot_general(
            left,
            right,
            (((1,), (1,)), ((), ())),
            preferred_element_type=jnp.float32,
            **options,
        )

    extra[...] = jnp.zeros_like(extra)
    for place in range(per_visit):
        for side in range(2):
            for fine in range(4):
                top = fine * FINE_ROWS
                shifted[place, side, top : top + 16, :width] = jnp.zeros(
                    (16, width), jnp.bfloat16
                )
                shifted[place, side, top + 48 : top + 64, width:] = jnp.zeros(
                    (16, width), jnp.bfloat16
                )
    eye = (iota((tile_count, tile_count), 0) == iota((tile_count, tile_count), 1)).astype(
        jnp.bfloat16
    )
    for copy in small:
        copy.wait()
    weights[...] = across(eye, jnp.broadcast_to(weight_ref[...], (width, tile_count)))
    entry = iota((1, table_ref.shape[1]), 1)
    chosen = jnp.concatenate(
        [(entry == index_ref[j]).astype(jnp.float32) for j in range(tile_count)], axis=0
    ).astype(jnp.bfloat16)
    rest_of = table_ref[...]
    coeffs = jnp.zeros((tile_count, basis), jnp.float32)
    for _ in range(3):
        piece = rest_of.astype(jnp.bfloat16)
        rest_of = rest_of - piece.astype(jnp.float32)
        coeffs += across(chosen, piece)

    line = iota((2 * VECTORS, taps), 0)
    column = iota((2 * VECTORS, taps), 1)
    block = lax.rem(line, VECTORS) // 2
    step = 4 * lax.rem(block, COARSE) + 2 * lax.rem(line, 2) + line // VECTORS
    wanted = jnp.where(block < COARSE, half + step, half - 1 - step)
    wanted = jnp.where(lax.rem(line, VECTORS) < 4 * COARSE, wanted, -1)
    col_taps = across((wanted == column).astype(jnp.bfloat16), colk_ref[...])
    tap = iota((taps, width), 0)
    lane = iota((taps, width), 1)
    total = None
    for side in range(2):
        place = (lane == tap + LEAD + side * FINE_ROWS).astype(jnp.bfloat16)
        row_taps = jnp.dot(
            rowk_ref[...], place, preferred_element_type=jnp.float32
        ).astype(jnp.bfloat16)
        part = col_taps[side * VECTORS : (side + 1) * VECTORS]
        mix = jnp.concatenate([part * coeffs[j : j + 1] for j in range(tile_count)], axis=0)
        high = mix.astype(jnp.bfloat16)
        low = (mix - high.astype(jnp.float32)).astype(jnp.bfloat16)
        term = jnp.dot(high, row_taps, preferred_element_type=jnp.float32) + jnp.dot(
            low, row_taps, preferred_element_type=jnp.float32
        )
        total = term if total is None else total + term
    kernels[...] = total

    lane = iota((rows, width), 1)
    column = iota((1, width), 1)

    def edge(distance):
        here = iota((16, width), 1) + distance
        return ((here >= 0) & (here < width)).astype(jnp.float32).astype(jnp.bfloat16)

    edges = {distance: edge(distance) for distance in range(-4, 4) if distance != 0}

    def moved_tile(value, distance):
        if distance == 0:
            return value
        turned = pltpu.roll(value, -distance % width, 1).reshape(rows // 16, 16, width)
        return (turned * edges[distance][None]).reshape(rows, width)

    def moved(value, distance):
        if distance == 0:
            return value
        turned = pltpu.roll(value, -distance % width, 1)
        here = lane[: value.shape[0]] + distance
        return jnp.where((here >= 0) & (here < width), turned, jnp.zeros_like(turned))

    def one_visit(visit, unused):
        fetch(visit).wait()
        sums[...] = jnp.zeros_like(sums)
        first = visit * per_visit
        for place in range(per_visit):
            tile = first + place
            pixels = tiles_ref[tile]
            for side in range(2):
                for fine in range(4):
                    part = moved_tile(pixels, -1 - fine if side else fine)
                    top = fine * FINE_ROWS
                    shifted[place, side, top + 16 : top + 64, :width] = part[:48]
                    shifted[place, side, top : top + 48, width:] = part[16:]
                for coarse in range(COARSE):
                    for pair in range(2):
                        vector = pl.ds(
                            tile * VECTORS + (side * COARSE + coarse) * 2 + pair, 1
                        )
                        spread = jnp.broadcast_to(kernels[vector, :], (BLOCK, width))
                        turned = pltpu.roll(spread, 0, 1, stride=1, stride_axis=0)
                        toeplitz[
                            place,
                            side,
                            coarse * BLOCK : (coarse + 1) * BLOCK,
                            pair * width : (pair + 1) * width,
                        ] = turned.astype(jnp.bfloat16)
        for place in range(per_visit):
            matched = [jnp.zeros((BLOCK, width), jnp.float32) for _ in range(2)]
            for side in range(2):
                passed = jnp.dot(
                    toeplitz[place, side],
                    shifted[place, side],
                    preferred_element_type=jnp.float32,
                )
                for part in range(2):
                    for coarse in range(COARSE):
                        matched[part] += moved(
                            passed[
                                coarse * BLOCK : (coarse + 1) * BLOCK,
                                part * width : (part + 1) * width,
                            ],
                            -4 * coarse if side else 4 * coarse,
                        )
            matches[place] = jnp.concatenate(matched, axis=0)
        for place in range(per_visit):
            tile = first + place
            offset = offset_ref[tile]
            bucket = lax.rem(patch_ref[tile] - owner + REACH + patches, patches)
            weight = weights[pl.ds(tile, 1), :]
            turned = pltpu.roll(
                matches[place] * weight, lax.rem(offset, width), 1
            )
            sums[bucket, :, :width] += jnp.where(lane >= offset, turned, 0.0)
            sums[bucket, :, width:] += jnp.where(lane < offset, turned, 0.0)
            extra[bucket, pl.ds(visit, 1), :] += jnp.concatenate(
                [
                    jnp.where(column >= offset, weight, 0.0),
                    jnp.where(column < offset, weight, 0.0),
                ],
                axis=1,
            )

        for bucket in range(SPREAD):
            for turn in range(groups):
                part = lax.rem(group + turn, groups)
                own = sums[bucket, pl.ds(pl.multiple_of(part * row_share, row_share), row_share), :]
                if slot > row_share:
                    own = jnp.concatenate(
                        [own, jnp.zeros((slot - row_share, PW), jnp.float32)], axis=0
                    )
                messages[bucket * groups + turn][
                    pl.ds(pl.multiple_of(visit * slot, slot), slot), :
                ] = own.astype(jnp.bfloat16)
        return unused

    lax.fori_loop(0, visits, one_visit, 0)

    row = iota((EXTRA, PW), 0)
    lane = iota((1, PW), 1)
    by_row = jnp.zeros((1, PW), jnp.float32)
    by_weight = jnp.full((1, PW), -1.0, jnp.float32)
    for visit in range(visits):
        band = band_ref[visit].astype(jnp.float32)
        by_row = jnp.where(lane // slot == visit, band, by_row)
        by_weight = jnp.where(
            (lane < 2 * visits) & (lax.rem(lane, visits) == visit), band, by_weight
        )
    for bucket in range(SPREAD):
        held = extra[bucket]
        high = held.astype(jnp.bfloat16).astype(jnp.float32)
        low = jnp.concatenate([held[-visits:], (held - high)[:-visits]], axis=0)
        mixed = jnp.where((row >= visits) & (row < 2 * visits), low, high)
        mixed = jnp.where(row == 2 * visits, by_row, mixed)
        mixed = jnp.where(row == 2 * visits + 1, by_weight, mixed).astype(jnp.bfloat16)
        for turn in range(groups):
            messages[bucket * groups + turn][slot * visits :, :] = mixed


def add_messages(count, row_share, messages):
    slot = slot_rows(row_share)
    depth = slot * count
    line = lax.broadcasted_iota(jnp.int32, (row_share, depth), 0)
    lane = lax.broadcasted_iota(jnp.int32, (row_share, depth), 1)
    same = (lax.rem(lane, slot) == line).astype(jnp.float32)
    band_line = lax.broadcasted_iota(jnp.int32, (8, EXTRA), 0).astype(jnp.float32)
    totals = jnp.zeros((BANDS * row_share, PW), jnp.float32)
    weight_totals = jnp.zeros((8, PW), jnp.float32)
    for message in messages:
        extra = message[depth:, :]
        bands = extra[2 * count : 2 * count + 2].astype(jnp.float32)
        pick = jnp.concatenate(
            [jnp.where(bands[:1, :depth] == float(b), same, 0.0) for b in range(BANDS)], axis=0
        ).astype(jnp.bfloat16)
        totals += jnp.dot(pick, message[:depth, :], preferred_element_type=jnp.float32)
        pick = (bands[1:, :EXTRA] == band_line).astype(jnp.bfloat16)
        weight_totals += jnp.dot(pick, extra, preferred_element_type=jnp.float32)
    return totals, weight_totals


def early_kernel(count, row_share, weight_ref, *refs):
    totals_ref, rows_ref = refs[-2:]
    totals_ref[...], rows_ref[:8] = add_messages(count, row_share, refs[:-2])
    line = lax.broadcasted_iota(jnp.int32, (8, PW), 0)
    band_weights = jnp.zeros((8, PW), jnp.float32)
    for b in range(BANDS):
        band_weights = jnp.where(line == b, weight_ref[b], band_weights)
    rows_ref[8:] = band_weights


def combine_kernel(count, totals_ref, rows_ref, *refs):
    coadd_ref, detection_ref = refs[-2:]
    row_share = coadd_ref.shape[1]
    totals, weight_totals = add_messages(count, row_share, refs[:-2])
    weight_totals = jnp.maximum(weight_totals + rows_ref[:8], 1.0)
    detection = jnp.zeros((row_share, PW), jnp.float32)
    for b in range(BANDS):
        held = pl.ds(b * row_share, row_share)
        coadd = (totals[b * row_share : (b + 1) * row_share] + totals_ref[held, :]) / (
            weight_totals[b : b + 1]
        )
        coadd_ref[b] = coadd
        detection += rows_ref[8 + b : 9 + b] * coadd
    detection_ref[...] = detection


def local(
    tiles,
    tile_patch,
    tile_offset,
    tile_weight,
    visit_band,
    coeff_index,
    coeff_table,
    row_kernels,
    column_kernels,
    band_weight,
):
    tile_count, rows, width = tiles.shape
    visits = visit_band.shape[0]
    per_visit = tile_count // visits
    basis, taps = row_kernels.shape
    patches = lax.axis_size("ra")
    groups = lax.axis_size("band")
    row_share = rows // groups
    slot = slot_rows(row_share)
    length = visits * slot + EXTRA
    smem = pl.BlockSpec(memory_space=pltpu.SMEM)

    vmem = pl.BlockSpec(memory_space=pltpu.VMEM)
    anywhere = pl.BlockSpec(memory_space=pl.ANY)
    messages = pl.pallas_call(
        functools.partial(match_kernel, patches, groups),
        in_specs=[anywhere] * 9,
        out_specs=[vmem] * (SPREAD * groups),
        out_shape=[jax.ShapeDtypeStruct((length, PW), jnp.bfloat16)] * (SPREAD * groups),
        scratch_shapes=[
            pltpu.SMEM((tile_count,), jnp.int32),
            pltpu.SMEM((tile_count,), jnp.int32),
            pltpu.SMEM((tile_count,), jnp.int32),
            pltpu.SMEM((visits,), jnp.int32),
            pltpu.VMEM(coeff_table.shape[::-1], jnp.float32),
            pltpu.VMEM((1, tile_count), jnp.bfloat16),
            pltpu.VMEM((basis, taps), jnp.bfloat16),
            pltpu.VMEM((basis, taps), jnp.bfloat16),
            pltpu.VMEM((tile_count, rows, width), jnp.bfloat16),
            pltpu.VMEM((tile_count * VECTORS, width), jnp.float32),
            pltpu.VMEM((tile_count, width), jnp.float32),
            pltpu.VMEM((per_visit, 2, 4 * FINE_ROWS, 2 * width), jnp.bfloat16),
            pltpu.VMEM((per_visit, 2, COARSE * BLOCK, 2 * width), jnp.bfloat16),
            pltpu.VMEM((per_visit, rows, width), jnp.float32),
            pltpu.VMEM((SPREAD, rows, PW), jnp.float32),
            pltpu.VMEM((SPREAD, EXTRA, PW), jnp.float32),
            pltpu.SemaphoreType.DMA((visits,)),
            pltpu.SemaphoreType.DMA((8,)),
        ],
        compiler_params=pltpu.CompilerParams(vmem_limit_bytes=62 * 1024 * 1024),
        name="match_and_sum",
    )(
        tile_patch,
        tile_offset,
        coeff_index,
        visit_band,
        coeff_table.T,
        tile_weight.reshape(1, tile_count),
        row_kernels,
        column_kernels,
        tiles,
    )

    order = [(d, t) for d in range(1, REACH + 1) for t in range(groups)]
    early = len(order)
    order += [(d, t) for d in range(-REACH, 0) for t in range(groups)]
    order += [(0, t) for t in range(1, groups)]
    arrived = []
    for distance, turn in order:
        route = [
            (o * groups + g, (o + distance) % patches * groups + (g + turn) % groups)
            for o in range(patches)
            for g in range(groups)
        ]
        arrived.append(
            lax.ppermute(messages[(distance + REACH) * groups + turn], ("ra", "band"), route)
        )

    params = pltpu.CompilerParams(vmem_limit_bytes=40 * 1024 * 1024)
    first = [messages[REACH * groups]] + arrived[:early]
    totals = pl.pallas_call(
        functools.partial(early_kernel, visits, row_share),
        in_specs=[smem] + [vmem] * len(first),
        out_specs=(vmem, vmem),
        out_shape=(
            jax.ShapeDtypeStruct((BANDS * row_share, PW), jnp.float32),
            jax.ShapeDtypeStruct((16, PW), jnp.float32),
        ),
        compiler_params=params,
        name="combine_early",
    )(band_weight, *first)
    return pl.pallas_call(
        functools.partial(combine_kernel, visits),
        in_specs=[vmem] * (len(arrived) - early + 2),
        out_specs=(vmem, vmem),
        out_shape=(
            jax.ShapeDtypeStruct((BANDS, row_share, PW), jnp.float32),
            jax.ShapeDtypeStruct((row_share, PW), jnp.float32),
        ),
        compiler_params=params,
        name="combine",
    )(*totals, *arrived[early:])


def solution(mesh):
    return jax.shard_map(
        local,
        mesh=mesh,
        in_specs=(
            P(("ra", "band"), None, None),
            P(("ra", "band")),
            P(("ra", "band")),
            P(("ra", "band")),
            P(("ra", "band")),
            P(("ra", "band")),
            P(),
            P(),
            P(),
            P(),
        ),
        out_specs=(P(None, "band", "ra"), P("band", "ra")),
        check_vma=False,
    )
```

```python
import functools

import jax
import jax.numpy as jnp
from jax import lax
from jax.experimental import pallas as pl
from jax.experimental.pallas import tpu as pltpu
from jax.sharding import PartitionSpec as P

PW = 256
BANDS = 6
REACH = 2
SPREAD = 2 * REACH + 1
EXTRA = 16
DETECT = 10
BLOCK = 32
COARSE = 3
VECTORS = 16
FINE_ROWS = 64
LEAD = 6


def match_kernel(
    patches,
    patch_hbm,
    offset_hbm,
    index_hbm,
    band_hbm,
    detect_hbm,
    table_hbm,
    weight_hbm,
    rowk_hbm,
    colk_hbm,
    tiles_hbm,
    far,
    cross,
    kept,
    patch_ref,
    offset_ref,
    index_ref,
    band_ref,
    detect_ref,
    table_ref,
    weight_ref,
    rowk_ref,
    colk_ref,
    tiles_ref,
    kernels,
    weights,
    shifted,
    toeplitz,
    matches,
    sums,
    extra,
    arrival,
    ready,
):
    visits = band_ref.shape[0]
    tile_count, rows, width = tiles_ref.shape
    per_visit = tile_count // visits
    basis, taps = rowk_ref.shape
    half = taps // 2
    owner = lax.axis_index("ra")
    way = 2 * lax.rem(owner, 2) - 1

    small = [
        pltpu.make_async_copy(source, target, ready.at[place])
        for place, (source, target) in enumerate(
            (
                (index_hbm, index_ref),
                (table_hbm, table_ref),
                (weight_hbm, weight_ref),
                (rowk_hbm, rowk_ref),
                (colk_hbm, colk_ref),
                (patch_hbm, patch_ref),
                (offset_hbm, offset_ref),
                (band_hbm, band_ref),
                (detect_hbm, detect_ref),
            )
        )
    ]
    for copy in small:
        copy.start()

    def fetch(visit):
        held = pl.ds(visit * per_visit, per_visit)
        return pltpu.make_async_copy(tiles_hbm.at[held], tiles_ref.at[held], arrival.at[visit])

    for visit in range(visits):
        fetch(visit).start()

    def iota(shape, axis):
        return lax.broadcasted_iota(jnp.int32, shape, axis)

    def across(left, right, **options):
        return lax.dot_general(
            left,
            right,
            (((1,), (1,)), ((), ())),
            preferred_element_type=jnp.float32,
            **options,
        )

    extra[...] = jnp.zeros_like(extra)
    for place in range(per_visit):
        for side in range(2):
            for fine in range(4):
                top = fine * FINE_ROWS
                shifted[place, side, top : top + 16, :width] = jnp.zeros(
                    (16, width), jnp.bfloat16
                )
                shifted[place, side, top + 48 : top + 64, width:] = jnp.zeros(
                    (16, width), jnp.bfloat16
                )
    eye = (iota((tile_count, tile_count), 0) == iota((tile_count, tile_count), 1)).astype(
        jnp.bfloat16
    )
    for copy in small:
        copy.wait()
    weights[...] = across(eye, jnp.broadcast_to(weight_ref[...], (width, tile_count)))
    entry = iota((1, table_ref.shape[1]), 1)
    chosen = jnp.concatenate(
        [(entry == index_ref[j]).astype(jnp.float32) for j in range(tile_count)], axis=0
    ).astype(jnp.bfloat16)
    rest_of = table_ref[...]
    coeffs = jnp.zeros((tile_count, basis), jnp.float32)
    for _ in range(3):
        piece = rest_of.astype(jnp.bfloat16)
        rest_of = rest_of - piece.astype(jnp.float32)
        coeffs += across(chosen, piece)

    line = iota((2 * VECTORS, taps), 0)
    column = iota((2 * VECTORS, taps), 1)
    block = lax.rem(line, VECTORS) // 2
    step = 4 * lax.rem(block, COARSE) + 2 * lax.rem(line, 2) + line // VECTORS
    wanted = jnp.where(block < COARSE, half + step, half - 1 - step)
    wanted = jnp.where(lax.rem(line, VECTORS) < 4 * COARSE, wanted, -1)
    col_taps = across((wanted == column).astype(jnp.bfloat16), colk_ref[...])
    tap = iota((taps, width), 0)
    lane = iota((taps, width), 1)
    total = None
    for side in range(2):
        place = (lane == tap + LEAD + side * FINE_ROWS).astype(jnp.bfloat16)
        row_taps = jnp.dot(
            rowk_ref[...], place, preferred_element_type=jnp.float32
        ).astype(jnp.bfloat16)
        part = col_taps[side * VECTORS : (side + 1) * VECTORS]
        mix = jnp.concatenate([part * coeffs[j : j + 1] for j in range(tile_count)], axis=0)
        high = mix.astype(jnp.bfloat16)
        low = (mix - high.astype(jnp.float32)).astype(jnp.bfloat16)
        term = jnp.dot(high, row_taps, preferred_element_type=jnp.float32) + jnp.dot(
            low, row_taps, preferred_element_type=jnp.float32
        )
        total = term if total is None else total + term
    kernels[...] = total

    lane = iota((rows, width), 1)
    column = iota((1, width), 1)

    def edge(distance):
        here = iota((16, width), 1) + distance
        return ((here >= 0) & (here < width)).astype(jnp.float32).astype(jnp.bfloat16)

    edges = {distance: edge(distance) for distance in range(-4, 4) if distance != 0}

    def moved_tile(value, distance):
        if distance == 0:
            return value
        turned = pltpu.roll(value, -distance % width, 1).reshape(rows // 16, 16, width)
        return (turned * edges[distance][None]).reshape(rows, width)

    def moved(value, distance):
        if distance == 0:
            return value
        turned = pltpu.roll(value, -distance % width, 1)
        here = lane[: value.shape[0]] + distance
        return jnp.where((here >= 0) & (here < width), turned, jnp.zeros_like(turned))

    def one_visit(visit, unused):
        fetch(visit).wait()
        sums[...] = jnp.zeros_like(sums)
        first = visit * per_visit
        for place in range(per_visit):
            tile = first + place
            pixels = tiles_ref[tile]
            for side in range(2):
                for fine in range(4):
                    part = moved_tile(pixels, -1 - fine if side else fine)
                    top = fine * FINE_ROWS
                    shifted[place, side, top + 16 : top + 64, :width] = part[:48]
                    shifted[place, side, top : top + 48, width:] = part[16:]
                for coarse in range(COARSE):
                    for pair in range(2):
                        vector = pl.ds(
                            tile * VECTORS + (side * COARSE + coarse) * 2 + pair, 1
                        )
                        spread = jnp.broadcast_to(kernels[vector, :], (BLOCK, width))
                        turned = pltpu.roll(spread, 0, 1, stride=1, stride_axis=0)
                        toeplitz[
                            place,
                            side,
                            coarse * BLOCK : (coarse + 1) * BLOCK,
                            pair * width : (pair + 1) * width,
                        ] = turned.astype(jnp.bfloat16)
        for place in range(per_visit):
            matched = [jnp.zeros((BLOCK, width), jnp.float32) for _ in range(2)]
            for side in range(2):
                passed = jnp.dot(
                    toeplitz[place, side],
                    shifted[place, side],
                    preferred_element_type=jnp.float32,
                )
                for part in range(2):
                    for coarse in range(COARSE):
                        matched[part] += moved(
                            passed[
                                coarse * BLOCK : (coarse + 1) * BLOCK,
                                part * width : (part + 1) * width,
                            ],
                            -4 * coarse if side else 4 * coarse,
                        )
            matches[place] = jnp.concatenate(matched, axis=0)
        for place in range(per_visit):
            tile = first + place
            offset = offset_ref[tile]
            bucket = lax.rem(patch_ref[tile] - owner + REACH + patches, patches)
            weight = weights[pl.ds(tile, 1), :]
            turned = pltpu.roll(
                matches[place] * weight, lax.rem(offset, width), 1
            )
            sums[bucket, :, :width] += jnp.where(lane >= offset, turned, 0.0)
            sums[bucket, :, width:] += jnp.where(lane < offset, turned, 0.0)
            extra[bucket, pl.ds(visit, 1), :] += jnp.concatenate(
                [
                    jnp.where(column >= offset, weight, 0.0),
                    jnp.where(column < offset, weight, 0.0),
                ],
                axis=1,
            )

        held = pl.ds(pl.multiple_of(visit * rows, rows), rows)
        far[held, :] = sums[REACH + 2 * way].astype(jnp.bfloat16)
        cross[0, held, :] = sums[REACH - 2 * way].astype(jnp.bfloat16)
        cross[1, held, :] = sums[REACH - way].astype(jnp.bfloat16)
        kept[0, held, :] = sums[REACH + way].astype(jnp.bfloat16)
        kept[1, held, :] = sums[REACH].astype(jnp.bfloat16)
        return unused

    lax.fori_loop(0, visits, one_visit, 0)

    row = iota((EXTRA, PW), 0)
    lane = iota((1, PW), 1)

    def spread_bands(visit_of, limit):
        line = jnp.full((1, PW), -1.0, jnp.float32)
        for visit in range(visits):
            line = jnp.where(
                (lane < limit) & (visit_of == visit), band_ref[visit].astype(jnp.float32), line
            )
        return line

    by_row = spread_bands(lane // rows, visits * rows)
    by_weight = spread_bands(lax.rem(lane, visits), 2 * visits)
    detect = jnp.zeros((1, PW), jnp.float32)
    for b in range(BANDS):
        detect = jnp.where(lane == b, detect_ref[b], detect)

    def footer(bucket):
        held = extra[bucket]
        high = held.astype(jnp.bfloat16).astype(jnp.float32)
        low = jnp.concatenate([held[-visits:], (held - high)[:-visits]], axis=0)
        mixed = jnp.where((row >= visits) & (row < 2 * visits), low, high)
        mixed = jnp.where(row == 2 * visits, by_row, mixed)
        mixed = jnp.where(row == 2 * visits + 1, by_weight, mixed)
        rest = detect
        for place in range(DETECT, DETECT + 3):
            piece = rest.astype(jnp.bfloat16).astype(jnp.float32)
            rest = rest - piece
            mixed = jnp.where(row == place, piece, mixed)
        return mixed.astype(jnp.bfloat16)

    far[rows * visits :, :] = footer(REACH + 2 * way)
    cross[0, rows * visits :, :] = footer(REACH - 2 * way)
    cross[1, rows * visits :, :] = footer(REACH - way)
    kept[0, rows * visits :, :] = footer(REACH + way)
    kept[1, rows * visits :, :] = footer(REACH)


def add_message(count, groups, message):
    depth = message.shape[0] - EXTRA
    span = depth // count
    row_share = span // groups
    line = lax.broadcasted_iota(jnp.int32, (row_share, depth), 0)
    lane = lax.rem(lax.broadcasted_iota(jnp.int32, (row_share, depth), 1), span)
    band_line = lax.broadcasted_iota(jnp.int32, (8, EXTRA), 0).astype(jnp.float32)
    extra = message[depth:, :]
    bands = extra[2 * count : 2 * count + 2].astype(jnp.float32)
    pick = jnp.concatenate(
        [
            jnp.where(
                (lane == line + part * row_share) & (bands[:1, :depth] == float(b)), 1.0, 0.0
            )
            for part in range(groups)
            for b in range(BANDS)
        ],
        axis=0,
    ).astype(jnp.bfloat16)
    totals = jnp.dot(pick, message[:depth, :], preferred_element_type=jnp.float32)
    pick = (bands[1:, :EXTRA] == band_line).astype(jnp.bfloat16)
    return totals, jnp.dot(pick, extra, preferred_element_type=jnp.float32)


def add_banded(totals, weights, messages):
    depth = totals.shape[0]
    for message in messages:
        totals += message[:depth, :].astype(jnp.float32)
        footer = message[depth:, :].astype(jnp.float32)
        weights += footer[:8] + footer[8:]
    return totals, weights


def write_banded(message, totals, weights):
    depth = totals.shape[0]
    high = weights.astype(jnp.bfloat16).astype(jnp.float32)
    message[:depth, :] = totals.astype(jnp.bfloat16)
    message[depth:, :] = jnp.concatenate([high, weights - high], axis=0).astype(jnp.bfloat16)


def part_of(held, turn, groups):
    depth = held.shape[0] // groups
    part = lax.rem(lax.axis_index("band") + turn, groups)
    return held[pl.ds(pl.multiple_of(part * depth, depth), depth), :]


def keep_kernel(count, groups, kept_ref, totals_ref, weights_ref, detect_ref):
    for place in range(2):
        totals_ref[place], weights_ref[place] = add_message(count, groups, kept_ref.at[place])
    extra = kept_ref[0, kept_ref.shape[1] - EXTRA :, :].astype(jnp.float32)
    detect = extra[DETECT : DETECT + 1] + extra[DETECT + 1 : DETECT + 2]
    detect += extra[DETECT + 2 : DETECT + 3]
    line = lax.broadcasted_iota(jnp.int32, (8, PW), 0)
    lane = lax.broadcasted_iota(jnp.int32, (8, PW), 1)
    chosen = jnp.sum(jnp.where(line == lane, detect, 0.0), axis=1, keepdims=True)
    detect_ref[...] = jnp.broadcast_to(chosen, (8, PW))


def merge_kernel(count, groups, totals_ref, weights_ref, cross_ref, *refs):
    messages = refs[:groups]
    home_ref, home_weight_ref, held = refs[groups:]
    totals, weights = add_message(count, groups, cross_ref.at[0])
    held[...] = totals + totals_ref[0]
    weights += weights_ref[0]
    for turn, message in enumerate(messages):
        write_banded(message, part_of(held, turn, groups), weights)
    totals, weights = add_message(count, groups, cross_ref.at[1])
    home_ref[...] = totals + totals_ref[1]
    home_weight_ref[...] = weights + weights_ref[1]


def home_kernel(count, groups, home_ref, home_weight_ref, far_ref, *refs):
    messages = refs[: groups - 1]
    own_ref, own_weight_ref, held = refs[groups - 1 :]
    totals, weights = add_message(count, groups, far_ref)
    held[...] = totals + home_ref[...]
    weights += home_weight_ref[...]
    for turn, message in enumerate(messages, 1):
        write_banded(message, part_of(held, turn, groups), weights)
    own_ref[...] = part_of(held, 0, groups)
    own_weight_ref[...] = weights


def early_kernel(*refs):
    messages = refs[:-2]
    totals_ref, weights_ref = refs[-2:]
    depth = totals_ref.shape[0]
    totals_ref[...], weights_ref[...] = add_banded(
        jnp.zeros((depth, PW), jnp.float32), jnp.zeros((8, PW), jnp.float32), messages
    )


def combine_kernel(
    detect_ref, own_ref, own_weight_ref, near_ref, near_weight_ref, *refs
):
    coadd_ref, detection_ref = refs[-2:]
    row_share = coadd_ref.shape[1]
    totals, weights = add_banded(
        own_ref[...] + near_ref[...], own_weight_ref[...] + near_weight_ref[...], refs[:-2]
    )
    weights = jnp.maximum(weights, 1.0)
    detection = jnp.zeros((row_share, PW), jnp.float32)
    for b in range(BANDS):
        coadd = totals[b * row_share : (b + 1) * row_share] / weights[b : b + 1]
        coadd_ref[b] = coadd
        detection += detect_ref[b : b + 1] * coadd
    detection_ref[...] = detection


def local(
    tiles,
    tile_patch,
    tile_offset,
    tile_weight,
    visit_band,
    coeff_index,
    coeff_table,
    row_kernels,
    column_kernels,
    band_weight,
):
    tile_count, rows, width = tiles.shape
    visits = visit_band.shape[0]
    per_visit = tile_count // visits
    basis, taps = row_kernels.shape
    patches = lax.axis_size("ra")
    groups = lax.axis_size("band")
    row_share = rows // groups
    length = visits * rows + EXTRA
    message_shape = jax.ShapeDtypeStruct((length, PW), jnp.bfloat16)
    pair_shape = jax.ShapeDtypeStruct((2, length, PW), jnp.bfloat16)
    band_shape = jax.ShapeDtypeStruct((BANDS * row_share + EXTRA, PW), jnp.bfloat16)
    part_shape = jax.ShapeDtypeStruct((BANDS * row_share, PW), jnp.float32)
    whole_shape = jax.ShapeDtypeStruct((BANDS * rows, PW), jnp.float32)
    weight_shape = jax.ShapeDtypeStruct((8, PW), jnp.float32)

    vmem = pl.BlockSpec(memory_space=pltpu.VMEM)
    anywhere = pl.BlockSpec(memory_space=pl.ANY)
    far, cross, kept = pl.pallas_call(
        functools.partial(match_kernel, patches),
        in_specs=[anywhere] * 10,
        out_specs=[vmem] * 3,
        out_shape=[message_shape, pair_shape, pair_shape],
        scratch_shapes=[
            pltpu.SMEM((tile_count,), jnp.int32),
            pltpu.SMEM((tile_count,), jnp.int32),
            pltpu.SMEM((tile_count,), jnp.int32),
            pltpu.SMEM((visits,), jnp.int32),
            pltpu.SMEM((BANDS,), jnp.float32),
            pltpu.VMEM(coeff_table.shape[::-1], jnp.float32),
            pltpu.VMEM((1, tile_count), jnp.bfloat16),
            pltpu.VMEM((basis, taps), jnp.bfloat16),
            pltpu.VMEM((basis, taps), jnp.bfloat16),
            pltpu.VMEM((tile_count, rows, width), jnp.bfloat16),
            pltpu.VMEM((tile_count * VECTORS, width), jnp.float32),
            pltpu.VMEM((tile_count, width), jnp.float32),
            pltpu.VMEM((per_visit, 2, 4 * FINE_ROWS, 2 * width), jnp.bfloat16),
            pltpu.VMEM((per_visit, 2, COARSE * BLOCK, 2 * width), jnp.bfloat16),
            pltpu.VMEM((per_visit, rows, width), jnp.float32),
            pltpu.VMEM((SPREAD, rows, PW), jnp.float32),
            pltpu.VMEM((SPREAD, EXTRA, PW), jnp.float32),
            pltpu.SemaphoreType.DMA((visits,)),
            pltpu.SemaphoreType.DMA((9,)),
        ],
        compiler_params=pltpu.CompilerParams(vmem_limit_bytes=62 * 1024 * 1024),
        name="match_and_sum",
    )(
        tile_patch,
        tile_offset,
        coeff_index,
        visit_band,
        band_weight,
        coeff_table.T,
        tile_weight.reshape(1, tile_count),
        row_kernels,
        column_kernels,
        tiles,
    )

    def send(message, goal, turn):
        route = [
            (o * groups + g, goal(o) % patches * groups + (g + turn) % groups)
            for o in range(patches)
            for g in range(groups)
        ]
        return lax.ppermute(message, ("ra", "band"), route)

    def onward(distance):
        return lambda o: o + distance if o % 2 else o - distance

    def local_call(kernel, name, out_shape, *operands, **options):
        return pl.pallas_call(
            kernel,
            in_specs=[vmem] * len(operands),
            out_specs=[vmem] * len(out_shape),
            out_shape=out_shape,
            compiler_params=pltpu.CompilerParams(vmem_limit_bytes=40 * 1024 * 1024),
            name=name,
            **options,
        )(*operands)

    held = [pltpu.VMEM(whole_shape.shape, jnp.float32)]
    cross = send(cross, onward(-1), 0)
    far = send(far, onward(2), 0)
    *kept, detect = local_call(
        functools.partial(keep_kernel, visits, groups),
        "keep",
        [
            jax.ShapeDtypeStruct((2,) + whole_shape.shape, jnp.float32),
            jax.ShapeDtypeStruct((2,) + weight_shape.shape, jnp.float32),
            weight_shape,
        ],
        kept,
    )
    *near, home, home_weight = local_call(
        functools.partial(merge_kernel, visits, groups),
        "merge",
        [band_shape] * groups + [whole_shape, weight_shape],
        *kept,
        cross,
        scratch_shapes=held,
    )
    near = [send(near[turn], onward(1), turn) for turn in range(groups)]
    *others, own, own_weight = local_call(
        functools.partial(home_kernel, visits, groups),
        "home",
        [band_shape] * (groups - 1) + [part_shape, weight_shape],
        home,
        home_weight,
        far,
        scratch_shapes=held,
    )
    others = [send(others[turn - 1], onward(0), turn) for turn in range(1, groups)]
    near = local_call(early_kernel, "combine_early", [part_shape, weight_shape], *near)
    return local_call(
        combine_kernel,
        "combine",
        (
            jax.ShapeDtypeStruct((BANDS, row_share, PW), jnp.float32),
            jax.ShapeDtypeStruct((row_share, PW), jnp.float32),
        ),
        detect,
        own,
        own_weight,
        *near,
        *others,
    )


def solution(mesh):
    return jax.shard_map(
        local,
        mesh=mesh,
        in_specs=(
            P(("ra", "band"), None, None),
            P(("ra", "band")),
            P(("ra", "band")),
            P(("ra", "band")),
            P(("ra", "band")),
            P(("ra", "band")),
            P(),
            P(),
            P(),
            P(),
        ),
        out_specs=(P(None, "band", "ra"), P("band", "ra")),
        check_vma=False,
    )
```

```python
import functools

import jax
import jax.numpy as jnp
from jax import lax
from jax.experimental import pallas as pl
from jax.experimental.pallas import tpu as pltpu
from jax.sharding import PartitionSpec as P

PW = 256
BANDS = 6
REACH = 2
SPREAD = 2 * REACH + 1
EXTRA = 16
DETECT = 10
BLOCK = 32
COARSE = 3
VECTORS = 16
FINE_ROWS = 64
LEAD = 6


def slot_rows(row_share):
    return max(row_share, 16)


def match_kernel(
    patches,
    groups,
    patch_hbm,
    offset_hbm,
    index_hbm,
    band_hbm,
    detect_hbm,
    table_hbm,
    weight_hbm,
    rowk_hbm,
    colk_hbm,
    tiles_hbm,
    far,
    cross,
    kept,
    *rest,
):
    left = rest[:groups]
    (
        patch_ref,
        offset_ref,
        index_ref,
        band_ref,
        detect_ref,
        table_ref,
        weight_ref,
        rowk_ref,
        colk_ref,
        tiles_ref,
        kernels,
        weights,
        shifted,
        toeplitz,
        matches,
        sums,
        extra,
        arrival,
        ready,
    ) = rest[groups:]
    visits = band_ref.shape[0]
    tile_count, rows, width = tiles_ref.shape
    per_visit = tile_count // visits
    basis, taps = rowk_ref.shape
    half = taps // 2
    row_share = rows // groups
    slot = slot_rows(row_share)
    owner = lax.axis_index("ra")
    group = lax.axis_index("band")
    way = 2 * lax.rem(owner, 2) - 1

    small = [
        pltpu.make_async_copy(source, target, ready.at[place])
        for place, (source, target) in enumerate(
            (
                (index_hbm, index_ref),
                (table_hbm, table_ref),
                (weight_hbm, weight_ref),
                (rowk_hbm, rowk_ref),
                (colk_hbm, colk_ref),
                (patch_hbm, patch_ref),
                (offset_hbm, offset_ref),
                (band_hbm, band_ref),
                (detect_hbm, detect_ref),
            )
        )
    ]
    for copy in small:
        copy.start()

    def fetch(visit):
        held = pl.ds(visit * per_visit, per_visit)
        return pltpu.make_async_copy(tiles_hbm.at[held], tiles_ref.at[held], arrival.at[visit])

    for visit in range(visits):
        fetch(visit).start()

    def iota(shape, axis):
        return lax.broadcasted_iota(jnp.int32, shape, axis)

    def across(left, right, **options):
        return lax.dot_general(
            left,
            right,
            (((1,), (1,)), ((), ())),
            preferred_element_type=jnp.float32,
            **options,
        )

    extra[...] = jnp.zeros_like(extra)
    for place in range(per_visit):
        for side in range(2):
            for fine in range(4):
                top = fine * FINE_ROWS
                shifted[place, side, top : top + 16, :width] = jnp.zeros(
                    (16, width), jnp.bfloat16
                )
                shifted[place, side, top + 48 : top + 64, width:] = jnp.zeros(
                    (16, width), jnp.bfloat16
                )
    eye = (iota((tile_count, tile_count), 0) == iota((tile_count, tile_count), 1)).astype(
        jnp.bfloat16
    )
    for copy in small:
        copy.wait()
    weights[...] = across(eye, jnp.broadcast_to(weight_ref[...], (width, tile_count)))
    entry = iota((1, table_ref.shape[1]), 1)
    chosen = jnp.concatenate(
        [(entry == index_ref[j]).astype(jnp.float32) for j in range(tile_count)], axis=0
    ).astype(jnp.bfloat16)
    rest_of = table_ref[...]
    coeffs = jnp.zeros((tile_count, basis), jnp.float32)
    for _ in range(3):
        piece = rest_of.astype(jnp.bfloat16)
        rest_of = rest_of - piece.astype(jnp.float32)
        coeffs += across(chosen, piece)

    line = iota((2 * VECTORS, taps), 0)
    column = iota((2 * VECTORS, taps), 1)
    block = lax.rem(line, VECTORS) // 2
    step = 4 * lax.rem(block, COARSE) + 2 * lax.rem(line, 2) + line // VECTORS
    wanted = jnp.where(block < COARSE, half + step, half - 1 - step)
    wanted = jnp.where(lax.rem(line, VECTORS) < 4 * COARSE, wanted, -1)
    col_taps = across((wanted == column).astype(jnp.bfloat16), colk_ref[...])
    tap = iota((taps, width), 0)
    lane = iota((taps, width), 1)
    total = None
    for side in range(2):
        place = (lane == tap + LEAD + side * FINE_ROWS).astype(jnp.bfloat16)
        row_taps = jnp.dot(
            rowk_ref[...], place, preferred_element_type=jnp.float32
        ).astype(jnp.bfloat16)
        part = col_taps[side * VECTORS : (side + 1) * VECTORS]
        mix = jnp.concatenate([part * coeffs[j : j + 1] for j in range(tile_count)], axis=0)
        high = mix.astype(jnp.bfloat16)
        low = (mix - high.astype(jnp.float32)).astype(jnp.bfloat16)
        term = jnp.dot(high, row_taps, preferred_element_type=jnp.float32) + jnp.dot(
            low, row_taps, preferred_element_type=jnp.float32
        )
        total = term if total is None else total + term
    kernels[...] = total

    lane = iota((rows, width), 1)
    column = iota((1, width), 1)

    def edge(distance):
        here = iota((16, width), 1) + distance
        return ((here >= 0) & (here < width)).astype(jnp.float32).astype(jnp.bfloat16)

    edges = {distance: edge(distance) for distance in range(-4, 4) if distance != 0}

    def moved_tile(value, distance):
        if distance == 0:
            return value
        turned = pltpu.roll(value, -distance % width, 1).reshape(rows // 16, 16, width)
        return (turned * edges[distance][None]).reshape(rows, width)

    def moved(value, distance):
        if distance == 0:
            return value
        turned = pltpu.roll(value, -distance % width, 1)
        here = lane[: value.shape[0]] + distance
        return jnp.where((here >= 0) & (here < width), turned, jnp.zeros_like(turned))

    def one_visit(visit, unused):
        fetch(visit).wait()
        sums[...] = jnp.zeros_like(sums)
        first = visit * per_visit
        for place in range(per_visit):
            tile = first + place
            pixels = tiles_ref[tile]
            for side in range(2):
                for fine in range(4):
                    part = moved_tile(pixels, -1 - fine if side else fine)
                    top = fine * FINE_ROWS
                    shifted[place, side, top + 16 : top + 64, :width] = part[:48]
                    shifted[place, side, top : top + 48, width:] = part[16:]
                for coarse in range(COARSE):
                    for pair in range(2):
                        vector = pl.ds(
                            tile * VECTORS + (side * COARSE + coarse) * 2 + pair, 1
                        )
                        spread = jnp.broadcast_to(kernels[vector, :], (BLOCK, width))
                        turned = pltpu.roll(spread, 0, 1, stride=1, stride_axis=0)
                        toeplitz[
                            place,
                            side,
                            coarse * BLOCK : (coarse + 1) * BLOCK,
                            pair * width : (pair + 1) * width,
                        ] = turned.astype(jnp.bfloat16)
        for place in range(per_visit):
            matched = [jnp.zeros((BLOCK, width), jnp.float32) for _ in range(2)]
            for side in range(2):
                passed = jnp.dot(
                    toeplitz[place, side],
                    shifted[place, side],
                    preferred_element_type=jnp.float32,
                )
                for part in range(2):
                    for coarse in range(COARSE):
                        matched[part] += moved(
                            passed[
                                coarse * BLOCK : (coarse + 1) * BLOCK,
                                part * width : (part + 1) * width,
                            ],
                            -4 * coarse if side else 4 * coarse,
                        )
            matches[place] = jnp.concatenate(matched, axis=0)
        for place in range(per_visit):
            tile = first + place
            offset = offset_ref[tile]
            bucket = lax.rem(patch_ref[tile] - owner + REACH + patches, patches)
            weight = weights[pl.ds(tile, 1), :]
            turned = pltpu.roll(
                matches[place] * weight, lax.rem(offset, width), 1
            )
            sums[bucket, :, :width] += jnp.where(lane >= offset, turned, 0.0)
            sums[bucket, :, width:] += jnp.where(lane < offset, turned, 0.0)
            extra[bucket, pl.ds(visit, 1), :] += jnp.concatenate(
                [
                    jnp.where(column >= offset, weight, 0.0),
                    jnp.where(column < offset, weight, 0.0),
                ],
                axis=1,
            )

        for turn in range(groups):
            part = lax.rem(group + turn, groups)
            own = sums[
                REACH + 2 * way, pl.ds(pl.multiple_of(part * row_share, row_share), row_share), :
            ]
            if slot > row_share:
                own = jnp.concatenate(
                    [own, jnp.zeros((slot - row_share, PW), jnp.float32)], axis=0
                )
            left[turn][pl.ds(pl.multiple_of(visit * slot, slot), slot), :] = own.astype(
                jnp.bfloat16
            )
        held = pl.ds(pl.multiple_of(visit * rows, rows), rows)
        far[held, :] = sums[REACH + 2 * way].astype(jnp.bfloat16)
        cross[0, held, :] = sums[REACH - 2 * way].astype(jnp.bfloat16)
        cross[1, held, :] = sums[REACH - way].astype(jnp.bfloat16)
        kept[0, held, :] = sums[REACH + way].astype(jnp.bfloat16)
        kept[1, held, :] = sums[REACH].astype(jnp.bfloat16)
        return unused

    lax.fori_loop(0, visits, one_visit, 0)

    row = iota((EXTRA, PW), 0)
    lane = iota((1, PW), 1)

    def spread_bands(visit_of, limit):
        line = jnp.full((1, PW), -1.0, jnp.float32)
        for visit in range(visits):
            line = jnp.where(
                (lane < limit) & (visit_of == visit), band_ref[visit].astype(jnp.float32), line
            )
        return line

    by_row = spread_bands(lane // rows, visits * rows)
    by_slot = spread_bands(lane // slot, visits * slot)
    by_weight = spread_bands(lax.rem(lane, visits), 2 * visits)
    detect = jnp.zeros((1, PW), jnp.float32)
    for b in range(BANDS):
        detect = jnp.where(lane == b, detect_ref[b], detect)

    def footer(bucket, by_row):
        held = extra[bucket]
        high = held.astype(jnp.bfloat16).astype(jnp.float32)
        low = jnp.concatenate([held[-visits:], (held - high)[:-visits]], axis=0)
        mixed = jnp.where((row >= visits) & (row < 2 * visits), low, high)
        mixed = jnp.where(row == 2 * visits, by_row, mixed)
        mixed = jnp.where(row == 2 * visits + 1, by_weight, mixed)
        rest = detect
        for place in range(DETECT, DETECT + 3):
            piece = rest.astype(jnp.bfloat16).astype(jnp.float32)
            rest = rest - piece
            mixed = jnp.where(row == place, piece, mixed)
        return mixed.astype(jnp.bfloat16)

    for turn in range(groups):
        left[turn][slot * visits :, :] = footer(REACH + 2 * way, by_slot)
    far[rows * visits :, :] = footer(REACH + 2 * way, by_row)
    cross[0, rows * visits :, :] = footer(REACH - 2 * way, by_row)
    cross[1, rows * visits :, :] = footer(REACH - way, by_row)
    kept[0, rows * visits :, :] = footer(REACH + way, by_row)
    kept[1, rows * visits :, :] = footer(REACH, by_row)


def add_message(count, groups, message, row_share=None):
    depth = message.shape[0] - EXTRA
    span = depth // count
    row_share = row_share or span // groups
    line = lax.broadcasted_iota(jnp.int32, (row_share, depth), 0)
    lane = lax.rem(lax.broadcasted_iota(jnp.int32, (row_share, depth), 1), span)
    band_line = lax.broadcasted_iota(jnp.int32, (8, EXTRA), 0).astype(jnp.float32)
    extra = message[depth:, :]
    bands = extra[2 * count : 2 * count + 2].astype(jnp.float32)
    pick = jnp.concatenate(
        [
            jnp.where(
                (lane == line + part * row_share) & (bands[:1, :depth] == float(b)), 1.0, 0.0
            )
            for part in range(groups)
            for b in range(BANDS)
        ],
        axis=0,
    ).astype(jnp.bfloat16)
    totals = jnp.dot(pick, message[:depth, :], preferred_element_type=jnp.float32)
    pick = (bands[1:, :EXTRA] == band_line).astype(jnp.bfloat16)
    return totals, jnp.dot(pick, extra, preferred_element_type=jnp.float32)


def add_banded(totals, weights, messages):
    depth = totals.shape[0]
    for message in messages:
        totals += message[:depth, :].astype(jnp.float32)
        footer = message[depth:, :].astype(jnp.float32)
        weights += footer[:8] + footer[8:]
    return totals, weights


def write_banded(message, totals, weights):
    depth = totals.shape[0]
    high = weights.astype(jnp.bfloat16).astype(jnp.float32)
    message[:depth, :] = totals.astype(jnp.bfloat16)
    message[depth:, :] = jnp.concatenate([high, weights - high], axis=0).astype(jnp.bfloat16)


def part_of(held, turn, groups):
    depth = held.shape[0] // groups
    part = lax.rem(lax.axis_index("band") + turn, groups)
    return held[pl.ds(pl.multiple_of(part * depth, depth), depth), :]


def keep_kernel(count, groups, kept_ref, totals_ref, weights_ref, detect_ref):
    for place in range(2):
        totals_ref[place], weights_ref[place] = add_message(count, groups, kept_ref.at[place])
    extra = kept_ref[0, kept_ref.shape[1] - EXTRA :, :].astype(jnp.float32)
    detect = extra[DETECT : DETECT + 1] + extra[DETECT + 1 : DETECT + 2]
    detect += extra[DETECT + 2 : DETECT + 3]
    line = lax.broadcasted_iota(jnp.int32, (8, PW), 0)
    lane = lax.broadcasted_iota(jnp.int32, (8, PW), 1)
    chosen = jnp.sum(jnp.where(line == lane, detect, 0.0), axis=1, keepdims=True)
    detect_ref[...] = jnp.broadcast_to(chosen, (8, PW))


def merge_kernel(count, groups, totals_ref, weights_ref, cross_ref, *refs):
    messages = refs[:groups]
    home_ref, home_weight_ref, held = refs[groups:]
    totals, weights = add_message(count, groups, cross_ref.at[0])
    held[...] = totals + totals_ref[0]
    weights += weights_ref[0]
    for turn, message in enumerate(messages):
        write_banded(message, part_of(held, turn, groups), weights)
    totals, weights = add_message(count, groups, cross_ref.at[1])
    home_ref[...] = totals + totals_ref[1]
    home_weight_ref[...] = weights + weights_ref[1]


def home_kernel(count, groups, home_ref, home_weight_ref, far_ref, *refs):
    messages = refs[: groups - 1]
    own_ref, own_weight_ref, held = refs[groups - 1 :]
    totals, weights = add_message(count, groups, far_ref)
    held[...] = totals + home_ref[...]
    weights += home_weight_ref[...]
    for turn, message in enumerate(messages, 1):
        write_banded(message, part_of(held, turn, groups), weights)
    own_ref[...] = part_of(held, 0, groups)
    own_weight_ref[...] = weights


def early_kernel(*refs):
    messages = refs[:-2]
    totals_ref, weights_ref = refs[-2:]
    depth = totals_ref.shape[0]
    totals_ref[...], weights_ref[...] = add_banded(
        jnp.zeros((depth, PW), jnp.float32), jnp.zeros((8, PW), jnp.float32), messages
    )


def combine_kernel(
    count, groups, detect_ref, own_ref, own_weight_ref, near_ref, near_weight_ref, *refs
):
    coadd_ref, detection_ref = refs[-2:]
    row_share = coadd_ref.shape[1]
    totals, weights = add_banded(
        own_ref[...] + near_ref[...],
        own_weight_ref[...] + near_weight_ref[...],
        refs[: groups - 1],
    )
    for message in refs[groups - 1 : -2]:
        more, more_weights = add_message(count, 1, message, row_share)
        totals += more
        weights += more_weights
    weights = jnp.maximum(weights, 1.0)
    detection = jnp.zeros((row_share, PW), jnp.float32)
    for b in range(BANDS):
        coadd = totals[b * row_share : (b + 1) * row_share] / weights[b : b + 1]
        coadd_ref[b] = coadd
        detection += detect_ref[b : b + 1] * coadd
    detection_ref[...] = detection


def local(
    tiles,
    tile_patch,
    tile_offset,
    tile_weight,
    visit_band,
    coeff_index,
    coeff_table,
    row_kernels,
    column_kernels,
    band_weight,
):
    tile_count, rows, width = tiles.shape
    visits = visit_band.shape[0]
    per_visit = tile_count // visits
    basis, taps = row_kernels.shape
    patches = lax.axis_size("ra")
    groups = lax.axis_size("band")
    row_share = rows // groups
    length = visits * rows + EXTRA
    message_shape = jax.ShapeDtypeStruct((length, PW), jnp.bfloat16)
    left_shape = jax.ShapeDtypeStruct(
        (visits * slot_rows(row_share) + EXTRA, PW), jnp.bfloat16
    )
    pair_shape = jax.ShapeDtypeStruct((2, length, PW), jnp.bfloat16)
    band_shape = jax.ShapeDtypeStruct((BANDS * row_share + EXTRA, PW), jnp.bfloat16)
    part_shape = jax.ShapeDtypeStruct((BANDS * row_share, PW), jnp.float32)
    whole_shape = jax.ShapeDtypeStruct((BANDS * rows, PW), jnp.float32)
    weight_shape = jax.ShapeDtypeStruct((8, PW), jnp.float32)

    vmem = pl.BlockSpec(memory_space=pltpu.VMEM)
    anywhere = pl.BlockSpec(memory_space=pl.ANY)
    far, cross, kept, *left = pl.pallas_call(
        functools.partial(match_kernel, patches, groups),
        in_specs=[anywhere] * 10,
        out_specs=[vmem] * (3 + groups),
        out_shape=[message_shape, pair_shape, pair_shape] + [left_shape] * groups,
        scratch_shapes=[
            pltpu.SMEM((tile_count,), jnp.int32),
            pltpu.SMEM((tile_count,), jnp.int32),
            pltpu.SMEM((tile_count,), jnp.int32),
            pltpu.SMEM((visits,), jnp.int32),
            pltpu.SMEM((BANDS,), jnp.float32),
            pltpu.VMEM(coeff_table.shape[::-1], jnp.float32),
            pltpu.VMEM((1, tile_count), jnp.bfloat16),
            pltpu.VMEM((basis, taps), jnp.bfloat16),
            pltpu.VMEM((basis, taps), jnp.bfloat16),
            pltpu.VMEM((tile_count, rows, width), jnp.bfloat16),
            pltpu.VMEM((tile_count * VECTORS, width), jnp.float32),
            pltpu.VMEM((tile_count, width), jnp.float32),
            pltpu.VMEM((per_visit, 2, 4 * FINE_ROWS, 2 * width), jnp.bfloat16),
            pltpu.VMEM((per_visit, 2, COARSE * BLOCK, 2 * width), jnp.bfloat16),
            pltpu.VMEM((per_visit, rows, width), jnp.float32),
            pltpu.VMEM((SPREAD, rows, PW), jnp.float32),
            pltpu.VMEM((SPREAD, EXTRA, PW), jnp.float32),
            pltpu.SemaphoreType.DMA((visits,)),
            pltpu.SemaphoreType.DMA((9,)),
        ],
        compiler_params=pltpu.CompilerParams(vmem_limit_bytes=62 * 1024 * 1024),
        name="match_and_sum",
    )(
        tile_patch,
        tile_offset,
        coeff_index,
        visit_band,
        band_weight,
        coeff_table.T,
        tile_weight.reshape(1, tile_count),
        row_kernels,
        column_kernels,
        tiles,
    )

    def send(message, goal, turn, owners=range(patches)):
        route = [
            (o * groups + g, goal(o) % patches * groups + (g + turn) % groups)
            for o in owners
            for g in range(groups)
        ]
        return lax.ppermute(message, ("ra", "band"), route)

    def onward(distance):
        return lambda o: o + distance if o % 2 else o - distance

    def local_call(kernel, name, out_shape, *operands, **options):
        return pl.pallas_call(
            kernel,
            in_specs=[vmem] * len(operands),
            out_specs=[vmem] * len(out_shape),
            out_shape=out_shape,
            compiler_params=pltpu.CompilerParams(vmem_limit_bytes=40 * 1024 * 1024),
            name=name,
            **options,
        )(*operands)

    held = [pltpu.VMEM(whole_shape.shape, jnp.float32)]
    cross = send(cross, onward(-1), 0)
    far = send(far, onward(2), 0, range(1, patches, 2))
    left = [send(left[turn], onward(2), turn, range(0, patches, 2)) for turn in range(groups)]
    *kept, detect = local_call(
        functools.partial(keep_kernel, visits, groups),
        "keep",
        [
            jax.ShapeDtypeStruct((2,) + whole_shape.shape, jnp.float32),
            jax.ShapeDtypeStruct((2,) + weight_shape.shape, jnp.float32),
            weight_shape,
        ],
        kept,
    )
    *near, home, home_weight = local_call(
        functools.partial(merge_kernel, visits, groups),
        "merge",
        [band_shape] * groups + [whole_shape, weight_shape],
        *kept,
        cross,
        scratch_shapes=held,
    )
    near = [send(near[turn], onward(1), turn) for turn in range(groups)]
    *others, own, own_weight = local_call(
        functools.partial(home_kernel, visits, groups),
        "home",
        [band_shape] * (groups - 1) + [part_shape, weight_shape],
        home,
        home_weight,
        far,
        scratch_shapes=held,
    )
    others = [send(others[turn - 1], onward(0), turn) for turn in range(1, groups)]
    near = local_call(early_kernel, "combine_early", [part_shape, weight_shape], *near)
    return local_call(
        functools.partial(combine_kernel, visits, groups),
        "combine",
        (
            jax.ShapeDtypeStruct((BANDS, row_share, PW), jnp.float32),
            jax.ShapeDtypeStruct((row_share, PW), jnp.float32),
        ),
        detect,
        own,
        own_weight,
        *near,
        *others,
        *left,
    )


def solution(mesh):
    return jax.shard_map(
        local,
        mesh=mesh,
        in_specs=(
            P(("ra", "band"), None, None),
            P(("ra", "band")),
            P(("ra", "band")),
            P(("ra", "band")),
            P(("ra", "band")),
            P(("ra", "band")),
            P(),
            P(),
            P(),
            P(),
        ),
        out_specs=(P(None, "band", "ra"), P("band", "ra")),
        check_vma=False,
    )
```

```python
import functools

import jax
import jax.numpy as jnp
from jax import lax
from jax.experimental import pallas as pl
from jax.experimental.pallas import tpu as pltpu
from jax.sharding import PartitionSpec as P

PW = 256
BANDS = 6
REACH = 2
SPREAD = 2 * REACH + 1
EXTRA = 16
DETECT = 10
BLOCK = 32
COARSE = 3
VECTORS = 16
FINE_ROWS = 64
LEAD = 6


def match_kernel(
    patches,
    patch_hbm,
    offset_hbm,
    index_hbm,
    band_hbm,
    detect_hbm,
    table_hbm,
    weight_hbm,
    rowk_hbm,
    colk_hbm,
    tiles_hbm,
    far,
    cross,
    kept,
    patch_ref,
    offset_ref,
    index_ref,
    band_ref,
    detect_ref,
    table_ref,
    weight_ref,
    rowk_ref,
    colk_ref,
    tiles_ref,
    kernels,
    weights,
    shifted,
    toeplitz,
    matches,
    sums,
    extra,
    arrival,
    ready,
):
    visits = band_ref.shape[0]
    tile_count, rows, width = tiles_ref.shape
    per_visit = tile_count // visits
    basis, taps = rowk_ref.shape
    half = taps // 2
    owner = lax.axis_index("ra")
    way = 2 * lax.rem(owner, 2) - 1

    small = [
        pltpu.make_async_copy(source, target, ready.at[place])
        for place, (source, target) in enumerate(
            (
                (index_hbm, index_ref),
                (table_hbm, table_ref),
                (weight_hbm, weight_ref),
                (rowk_hbm, rowk_ref),
                (colk_hbm, colk_ref),
                (patch_hbm, patch_ref),
                (offset_hbm, offset_ref),
                (band_hbm, band_ref),
                (detect_hbm, detect_ref),
            )
        )
    ]
    for copy in small:
        copy.start()

    def fetch(visit):
        held = pl.ds(visit * per_visit, per_visit)
        return pltpu.make_async_copy(tiles_hbm.at[held], tiles_ref.at[held], arrival.at[visit])

    for visit in range(visits):
        fetch(visit).start()

    def iota(shape, axis):
        return lax.broadcasted_iota(jnp.int32, shape, axis)

    def across(left, right, **options):
        return lax.dot_general(
            left,
            right,
            (((1,), (1,)), ((), ())),
            preferred_element_type=jnp.float32,
            **options,
        )

    extra[...] = jnp.zeros_like(extra)
    for place in range(per_visit):
        for side in range(2):
            for fine in range(4):
                top = fine * FINE_ROWS
                shifted[place, side, top : top + 16, :width] = jnp.zeros(
                    (16, width), jnp.bfloat16
                )
                shifted[place, side, top + 48 : top + 64, width:] = jnp.zeros(
                    (16, width), jnp.bfloat16
                )
    eye = (iota((tile_count, tile_count), 0) == iota((tile_count, tile_count), 1)).astype(
        jnp.bfloat16
    )

    def edge(distance):
        here = iota((16, width), 1) + distance
        return ((here >= 0) & (here < width)).astype(jnp.float32).astype(jnp.bfloat16)

    edges = {distance: edge(distance) for distance in range(-4, 4) if distance != 0}

    def moved_tile(value, distance):
        if distance == 0:
            return value
        turned = pltpu.roll(value, -distance % width, 1).reshape(rows // 16, 16, width)
        return (turned * edges[distance][None]).reshape(rows, width)

    def shift_tiles(visit):
        for place in range(per_visit):
            pixels = tiles_ref[visit * per_visit + place]
            for side in range(2):
                for fine in range(4):
                    part = moved_tile(pixels, -1 - fine if side else fine)
                    top = fine * FINE_ROWS
                    shifted[place, side, top + 16 : top + 64, :width] = part[:48]
                    shifted[place, side, top : top + 48, width:] = part[16:]

    fetch(0).wait()
    shift_tiles(0)
    for copy in small:
        copy.wait()
    weights[...] = across(eye, jnp.broadcast_to(weight_ref[...], (width, tile_count)))
    entry = iota((1, table_ref.shape[1]), 1)
    chosen = jnp.concatenate(
        [(entry == index_ref[j]).astype(jnp.float32) for j in range(tile_count)], axis=0
    ).astype(jnp.bfloat16)
    rest_of = table_ref[...]
    coeffs = jnp.zeros((tile_count, basis), jnp.float32)
    for _ in range(3):
        piece = rest_of.astype(jnp.bfloat16)
        rest_of = rest_of - piece.astype(jnp.float32)
        coeffs += across(chosen, piece)

    line = iota((2 * VECTORS, taps), 0)
    column = iota((2 * VECTORS, taps), 1)
    block = lax.rem(line, VECTORS) // 2
    step = 4 * lax.rem(block, COARSE) + 2 * lax.rem(line, 2) + line // VECTORS
    wanted = jnp.where(block < COARSE, half + step, half - 1 - step)
    wanted = jnp.where(lax.rem(line, VECTORS) < 4 * COARSE, wanted, -1)
    col_taps = across((wanted == column).astype(jnp.bfloat16), colk_ref[...])
    tap = iota((taps, width), 0)
    lane = iota((taps, width), 1)
    total = None
    for side in range(2):
        place = (lane == tap + LEAD + side * FINE_ROWS).astype(jnp.bfloat16)
        row_taps = jnp.dot(
            rowk_ref[...], place, preferred_element_type=jnp.float32
        ).astype(jnp.bfloat16)
        part = col_taps[side * VECTORS : (side + 1) * VECTORS]
        mix = jnp.concatenate([part * coeffs[j : j + 1] for j in range(tile_count)], axis=0)
        high = mix.astype(jnp.bfloat16)
        low = (mix - high.astype(jnp.float32)).astype(jnp.bfloat16)
        term = jnp.dot(high, row_taps, preferred_element_type=jnp.float32) + jnp.dot(
            low, row_taps, preferred_element_type=jnp.float32
        )
        total = term if total is None else total + term
    kernels[...] = total

    lane = iota((rows, width), 1)
    column = iota((1, width), 1)

    def moved(value, distance):
        if distance == 0:
            return value
        turned = pltpu.roll(value, -distance % width, 1)
        here = lane[: value.shape[0]] + distance
        return jnp.where((here >= 0) & (here < width), turned, jnp.zeros_like(turned))

    def one_visit(visit, unused):
        sums[...] = jnp.zeros_like(sums)
        first = visit * per_visit
        for place in range(per_visit):
            tile = first + place
            for side in range(2):
                for coarse in range(COARSE):
                    for pair in range(2):
                        vector = pl.ds(
                            tile * VECTORS + (side * COARSE + coarse) * 2 + pair, 1
                        )
                        spread = jnp.broadcast_to(kernels[vector, :], (16, width))
                        turned = pltpu.roll(spread, 0, 1, stride=1, stride_axis=0).astype(
                            jnp.bfloat16
                        )
                        for lower in range(BLOCK // 16):
                            top = coarse * BLOCK + lower * 16
                            toeplitz[
                                place,
                                side,
                                top : top + 16,
                                pair * width : (pair + 1) * width,
                            ] = pltpu.roll(turned, lower * 16, 1) if lower else turned
        for place in range(per_visit):
            matched = [jnp.zeros((BLOCK, width), jnp.float32) for _ in range(2)]
            for side in range(2):
                passed = jnp.dot(
                    toeplitz[place, side],
                    shifted[place, side],
                    preferred_element_type=jnp.float32,
                )
                for part in range(2):
                    for coarse in range(COARSE):
                        matched[part] += moved(
                            passed[
                                coarse * BLOCK : (coarse + 1) * BLOCK,
                                part * width : (part + 1) * width,
                            ],
                            -4 * coarse if side else 4 * coarse,
                        )
            matches[place] = jnp.concatenate(matched, axis=0)
        for place in range(per_visit):
            tile = first + place
            offset = offset_ref[tile]
            bucket = lax.rem(patch_ref[tile] - owner + REACH + patches, patches)
            weight = weights[pl.ds(tile, 1), :]
            turned = pltpu.roll(
                matches[place] * weight, lax.rem(offset, width), 1
            )
            sums[bucket, :, :width] += jnp.where(lane >= offset, turned, 0.0)
            sums[bucket, :, width:] += jnp.where(lane < offset, turned, 0.0)
            extra[bucket, pl.ds(visit, 1), :] += jnp.concatenate(
                [
                    jnp.where(column >= offset, weight, 0.0),
                    jnp.where(column < offset, weight, 0.0),
                ],
                axis=1,
            )


        @pl.when(visit + 1 < visits)
        def prepare():
            fetch(visit + 1).wait()
            shift_tiles(visit + 1)

        held = pl.ds(pl.multiple_of(visit * rows, rows), rows)
        far[held, :] = sums[REACH + 2 * way].astype(jnp.bfloat16)
        cross[0, held, :] = sums[REACH - 2 * way].astype(jnp.bfloat16)
        cross[1, held, :] = sums[REACH - way].astype(jnp.bfloat16)
        kept[0, held, :] = sums[REACH + way].astype(jnp.bfloat16)
        kept[1, held, :] = sums[REACH].astype(jnp.bfloat16)
        return unused

    lax.fori_loop(0, visits, one_visit, 0)

    row = iota((EXTRA, PW), 0)
    lane = iota((1, PW), 1)

    def spread_bands(visit_of, limit):
        line = jnp.full((1, PW), -1.0, jnp.float32)
        for visit in range(visits):
            line = jnp.where(
                (lane < limit) & (visit_of == visit), band_ref[visit].astype(jnp.float32), line
            )
        return line

    by_row = spread_bands(lane // rows, visits * rows)
    by_weight = spread_bands(lax.rem(lane, visits), 2 * visits)
    detect = jnp.zeros((1, PW), jnp.float32)
    for b in range(BANDS):
        detect = jnp.where(lane == b, detect_ref[b], detect)

    def footer(bucket):
        held = extra[bucket]
        high = held.astype(jnp.bfloat16).astype(jnp.float32)
        low = jnp.concatenate([held[-visits:], (held - high)[:-visits]], axis=0)
        mixed = jnp.where((row >= visits) & (row < 2 * visits), low, high)
        mixed = jnp.where(row == 2 * visits, by_row, mixed)
        mixed = jnp.where(row == 2 * visits + 1, by_weight, mixed)
        rest = detect
        for place in range(DETECT, DETECT + 3):
            piece = rest.astype(jnp.bfloat16).astype(jnp.float32)
            rest = rest - piece
            mixed = jnp.where(row == place, piece, mixed)
        return mixed.astype(jnp.bfloat16)

    far[rows * visits :, :] = footer(REACH + 2 * way)
    cross[0, rows * visits :, :] = footer(REACH - 2 * way)
    cross[1, rows * visits :, :] = footer(REACH - way)
    kept[0, rows * visits :, :] = footer(REACH + way)
    kept[1, rows * visits :, :] = footer(REACH)


def add_message(count, groups, message):
    depth = message.shape[0] - EXTRA
    span = depth // count
    row_share = span // groups
    line = lax.broadcasted_iota(jnp.int32, (row_share, depth), 0)
    lane = lax.rem(lax.broadcasted_iota(jnp.int32, (row_share, depth), 1), span)
    band_line = lax.broadcasted_iota(jnp.int32, (8, EXTRA), 0).astype(jnp.float32)
    extra = message[depth:, :]
    bands = extra[2 * count : 2 * count + 2].astype(jnp.float32)
    pick = jnp.concatenate(
        [
            jnp.where(
                (lane == line + part * row_share) & (bands[:1, :depth] == float(b)), 1.0, 0.0
            )
            for part in range(groups)
            for b in range(BANDS)
        ],
        axis=0,
    ).astype(jnp.bfloat16)
    totals = jnp.dot(pick, message[:depth, :], preferred_element_type=jnp.float32)
    pick = (bands[1:, :EXTRA] == band_line).astype(jnp.bfloat16)
    return totals, jnp.dot(pick, extra, preferred_element_type=jnp.float32)


def add_banded(totals, weights, messages):
    depth = totals.shape[0]
    for message in messages:
        totals += message[:depth, :].astype(jnp.float32)
        footer = message[depth:, :].astype(jnp.float32)
        weights += footer[:8] + footer[8:]
    return totals, weights


def write_banded(message, totals, weights):
    depth = totals.shape[0]
    high = weights.astype(jnp.bfloat16).astype(jnp.float32)
    message[:depth, :] = totals.astype(jnp.bfloat16)
    message[depth:, :] = jnp.concatenate([high, weights - high], axis=0).astype(jnp.bfloat16)


def part_of(held, turn, groups):
    depth = held.shape[0] // groups
    part = lax.rem(lax.axis_index("band") + turn, groups)
    return held[pl.ds(pl.multiple_of(part * depth, depth), depth), :]


def keep_kernel(count, groups, kept_ref, totals_ref, weights_ref, detect_ref):
    for place in range(2):
        totals_ref[place], weights_ref[place] = add_message(count, groups, kept_ref.at[place])
    extra = kept_ref[0, kept_ref.shape[1] - EXTRA :, :].astype(jnp.float32)
    detect = extra[DETECT : DETECT + 1] + extra[DETECT + 1 : DETECT + 2]
    detect += extra[DETECT + 2 : DETECT + 3]
    line = lax.broadcasted_iota(jnp.int32, (8, PW), 0)
    lane = lax.broadcasted_iota(jnp.int32, (8, PW), 1)
    chosen = jnp.sum(jnp.where(line == lane, detect, 0.0), axis=1, keepdims=True)
    detect_ref[...] = jnp.broadcast_to(chosen, (8, PW))


def merge_kernel(count, groups, totals_ref, weights_ref, cross_ref, *refs):
    messages = refs[:groups]
    home_ref, home_weight_ref, held = refs[groups:]
    totals, weights = add_message(count, groups, cross_ref.at[0])
    held[...] = totals + totals_ref[0]
    weights += weights_ref[0]
    for turn, message in enumerate(messages):
        write_banded(message, part_of(held, turn, groups), weights)
    totals, weights = add_message(count, groups, cross_ref.at[1])
    home_ref[...] = totals + totals_ref[1]
    home_weight_ref[...] = weights + weights_ref[1]


def home_kernel(count, groups, home_ref, home_weight_ref, far_ref, *refs):
    messages = refs[: groups - 1]
    own_ref, own_weight_ref, held = refs[groups - 1 :]
    totals, weights = add_message(count, groups, far_ref)
    held[...] = totals + home_ref[...]
    weights += home_weight_ref[...]
    for turn, message in enumerate(messages, 1):
        write_banded(message, part_of(held, turn, groups), weights)
    own_ref[...] = part_of(held, 0, groups)
    own_weight_ref[...] = weights


def early_kernel(*refs):
    messages = refs[:-2]
    totals_ref, weights_ref = refs[-2:]
    depth = totals_ref.shape[0]
    totals_ref[...], weights_ref[...] = add_banded(
        jnp.zeros((depth, PW), jnp.float32), jnp.zeros((8, PW), jnp.float32), messages
    )


def combine_kernel(
    detect_ref, own_ref, own_weight_ref, near_ref, near_weight_ref, *refs
):
    coadd_ref, detection_ref = refs[-2:]
    row_share = coadd_ref.shape[1]
    totals, weights = add_banded(
        own_ref[...] + near_ref[...], own_weight_ref[...] + near_weight_ref[...], refs[:-2]
    )
    weights = jnp.maximum(weights, 1.0)
    detection = jnp.zeros((row_share, PW), jnp.float32)
    for b in range(BANDS):
        coadd = totals[b * row_share : (b + 1) * row_share] / weights[b : b + 1]
        coadd_ref[b] = coadd
        detection += detect_ref[b : b + 1] * coadd
    detection_ref[...] = detection


def local(
    tiles,
    tile_patch,
    tile_offset,
    tile_weight,
    visit_band,
    coeff_index,
    coeff_table,
    row_kernels,
    column_kernels,
    band_weight,
):
    tile_count, rows, width = tiles.shape
    visits = visit_band.shape[0]
    per_visit = tile_count // visits
    basis, taps = row_kernels.shape
    patches = lax.axis_size("ra")
    groups = lax.axis_size("band")
    row_share = rows // groups
    length = visits * rows + EXTRA
    message_shape = jax.ShapeDtypeStruct((length, PW), jnp.bfloat16)
    pair_shape = jax.ShapeDtypeStruct((2, length, PW), jnp.bfloat16)
    band_shape = jax.ShapeDtypeStruct((BANDS * row_share + EXTRA, PW), jnp.bfloat16)
    part_shape = jax.ShapeDtypeStruct((BANDS * row_share, PW), jnp.float32)
    whole_shape = jax.ShapeDtypeStruct((BANDS * rows, PW), jnp.float32)
    weight_shape = jax.ShapeDtypeStruct((8, PW), jnp.float32)

    vmem = pl.BlockSpec(memory_space=pltpu.VMEM)
    anywhere = pl.BlockSpec(memory_space=pl.ANY)
    far, cross, kept = pl.pallas_call(
        functools.partial(match_kernel, patches),
        in_specs=[anywhere] * 10,
        out_specs=[vmem] * 3,
        out_shape=[message_shape, pair_shape, pair_shape],
        scratch_shapes=[
            pltpu.SMEM((tile_count,), jnp.int32),
            pltpu.SMEM((tile_count,), jnp.int32),
            pltpu.SMEM((tile_count,), jnp.int32),
            pltpu.SMEM((visits,), jnp.int32),
            pltpu.SMEM((BANDS,), jnp.float32),
            pltpu.VMEM(coeff_table.shape[::-1], jnp.float32),
            pltpu.VMEM((1, tile_count), jnp.bfloat16),
            pltpu.VMEM((basis, taps), jnp.bfloat16),
            pltpu.VMEM((basis, taps), jnp.bfloat16),
            pltpu.VMEM((tile_count, rows, width), jnp.bfloat16),
            pltpu.VMEM((tile_count * VECTORS, width), jnp.float32),
            pltpu.VMEM((tile_count, width), jnp.float32),
            pltpu.VMEM((per_visit, 2, 4 * FINE_ROWS, 2 * width), jnp.bfloat16),
            pltpu.VMEM((per_visit, 2, COARSE * BLOCK, 2 * width), jnp.bfloat16),
            pltpu.VMEM((per_visit, rows, width), jnp.float32),
            pltpu.VMEM((SPREAD, rows, PW), jnp.float32),
            pltpu.VMEM((SPREAD, EXTRA, PW), jnp.float32),
            pltpu.SemaphoreType.DMA((visits,)),
            pltpu.SemaphoreType.DMA((9,)),
        ],
        compiler_params=pltpu.CompilerParams(vmem_limit_bytes=62 * 1024 * 1024),
        name="match_and_sum",
    )(
        tile_patch,
        tile_offset,
        coeff_index,
        visit_band,
        band_weight,
        coeff_table.T,
        tile_weight.reshape(1, tile_count),
        row_kernels,
        column_kernels,
        tiles,
    )

    def send(message, goal, turn):
        route = [
            (o * groups + g, goal(o) % patches * groups + (g + turn) % groups)
            for o in range(patches)
            for g in range(groups)
        ]
        return lax.ppermute(message, ("ra", "band"), route)

    def onward(distance):
        return lambda o: o + distance if o % 2 else o - distance

    def local_call(kernel, name, out_shape, *operands, **options):
        return pl.pallas_call(
            kernel,
            in_specs=[vmem] * len(operands),
            out_specs=[vmem] * len(out_shape),
            out_shape=out_shape,
            compiler_params=pltpu.CompilerParams(vmem_limit_bytes=40 * 1024 * 1024),
            name=name,
            **options,
        )(*operands)

    held = [pltpu.VMEM(whole_shape.shape, jnp.float32)]
    cross = send(cross, onward(-1), 0)
    far = send(far, onward(2), 0)
    *kept, detect = local_call(
        functools.partial(keep_kernel, visits, groups),
        "keep",
        [
            jax.ShapeDtypeStruct((2,) + whole_shape.shape, jnp.float32),
            jax.ShapeDtypeStruct((2,) + weight_shape.shape, jnp.float32),
            weight_shape,
        ],
        kept,
    )
    *near, home, home_weight = local_call(
        functools.partial(merge_kernel, visits, groups),
        "merge",
        [band_shape] * groups + [whole_shape, weight_shape],
        *kept,
        cross,
        scratch_shapes=held,
    )
    near = [send(near[turn], onward(1), turn) for turn in range(groups)]
    *others, own, own_weight = local_call(
        functools.partial(home_kernel, visits, groups),
        "home",
        [band_shape] * (groups - 1) + [part_shape, weight_shape],
        home,
        home_weight,
        far,
        scratch_shapes=held,
    )
    others = [send(others[turn - 1], onward(0), turn) for turn in range(1, groups)]
    near = local_call(early_kernel, "combine_early", [part_shape, weight_shape], *near)
    return local_call(
        combine_kernel,
        "combine",
        (
            jax.ShapeDtypeStruct((BANDS, row_share, PW), jnp.float32),
            jax.ShapeDtypeStruct((row_share, PW), jnp.float32),
        ),
        detect,
        own,
        own_weight,
        *near,
        *others,
    )


def solution(mesh):
    return jax.shard_map(
        local,
        mesh=mesh,
        in_specs=(
            P(("ra", "band"), None, None),
            P(("ra", "band")),
            P(("ra", "band")),
            P(("ra", "band")),
            P(("ra", "band")),
            P(("ra", "band")),
            P(),
            P(),
            P(),
            P(),
        ),
        out_specs=(P(None, "band", "ra"), P("band", "ra")),
        check_vma=False,
    )
```

```python
import functools

import jax
import jax.numpy as jnp
from jax import lax
from jax.experimental import pallas as pl
from jax.experimental.pallas import tpu as pltpu
from jax.sharding import PartitionSpec as P

PW = 256
BANDS = 6
REACH = 2
SPREAD = 2 * REACH + 1
EXTRA = 16
DETECT = 10
BLOCK = 32
COARSE = 3
VECTORS = 16
FINE_ROWS = 64
LEAD = 6


def match_kernel(
    patches,
    patch_hbm,
    offset_hbm,
    index_hbm,
    band_hbm,
    detect_hbm,
    table_hbm,
    weight_hbm,
    rowk_hbm,
    colk_hbm,
    tiles_hbm,
    far,
    cross,
    kept,
    patch_ref,
    offset_ref,
    index_ref,
    band_ref,
    detect_ref,
    table_ref,
    weight_ref,
    rowk_ref,
    colk_ref,
    tiles_ref,
    kernels,
    weights,
    shifted,
    toeplitz,
    matches,
    sums,
    extra,
    arrival,
    ready,
):
    visits = band_ref.shape[0]
    tile_count, rows, width = tiles_ref.shape
    per_visit = tile_count // visits
    basis, taps = rowk_ref.shape
    half = taps // 2
    owner = lax.axis_index("ra")
    way = 2 * lax.rem(owner, 2) - 1

    small = [
        pltpu.make_async_copy(source, target, ready.at[place])
        for place, (source, target) in enumerate(
            (
                (index_hbm, index_ref),
                (table_hbm, table_ref),
                (weight_hbm, weight_ref),
                (rowk_hbm, rowk_ref),
                (colk_hbm, colk_ref),
                (patch_hbm, patch_ref),
                (offset_hbm, offset_ref),
                (band_hbm, band_ref),
                (detect_hbm, detect_ref),
            )
        )
    ]
    for copy in small:
        copy.start()

    def fetch(visit):
        held = pl.ds(visit * per_visit, per_visit)
        return pltpu.make_async_copy(tiles_hbm.at[held], tiles_ref.at[held], arrival.at[visit])

    for visit in range(visits):
        fetch(visit).start()

    def iota(shape, axis):
        return lax.broadcasted_iota(jnp.int32, shape, axis)

    def across(left, right, **options):
        return lax.dot_general(
            left,
            right,
            (((1,), (1,)), ((), ())),
            preferred_element_type=jnp.float32,
            **options,
        )

    extra[...] = jnp.zeros_like(extra)
    for place in range(per_visit):
        for side in range(2):
            for fine in range(4):
                top = fine * FINE_ROWS
                shifted[place, side, top : top + 16, :width] = jnp.zeros(
                    (16, width), jnp.bfloat16
                )
                shifted[place, side, top + 48 : top + 64, width:] = jnp.zeros(
                    (16, width), jnp.bfloat16
                )
    eye = (iota((tile_count, tile_count), 0) == iota((tile_count, tile_count), 1)).astype(
        jnp.bfloat16
    )
    for copy in small:
        copy.wait()
    weights[...] = across(eye, jnp.broadcast_to(weight_ref[...], (width, tile_count)))
    entry = iota((1, table_ref.shape[1]), 1)
    chosen = jnp.concatenate(
        [(entry == index_ref[j]).astype(jnp.float32) for j in range(tile_count)], axis=0
    ).astype(jnp.bfloat16)
    rest_of = table_ref[...]
    coeffs = jnp.zeros((tile_count, basis), jnp.float32)
    for _ in range(3):
        piece = rest_of.astype(jnp.bfloat16)
        rest_of = rest_of - piece.astype(jnp.float32)
        coeffs += across(chosen, piece)

    line = iota((2 * VECTORS, taps), 0)
    column = iota((2 * VECTORS, taps), 1)
    block = lax.rem(line, VECTORS) // 2
    step = 4 * lax.rem(block, COARSE) + 2 * lax.rem(line, 2) + line // VECTORS
    wanted = jnp.where(block < COARSE, half + step, half - 1 - step)
    wanted = jnp.where(lax.rem(line, VECTORS) < 4 * COARSE, wanted, -1)
    col_taps = across((wanted == column).astype(jnp.bfloat16), colk_ref[...])
    tap = iota((taps, width), 0)
    lane = iota((taps, width), 1)
    total = None
    for side in range(2):
        place = (lane == tap + LEAD + side * FINE_ROWS).astype(jnp.bfloat16)
        row_taps = jnp.dot(
            rowk_ref[...], place, preferred_element_type=jnp.float32
        ).astype(jnp.bfloat16)
        part = col_taps[side * VECTORS : (side + 1) * VECTORS]
        mix = jnp.concatenate([part * coeffs[j : j + 1] for j in range(tile_count)], axis=0)
        high = mix.astype(jnp.bfloat16)
        low = (mix - high.astype(jnp.float32)).astype(jnp.bfloat16)
        term = jnp.dot(high, row_taps, preferred_element_type=jnp.float32) + jnp.dot(
            low, row_taps, preferred_element_type=jnp.float32
        )
        total = term if total is None else total + term
    kernels[...] = total

    lane = iota((rows, width), 1)
    column = iota((1, width), 1)

    def moved(value, distance):
        if distance == 0:
            return value
        turned = pltpu.roll(value, -distance % width, 1)
        here = lane[: value.shape[0]] + distance
        return jnp.where((here >= 0) & (here < width), turned, jnp.zeros_like(turned))

    def one_visit(visit, unused):
        fetch(visit).wait()
        sums[...] = jnp.zeros_like(sums)
        first = visit * per_visit
        for place in range(per_visit):
            tile = first + place
            pixels = tiles_ref[tile].astype(jnp.float32)
            for side in range(2):
                for fine in range(4):
                    part = moved(pixels, -1 - fine if side else fine).astype(jnp.bfloat16)
                    top = fine * FINE_ROWS
                    shifted[place, side, top + 16 : top + 64, :width] = part[:48]
                    shifted[place, side, top : top + 48, width:] = part[16:]
                for coarse in range(COARSE):
                    for pair in range(2):
                        vector = pl.ds(
                            tile * VECTORS + (side * COARSE + coarse) * 2 + pair, 1
                        )
                        spread = jnp.broadcast_to(kernels[vector, :], (BLOCK, width))
                        turned = pltpu.roll(spread, 0, 1, stride=1, stride_axis=0)
                        toeplitz[
                            place,
                            side,
                            coarse * BLOCK : (coarse + 1) * BLOCK,
                            pair * width : (pair + 1) * width,
                        ] = turned.astype(jnp.bfloat16)
        for place in range(per_visit):
            matched = [jnp.zeros((BLOCK, width), jnp.float32) for _ in range(2)]
            for side in range(2):
                passed = jnp.dot(
                    toeplitz[place, side],
                    shifted[place, side],
                    preferred_element_type=jnp.float32,
                )
                for part in range(2):
                    for coarse in range(COARSE):
                        matched[part] += moved(
                            passed[
                                coarse * BLOCK : (coarse + 1) * BLOCK,
                                part * width : (part + 1) * width,
                            ],
                            -4 * coarse if side else 4 * coarse,
                        )
            matches[place] = jnp.concatenate(matched, axis=0)
        for place in range(per_visit):
            tile = first + place
            offset = offset_ref[tile]
            bucket = lax.rem(patch_ref[tile] - owner + REACH + patches, patches)
            weight = weights[pl.ds(tile, 1), :]
            turned = pltpu.roll(
                matches[place] * weight, lax.rem(offset, width), 1
            )
            sums[bucket, :, :width] += jnp.where(lane >= offset, turned, 0.0)
            sums[bucket, :, width:] += jnp.where(lane < offset, turned, 0.0)
            extra[bucket, pl.ds(visit, 1), :] += jnp.concatenate(
                [
                    jnp.where(column >= offset, weight, 0.0),
                    jnp.where(column < offset, weight, 0.0),
                ],
                axis=1,
            )

        held = pl.ds(pl.multiple_of(visit * rows, rows), rows)
        far[held, :] = sums[REACH + 2 * way].astype(jnp.bfloat16)
        cross[0, held, :] = sums[REACH - 2 * way].astype(jnp.bfloat16)
        cross[1, held, :] = sums[REACH - way].astype(jnp.bfloat16)
        kept[0, held, :] = sums[REACH + way].astype(jnp.bfloat16)
        kept[1, held, :] = sums[REACH].astype(jnp.bfloat16)
        return unused

    lax.fori_loop(0, visits, one_visit, 0)

    row = iota((EXTRA, PW), 0)
    lane = iota((1, PW), 1)

    def spread_bands(visit_of, limit):
        line = jnp.full((1, PW), -1.0, jnp.float32)
        for visit in range(visits):
            line = jnp.where(
                (lane < limit) & (visit_of == visit), band_ref[visit].astype(jnp.float32), line
            )
        return line

    by_row = spread_bands(lane // rows, visits * rows)
    by_weight = spread_bands(lax.rem(lane, visits), 2 * visits)
    detect = jnp.zeros((1, PW), jnp.float32)
    for b in range(BANDS):
        detect = jnp.where(lane == b, detect_ref[b], detect)

    def footer(bucket):
        held = extra[bucket]
        high = held.astype(jnp.bfloat16).astype(jnp.float32)
        low = jnp.concatenate([held[-visits:], (held - high)[:-visits]], axis=0)
        mixed = jnp.where((row >= visits) & (row < 2 * visits), low, high)
        mixed = jnp.where(row == 2 * visits, by_row, mixed)
        mixed = jnp.where(row == 2 * visits + 1, by_weight, mixed)
        rest = detect
        for place in range(DETECT, DETECT + 3):
            piece = rest.astype(jnp.bfloat16).astype(jnp.float32)
            rest = rest - piece
            mixed = jnp.where(row == place, piece, mixed)
        return mixed.astype(jnp.bfloat16)

    far[rows * visits :, :] = footer(REACH + 2 * way)
    cross[0, rows * visits :, :] = footer(REACH - 2 * way)
    cross[1, rows * visits :, :] = footer(REACH - way)
    kept[0, rows * visits :, :] = footer(REACH + way)
    kept[1, rows * visits :, :] = footer(REACH)


def add_message(count, groups, message):
    depth = message.shape[0] - EXTRA
    span = depth // count
    row_share = span // groups
    line = lax.broadcasted_iota(jnp.int32, (row_share, depth), 0)
    lane = lax.rem(lax.broadcasted_iota(jnp.int32, (row_share, depth), 1), span)
    band_line = lax.broadcasted_iota(jnp.int32, (8, EXTRA), 0).astype(jnp.float32)
    extra = message[depth:, :]
    bands = extra[2 * count : 2 * count + 2].astype(jnp.float32)
    pick = jnp.concatenate(
        [
            jnp.where(
                (lane == line + part * row_share) & (bands[:1, :depth] == float(b)), 1.0, 0.0
            )
            for part in range(groups)
            for b in range(BANDS)
        ],
        axis=0,
    ).astype(jnp.bfloat16)
    totals = jnp.dot(pick, message[:depth, :], preferred_element_type=jnp.float32)
    pick = (bands[1:, :EXTRA] == band_line).astype(jnp.bfloat16)
    return totals, jnp.dot(pick, extra, preferred_element_type=jnp.float32)


def add_banded(totals, weights, messages):
    depth = totals.shape[0]
    for message in messages:
        totals += message[:depth, :].astype(jnp.float32)
        footer = message[depth:, :].astype(jnp.float32)
        weights += footer[:8] + footer[8:]
    return totals, weights


def write_banded(message, totals, weights):
    depth = totals.shape[0]
    high = weights.astype(jnp.bfloat16).astype(jnp.float32)
    message[:depth, :] = totals.astype(jnp.bfloat16)
    message[depth:, :] = jnp.concatenate([high, weights - high], axis=0).astype(jnp.bfloat16)


def part_of(held, turn, groups):
    depth = held.shape[0] // groups
    part = lax.rem(lax.axis_index("band") + turn, groups)
    return held[pl.ds(pl.multiple_of(part * depth, depth), depth), :]


def keep_kernel(count, groups, kept_ref, totals_ref, weights_ref, detect_ref):
    for place in range(2):
        totals_ref[place], weights_ref[place] = add_message(count, groups, kept_ref.at[place])
    extra = kept_ref[0, kept_ref.shape[1] - EXTRA :, :].astype(jnp.float32)
    detect = extra[DETECT : DETECT + 1] + extra[DETECT + 1 : DETECT + 2]
    detect += extra[DETECT + 2 : DETECT + 3]
    line = lax.broadcasted_iota(jnp.int32, (8, PW), 0)
    lane = lax.broadcasted_iota(jnp.int32, (8, PW), 1)
    chosen = jnp.sum(jnp.where(line == lane, detect, 0.0), axis=1, keepdims=True)
    detect_ref[...] = jnp.broadcast_to(chosen, (8, PW))


def merge_kernel(count, groups, totals_ref, weights_ref, cross_ref, *refs):
    messages = refs[:groups]
    home_ref, home_weight_ref, held = refs[groups:]
    totals, weights = add_message(count, groups, cross_ref.at[0])
    held[...] = totals + totals_ref[0]
    weights += weights_ref[0]
    for turn, message in enumerate(messages):
        write_banded(message, part_of(held, turn, groups), weights)
    totals, weights = add_message(count, groups, cross_ref.at[1])
    home_ref[...] = totals + totals_ref[1]
    home_weight_ref[...] = weights + weights_ref[1]


def home_kernel(count, groups, home_ref, home_weight_ref, far_ref, *refs):
    messages = refs[: groups - 1]
    own_ref, own_weight_ref, held = refs[groups - 1 :]
    totals, weights = add_message(count, groups, far_ref)
    held[...] = totals + home_ref[...]
    weights += home_weight_ref[...]
    for turn, message in enumerate(messages, 1):
        write_banded(message, part_of(held, turn, groups), weights)
    own_ref[...] = part_of(held, 0, groups)
    own_weight_ref[...] = weights


def early_kernel(*refs):
    messages = refs[:-2]
    totals_ref, weights_ref = refs[-2:]
    depth = totals_ref.shape[0]
    totals_ref[...], weights_ref[...] = add_banded(
        jnp.zeros((depth, PW), jnp.float32), jnp.zeros((8, PW), jnp.float32), messages
    )


def combine_kernel(
    detect_ref, own_ref, own_weight_ref, near_ref, near_weight_ref, *refs
):
    coadd_ref, detection_ref = refs[-2:]
    row_share = coadd_ref.shape[1]
    totals, weights = add_banded(
        own_ref[...] + near_ref[...], own_weight_ref[...] + near_weight_ref[...], refs[:-2]
    )
    weights = jnp.maximum(weights, 1.0)
    detection = jnp.zeros((row_share, PW), jnp.float32)
    for b in range(BANDS):
        coadd = totals[b * row_share : (b + 1) * row_share] / weights[b : b + 1]
        coadd_ref[b] = coadd
        detection += detect_ref[b : b + 1] * coadd
    detection_ref[...] = detection


def local(
    tiles,
    tile_patch,
    tile_offset,
    tile_weight,
    visit_band,
    coeff_index,
    coeff_table,
    row_kernels,
    column_kernels,
    band_weight,
):
    tile_count, rows, width = tiles.shape
    visits = visit_band.shape[0]
    per_visit = tile_count // visits
    basis, taps = row_kernels.shape
    patches = lax.axis_size("ra")
    groups = lax.axis_size("band")
    row_share = rows // groups
    length = visits * rows + EXTRA
    message_shape = jax.ShapeDtypeStruct((length, PW), jnp.bfloat16)
    pair_shape = jax.ShapeDtypeStruct((2, length, PW), jnp.bfloat16)
    band_shape = jax.ShapeDtypeStruct((BANDS * row_share + EXTRA, PW), jnp.bfloat16)
    part_shape = jax.ShapeDtypeStruct((BANDS * row_share, PW), jnp.float32)
    whole_shape = jax.ShapeDtypeStruct((BANDS * rows, PW), jnp.float32)
    weight_shape = jax.ShapeDtypeStruct((8, PW), jnp.float32)

    vmem = pl.BlockSpec(memory_space=pltpu.VMEM)
    anywhere = pl.BlockSpec(memory_space=pl.ANY)
    far, cross, kept = pl.pallas_call(
        functools.partial(match_kernel, patches),
        in_specs=[anywhere] * 10,
        out_specs=[vmem] * 3,
        out_shape=[message_shape, pair_shape, pair_shape],
        scratch_shapes=[
            pltpu.SMEM((tile_count,), jnp.int32),
            pltpu.SMEM((tile_count,), jnp.int32),
            pltpu.SMEM((tile_count,), jnp.int32),
            pltpu.SMEM((visits,), jnp.int32),
            pltpu.SMEM((BANDS,), jnp.float32),
            pltpu.VMEM(coeff_table.shape[::-1], jnp.float32),
            pltpu.VMEM((1, tile_count), jnp.bfloat16),
            pltpu.VMEM((basis, taps), jnp.bfloat16),
            pltpu.VMEM((basis, taps), jnp.bfloat16),
            pltpu.VMEM((tile_count, rows, width), jnp.bfloat16),
            pltpu.VMEM((tile_count * VECTORS, width), jnp.float32),
            pltpu.VMEM((tile_count, width), jnp.float32),
            pltpu.VMEM((per_visit, 2, 4 * FINE_ROWS, 2 * width), jnp.bfloat16),
            pltpu.VMEM((per_visit, 2, COARSE * BLOCK, 2 * width), jnp.bfloat16),
            pltpu.VMEM((per_visit, rows, width), jnp.float32),
            pltpu.VMEM((SPREAD, rows, PW), jnp.float32),
            pltpu.VMEM((SPREAD, EXTRA, PW), jnp.float32),
            pltpu.SemaphoreType.DMA((visits,)),
            pltpu.SemaphoreType.DMA((9,)),
        ],
        compiler_params=pltpu.CompilerParams(vmem_limit_bytes=62 * 1024 * 1024),
        name="match_and_sum",
    )(
        tile_patch,
        tile_offset,
        coeff_index,
        visit_band,
        band_weight,
        coeff_table.T,
        tile_weight.reshape(1, tile_count),
        row_kernels,
        column_kernels,
        tiles,
    )

    def send(message, goal, turn):
        route = [
            (o * groups + g, goal(o) % patches * groups + (g + turn) % groups)
            for o in range(patches)
            for g in range(groups)
        ]
        return lax.ppermute(message, ("ra", "band"), route)

    def onward(distance):
        return lambda o: o + distance if o % 2 else o - distance

    def local_call(kernel, name, out_shape, *operands, **options):
        return pl.pallas_call(
            kernel,
            in_specs=[vmem] * len(operands),
            out_specs=[vmem] * len(out_shape),
            out_shape=out_shape,
            compiler_params=pltpu.CompilerParams(vmem_limit_bytes=40 * 1024 * 1024),
            name=name,
            **options,
        )(*operands)

    held = [pltpu.VMEM(whole_shape.shape, jnp.float32)]
    cross = send(cross, onward(-1), 0)
    far = send(far, onward(2), 0)
    *kept, detect = local_call(
        functools.partial(keep_kernel, visits, groups),
        "keep",
        [
            jax.ShapeDtypeStruct((2,) + whole_shape.shape, jnp.float32),
            jax.ShapeDtypeStruct((2,) + weight_shape.shape, jnp.float32),
            weight_shape,
        ],
        kept,
    )
    *near, home, home_weight = local_call(
        functools.partial(merge_kernel, visits, groups),
        "merge",
        [band_shape] * groups + [whole_shape, weight_shape],
        *kept,
        cross,
        scratch_shapes=held,
    )
    near = [send(near[turn], onward(1), turn) for turn in range(groups)]
    *others, own, own_weight = local_call(
        functools.partial(home_kernel, visits, groups),
        "home",
        [band_shape] * (groups - 1) + [part_shape, weight_shape],
        home,
        home_weight,
        far,
        scratch_shapes=held,
    )
    others = [send(others[turn - 1], onward(0), turn) for turn in range(1, groups)]
    near = local_call(early_kernel, "combine_early", [part_shape, weight_shape], *near)
    return local_call(
        combine_kernel,
        "combine",
        (
            jax.ShapeDtypeStruct((BANDS, row_share, PW), jnp.float32),
            jax.ShapeDtypeStruct((row_share, PW), jnp.float32),
        ),
        detect,
        own,
        own_weight,
        *near,
        *others,
    )


def solution(mesh):
    return jax.shard_map(
        local,
        mesh=mesh,
        in_specs=(
            P(("ra", "band"), None, None),
            P(("ra", "band")),
            P(("ra", "band")),
            P(("ra", "band")),
            P(("ra", "band")),
            P(("ra", "band")),
            P(),
            P(),
            P(),
            P(),
        ),
        out_specs=(P(None, "band", "ra"), P("band", "ra")),
        check_vma=False,
    )
```

```python
import functools

import jax
import jax.numpy as jnp
from jax import lax
from jax.experimental import pallas as pl
from jax.experimental.pallas import tpu as pltpu
from jax.sharding import PartitionSpec as P

PW = 256
BANDS = 6
REACH = 2
SPREAD = 2 * REACH + 1
EXTRA = 16
DETECT = 10
BLOCK = 32
COARSE = 3
VECTORS = 16
FINE_ROWS = 64
LEAD = 6


def match_kernel(
    patches,
    patch_hbm,
    offset_hbm,
    index_hbm,
    band_hbm,
    detect_hbm,
    table_hbm,
    weight_hbm,
    rowk_hbm,
    colk_hbm,
    tiles_hbm,
    far,
    cross,
    kept,
    patch_ref,
    offset_ref,
    index_ref,
    band_ref,
    detect_ref,
    table_ref,
    weight_ref,
    rowk_ref,
    colk_ref,
    tiles_ref,
    kernels,
    weights,
    shifted,
    toeplitz,
    matches,
    sums,
    extra,
    arrival,
    ready,
):
    visits = band_ref.shape[0]
    tile_count, rows, width = tiles_ref.shape
    per_visit = tile_count // visits
    basis, taps = rowk_ref.shape
    half = taps // 2
    owner = lax.axis_index("ra")
    way = 2 * lax.rem(owner, 2) - 1

    small = [
        pltpu.make_async_copy(source, target, ready.at[place])
        for place, (source, target) in enumerate(
            (
                (index_hbm, index_ref),
                (table_hbm, table_ref),
                (weight_hbm, weight_ref),
                (rowk_hbm, rowk_ref),
                (colk_hbm, colk_ref),
                (patch_hbm, patch_ref),
                (offset_hbm, offset_ref),
                (band_hbm, band_ref),
                (detect_hbm, detect_ref),
            )
        )
    ]
    for copy in small:
        copy.start()

    def fetch(visit):
        held = pl.ds(visit * per_visit, per_visit)
        return pltpu.make_async_copy(tiles_hbm.at[held], tiles_ref.at[held], arrival.at[visit])

    for visit in range(visits):
        fetch(visit).start()

    def iota(shape, axis):
        return lax.broadcasted_iota(jnp.int32, shape, axis)

    def across(left, right, **options):
        return lax.dot_general(
            left,
            right,
            (((1,), (1,)), ((), ())),
            preferred_element_type=jnp.float32,
            **options,
        )

    extra[...] = jnp.zeros_like(extra)
    for place in range(per_visit):
        for side in range(2):
            for fine in range(4):
                top = fine * FINE_ROWS
                shifted[place, side, top : top + 16, :width] = jnp.zeros(
                    (16, width), jnp.bfloat16
                )
                shifted[place, side, top + 48 : top + 64, width:] = jnp.zeros(
                    (16, width), jnp.bfloat16
                )
    eye = (iota((tile_count, tile_count), 0) == iota((tile_count, tile_count), 1)).astype(
        jnp.bfloat16
    )
    for copy in small:
        copy.wait()
    weights[...] = across(eye, jnp.broadcast_to(weight_ref[...], (width, tile_count)))
    entry = iota((1, table_ref.shape[1]), 1)
    chosen = jnp.concatenate(
        [(entry == index_ref[j]).astype(jnp.float32) for j in range(tile_count)], axis=0
    ).astype(jnp.bfloat16)
    rest_of = table_ref[...]
    coeffs = jnp.zeros((tile_count, basis), jnp.float32)
    for _ in range(3):
        piece = rest_of.astype(jnp.bfloat16)
        rest_of = rest_of - piece.astype(jnp.float32)
        coeffs += across(chosen, piece)

    line = iota((2 * VECTORS, taps), 0)
    column = iota((2 * VECTORS, taps), 1)
    block = lax.rem(line, VECTORS) // 2
    step = 4 * lax.rem(block, COARSE) + 2 * lax.rem(line, 2) + line // VECTORS
    wanted = jnp.where(block < COARSE, half + step, half - 1 - step)
    wanted = jnp.where(lax.rem(line, VECTORS) < 4 * COARSE, wanted, -1)
    col_taps = across((wanted == column).astype(jnp.bfloat16), colk_ref[...])
    tap = iota((taps, width), 0)
    lane = iota((taps, width), 1)
    total = None
    for side in range(2):
        place = (lane == tap + LEAD + side * FINE_ROWS).astype(jnp.bfloat16)
        row_taps = jnp.dot(
            rowk_ref[...], place, preferred_element_type=jnp.float32
        ).astype(jnp.bfloat16)
        part = col_taps[side * VECTORS : (side + 1) * VECTORS]
        mix = jnp.concatenate([part * coeffs[j : j + 1] for j in range(tile_count)], axis=0)
        high = mix.astype(jnp.bfloat16)
        low = (mix - high.astype(jnp.float32)).astype(jnp.bfloat16)
        term = jnp.dot(high, row_taps, preferred_element_type=jnp.float32) + jnp.dot(
            low, row_taps, preferred_element_type=jnp.float32
        )
        total = term if total is None else total + term
    kernels[...] = total

    lane = iota((rows, width), 1)
    column = iota((1, width), 1)

    def edge(distance):
        here = iota((16, width), 1) + distance
        return ((here >= 0) & (here < width)).astype(jnp.float32).astype(jnp.bfloat16)

    edges = {distance: edge(distance) for distance in range(-4, 4) if distance != 0}

    def moved_tile(value, distance):
        if distance == 0:
            return value
        turned = pltpu.roll(value, -distance % width, 1).reshape(rows // 16, 16, width)
        return (turned * edges[distance][None]).reshape(rows, width)

    def moved(value, distance):
        if distance == 0:
            return value
        turned = pltpu.roll(value, -distance % width, 1)
        here = lane[: value.shape[0]] + distance
        return jnp.where((here >= 0) & (here < width), turned, jnp.zeros_like(turned))

    def one_visit(visit, unused):
        fetch(visit).wait()
        sums[...] = jnp.zeros_like(sums)
        first = visit * per_visit
        for place in range(per_visit):
            tile = first + place
            pixels = tiles_ref[tile]
            for side in range(2):
                for fine in range(4):
                    part = moved_tile(pixels, -1 - fine if side else fine)
                    top = fine * FINE_ROWS
                    shifted[place, side, top + 16 : top + 64, :width] = part[:48]
                    shifted[place, side, top : top + 48, width:] = part[16:]
                for coarse in range(COARSE):
                    for pair in range(2):
                        vector = pl.ds(
                            tile * VECTORS + (side * COARSE + coarse) * 2 + pair, 1
                        )
                        spread = jnp.broadcast_to(kernels[vector, :], (8, width))
                        turned = pltpu.roll(spread, 0, 1, stride=1, stride_axis=0)
                        turned = jnp.concatenate(
                            [turned] + [pltpu.roll(turned, top, 1) for top in range(8, BLOCK, 8)],
                            axis=0,
                        )
                        toeplitz[
                            place,
                            side,
                            coarse * BLOCK : (coarse + 1) * BLOCK,
                            pair * width : (pair + 1) * width,
                        ] = turned.astype(jnp.bfloat16)
        for place in range(per_visit):
            matched = [jnp.zeros((BLOCK, width), jnp.float32) for _ in range(2)]
            for side in range(2):
                passed = jnp.dot(
                    toeplitz[place, side],
                    shifted[place, side],
                    preferred_element_type=jnp.float32,
                )
                for part in range(2):
                    for coarse in range(COARSE):
                        matched[part] += moved(
                            passed[
                                coarse * BLOCK : (coarse + 1) * BLOCK,
                                part * width : (part + 1) * width,
                            ],
                            -4 * coarse if side else 4 * coarse,
                        )
            matches[place] = jnp.concatenate(matched, axis=0)
        for place in range(per_visit):
            tile = first + place
            offset = offset_ref[tile]
            bucket = lax.rem(patch_ref[tile] - owner + REACH + patches, patches)
            weight = weights[pl.ds(tile, 1), :]
            turned = pltpu.roll(
                matches[place] * weight, lax.rem(offset, width), 1
            )
            sums[bucket, :, :width] += jnp.where(lane >= offset, turned, 0.0)
            sums[bucket, :, width:] += jnp.where(lane < offset, turned, 0.0)
            extra[bucket, pl.ds(visit, 1), :] += jnp.concatenate(
                [
                    jnp.where(column >= offset, weight, 0.0),
                    jnp.where(column < offset, weight, 0.0),
                ],
                axis=1,
            )

        held = pl.ds(pl.multiple_of(visit * rows, rows), rows)
        far[held, :] = sums[REACH + 2 * way].astype(jnp.bfloat16)
        cross[0, held, :] = sums[REACH - 2 * way].astype(jnp.bfloat16)
        cross[1, held, :] = sums[REACH - way].astype(jnp.bfloat16)
        kept[0, held, :] = sums[REACH + way].astype(jnp.bfloat16)
        kept[1, held, :] = sums[REACH].astype(jnp.bfloat16)
        return unused

    lax.fori_loop(0, visits, one_visit, 0)

    row = iota((EXTRA, PW), 0)
    lane = iota((1, PW), 1)

    def spread_bands(visit_of, limit):
        line = jnp.full((1, PW), -1.0, jnp.float32)
        for visit in range(visits):
            line = jnp.where(
                (lane < limit) & (visit_of == visit), band_ref[visit].astype(jnp.float32), line
            )
        return line

    by_row = spread_bands(lane // rows, visits * rows)
    by_weight = spread_bands(lax.rem(lane, visits), 2 * visits)
    detect = jnp.zeros((1, PW), jnp.float32)
    for b in range(BANDS):
        detect = jnp.where(lane == b, detect_ref[b], detect)

    def footer(bucket):
        held = extra[bucket]
        high = held.astype(jnp.bfloat16).astype(jnp.float32)
        low = jnp.concatenate([held[-visits:], (held - high)[:-visits]], axis=0)
        mixed = jnp.where((row >= visits) & (row < 2 * visits), low, high)
        mixed = jnp.where(row == 2 * visits, by_row, mixed)
        mixed = jnp.where(row == 2 * visits + 1, by_weight, mixed)
        rest = detect
        for place in range(DETECT, DETECT + 3):
            piece = rest.astype(jnp.bfloat16).astype(jnp.float32)
            rest = rest - piece
            mixed = jnp.where(row == place, piece, mixed)
        return mixed.astype(jnp.bfloat16)

    far[rows * visits :, :] = footer(REACH + 2 * way)
    cross[0, rows * visits :, :] = footer(REACH - 2 * way)
    cross[1, rows * visits :, :] = footer(REACH - way)
    kept[0, rows * visits :, :] = footer(REACH + way)
    kept[1, rows * visits :, :] = footer(REACH)


def add_message(count, groups, message):
    depth = message.shape[0] - EXTRA
    span = depth // count
    row_share = span // groups
    line = lax.broadcasted_iota(jnp.int32, (row_share, depth), 0)
    lane = lax.rem(lax.broadcasted_iota(jnp.int32, (row_share, depth), 1), span)
    band_line = lax.broadcasted_iota(jnp.int32, (8, EXTRA), 0).astype(jnp.float32)
    extra = message[depth:, :]
    bands = extra[2 * count : 2 * count + 2].astype(jnp.float32)
    pick = jnp.concatenate(
        [
            jnp.where(
                (lane == line + part * row_share) & (bands[:1, :depth] == float(b)), 1.0, 0.0
            )
            for part in range(groups)
            for b in range(BANDS)
        ],
        axis=0,
    ).astype(jnp.bfloat16)
    totals = jnp.dot(pick, message[:depth, :], preferred_element_type=jnp.float32)
    pick = (bands[1:, :EXTRA] == band_line).astype(jnp.bfloat16)
    return totals, jnp.dot(pick, extra, preferred_element_type=jnp.float32)


def add_banded(totals, weights, messages):
    depth = totals.shape[0]
    for message in messages:
        totals += message[:depth, :].astype(jnp.float32)
        footer = message[depth:, :].astype(jnp.float32)
        weights += footer[:8] + footer[8:]
    return totals, weights


def write_banded(message, totals, weights):
    depth = totals.shape[0]
    high = weights.astype(jnp.bfloat16).astype(jnp.float32)
    message[:depth, :] = totals.astype(jnp.bfloat16)
    message[depth:, :] = jnp.concatenate([high, weights - high], axis=0).astype(jnp.bfloat16)


def part_of(held, turn, groups):
    depth = held.shape[0] // groups
    part = lax.rem(lax.axis_index("band") + turn, groups)
    return held[pl.ds(pl.multiple_of(part * depth, depth), depth), :]


def keep_kernel(count, groups, kept_ref, totals_ref, weights_ref, detect_ref):
    for place in range(2):
        totals_ref[place], weights_ref[place] = add_message(count, groups, kept_ref.at[place])
    extra = kept_ref[0, kept_ref.shape[1] - EXTRA :, :].astype(jnp.float32)
    detect = extra[DETECT : DETECT + 1] + extra[DETECT + 1 : DETECT + 2]
    detect += extra[DETECT + 2 : DETECT + 3]
    line = lax.broadcasted_iota(jnp.int32, (8, PW), 0)
    lane = lax.broadcasted_iota(jnp.int32, (8, PW), 1)
    chosen = jnp.sum(jnp.where(line == lane, detect, 0.0), axis=1, keepdims=True)
    detect_ref[...] = jnp.broadcast_to(chosen, (8, PW))


def merge_kernel(count, groups, totals_ref, weights_ref, cross_ref, *refs):
    messages = refs[:groups]
    home_ref, home_weight_ref, held = refs[groups:]
    totals, weights = add_message(count, groups, cross_ref.at[0])
    held[...] = totals + totals_ref[0]
    weights += weights_ref[0]
    for turn, message in enumerate(messages):
        write_banded(message, part_of(held, turn, groups), weights)
    totals, weights = add_message(count, groups, cross_ref.at[1])
    home_ref[...] = totals + totals_ref[1]
    home_weight_ref[...] = weights + weights_ref[1]


def home_kernel(count, groups, home_ref, home_weight_ref, far_ref, *refs):
    messages = refs[: groups - 1]
    own_ref, own_weight_ref, held = refs[groups - 1 :]
    totals, weights = add_message(count, groups, far_ref)
    held[...] = totals + home_ref[...]
    weights += home_weight_ref[...]
    for turn, message in enumerate(messages, 1):
        write_banded(message, part_of(held, turn, groups), weights)
    own_ref[...] = part_of(held, 0, groups)
    own_weight_ref[...] = weights


def early_kernel(*refs):
    messages = refs[:-2]
    totals_ref, weights_ref = refs[-2:]
    depth = totals_ref.shape[0]
    totals_ref[...], weights_ref[...] = add_banded(
        jnp.zeros((depth, PW), jnp.float32), jnp.zeros((8, PW), jnp.float32), messages
    )


def combine_kernel(
    detect_ref, own_ref, own_weight_ref, near_ref, near_weight_ref, *refs
):
    coadd_ref, detection_ref = refs[-2:]
    row_share = coadd_ref.shape[1]
    totals, weights = add_banded(
        own_ref[...] + near_ref[...], own_weight_ref[...] + near_weight_ref[...], refs[:-2]
    )
    weights = jnp.maximum(weights, 1.0)
    detection = jnp.zeros((row_share, PW), jnp.float32)
    for b in range(BANDS):
        coadd = totals[b * row_share : (b + 1) * row_share] / weights[b : b + 1]
        coadd_ref[b] = coadd
        detection += detect_ref[b : b + 1] * coadd
    detection_ref[...] = detection


def local(
    tiles,
    tile_patch,
    tile_offset,
    tile_weight,
    visit_band,
    coeff_index,
    coeff_table,
    row_kernels,
    column_kernels,
    band_weight,
):
    tile_count, rows, width = tiles.shape
    visits = visit_band.shape[0]
    per_visit = tile_count // visits
    basis, taps = row_kernels.shape
    patches = lax.axis_size("ra")
    groups = lax.axis_size("band")
    row_share = rows // groups
    length = visits * rows + EXTRA
    message_shape = jax.ShapeDtypeStruct((length, PW), jnp.bfloat16)
    pair_shape = jax.ShapeDtypeStruct((2, length, PW), jnp.bfloat16)
    band_shape = jax.ShapeDtypeStruct((BANDS * row_share + EXTRA, PW), jnp.bfloat16)
    part_shape = jax.ShapeDtypeStruct((BANDS * row_share, PW), jnp.float32)
    whole_shape = jax.ShapeDtypeStruct((BANDS * rows, PW), jnp.float32)
    weight_shape = jax.ShapeDtypeStruct((8, PW), jnp.float32)

    vmem = pl.BlockSpec(memory_space=pltpu.VMEM)
    anywhere = pl.BlockSpec(memory_space=pl.ANY)
    far, cross, kept = pl.pallas_call(
        functools.partial(match_kernel, patches),
        in_specs=[anywhere] * 10,
        out_specs=[vmem] * 3,
        out_shape=[message_shape, pair_shape, pair_shape],
        scratch_shapes=[
            pltpu.SMEM((tile_count,), jnp.int32),
            pltpu.SMEM((tile_count,), jnp.int32),
            pltpu.SMEM((tile_count,), jnp.int32),
            pltpu.SMEM((visits,), jnp.int32),
            pltpu.SMEM((BANDS,), jnp.float32),
            pltpu.VMEM(coeff_table.shape[::-1], jnp.float32),
            pltpu.VMEM((1, tile_count), jnp.bfloat16),
            pltpu.VMEM((basis, taps), jnp.bfloat16),
            pltpu.VMEM((basis, taps), jnp.bfloat16),
            pltpu.VMEM((tile_count, rows, width), jnp.bfloat16),
            pltpu.VMEM((tile_count * VECTORS, width), jnp.float32),
            pltpu.VMEM((tile_count, width), jnp.float32),
            pltpu.VMEM((per_visit, 2, 4 * FINE_ROWS, 2 * width), jnp.bfloat16),
            pltpu.VMEM((per_visit, 2, COARSE * BLOCK, 2 * width), jnp.bfloat16),
            pltpu.VMEM((per_visit, rows, width), jnp.float32),
            pltpu.VMEM((SPREAD, rows, PW), jnp.float32),
            pltpu.VMEM((SPREAD, EXTRA, PW), jnp.float32),
            pltpu.SemaphoreType.DMA((visits,)),
            pltpu.SemaphoreType.DMA((9,)),
        ],
        compiler_params=pltpu.CompilerParams(vmem_limit_bytes=62 * 1024 * 1024),
        name="match_and_sum",
    )(
        tile_patch,
        tile_offset,
        coeff_index,
        visit_band,
        band_weight,
        coeff_table.T,
        tile_weight.reshape(1, tile_count),
        row_kernels,
        column_kernels,
        tiles,
    )

    def send(message, goal, turn):
        route = [
            (o * groups + g, goal(o) % patches * groups + (g + turn) % groups)
            for o in range(patches)
            for g in range(groups)
        ]
        return lax.ppermute(message, ("ra", "band"), route)

    def onward(distance):
        return lambda o: o + distance if o % 2 else o - distance

    def local_call(kernel, name, out_shape, *operands, **options):
        return pl.pallas_call(
            kernel,
            in_specs=[vmem] * len(operands),
            out_specs=[vmem] * len(out_shape),
            out_shape=out_shape,
            compiler_params=pltpu.CompilerParams(vmem_limit_bytes=40 * 1024 * 1024),
            name=name,
            **options,
        )(*operands)

    held = [pltpu.VMEM(whole_shape.shape, jnp.float32)]
    cross = send(cross, onward(-1), 0)
    far = send(far, onward(2), 0)
    *kept, detect = local_call(
        functools.partial(keep_kernel, visits, groups),
        "keep",
        [
            jax.ShapeDtypeStruct((2,) + whole_shape.shape, jnp.float32),
            jax.ShapeDtypeStruct((2,) + weight_shape.shape, jnp.float32),
            weight_shape,
        ],
        kept,
    )
    *near, home, home_weight = local_call(
        functools.partial(merge_kernel, visits, groups),
        "merge",
        [band_shape] * groups + [whole_shape, weight_shape],
        *kept,
        cross,
        scratch_shapes=held,
    )
    near = [send(near[turn], onward(1), turn) for turn in range(groups)]
    *others, own, own_weight = local_call(
        functools.partial(home_kernel, visits, groups),
        "home",
        [band_shape] * (groups - 1) + [part_shape, weight_shape],
        home,
        home_weight,
        far,
        scratch_shapes=held,
    )
    others = [send(others[turn - 1], onward(0), turn) for turn in range(1, groups)]
    near = local_call(early_kernel, "combine_early", [part_shape, weight_shape], *near)
    return local_call(
        combine_kernel,
        "combine",
        (
            jax.ShapeDtypeStruct((BANDS, row_share, PW), jnp.float32),
            jax.ShapeDtypeStruct((row_share, PW), jnp.float32),
        ),
        detect,
        own,
        own_weight,
        *near,
        *others,
    )


def solution(mesh):
    return jax.shard_map(
        local,
        mesh=mesh,
        in_specs=(
            P(("ra", "band"), None, None),
            P(("ra", "band")),
            P(("ra", "band")),
            P(("ra", "band")),
            P(("ra", "band")),
            P(("ra", "band")),
            P(),
            P(),
            P(),
            P(),
        ),
        out_specs=(P(None, "band", "ra"), P("band", "ra")),
        check_vma=False,
    )
```

```python
import functools

import jax
import jax.numpy as jnp
from jax import lax
from jax.experimental import pallas as pl
from jax.experimental.pallas import tpu as pltpu
from jax.sharding import PartitionSpec as P

PW = 256
BANDS = 6
REACH = 2
SPREAD = 2 * REACH + 1
EXTRA = 16
DETECT = 10
BLOCK = 32
COARSE = 3
VECTORS = 16
FINE_ROWS = 64
LEAD = 6


def match_kernel(
    patches,
    patch_hbm,
    offset_hbm,
    index_hbm,
    band_hbm,
    detect_hbm,
    table_hbm,
    weight_hbm,
    rowk_hbm,
    colk_hbm,
    tiles_hbm,
    far,
    cross,
    kept,
    patch_ref,
    offset_ref,
    index_ref,
    band_ref,
    detect_ref,
    table_ref,
    weight_ref,
    rowk_ref,
    colk_ref,
    tiles_ref,
    kernels,
    weights,
    shifted,
    toeplitz,
    matches,
    sums,
    extra,
    arrival,
    ready,
):
    visits = band_ref.shape[0]
    tile_count, rows, width = tiles_ref.shape
    per_visit = tile_count // visits
    basis, taps = rowk_ref.shape
    half = taps // 2
    owner = lax.axis_index("ra")
    way = 2 * lax.rem(owner, 2) - 1

    small = [
        pltpu.make_async_copy(source, target, ready.at[place])
        for place, (source, target) in enumerate(
            (
                (index_hbm, index_ref),
                (table_hbm, table_ref),
                (weight_hbm, weight_ref),
                (rowk_hbm, rowk_ref),
                (colk_hbm, colk_ref),
                (patch_hbm, patch_ref),
                (offset_hbm, offset_ref),
                (band_hbm, band_ref),
                (detect_hbm, detect_ref),
            )
        )
    ]
    for copy in small:
        copy.start()

    def fetch(visit):
        held = pl.ds(visit * per_visit, per_visit)
        return pltpu.make_async_copy(tiles_hbm.at[held], tiles_ref.at[held], arrival.at[visit])

    for visit in range(visits):
        fetch(visit).start()

    def iota(shape, axis):
        return lax.broadcasted_iota(jnp.int32, shape, axis)

    def across(left, right, **options):
        return lax.dot_general(
            left,
            right,
            (((1,), (1,)), ((), ())),
            preferred_element_type=jnp.float32,
            **options,
        )

    extra[...] = jnp.zeros_like(extra)
    for place in range(per_visit):
        for side in range(2):
            for fine in range(4):
                top = fine * FINE_ROWS
                shifted[place, side, top : top + 16, :width] = jnp.zeros(
                    (16, width), jnp.bfloat16
                )
                shifted[place, side, top + 48 : top + 64, width:] = jnp.zeros(
                    (16, width), jnp.bfloat16
                )
    eye = (iota((tile_count, tile_count), 0) == iota((tile_count, tile_count), 1)).astype(
        jnp.bfloat16
    )
    for copy in small:
        copy.wait()
    weights[...] = across(eye, jnp.broadcast_to(weight_ref[...], (width, tile_count)))
    entry = iota((1, table_ref.shape[1]), 1)
    chosen = jnp.concatenate(
        [(entry == index_ref[j]).astype(jnp.float32) for j in range(tile_count)], axis=0
    ).astype(jnp.bfloat16)
    rest_of = table_ref[...]
    coeffs = jnp.zeros((tile_count, basis), jnp.float32)
    for _ in range(3):
        piece = rest_of.astype(jnp.bfloat16)
        rest_of = rest_of - piece.astype(jnp.float32)
        coeffs += across(chosen, piece)

    line = iota((2 * VECTORS, taps), 0)
    column = iota((2 * VECTORS, taps), 1)
    block = lax.rem(line, VECTORS) // 2
    step = 4 * lax.rem(block, COARSE) + 2 * lax.rem(line, 2) + line // VECTORS
    wanted = jnp.where(block < COARSE, half + step, half - 1 - step)
    wanted = jnp.where(lax.rem(line, VECTORS) < 4 * COARSE, wanted, -1)
    col_taps = across((wanted == column).astype(jnp.bfloat16), colk_ref[...])
    tap = iota((taps, width), 0)
    lane = iota((taps, width), 1)
    total = None
    for side in range(2):
        place = (lane == tap + LEAD + side * FINE_ROWS).astype(jnp.bfloat16)
        row_taps = jnp.dot(
            rowk_ref[...], place, preferred_element_type=jnp.float32
        ).astype(jnp.bfloat16)
        part = col_taps[side * VECTORS : (side + 1) * VECTORS]
        mix = jnp.concatenate([part * coeffs[j : j + 1] for j in range(tile_count)], axis=0)
        high = mix.astype(jnp.bfloat16)
        low = (mix - high.astype(jnp.float32)).astype(jnp.bfloat16)
        term = jnp.dot(high, row_taps, preferred_element_type=jnp.float32) + jnp.dot(
            low, row_taps, preferred_element_type=jnp.float32
        )
        total = term if total is None else total + term
    kernels[...] = total

    lane = iota((rows, width), 1)
    column = iota((1, width), 1)

    def edge(distance):
        here = iota((16, width), 1) + distance
        return ((here >= 0) & (here < width)).astype(jnp.float32).astype(jnp.bfloat16)

    edges = {distance: edge(distance) for distance in range(-4, 4) if distance != 0}

    def moved_tile(value, distance):
        if distance == 0:
            return value
        turned = pltpu.roll(value, -distance % width, 1).reshape(rows // 16, 16, width)
        return (turned * edges[distance][None]).reshape(rows, width)

    def moved(value, distance):
        if distance == 0:
            return value
        turned = pltpu.roll(value, -distance % width, 1)
        here = lane[: value.shape[0]] + distance
        return jnp.where((here >= 0) & (here < width), turned, jnp.zeros_like(turned))

    def one_visit(visit, unused):
        fetch(visit).wait()
        sums[...] = jnp.zeros_like(sums)
        first = visit * per_visit
        for place in range(per_visit):
            tile = first + place
            pixels = tiles_ref[tile]
            for side in range(2):
                for fine in range(4):
                    part = moved_tile(pixels, -1 - fine if side else fine)
                    top = fine * FINE_ROWS
                    shifted[place, side, top + 16 : top + 64, :width] = part[:48]
                    shifted[place, side, top : top + 48, width:] = part[16:]
                for coarse in range(COARSE):
                    for pair in range(2):
                        vector = pl.ds(
                            tile * VECTORS + (side * COARSE + coarse) * 2 + pair, 1
                        )
                        spread = jnp.broadcast_to(kernels[vector, :], (BLOCK, width))
                        turned = pltpu.roll(spread, 0, 1, stride=1, stride_axis=0)
                        toeplitz[
                            place,
                            side,
                            coarse * BLOCK : (coarse + 1) * BLOCK,
                            pair * width : (pair + 1) * width,
                        ] = turned.astype(jnp.bfloat16)
        for place in range(per_visit):
            matched = [jnp.zeros((BLOCK, width), jnp.float32) for _ in range(2)]
            for side in range(2):
                passed = jnp.dot(
                    toeplitz[place, side],
                    shifted[place, side],
                    preferred_element_type=jnp.float32,
                )
                for part in range(2):
                    for coarse in range(COARSE):
                        matched[part] += moved(
                            passed[
                                coarse * BLOCK : (coarse + 1) * BLOCK,
                                part * width : (part + 1) * width,
                            ],
                            -4 * coarse if side else 4 * coarse,
                        )
            matches[place] = jnp.concatenate(matched, axis=0)
        for place in range(per_visit):
            tile = first + place
            matches[place] = pltpu.roll(
                matches[place] * weights[pl.ds(tile, 1), :], lax.rem(offset_ref[tile], width), 1
            )
        for place in range(per_visit):
            tile = first + place
            offset = offset_ref[tile]
            bucket = lax.rem(patch_ref[tile] - owner + REACH + patches, patches)
            weight = weights[pl.ds(tile, 1), :]
            turned = matches[place]
            sums[bucket, :, :width] += jnp.where(lane >= offset, turned, 0.0)
            sums[bucket, :, width:] += jnp.where(lane < offset, turned, 0.0)
            extra[bucket, pl.ds(visit, 1), :] += jnp.concatenate(
                [
                    jnp.where(column >= offset, weight, 0.0),
                    jnp.where(column < offset, weight, 0.0),
                ],
                axis=1,
            )

        held = pl.ds(pl.multiple_of(visit * rows, rows), rows)
        far[held, :] = sums[REACH + 2 * way].astype(jnp.bfloat16)
        cross[0, held, :] = sums[REACH - 2 * way].astype(jnp.bfloat16)
        cross[1, held, :] = sums[REACH - way].astype(jnp.bfloat16)
        kept[0, held, :] = sums[REACH + way].astype(jnp.bfloat16)
        kept[1, held, :] = sums[REACH].astype(jnp.bfloat16)
        return unused

    lax.fori_loop(0, visits, one_visit, 0)

    row = iota((EXTRA, PW), 0)
    lane = iota((1, PW), 1)

    def spread_bands(visit_of, limit):
        line = jnp.full((1, PW), -1.0, jnp.float32)
        for visit in range(visits):
            line = jnp.where(
                (lane < limit) & (visit_of == visit), band_ref[visit].astype(jnp.float32), line
            )
        return line

    by_row = spread_bands(lane // rows, visits * rows)
    by_weight = spread_bands(lax.rem(lane, visits), 2 * visits)
    detect = jnp.zeros((1, PW), jnp.float32)
    for b in range(BANDS):
        detect = jnp.where(lane == b, detect_ref[b], detect)

    def footer(bucket):
        held = extra[bucket]
        high = held.astype(jnp.bfloat16).astype(jnp.float32)
        low = jnp.concatenate([held[-visits:], (held - high)[:-visits]], axis=0)
        mixed = jnp.where((row >= visits) & (row < 2 * visits), low, high)
        mixed = jnp.where(row == 2 * visits, by_row, mixed)
        mixed = jnp.where(row == 2 * visits + 1, by_weight, mixed)
        rest = detect
        for place in range(DETECT, DETECT + 3):
            piece = rest.astype(jnp.bfloat16).astype(jnp.float32)
            rest = rest - piece
            mixed = jnp.where(row == place, piece, mixed)
        return mixed.astype(jnp.bfloat16)

    far[rows * visits :, :] = footer(REACH + 2 * way)
    cross[0, rows * visits :, :] = footer(REACH - 2 * way)
    cross[1, rows * visits :, :] = footer(REACH - way)
    kept[0, rows * visits :, :] = footer(REACH + way)
    kept[1, rows * visits :, :] = footer(REACH)


def add_message(count, groups, message):
    depth = message.shape[0] - EXTRA
    span = depth // count
    row_share = span // groups
    line = lax.broadcasted_iota(jnp.int32, (row_share, depth), 0)
    lane = lax.rem(lax.broadcasted_iota(jnp.int32, (row_share, depth), 1), span)
    band_line = lax.broadcasted_iota(jnp.int32, (8, EXTRA), 0).astype(jnp.float32)
    extra = message[depth:, :]
    bands = extra[2 * count : 2 * count + 2].astype(jnp.float32)
    pick = jnp.concatenate(
        [
            jnp.where(
                (lane == line + part * row_share) & (bands[:1, :depth] == float(b)), 1.0, 0.0
            )
            for part in range(groups)
            for b in range(BANDS)
        ],
        axis=0,
    ).astype(jnp.bfloat16)
    totals = jnp.dot(pick, message[:depth, :], preferred_element_type=jnp.float32)
    pick = (bands[1:, :EXTRA] == band_line).astype(jnp.bfloat16)
    return totals, jnp.dot(pick, extra, preferred_element_type=jnp.float32)


def add_banded(totals, weights, messages):
    depth = totals.shape[0]
    for message in messages:
        totals += message[:depth, :].astype(jnp.float32)
        footer = message[depth:, :].astype(jnp.float32)
        weights += footer[:8] + footer[8:]
    return totals, weights


def write_banded(message, totals, weights):
    depth = totals.shape[0]
    high = weights.astype(jnp.bfloat16).astype(jnp.float32)
    message[:depth, :] = totals.astype(jnp.bfloat16)
    message[depth:, :] = jnp.concatenate([high, weights - high], axis=0).astype(jnp.bfloat16)


def part_of(held, turn, groups):
    depth = held.shape[0] // groups
    part = lax.rem(lax.axis_index("band") + turn, groups)
    return held[pl.ds(pl.multiple_of(part * depth, depth), depth), :]


def keep_kernel(count, groups, kept_ref, totals_ref, weights_ref, detect_ref):
    for place in range(2):
        totals_ref[place], weights_ref[place] = add_message(count, groups, kept_ref.at[place])
    extra = kept_ref[0, kept_ref.shape[1] - EXTRA :, :].astype(jnp.float32)
    detect = extra[DETECT : DETECT + 1] + extra[DETECT + 1 : DETECT + 2]
    detect += extra[DETECT + 2 : DETECT + 3]
    line = lax.broadcasted_iota(jnp.int32, (8, PW), 0)
    lane = lax.broadcasted_iota(jnp.int32, (8, PW), 1)
    chosen = jnp.sum(jnp.where(line == lane, detect, 0.0), axis=1, keepdims=True)
    detect_ref[...] = jnp.broadcast_to(chosen, (8, PW))


def merge_kernel(count, groups, totals_ref, weights_ref, cross_ref, *refs):
    messages = refs[:groups]
    home_ref, home_weight_ref, held = refs[groups:]
    totals, weights = add_message(count, groups, cross_ref.at[0])
    held[...] = totals + totals_ref[0]
    weights += weights_ref[0]
    for turn, message in enumerate(messages):
        write_banded(message, part_of(held, turn, groups), weights)
    totals, weights = add_message(count, groups, cross_ref.at[1])
    home_ref[...] = totals + totals_ref[1]
    home_weight_ref[...] = weights + weights_ref[1]


def home_kernel(count, groups, home_ref, home_weight_ref, far_ref, *refs):
    messages = refs[: groups - 1]
    own_ref, own_weight_ref, held = refs[groups - 1 :]
    totals, weights = add_message(count, groups, far_ref)
    held[...] = totals + home_ref[...]
    weights += home_weight_ref[...]
    for turn, message in enumerate(messages, 1):
        write_banded(message, part_of(held, turn, groups), weights)
    own_ref[...] = part_of(held, 0, groups)
    own_weight_ref[...] = weights


def early_kernel(*refs):
    messages = refs[:-2]
    totals_ref, weights_ref = refs[-2:]
    depth = totals_ref.shape[0]
    totals_ref[...], weights_ref[...] = add_banded(
        jnp.zeros((depth, PW), jnp.float32), jnp.zeros((8, PW), jnp.float32), messages
    )


def combine_kernel(
    detect_ref, own_ref, own_weight_ref, near_ref, near_weight_ref, *refs
):
    coadd_ref, detection_ref = refs[-2:]
    row_share = coadd_ref.shape[1]
    totals, weights = add_banded(
        own_ref[...] + near_ref[...], own_weight_ref[...] + near_weight_ref[...], refs[:-2]
    )
    weights = jnp.maximum(weights, 1.0)
    detection = jnp.zeros((row_share, PW), jnp.float32)
    for b in range(BANDS):
        coadd = totals[b * row_share : (b + 1) * row_share] / weights[b : b + 1]
        coadd_ref[b] = coadd
        detection += detect_ref[b : b + 1] * coadd
    detection_ref[...] = detection


def local(
    tiles,
    tile_patch,
    tile_offset,
    tile_weight,
    visit_band,
    coeff_index,
    coeff_table,
    row_kernels,
    column_kernels,
    band_weight,
):
    tile_count, rows, width = tiles.shape
    visits = visit_band.shape[0]
    per_visit = tile_count // visits
    basis, taps = row_kernels.shape
    patches = lax.axis_size("ra")
    groups = lax.axis_size("band")
    row_share = rows // groups
    length = visits * rows + EXTRA
    message_shape = jax.ShapeDtypeStruct((length, PW), jnp.bfloat16)
    pair_shape = jax.ShapeDtypeStruct((2, length, PW), jnp.bfloat16)
    band_shape = jax.ShapeDtypeStruct((BANDS * row_share + EXTRA, PW), jnp.bfloat16)
    part_shape = jax.ShapeDtypeStruct((BANDS * row_share, PW), jnp.float32)
    whole_shape = jax.ShapeDtypeStruct((BANDS * rows, PW), jnp.float32)
    weight_shape = jax.ShapeDtypeStruct((8, PW), jnp.float32)

    vmem = pl.BlockSpec(memory_space=pltpu.VMEM)
    anywhere = pl.BlockSpec(memory_space=pl.ANY)
    far, cross, kept = pl.pallas_call(
        functools.partial(match_kernel, patches),
        in_specs=[anywhere] * 10,
        out_specs=[vmem] * 3,
        out_shape=[message_shape, pair_shape, pair_shape],
        scratch_shapes=[
            pltpu.SMEM((tile_count,), jnp.int32),
            pltpu.SMEM((tile_count,), jnp.int32),
            pltpu.SMEM((tile_count,), jnp.int32),
            pltpu.SMEM((visits,), jnp.int32),
            pltpu.SMEM((BANDS,), jnp.float32),
            pltpu.VMEM(coeff_table.shape[::-1], jnp.float32),
            pltpu.VMEM((1, tile_count), jnp.bfloat16),
            pltpu.VMEM((basis, taps), jnp.bfloat16),
            pltpu.VMEM((basis, taps), jnp.bfloat16),
            pltpu.VMEM((tile_count, rows, width), jnp.bfloat16),
            pltpu.VMEM((tile_count * VECTORS, width), jnp.float32),
            pltpu.VMEM((tile_count, width), jnp.float32),
            pltpu.VMEM((per_visit, 2, 4 * FINE_ROWS, 2 * width), jnp.bfloat16),
            pltpu.VMEM((per_visit, 2, COARSE * BLOCK, 2 * width), jnp.bfloat16),
            pltpu.VMEM((per_visit, rows, width), jnp.float32),
            pltpu.VMEM((SPREAD, rows, PW), jnp.float32),
            pltpu.VMEM((SPREAD, EXTRA, PW), jnp.float32),
            pltpu.SemaphoreType.DMA((visits,)),
            pltpu.SemaphoreType.DMA((9,)),
        ],
        compiler_params=pltpu.CompilerParams(vmem_limit_bytes=62 * 1024 * 1024),
        name="match_and_sum",
    )(
        tile_patch,
        tile_offset,
        coeff_index,
        visit_band,
        band_weight,
        coeff_table.T,
        tile_weight.reshape(1, tile_count),
        row_kernels,
        column_kernels,
        tiles,
    )

    def send(message, goal, turn):
        route = [
            (o * groups + g, goal(o) % patches * groups + (g + turn) % groups)
            for o in range(patches)
            for g in range(groups)
        ]
        return lax.ppermute(message, ("ra", "band"), route)

    def onward(distance):
        return lambda o: o + distance if o % 2 else o - distance

    def local_call(kernel, name, out_shape, *operands, **options):
        return pl.pallas_call(
            kernel,
            in_specs=[vmem] * len(operands),
            out_specs=[vmem] * len(out_shape),
            out_shape=out_shape,
            compiler_params=pltpu.CompilerParams(vmem_limit_bytes=40 * 1024 * 1024),
            name=name,
            **options,
        )(*operands)

    held = [pltpu.VMEM(whole_shape.shape, jnp.float32)]
    cross = send(cross, onward(-1), 0)
    far = send(far, onward(2), 0)
    *kept, detect = local_call(
        functools.partial(keep_kernel, visits, groups),
        "keep",
        [
            jax.ShapeDtypeStruct((2,) + whole_shape.shape, jnp.float32),
            jax.ShapeDtypeStruct((2,) + weight_shape.shape, jnp.float32),
            weight_shape,
        ],
        kept,
    )
    *near, home, home_weight = local_call(
        functools.partial(merge_kernel, visits, groups),
        "merge",
        [band_shape] * groups + [whole_shape, weight_shape],
        *kept,
        cross,
        scratch_shapes=held,
    )
    near = [send(near[turn], onward(1), turn) for turn in range(groups)]
    *others, own, own_weight = local_call(
        functools.partial(home_kernel, visits, groups),
        "home",
        [band_shape] * (groups - 1) + [part_shape, weight_shape],
        home,
        home_weight,
        far,
        scratch_shapes=held,
    )
    others = [send(others[turn - 1], onward(0), turn) for turn in range(1, groups)]
    near = local_call(early_kernel, "combine_early", [part_shape, weight_shape], *near)
    return local_call(
        combine_kernel,
        "combine",
        (
            jax.ShapeDtypeStruct((BANDS, row_share, PW), jnp.float32),
            jax.ShapeDtypeStruct((row_share, PW), jnp.float32),
        ),
        detect,
        own,
        own_weight,
        *near,
        *others,
    )


def solution(mesh):
    return jax.shard_map(
        local,
        mesh=mesh,
        in_specs=(
            P(("ra", "band"), None, None),
            P(("ra", "band")),
            P(("ra", "band")),
            P(("ra", "band")),
            P(("ra", "band")),
            P(("ra", "band")),
            P(),
            P(),
            P(),
            P(),
        ),
        out_specs=(P(None, "band", "ra"), P("band", "ra")),
        check_vma=False,
    )
```

```python
import functools

import jax
import jax.numpy as jnp
from jax import lax
from jax.experimental import pallas as pl
from jax.experimental.pallas import tpu as pltpu
from jax.sharding import PartitionSpec as P

PW = 256
BANDS = 6
REACH = 2
SPREAD = 2 * REACH + 1
EXTRA = 16
DETECT = 10
BLOCK = 32
COARSE = 3
VECTORS = 16
FINE_ROWS = 64
LEAD = 6


def match_kernel(
    patches,
    patch_hbm,
    offset_hbm,
    index_hbm,
    band_hbm,
    detect_hbm,
    table_hbm,
    weight_hbm,
    rowk_hbm,
    colk_hbm,
    tiles_hbm,
    far,
    cross,
    kept,
    patch_ref,
    offset_ref,
    index_ref,
    band_ref,
    detect_ref,
    table_ref,
    weight_ref,
    rowk_ref,
    colk_ref,
    tiles_ref,
    kernels,
    weights,
    shifted,
    toeplitz,
    matches,
    sums,
    extra,
    arrival,
    ready,
):
    visits = band_ref.shape[0]
    tile_count, rows, width = tiles_ref.shape
    per_visit = tile_count // visits
    basis, taps = rowk_ref.shape
    half = taps // 2
    owner = lax.axis_index("ra")
    way = 2 * lax.rem(owner, 2) - 1

    small = [
        pltpu.make_async_copy(source, target, ready.at[place])
        for place, (source, target) in enumerate(
            (
                (index_hbm, index_ref),
                (table_hbm, table_ref),
                (weight_hbm, weight_ref),
                (rowk_hbm, rowk_ref),
                (colk_hbm, colk_ref),
                (patch_hbm, patch_ref),
                (offset_hbm, offset_ref),
                (band_hbm, band_ref),
                (detect_hbm, detect_ref),
            )
        )
    ]
    for copy in small:
        copy.start()

    def fetch(visit):
        held = pl.ds(visit * per_visit, per_visit)
        return pltpu.make_async_copy(tiles_hbm.at[held], tiles_ref.at[held], arrival.at[visit])

    for visit in range(visits):
        fetch(visit).start()

    def iota(shape, axis):
        return lax.broadcasted_iota(jnp.int32, shape, axis)

    def across(left, right, **options):
        return lax.dot_general(
            left,
            right,
            (((1,), (1,)), ((), ())),
            preferred_element_type=jnp.float32,
            **options,
        )

    extra[...] = jnp.zeros_like(extra)
    for place in range(per_visit):
        for side in range(2):
            for fine in range(4):
                top = fine * FINE_ROWS
                shifted[place, side, top : top + 16, :width] = jnp.zeros(
                    (16, width), jnp.bfloat16
                )
                shifted[place, side, top + 48 : top + 64, width:] = jnp.zeros(
                    (16, width), jnp.bfloat16
                )
    eye = (iota((tile_count, tile_count), 0) == iota((tile_count, tile_count), 1)).astype(
        jnp.bfloat16
    )
    for copy in small:
        copy.wait()
    weights[...] = across(eye, jnp.broadcast_to(weight_ref[...], (width, tile_count)))
    entry = iota((1, table_ref.shape[1]), 1)
    chosen = jnp.concatenate(
        [(entry == index_ref[j]).astype(jnp.float32) for j in range(tile_count)], axis=0
    ).astype(jnp.bfloat16)
    rest_of = table_ref[...]
    coeffs = jnp.zeros((tile_count, basis), jnp.float32)
    for _ in range(3):
        piece = rest_of.astype(jnp.bfloat16)
        rest_of = rest_of - piece.astype(jnp.float32)
        coeffs += across(chosen, piece)

    line = iota((2 * VECTORS, taps), 0)
    column = iota((2 * VECTORS, taps), 1)
    block = lax.rem(line, VECTORS) // 2
    step = 4 * lax.rem(block, COARSE) + 2 * lax.rem(line, 2) + line // VECTORS
    wanted = jnp.where(block < COARSE, half + step, half - 1 - step)
    wanted = jnp.where(lax.rem(line, VECTORS) < 4 * COARSE, wanted, -1)
    col_taps = across((wanted == column).astype(jnp.bfloat16), colk_ref[...])
    tap = iota((taps, width), 0)
    lane = iota((taps, width), 1)
    total = None
    for side in range(2):
        place = (lane == tap + LEAD + side * FINE_ROWS).astype(jnp.bfloat16)
        row_taps = jnp.dot(
            rowk_ref[...], place, preferred_element_type=jnp.float32
        ).astype(jnp.bfloat16)
        part = col_taps[side * VECTORS : (side + 1) * VECTORS]
        mix = jnp.concatenate([part * coeffs[j : j + 1] for j in range(tile_count)], axis=0)
        high = mix.astype(jnp.bfloat16)
        low = (mix - high.astype(jnp.float32)).astype(jnp.bfloat16)
        term = jnp.dot(high, row_taps, preferred_element_type=jnp.float32) + jnp.dot(
            low, row_taps, preferred_element_type=jnp.float32
        )
        total = term if total is None else total + term
    kernels[...] = total

    lane = iota((rows, width), 1)
    column = iota((1, width), 1)

    def edge(distance):
        here = iota((16, width), 1) + distance
        return ((here >= 0) & (here < width)).astype(jnp.float32).astype(jnp.bfloat16)

    edges = {distance: edge(distance) for distance in range(-4, 4) if distance != 0}

    def moved_tile(value, distance):
        if distance == 0:
            return value
        turned = pltpu.roll(value, -distance % width, 1).reshape(rows // 16, 16, width)
        return (turned * edges[distance][None]).reshape(rows, width)

    def moved(value, distance):
        if distance == 0:
            return value
        turned = pltpu.roll(value, -distance % width, 1)
        here = lane[: value.shape[0]] + distance
        return jnp.where((here >= 0) & (here < width), turned, jnp.zeros_like(turned))

    def one_visit(visit, unused):
        fetch(visit).wait()
        sums[...] = jnp.zeros_like(sums)
        first = visit * per_visit
        for place in range(per_visit):
            tile = first + place
            pixels = tiles_ref[tile]
            for side in range(2):
                for fine in range(4):
                    part = moved_tile(pixels, -1 - fine if side else fine)
                    top = fine * FINE_ROWS
                    shifted[place, side, top + 16 : top + 64, :width] = part[:48]
                    shifted[place, side, top : top + 48, width:] = part[16:]
        for place in range(per_visit):
            tile = first + place
            for side in range(2):
                for coarse in range(COARSE):
                    for pair in range(2):
                        vector = pl.ds(
                            tile * VECTORS + (side * COARSE + coarse) * 2 + pair, 1
                        )
                        spread = jnp.broadcast_to(kernels[vector, :], (BLOCK, width))
                        turned = pltpu.roll(spread, 0, 1, stride=1, stride_axis=0)
                        toeplitz[
                            place,
                            side,
                            coarse * BLOCK : (coarse + 1) * BLOCK,
                            pair * width : (pair + 1) * width,
                        ] = turned.astype(jnp.bfloat16)
        for place in range(per_visit):
            matched = [jnp.zeros((BLOCK, width), jnp.float32) for _ in range(2)]
            for side in range(2):
                passed = jnp.dot(
                    toeplitz[place, side],
                    shifted[place, side],
                    preferred_element_type=jnp.float32,
                )
                for part in range(2):
                    for coarse in range(COARSE):
                        matched[part] += moved(
                            passed[
                                coarse * BLOCK : (coarse + 1) * BLOCK,
                                part * width : (part + 1) * width,
                            ],
                            -4 * coarse if side else 4 * coarse,
                        )
            matches[place] = jnp.concatenate(matched, axis=0)
        for place in range(per_visit):
            tile = first + place
            matches[place] = pltpu.roll(
                matches[place] * weights[pl.ds(tile, 1), :], lax.rem(offset_ref[tile], width), 1
            )
        for place in range(per_visit):
            tile = first + place
            offset = offset_ref[tile]
            bucket = lax.rem(patch_ref[tile] - owner + REACH + patches, patches)
            weight = weights[pl.ds(tile, 1), :]
            turned = matches[place]
            sums[bucket, :, :width] += jnp.where(lane >= offset, turned, 0.0)
            sums[bucket, :, width:] += jnp.where(lane < offset, turned, 0.0)
            extra[bucket, pl.ds(visit, 1), :] += jnp.concatenate(
                [
                    jnp.where(column >= offset, weight, 0.0),
                    jnp.where(column < offset, weight, 0.0),
                ],
                axis=1,
            )

        held = pl.ds(pl.multiple_of(visit * rows, rows), rows)
        far[held, :] = sums[REACH + 2 * way].astype(jnp.bfloat16)
        cross[0, held, :] = sums[REACH - 2 * way].astype(jnp.bfloat16)
        cross[1, held, :] = sums[REACH - way].astype(jnp.bfloat16)
        kept[0, held, :] = sums[REACH + way].astype(jnp.bfloat16)
        kept[1, held, :] = sums[REACH].astype(jnp.bfloat16)
        return unused

    lax.fori_loop(0, visits, one_visit, 0)

    row = iota((EXTRA, PW), 0)
    lane = iota((1, PW), 1)

    def spread_bands(visit_of, limit):
        line = jnp.full((1, PW), -1.0, jnp.float32)
        for visit in range(visits):
            line = jnp.where(
                (lane < limit) & (visit_of == visit), band_ref[visit].astype(jnp.float32), line
            )
        return line

    by_row = spread_bands(lane // rows, visits * rows)
    by_weight = spread_bands(lax.rem(lane, visits), 2 * visits)
    detect = jnp.zeros((1, PW), jnp.float32)
    for b in range(BANDS):
        detect = jnp.where(lane == b, detect_ref[b], detect)

    def footer(bucket):
        held = extra[bucket]
        high = held.astype(jnp.bfloat16).astype(jnp.float32)
        low = jnp.concatenate([held[-visits:], (held - high)[:-visits]], axis=0)
        mixed = jnp.where((row >= visits) & (row < 2 * visits), low, high)
        mixed = jnp.where(row == 2 * visits, by_row, mixed)
        mixed = jnp.where(row == 2 * visits + 1, by_weight, mixed)
        rest = detect
        for place in range(DETECT, DETECT + 3):
            piece = rest.astype(jnp.bfloat16).astype(jnp.float32)
            rest = rest - piece
            mixed = jnp.where(row == place, piece, mixed)
        return mixed.astype(jnp.bfloat16)

    far[rows * visits :, :] = footer(REACH + 2 * way)
    cross[0, rows * visits :, :] = footer(REACH - 2 * way)
    cross[1, rows * visits :, :] = footer(REACH - way)
    kept[0, rows * visits :, :] = footer(REACH + way)
    kept[1, rows * visits :, :] = footer(REACH)


def add_message(count, groups, message):
    depth = message.shape[0] - EXTRA
    span = depth // count
    row_share = span // groups
    line = lax.broadcasted_iota(jnp.int32, (row_share, depth), 0)
    lane = lax.rem(lax.broadcasted_iota(jnp.int32, (row_share, depth), 1), span)
    band_line = lax.broadcasted_iota(jnp.int32, (8, EXTRA), 0).astype(jnp.float32)
    extra = message[depth:, :]
    bands = extra[2 * count : 2 * count + 2].astype(jnp.float32)
    pick = jnp.concatenate(
        [
            jnp.where(
                (lane == line + part * row_share) & (bands[:1, :depth] == float(b)), 1.0, 0.0
            )
            for part in range(groups)
            for b in range(BANDS)
        ],
        axis=0,
    ).astype(jnp.bfloat16)
    totals = jnp.dot(pick, message[:depth, :], preferred_element_type=jnp.float32)
    pick = (bands[1:, :EXTRA] == band_line).astype(jnp.bfloat16)
    return totals, jnp.dot(pick, extra, preferred_element_type=jnp.float32)


def add_banded(totals, weights, messages):
    depth = totals.shape[0]
    for message in messages:
        totals += message[:depth, :].astype(jnp.float32)
        footer = message[depth:, :].astype(jnp.float32)
        weights += footer[:8] + footer[8:]
    return totals, weights


def write_banded(message, totals, weights):
    depth = totals.shape[0]
    high = weights.astype(jnp.bfloat16).astype(jnp.float32)
    message[:depth, :] = totals.astype(jnp.bfloat16)
    message[depth:, :] = jnp.concatenate([high, weights - high], axis=0).astype(jnp.bfloat16)


def part_of(held, turn, groups):
    depth = held.shape[0] // groups
    part = lax.rem(lax.axis_index("band") + turn, groups)
    return held[pl.ds(pl.multiple_of(part * depth, depth), depth), :]


def keep_kernel(count, groups, kept_ref, totals_ref, weights_ref, detect_ref):
    for place in range(2):
        totals_ref[place], weights_ref[place] = add_message(count, groups, kept_ref.at[place])
    extra = kept_ref[0, kept_ref.shape[1] - EXTRA :, :].astype(jnp.float32)
    detect = extra[DETECT : DETECT + 1] + extra[DETECT + 1 : DETECT + 2]
    detect += extra[DETECT + 2 : DETECT + 3]
    line = lax.broadcasted_iota(jnp.int32, (8, PW), 0)
    lane = lax.broadcasted_iota(jnp.int32, (8, PW), 1)
    chosen = jnp.sum(jnp.where(line == lane, detect, 0.0), axis=1, keepdims=True)
    detect_ref[...] = jnp.broadcast_to(chosen, (8, PW))


def merge_kernel(count, groups, totals_ref, weights_ref, cross_ref, *refs):
    messages = refs[:groups]
    home_ref, home_weight_ref, held = refs[groups:]
    totals, weights = add_message(count, groups, cross_ref.at[0])
    held[...] = totals + totals_ref[0]
    weights += weights_ref[0]
    for turn, message in enumerate(messages):
        write_banded(message, part_of(held, turn, groups), weights)
    totals, weights = add_message(count, groups, cross_ref.at[1])
    home_ref[...] = totals + totals_ref[1]
    home_weight_ref[...] = weights + weights_ref[1]


def home_kernel(count, groups, home_ref, home_weight_ref, far_ref, *refs):
    messages = refs[: groups - 1]
    own_ref, own_weight_ref, held = refs[groups - 1 :]
    totals, weights = add_message(count, groups, far_ref)
    held[...] = totals + home_ref[...]
    weights += home_weight_ref[...]
    for turn, message in enumerate(messages, 1):
        write_banded(message, part_of(held, turn, groups), weights)
    own_ref[...] = part_of(held, 0, groups)
    own_weight_ref[...] = weights


def early_kernel(*refs):
    messages = refs[:-2]
    totals_ref, weights_ref = refs[-2:]
    depth = totals_ref.shape[0]
    totals_ref[...], weights_ref[...] = add_banded(
        jnp.zeros((depth, PW), jnp.float32), jnp.zeros((8, PW), jnp.float32), messages
    )


def combine_kernel(
    detect_ref, own_ref, own_weight_ref, near_ref, near_weight_ref, *refs
):
    coadd_ref, detection_ref = refs[-2:]
    row_share = coadd_ref.shape[1]
    totals, weights = add_banded(
        own_ref[...] + near_ref[...], own_weight_ref[...] + near_weight_ref[...], refs[:-2]
    )
    weights = jnp.maximum(weights, 1.0)
    detection = jnp.zeros((row_share, PW), jnp.float32)
    for b in range(BANDS):
        coadd = totals[b * row_share : (b + 1) * row_share] / weights[b : b + 1]
        coadd_ref[b] = coadd
        detection += detect_ref[b : b + 1] * coadd
    detection_ref[...] = detection


def local(
    tiles,
    tile_patch,
    tile_offset,
    tile_weight,
    visit_band,
    coeff_index,
    coeff_table,
    row_kernels,
    column_kernels,
    band_weight,
):
    tile_count, rows, width = tiles.shape
    visits = visit_band.shape[0]
    per_visit = tile_count // visits
    basis, taps = row_kernels.shape
    patches = lax.axis_size("ra")
    groups = lax.axis_size("band")
    row_share = rows // groups
    length = visits * rows + EXTRA
    message_shape = jax.ShapeDtypeStruct((length, PW), jnp.bfloat16)
    pair_shape = jax.ShapeDtypeStruct((2, length, PW), jnp.bfloat16)
    band_shape = jax.ShapeDtypeStruct((BANDS * row_share + EXTRA, PW), jnp.bfloat16)
    part_shape = jax.ShapeDtypeStruct((BANDS * row_share, PW), jnp.float32)
    whole_shape = jax.ShapeDtypeStruct((BANDS * rows, PW), jnp.float32)
    weight_shape = jax.ShapeDtypeStruct((8, PW), jnp.float32)

    vmem = pl.BlockSpec(memory_space=pltpu.VMEM)
    anywhere = pl.BlockSpec(memory_space=pl.ANY)
    far, cross, kept = pl.pallas_call(
        functools.partial(match_kernel, patches),
        in_specs=[anywhere] * 10,
        out_specs=[vmem] * 3,
        out_shape=[message_shape, pair_shape, pair_shape],
        scratch_shapes=[
            pltpu.SMEM((tile_count,), jnp.int32),
            pltpu.SMEM((tile_count,), jnp.int32),
            pltpu.SMEM((tile_count,), jnp.int32),
            pltpu.SMEM((visits,), jnp.int32),
            pltpu.SMEM((BANDS,), jnp.float32),
            pltpu.VMEM(coeff_table.shape[::-1], jnp.float32),
            pltpu.VMEM((1, tile_count), jnp.bfloat16),
            pltpu.VMEM((basis, taps), jnp.bfloat16),
            pltpu.VMEM((basis, taps), jnp.bfloat16),
            pltpu.VMEM((tile_count, rows, width), jnp.bfloat16),
            pltpu.VMEM((tile_count * VECTORS, width), jnp.float32),
            pltpu.VMEM((tile_count, width), jnp.float32),
            pltpu.VMEM((per_visit, 2, 4 * FINE_ROWS, 2 * width), jnp.bfloat16),
            pltpu.VMEM((per_visit, 2, COARSE * BLOCK, 2 * width), jnp.bfloat16),
            pltpu.VMEM((per_visit, rows, width), jnp.float32),
            pltpu.VMEM((SPREAD, rows, PW), jnp.float32),
            pltpu.VMEM((SPREAD, EXTRA, PW), jnp.float32),
            pltpu.SemaphoreType.DMA((visits,)),
            pltpu.SemaphoreType.DMA((9,)),
        ],
        compiler_params=pltpu.CompilerParams(vmem_limit_bytes=62 * 1024 * 1024),
        name="match_and_sum",
    )(
        tile_patch,
        tile_offset,
        coeff_index,
        visit_band,
        band_weight,
        coeff_table.T,
        tile_weight.reshape(1, tile_count),
        row_kernels,
        column_kernels,
        tiles,
    )

    def send(message, goal, turn):
        route = [
            (o * groups + g, goal(o) % patches * groups + (g + turn) % groups)
            for o in range(patches)
            for g in range(groups)
        ]
        return lax.ppermute(message, ("ra", "band"), route)

    def onward(distance):
        return lambda o: o + distance if o % 2 else o - distance

    def local_call(kernel, name, out_shape, *operands, **options):
        return pl.pallas_call(
            kernel,
            in_specs=[vmem] * len(operands),
            out_specs=[vmem] * len(out_shape),
            out_shape=out_shape,
            compiler_params=pltpu.CompilerParams(vmem_limit_bytes=40 * 1024 * 1024),
            name=name,
            **options,
        )(*operands)

    held = [pltpu.VMEM(whole_shape.shape, jnp.float32)]
    cross = send(cross, onward(-1), 0)
    far = send(far, onward(2), 0)
    *kept, detect = local_call(
        functools.partial(keep_kernel, visits, groups),
        "keep",
        [
            jax.ShapeDtypeStruct((2,) + whole_shape.shape, jnp.float32),
            jax.ShapeDtypeStruct((2,) + weight_shape.shape, jnp.float32),
            weight_shape,
        ],
        kept,
    )
    *near, home, home_weight = local_call(
        functools.partial(merge_kernel, visits, groups),
        "merge",
        [band_shape] * groups + [whole_shape, weight_shape],
        *kept,
        cross,
        scratch_shapes=held,
    )
    near = [send(near[turn], onward(1), turn) for turn in range(groups)]
    *others, own, own_weight = local_call(
        functools.partial(home_kernel, visits, groups),
        "home",
        [band_shape] * (groups - 1) + [part_shape, weight_shape],
        home,
        home_weight,
        far,
        scratch_shapes=held,
    )
    others = [send(others[turn - 1], onward(0), turn) for turn in range(1, groups)]
    near = local_call(early_kernel, "combine_early", [part_shape, weight_shape], *near)
    return local_call(
        combine_kernel,
        "combine",
        (
            jax.ShapeDtypeStruct((BANDS, row_share, PW), jnp.float32),
            jax.ShapeDtypeStruct((row_share, PW), jnp.float32),
        ),
        detect,
        own,
        own_weight,
        *near,
        *others,
    )


def solution(mesh):
    return jax.shard_map(
        local,
        mesh=mesh,
        in_specs=(
            P(("ra", "band"), None, None),
            P(("ra", "band")),
            P(("ra", "band")),
            P(("ra", "band")),
            P(("ra", "band")),
            P(("ra", "band")),
            P(),
            P(),
            P(),
            P(),
        ),
        out_specs=(P(None, "band", "ra"), P("band", "ra")),
        check_vma=False,
    )
```

```python
import functools

import jax
import jax.numpy as jnp
from jax import lax
from jax.experimental import pallas as pl
from jax.experimental.pallas import tpu as pltpu
from jax.sharding import PartitionSpec as P

PW = 256
BANDS = 6
REACH = 2
SPREAD = 2 * REACH + 1
EXTRA = 16
DETECT = 10
BLOCK = 32
COARSE = 3
VECTORS = 16
FINE_ROWS = 64
LEAD = 6


def match_kernel(
    patches,
    patch_hbm,
    offset_hbm,
    index_hbm,
    band_hbm,
    detect_hbm,
    table_hbm,
    weight_hbm,
    rowk_hbm,
    colk_hbm,
    tiles_hbm,
    far,
    cross,
    kept,
    patch_ref,
    offset_ref,
    index_ref,
    band_ref,
    detect_ref,
    table_ref,
    weight_ref,
    rowk_ref,
    colk_ref,
    tiles_ref,
    kernels,
    weights,
    shifted,
    toeplitz,
    matches,
    sums,
    extra,
    arrival,
    ready,
):
    visits = band_ref.shape[0]
    tile_count, rows, width = tiles_ref.shape
    per_visit = tile_count // visits
    basis, taps = rowk_ref.shape
    half = taps // 2
    owner = lax.axis_index("ra")
    way = 2 * lax.rem(owner, 2) - 1

    small = [
        pltpu.make_async_copy(source, target, ready.at[place])
        for place, (source, target) in enumerate(
            (
                (index_hbm, index_ref),
                (table_hbm, table_ref),
                (weight_hbm, weight_ref),
                (rowk_hbm, rowk_ref),
                (colk_hbm, colk_ref),
                (patch_hbm, patch_ref),
                (offset_hbm, offset_ref),
                (band_hbm, band_ref),
                (detect_hbm, detect_ref),
            )
        )
    ]
    for copy in small:
        copy.start()

    def fetch(visit):
        held = pl.ds(visit * per_visit, per_visit)
        return pltpu.make_async_copy(tiles_hbm.at[held], tiles_ref.at[held], arrival.at[visit])

    for visit in range(visits):
        fetch(visit).start()

    def iota(shape, axis):
        return lax.broadcasted_iota(jnp.int32, shape, axis)

    def across(left, right, **options):
        return lax.dot_general(
            left,
            right,
            (((1,), (1,)), ((), ())),
            preferred_element_type=jnp.float32,
            **options,
        )

    extra[...] = jnp.zeros_like(extra)
    for place in range(per_visit):
        for side in range(2):
            for fine in range(4):
                top = fine * FINE_ROWS
                shifted[place, side, top : top + 16, :width] = jnp.zeros(
                    (16, width), jnp.bfloat16
                )
                shifted[place, side, top + 48 : top + 64, width:] = jnp.zeros(
                    (16, width), jnp.bfloat16
                )
    eye = (iota((tile_count, tile_count), 0) == iota((tile_count, tile_count), 1)).astype(
        jnp.bfloat16
    )
    for copy in small:
        copy.wait()
    weights[...] = across(eye, jnp.broadcast_to(weight_ref[...], (width, tile_count)))
    entry = iota((1, table_ref.shape[1]), 1)
    chosen = jnp.concatenate(
        [(entry == index_ref[j]).astype(jnp.float32) for j in range(tile_count)], axis=0
    ).astype(jnp.bfloat16)
    rest_of = table_ref[...]
    coeffs = jnp.zeros((tile_count, basis), jnp.float32)
    for _ in range(3):
        piece = rest_of.astype(jnp.bfloat16)
        rest_of = rest_of - piece.astype(jnp.float32)
        coeffs += across(chosen, piece)

    line = iota((2 * VECTORS, taps), 0)
    column = iota((2 * VECTORS, taps), 1)
    block = lax.rem(line, VECTORS) // 2
    step = 4 * lax.rem(block, COARSE) + 2 * lax.rem(line, 2) + line // VECTORS
    wanted = jnp.where(block < COARSE, half + step, half - 1 - step)
    wanted = jnp.where(lax.rem(line, VECTORS) < 4 * COARSE, wanted, -1)
    col_taps = across((wanted == column).astype(jnp.bfloat16), colk_ref[...])
    tap = iota((taps, width), 0)
    lane = iota((taps, width), 1)
    total = None
    for side in range(2):
        place = (lane == tap + LEAD + side * FINE_ROWS).astype(jnp.bfloat16)
        row_taps = jnp.dot(
            rowk_ref[...], place, preferred_element_type=jnp.float32
        ).astype(jnp.bfloat16)
        part = col_taps[side * VECTORS : (side + 1) * VECTORS]
        mix = jnp.concatenate([part * coeffs[j : j + 1] for j in range(tile_count)], axis=0)
        high = mix.astype(jnp.bfloat16)
        low = (mix - high.astype(jnp.float32)).astype(jnp.bfloat16)
        term = jnp.dot(high, row_taps, preferred_element_type=jnp.float32) + jnp.dot(
            low, row_taps, preferred_element_type=jnp.float32
        )
        total = term if total is None else total + term
    kernels[...] = total

    lane = iota((rows, width), 1)
    column = iota((1, width), 1)

    def edge(distance):
        here = iota((16, width), 1) + distance
        return ((here >= 0) & (here < width)).astype(jnp.float32).astype(jnp.bfloat16)

    edges = {distance: edge(distance) for distance in range(-4, 4) if distance != 0}

    def moved_tile(value, distance):
        if distance == 0:
            return value
        turned = pltpu.roll(value, -distance % width, 1).reshape(rows // 16, 16, width)
        return (turned * edges[distance][None]).reshape(rows, width)

    def moved(value, distance):
        if distance == 0:
            return value
        turned = pltpu.roll(value, -distance % width, 1)
        here = lane[: value.shape[0]] + distance
        return jnp.where((here >= 0) & (here < width), turned, jnp.zeros_like(turned))

    def one_visit(visit, unused):
        fetch(visit).wait()
        sums[...] = jnp.zeros_like(sums)
        first = visit * per_visit
        for place in range(per_visit):
            tile = first + place
            pixels = tiles_ref[tile]
            for side in range(2):
                for fine in range(4):
                    part = moved_tile(pixels, -1 - fine if side else fine)
                    top = fine * FINE_ROWS
                    shifted[place, side, top + 16 : top + 64, :width] = part[:48]
                    shifted[place, side, top : top + 48, width:] = part[16:]
        for place in range(per_visit):
            tile = first + place
            for side in range(2):
                for coarse in range(COARSE):
                    for pair in range(2):
                        vector = pl.ds(
                            tile * VECTORS + (side * COARSE + coarse) * 2 + pair, 1
                        )
                        spread = jnp.broadcast_to(kernels[vector, :], (BLOCK, width))
                        turned = pltpu.roll(spread, 0, 1, stride=1, stride_axis=0)
                        toeplitz[
                            place,
                            side,
                            coarse * BLOCK : (coarse + 1) * BLOCK,
                            pair * width : (pair + 1) * width,
                        ] = turned.astype(jnp.bfloat16)
        for place in range(per_visit):
            matched = [jnp.zeros((BLOCK, width), jnp.float32) for _ in range(2)]
            for side in range(2):
                passed = jnp.dot(
                    toeplitz[place, side],
                    shifted[place, side],
                    preferred_element_type=jnp.float32,
                )
                for part in range(2):
                    for coarse in range(COARSE):
                        matched[part] += moved(
                            passed[
                                coarse * BLOCK : (coarse + 1) * BLOCK,
                                part * width : (part + 1) * width,
                            ],
                            -4 * coarse if side else 4 * coarse,
                        )
            matches[place] = jnp.concatenate(matched, axis=0)
        for place in range(per_visit):
            tile = first + place
            matches[place] = pltpu.roll(
                matches[place] * weights[pl.ds(tile, 1), :], lax.rem(offset_ref[tile], width), 1
            )
        for place in range(per_visit):
            tile = first + place
            offset = offset_ref[tile]
            bucket = lax.rem(patch_ref[tile] - owner + REACH + patches, patches)
            weight = weights[pl.ds(tile, 1), :]
            turned = matches[place]
            sums[bucket, :, :width] += jnp.where(lane >= offset, turned, 0.0)
            sums[bucket, :, width:] += jnp.where(lane < offset, turned, 0.0)
            extra[bucket, pl.ds(visit, 1), :] += jnp.concatenate(
                [
                    jnp.where(column >= offset, weight, 0.0),
                    jnp.where(column < offset, weight, 0.0),
                ],
                axis=1,
            )

        held = pl.ds(pl.multiple_of(visit * rows, rows), rows)
        far[held, :] = sums[REACH + 2 * way].astype(jnp.bfloat16)
        cross[0, held, :] = sums[REACH - 2 * way].astype(jnp.bfloat16)
        cross[1, held, :] = sums[REACH - way].astype(jnp.bfloat16)
        kept[0, held, :] = sums[REACH + way].astype(jnp.bfloat16)
        kept[1, held, :] = sums[REACH].astype(jnp.bfloat16)
        return unused

    lax.fori_loop(0, visits, one_visit, 0)

    row = iota((EXTRA, PW), 0)
    lane = iota((1, PW), 1)

    def spread_bands(visit_of, limit):
        line = jnp.full((1, PW), -1.0, jnp.float32)
        for visit in range(visits):
            line = jnp.where(
                (lane < limit) & (visit_of == visit), band_ref[visit].astype(jnp.float32), line
            )
        return line

    by_row = spread_bands(lane // rows, visits * rows)
    by_weight = spread_bands(lax.rem(lane, visits), 2 * visits)
    detect = jnp.zeros((1, PW), jnp.float32)
    for b in range(BANDS):
        detect = jnp.where(lane == b, detect_ref[b], detect)

    def footer(bucket):
        held = extra[bucket]
        high = held.astype(jnp.bfloat16).astype(jnp.float32)
        low = jnp.concatenate([held[-visits:], (held - high)[:-visits]], axis=0)
        mixed = jnp.where((row >= visits) & (row < 2 * visits), low, high)
        mixed = jnp.where(row == 2 * visits, by_row, mixed)
        mixed = jnp.where(row == 2 * visits + 1, by_weight, mixed)
        rest = detect
        for place in range(DETECT, DETECT + 3):
            piece = rest.astype(jnp.bfloat16).astype(jnp.float32)
            rest = rest - piece
            mixed = jnp.where(row == place, piece, mixed)
        return mixed.astype(jnp.bfloat16)

    far[rows * visits :, :] = footer(REACH + 2 * way)
    cross[0, rows * visits :, :] = footer(REACH - 2 * way)
    cross[1, rows * visits :, :] = footer(REACH - way)
    kept[0, rows * visits :, :] = footer(REACH + way)
    kept[1, rows * visits :, :] = footer(REACH)


def add_message(count, groups, message):
    depth = message.shape[0] - EXTRA
    span = depth // count
    row_share = span // groups
    line = lax.broadcasted_iota(jnp.int32, (row_share, depth), 0)
    lane = lax.rem(lax.broadcasted_iota(jnp.int32, (row_share, depth), 1), span)
    band_line = lax.broadcasted_iota(jnp.int32, (8, EXTRA), 0).astype(jnp.float32)
    extra = message[depth:, :]
    bands = extra[2 * count : 2 * count + 2].astype(jnp.float32)
    pick = jnp.concatenate(
        [
            jnp.where(
                (lane == line + part * row_share) & (bands[:1, :depth] == float(b)), 1.0, 0.0
            )
            for part in range(groups)
            for b in range(BANDS)
        ],
        axis=0,
    ).astype(jnp.bfloat16)
    totals = jnp.dot(pick, message[:depth, :], preferred_element_type=jnp.float32)
    pick = (bands[1:, :EXTRA] == band_line).astype(jnp.bfloat16)
    return totals, jnp.dot(pick, extra, preferred_element_type=jnp.float32)


def add_banded(totals, weights, messages):
    depth = totals.shape[0]
    for message in messages:
        totals += message[:depth, :].astype(jnp.float32)
        footer = message[depth:, :].astype(jnp.float32)
        weights += footer[:8] + footer[8:]
    return totals, weights


def write_banded(message, totals, weights):
    depth = totals.shape[0]
    high = weights.astype(jnp.bfloat16).astype(jnp.float32)
    message[:depth, :] = totals.astype(jnp.bfloat16)
    message[depth:, :] = jnp.concatenate([high, weights - high], axis=0).astype(jnp.bfloat16)


def part_of(held, turn, groups):
    depth = held.shape[0] // groups
    part = lax.rem(lax.axis_index("band") + turn, groups)
    return held[pl.ds(pl.multiple_of(part * depth, depth), depth), :]


def keep_kernel(count, groups, kept_ref, totals_ref, weights_ref, detect_ref):
    for place in range(2):
        totals_ref[place], weights_ref[place] = add_message(count, groups, kept_ref.at[place])
    extra = kept_ref[0, kept_ref.shape[1] - EXTRA :, :].astype(jnp.float32)
    detect = extra[DETECT : DETECT + 1] + extra[DETECT + 1 : DETECT + 2]
    detect += extra[DETECT + 2 : DETECT + 3]
    line = lax.broadcasted_iota(jnp.int32, (8, PW), 0)
    lane = lax.broadcasted_iota(jnp.int32, (8, PW), 1)
    chosen = jnp.sum(jnp.where(line == lane, detect, 0.0), axis=1, keepdims=True)
    detect_ref[...] = jnp.broadcast_to(chosen, (8, PW))


def merge_kernel(count, groups, totals_ref, weights_ref, cross_ref, *refs):
    messages = refs[:groups]
    home_ref, home_weight_ref, held = refs[groups:]
    totals, weights = add_message(count, groups, cross_ref.at[0])
    held[...] = totals + totals_ref[0]
    weights += weights_ref[0]
    for turn, message in enumerate(messages):
        write_banded(message, part_of(held, turn, groups), weights)
    totals, weights = add_message(count, groups, cross_ref.at[1])
    home_ref[...] = totals + totals_ref[1]
    home_weight_ref[...] = weights + weights_ref[1]


def home_kernel(count, groups, home_ref, home_weight_ref, far_ref, *refs):
    passing = refs[: groups - 1]
    messages = refs[groups - 1 : 2 * (groups - 1)]
    passed = refs[2 * (groups - 1) : 3 * (groups - 1)]
    own_ref, own_weight_ref, held = refs[3 * (groups - 1) :]
    for source, target in zip(passing, passed):
        target[...] = source[...]
    totals, weights = add_message(count, groups, far_ref)
    held[...] = totals + home_ref[...]
    weights += home_weight_ref[...]
    for turn, message in enumerate(messages, 1):
        write_banded(message, part_of(held, turn, groups), weights)
    own_ref[...] = part_of(held, 0, groups)
    own_weight_ref[...] = weights


def early_kernel(*refs):
    messages = refs[:-2]
    totals_ref, weights_ref = refs[-2:]
    depth = totals_ref.shape[0]
    totals_ref[...], weights_ref[...] = add_banded(
        jnp.zeros((depth, PW), jnp.float32), jnp.zeros((8, PW), jnp.float32), messages
    )


def later_kernel(near_ref, near_weight_ref, *refs):
    refs[-2][...], refs[-1][...] = add_banded(near_ref[...], near_weight_ref[...], refs[:-2])


def combine_kernel(
    detect_ref, own_ref, own_weight_ref, near_ref, near_weight_ref, *refs
):
    coadd_ref, detection_ref = refs[-2:]
    row_share = coadd_ref.shape[1]
    totals, weights = add_banded(
        own_ref[...] + near_ref[...], own_weight_ref[...] + near_weight_ref[...], refs[:-2]
    )
    weights = jnp.maximum(weights, 1.0)
    detection = jnp.zeros((row_share, PW), jnp.float32)
    for b in range(BANDS):
        coadd = totals[b * row_share : (b + 1) * row_share] / weights[b : b + 1]
        coadd_ref[b] = coadd
        detection += detect_ref[b : b + 1] * coadd
    detection_ref[...] = detection


def local(
    tiles,
    tile_patch,
    tile_offset,
    tile_weight,
    visit_band,
    coeff_index,
    coeff_table,
    row_kernels,
    column_kernels,
    band_weight,
):
    tile_count, rows, width = tiles.shape
    visits = visit_band.shape[0]
    per_visit = tile_count // visits
    basis, taps = row_kernels.shape
    patches = lax.axis_size("ra")
    groups = lax.axis_size("band")
    row_share = rows // groups
    length = visits * rows + EXTRA
    message_shape = jax.ShapeDtypeStruct((length, PW), jnp.bfloat16)
    pair_shape = jax.ShapeDtypeStruct((2, length, PW), jnp.bfloat16)
    band_shape = jax.ShapeDtypeStruct((BANDS * row_share + EXTRA, PW), jnp.bfloat16)
    part_shape = jax.ShapeDtypeStruct((BANDS * row_share, PW), jnp.float32)
    whole_shape = jax.ShapeDtypeStruct((BANDS * rows, PW), jnp.float32)
    weight_shape = jax.ShapeDtypeStruct((8, PW), jnp.float32)

    vmem = pl.BlockSpec(memory_space=pltpu.VMEM)
    anywhere = pl.BlockSpec(memory_space=pl.ANY)
    far, cross, kept = pl.pallas_call(
        functools.partial(match_kernel, patches),
        in_specs=[anywhere] * 10,
        out_specs=[vmem] * 3,
        out_shape=[message_shape, pair_shape, pair_shape],
        scratch_shapes=[
            pltpu.SMEM((tile_count,), jnp.int32),
            pltpu.SMEM((tile_count,), jnp.int32),
            pltpu.SMEM((tile_count,), jnp.int32),
            pltpu.SMEM((visits,), jnp.int32),
            pltpu.SMEM((BANDS,), jnp.float32),
            pltpu.VMEM(coeff_table.shape[::-1], jnp.float32),
            pltpu.VMEM((1, tile_count), jnp.bfloat16),
            pltpu.VMEM((basis, taps), jnp.bfloat16),
            pltpu.VMEM((basis, taps), jnp.bfloat16),
            pltpu.VMEM((tile_count, rows, width), jnp.bfloat16),
            pltpu.VMEM((tile_count * VECTORS, width), jnp.float32),
            pltpu.VMEM((tile_count, width), jnp.float32),
            pltpu.VMEM((per_visit, 2, 4 * FINE_ROWS, 2 * width), jnp.bfloat16),
            pltpu.VMEM((per_visit, 2, COARSE * BLOCK, 2 * width), jnp.bfloat16),
            pltpu.VMEM((per_visit, rows, width), jnp.float32),
            pltpu.VMEM((SPREAD, rows, PW), jnp.float32),
            pltpu.VMEM((SPREAD, EXTRA, PW), jnp.float32),
            pltpu.SemaphoreType.DMA((visits,)),
            pltpu.SemaphoreType.DMA((9,)),
        ],
        compiler_params=pltpu.CompilerParams(vmem_limit_bytes=62 * 1024 * 1024),
        name="match_and_sum",
    )(
        tile_patch,
        tile_offset,
        coeff_index,
        visit_band,
        band_weight,
        coeff_table.T,
        tile_weight.reshape(1, tile_count),
        row_kernels,
        column_kernels,
        tiles,
    )

    def send(message, goal, turn):
        route = [
            (o * groups + g, goal(o) % patches * groups + (g + turn) % groups)
            for o in range(patches)
            for g in range(groups)
        ]
        return lax.ppermute(message, ("ra", "band"), route)

    def onward(distance):
        return lambda o: o + distance if o % 2 else o - distance

    def local_call(kernel, name, out_shape, *operands, **options):
        return pl.pallas_call(
            kernel,
            in_specs=[vmem] * len(operands),
            out_specs=[vmem] * len(out_shape),
            out_shape=out_shape,
            compiler_params=pltpu.CompilerParams(vmem_limit_bytes=40 * 1024 * 1024),
            name=name,
            **options,
        )(*operands)

    held = [pltpu.VMEM(whole_shape.shape, jnp.float32)]
    cross = send(cross, onward(-1), 0)
    far = send(far, onward(2), 0)
    *kept, detect = local_call(
        functools.partial(keep_kernel, visits, groups),
        "keep",
        [
            jax.ShapeDtypeStruct((2,) + whole_shape.shape, jnp.float32),
            jax.ShapeDtypeStruct((2,) + weight_shape.shape, jnp.float32),
            weight_shape,
        ],
        kept,
    )
    *near, home, home_weight = local_call(
        functools.partial(merge_kernel, visits, groups),
        "merge",
        [band_shape] * groups + [whole_shape, weight_shape],
        *kept,
        cross,
        scratch_shapes=held,
    )
    first = send(near[0], onward(1), 0)
    *others, own, own_weight = local_call(
        functools.partial(home_kernel, visits, groups),
        "home",
        [band_shape] * (2 * groups - 2) + [part_shape, weight_shape],
        home,
        home_weight,
        far,
        *near[1:],
        scratch_shapes=held,
    )
    others, near = others[: groups - 1], others[groups - 1 :]
    others = [send(others[turn - 1], onward(0), turn) for turn in range(1, groups)]
    near = [send(near[turn - 1], onward(1), turn) for turn in range(1, groups)]
    early = local_call(early_kernel, "combine_early", [part_shape, weight_shape], first)
    early = local_call(
        later_kernel, "combine_later", [part_shape, weight_shape], *early, *others
    )
    return local_call(
        combine_kernel,
        "combine",
        (
            jax.ShapeDtypeStruct((BANDS, row_share, PW), jnp.float32),
            jax.ShapeDtypeStruct((row_share, PW), jnp.float32),
        ),
        detect,
        own,
        own_weight,
        *early,
        *near,
    )


def solution(mesh):
    return jax.shard_map(
        local,
        mesh=mesh,
        in_specs=(
            P(("ra", "band"), None, None),
            P(("ra", "band")),
            P(("ra", "band")),
            P(("ra", "band")),
            P(("ra", "band")),
            P(("ra", "band")),
            P(),
            P(),
            P(),
            P(),
        ),
        out_specs=(P(None, "band", "ra"), P("band", "ra")),
        check_vma=False,
    )
```

```python
import functools

import jax
import jax.numpy as jnp
from jax import lax
from jax.experimental import pallas as pl
from jax.experimental.pallas import tpu as pltpu
from jax.sharding import PartitionSpec as P

PW = 256
BANDS = 6
REACH = 2
SPREAD = 2 * REACH + 1
EXTRA = 16
DETECT = 10
BLOCK = 32
COARSE = 3
VECTORS = 16
FINE_ROWS = 64
LEAD = 6


def match_kernel(
    patches,
    patch_hbm,
    offset_hbm,
    index_hbm,
    band_hbm,
    detect_hbm,
    table_hbm,
    weight_hbm,
    rowk_hbm,
    colk_hbm,
    tiles_hbm,
    far,
    cross,
    kept,
    patch_ref,
    offset_ref,
    index_ref,
    band_ref,
    detect_ref,
    table_ref,
    weight_ref,
    rowk_ref,
    colk_ref,
    tiles_ref,
    kernels,
    weights,
    shifted,
    toeplitz,
    matches,
    sums,
    extra,
    arrival,
    ready,
):
    visits = band_ref.shape[0]
    tile_count, rows, width = tiles_ref.shape
    per_visit = tile_count // visits
    basis, taps = rowk_ref.shape
    half = taps // 2
    owner = lax.axis_index("ra")
    way = 2 * lax.rem(owner, 2) - 1

    small = [
        pltpu.make_async_copy(source, target, ready.at[place])
        for place, (source, target) in enumerate(
            (
                (index_hbm, index_ref),
                (table_hbm, table_ref),
                (weight_hbm, weight_ref),
                (rowk_hbm, rowk_ref),
                (colk_hbm, colk_ref),
                (patch_hbm, patch_ref),
                (offset_hbm, offset_ref),
                (band_hbm, band_ref),
                (detect_hbm, detect_ref),
            )
        )
    ]
    for copy in small:
        copy.start()

    def fetch(visit):
        held = pl.ds(visit * per_visit, per_visit)
        return pltpu.make_async_copy(tiles_hbm.at[held], tiles_ref.at[held], arrival.at[visit])

    for visit in range(visits):
        fetch(visit).start()

    def iota(shape, axis):
        return lax.broadcasted_iota(jnp.int32, shape, axis)

    def across(left, right, **options):
        return lax.dot_general(
            left,
            right,
            (((1,), (1,)), ((), ())),
            preferred_element_type=jnp.float32,
            **options,
        )

    extra[...] = jnp.zeros_like(extra)
    for place in range(per_visit):
        for side in range(2):
            for fine in range(4):
                top = fine * FINE_ROWS
                shifted[place, side, top : top + 16, :width] = jnp.zeros(
                    (16, width), jnp.bfloat16
                )
                shifted[place, side, top + 48 : top + 64, width:] = jnp.zeros(
                    (16, width), jnp.bfloat16
                )
    eye = (iota((tile_count, tile_count), 0) == iota((tile_count, tile_count), 1)).astype(
        jnp.bfloat16
    )
    for copy in small:
        copy.wait()
    weights[...] = across(eye, jnp.broadcast_to(weight_ref[...], (width, tile_count)))
    entry = iota((1, table_ref.shape[1]), 1)
    chosen = jnp.concatenate(
        [(entry == index_ref[j]).astype(jnp.float32) for j in range(tile_count)], axis=0
    ).astype(jnp.bfloat16)
    rest_of = table_ref[...]
    coeffs = jnp.zeros((tile_count, basis), jnp.float32)
    for _ in range(3):
        piece = rest_of.astype(jnp.bfloat16)
        rest_of = rest_of - piece.astype(jnp.float32)
        coeffs += across(chosen, piece)

    line = iota((2 * VECTORS, taps), 0)
    column = iota((2 * VECTORS, taps), 1)
    block = lax.rem(line, VECTORS) // 2
    step = 4 * lax.rem(block, COARSE) + 2 * lax.rem(line, 2) + line // VECTORS
    wanted = jnp.where(block < COARSE, half + step, half - 1 - step)
    wanted = jnp.where(lax.rem(line, VECTORS) < 4 * COARSE, wanted, -1)
    col_taps = across((wanted == column).astype(jnp.bfloat16), colk_ref[...])
    tap = iota((taps, width), 0)
    lane = iota((taps, width), 1)
    total = None
    for side in range(2):
        place = (lane == tap + LEAD + side * FINE_ROWS).astype(jnp.bfloat16)
        row_taps = jnp.dot(
            rowk_ref[...], place, preferred_element_type=jnp.float32
        ).astype(jnp.bfloat16)
        part = col_taps[side * VECTORS : (side + 1) * VECTORS]
        mix = jnp.concatenate([part * coeffs[j : j + 1] for j in range(tile_count)], axis=0)
        high = mix.astype(jnp.bfloat16)
        low = (mix - high.astype(jnp.float32)).astype(jnp.bfloat16)
        term = jnp.dot(high, row_taps, preferred_element_type=jnp.float32) + jnp.dot(
            low, row_taps, preferred_element_type=jnp.float32
        )
        total = term if total is None else total + term
    kernels[...] = total

    lane = iota((rows, width), 1)
    column = iota((1, width), 1)

    def edge(distance):
        here = iota((16, width), 1) + distance
        return ((here >= 0) & (here < width)).astype(jnp.float32).astype(jnp.bfloat16)

    edges = {distance: edge(distance) for distance in range(-4, 4) if distance != 0}

    def moved_tile(value, distance):
        if distance == 0:
            return value
        turned = pltpu.roll(value, -distance % width, 1).reshape(rows // 16, 16, width)
        return (turned * edges[distance][None]).reshape(rows, width)

    def moved(value, distance):
        if distance == 0:
            return value
        turned = pltpu.roll(value, -distance % width, 1)
        here = lane[: value.shape[0]] + distance
        return jnp.where((here >= 0) & (here < width), turned, jnp.zeros_like(turned))

    def one_visit(visit):
        fetch(visit).wait()
        sums[...] = jnp.zeros_like(sums)
        first = visit * per_visit
        for place in range(per_visit):
            tile = first + place
            pixels = tiles_ref[tile]
            for side in range(2):
                for fine in range(4):
                    part = moved_tile(pixels, -1 - fine if side else fine)
                    top = fine * FINE_ROWS
                    shifted[place, side, top + 16 : top + 64, :width] = part[:48]
                    shifted[place, side, top : top + 48, width:] = part[16:]
        for place in range(per_visit):
            tile = first + place
            for side in range(2):
                for coarse in range(COARSE):
                    for pair in range(2):
                        vector = pl.ds(
                            tile * VECTORS + (side * COARSE + coarse) * 2 + pair, 1
                        )
                        spread = jnp.broadcast_to(kernels[vector, :], (BLOCK, width))
                        turned = pltpu.roll(spread, 0, 1, stride=1, stride_axis=0)
                        toeplitz[
                            place,
                            side,
                            coarse * BLOCK : (coarse + 1) * BLOCK,
                            pair * width : (pair + 1) * width,
                        ] = turned.astype(jnp.bfloat16)
        for place in range(per_visit):
            matched = [jnp.zeros((BLOCK, width), jnp.float32) for _ in range(2)]
            for side in range(2):
                passed = jnp.dot(
                    toeplitz[place, side],
                    shifted[place, side],
                    preferred_element_type=jnp.float32,
                )
                for part in range(2):
                    for coarse in range(COARSE):
                        matched[part] += moved(
                            passed[
                                coarse * BLOCK : (coarse + 1) * BLOCK,
                                part * width : (part + 1) * width,
                            ],
                            -4 * coarse if side else 4 * coarse,
                        )
            matches[place] = jnp.concatenate(matched, axis=0)
        for place in range(per_visit):
            tile = first + place
            matches[place] = pltpu.roll(
                matches[place] * weights[pl.ds(tile, 1), :], lax.rem(offset_ref[tile], width), 1
            )
        for place in range(per_visit):
            tile = first + place
            offset = offset_ref[tile]
            bucket = lax.rem(patch_ref[tile] - owner + REACH + patches, patches)
            weight = weights[pl.ds(tile, 1), :]
            turned = matches[place]
            sums[bucket, :, :width] += jnp.where(lane >= offset, turned, 0.0)
            sums[bucket, :, width:] += jnp.where(lane < offset, turned, 0.0)
            extra[bucket, pl.ds(visit, 1), :] += jnp.concatenate(
                [
                    jnp.where(column >= offset, weight, 0.0),
                    jnp.where(column < offset, weight, 0.0),
                ],
                axis=1,
            )

        held = pl.ds(pl.multiple_of(visit * rows, rows), rows)
        far[held, :] = sums[REACH + 2 * way].astype(jnp.bfloat16)
        cross[0, held, :] = sums[REACH - 2 * way].astype(jnp.bfloat16)
        cross[1, held, :] = sums[REACH - way].astype(jnp.bfloat16)
        kept[0, held, :] = sums[REACH + way].astype(jnp.bfloat16)
        kept[1, held, :] = sums[REACH].astype(jnp.bfloat16)

    for visit in range(visits):
        one_visit(visit)

    row = iota((EXTRA, PW), 0)
    lane = iota((1, PW), 1)

    def spread_bands(visit_of, limit):
        line = jnp.full((1, PW), -1.0, jnp.float32)
        for visit in range(visits):
            line = jnp.where(
                (lane < limit) & (visit_of == visit), band_ref[visit].astype(jnp.float32), line
            )
        return line

    by_row = spread_bands(lane // rows, visits * rows)
    by_weight = spread_bands(lax.rem(lane, visits), 2 * visits)
    detect = jnp.zeros((1, PW), jnp.float32)
    for b in range(BANDS):
        detect = jnp.where(lane == b, detect_ref[b], detect)

    def footer(bucket):
        held = extra[bucket]
        high = held.astype(jnp.bfloat16).astype(jnp.float32)
        low = jnp.concatenate([held[-visits:], (held - high)[:-visits]], axis=0)
        mixed = jnp.where((row >= visits) & (row < 2 * visits), low, high)
        mixed = jnp.where(row == 2 * visits, by_row, mixed)
        mixed = jnp.where(row == 2 * visits + 1, by_weight, mixed)
        rest = detect
        for place in range(DETECT, DETECT + 3):
            piece = rest.astype(jnp.bfloat16).astype(jnp.float32)
            rest = rest - piece
            mixed = jnp.where(row == place, piece, mixed)
        return mixed.astype(jnp.bfloat16)

    far[rows * visits :, :] = footer(REACH + 2 * way)
    cross[0, rows * visits :, :] = footer(REACH - 2 * way)
    cross[1, rows * visits :, :] = footer(REACH - way)
    kept[0, rows * visits :, :] = footer(REACH + way)
    kept[1, rows * visits :, :] = footer(REACH)


def add_message(count, groups, message):
    depth = message.shape[0] - EXTRA
    span = depth // count
    row_share = span // groups
    line = lax.broadcasted_iota(jnp.int32, (row_share, depth), 0)
    lane = lax.rem(lax.broadcasted_iota(jnp.int32, (row_share, depth), 1), span)
    band_line = lax.broadcasted_iota(jnp.int32, (8, EXTRA), 0).astype(jnp.float32)
    extra = message[depth:, :]
    bands = extra[2 * count : 2 * count + 2].astype(jnp.float32)
    pick = jnp.concatenate(
        [
            jnp.where(
                (lane == line + part * row_share) & (bands[:1, :depth] == float(b)), 1.0, 0.0
            )
            for part in range(groups)
            for b in range(BANDS)
        ],
        axis=0,
    ).astype(jnp.bfloat16)
    totals = jnp.dot(pick, message[:depth, :], preferred_element_type=jnp.float32)
    pick = (bands[1:, :EXTRA] == band_line).astype(jnp.bfloat16)
    return totals, jnp.dot(pick, extra, preferred_element_type=jnp.float32)


def add_banded(totals, weights, messages):
    depth = totals.shape[0]
    for message in messages:
        totals += message[:depth, :].astype(jnp.float32)
        footer = message[depth:, :].astype(jnp.float32)
        weights += footer[:8] + footer[8:]
    return totals, weights


def write_banded(message, totals, weights):
    depth = totals.shape[0]
    high = weights.astype(jnp.bfloat16).astype(jnp.float32)
    message[:depth, :] = totals.astype(jnp.bfloat16)
    message[depth:, :] = jnp.concatenate([high, weights - high], axis=0).astype(jnp.bfloat16)


def part_of(held, turn, groups):
    depth = held.shape[0] // groups
    part = lax.rem(lax.axis_index("band") + turn, groups)
    return held[pl.ds(pl.multiple_of(part * depth, depth), depth), :]


def keep_kernel(count, groups, kept_ref, totals_ref, weights_ref, detect_ref):
    for place in range(2):
        totals_ref[place], weights_ref[place] = add_message(count, groups, kept_ref.at[place])
    extra = kept_ref[0, kept_ref.shape[1] - EXTRA :, :].astype(jnp.float32)
    detect = extra[DETECT : DETECT + 1] + extra[DETECT + 1 : DETECT + 2]
    detect += extra[DETECT + 2 : DETECT + 3]
    line = lax.broadcasted_iota(jnp.int32, (8, PW), 0)
    lane = lax.broadcasted_iota(jnp.int32, (8, PW), 1)
    chosen = jnp.sum(jnp.where(line == lane, detect, 0.0), axis=1, keepdims=True)
    detect_ref[...] = jnp.broadcast_to(chosen, (8, PW))


def merge_kernel(count, groups, totals_ref, weights_ref, cross_ref, *refs):
    messages = refs[:groups]
    home_ref, home_weight_ref, held = refs[groups:]
    totals, weights = add_message(count, groups, cross_ref.at[0])
    held[...] = totals + totals_ref[0]
    weights += weights_ref[0]
    for turn, message in enumerate(messages):
        write_banded(message, part_of(held, turn, groups), weights)
    totals, weights = add_message(count, groups, cross_ref.at[1])
    home_ref[...] = totals + totals_ref[1]
    home_weight_ref[...] = weights + weights_ref[1]


def home_kernel(count, groups, home_ref, home_weight_ref, far_ref, *refs):
    messages = refs[: groups - 1]
    own_ref, own_weight_ref, held = refs[groups - 1 :]
    totals, weights = add_message(count, groups, far_ref)
    held[...] = totals + home_ref[...]
    weights += home_weight_ref[...]
    for turn, message in enumerate(messages, 1):
        write_banded(message, part_of(held, turn, groups), weights)
    own_ref[...] = part_of(held, 0, groups)
    own_weight_ref[...] = weights


def early_kernel(*refs):
    messages = refs[:-2]
    totals_ref, weights_ref = refs[-2:]
    depth = totals_ref.shape[0]
    totals_ref[...], weights_ref[...] = add_banded(
        jnp.zeros((depth, PW), jnp.float32), jnp.zeros((8, PW), jnp.float32), messages
    )


def combine_kernel(
    detect_ref, own_ref, own_weight_ref, near_ref, near_weight_ref, *refs
):
    coadd_ref, detection_ref = refs[-2:]
    row_share = coadd_ref.shape[1]
    totals, weights = add_banded(
        own_ref[...] + near_ref[...], own_weight_ref[...] + near_weight_ref[...], refs[:-2]
    )
    weights = jnp.maximum(weights, 1.0)
    detection = jnp.zeros((row_share, PW), jnp.float32)
    for b in range(BANDS):
        coadd = totals[b * row_share : (b + 1) * row_share] / weights[b : b + 1]
        coadd_ref[b] = coadd
        detection += detect_ref[b : b + 1] * coadd
    detection_ref[...] = detection


def local(
    tiles,
    tile_patch,
    tile_offset,
    tile_weight,
    visit_band,
    coeff_index,
    coeff_table,
    row_kernels,
    column_kernels,
    band_weight,
):
    tile_count, rows, width = tiles.shape
    visits = visit_band.shape[0]
    per_visit = tile_count // visits
    basis, taps = row_kernels.shape
    patches = lax.axis_size("ra")
    groups = lax.axis_size("band")
    row_share = rows // groups
    length = visits * rows + EXTRA
    message_shape = jax.ShapeDtypeStruct((length, PW), jnp.bfloat16)
    pair_shape = jax.ShapeDtypeStruct((2, length, PW), jnp.bfloat16)
    band_shape = jax.ShapeDtypeStruct((BANDS * row_share + EXTRA, PW), jnp.bfloat16)
    part_shape = jax.ShapeDtypeStruct((BANDS * row_share, PW), jnp.float32)
    whole_shape = jax.ShapeDtypeStruct((BANDS * rows, PW), jnp.float32)
    weight_shape = jax.ShapeDtypeStruct((8, PW), jnp.float32)

    vmem = pl.BlockSpec(memory_space=pltpu.VMEM)
    anywhere = pl.BlockSpec(memory_space=pl.ANY)
    far, cross, kept = pl.pallas_call(
        functools.partial(match_kernel, patches),
        in_specs=[anywhere] * 10,
        out_specs=[vmem] * 3,
        out_shape=[message_shape, pair_shape, pair_shape],
        scratch_shapes=[
            pltpu.SMEM((tile_count,), jnp.int32),
            pltpu.SMEM((tile_count,), jnp.int32),
            pltpu.SMEM((tile_count,), jnp.int32),
            pltpu.SMEM((visits,), jnp.int32),
            pltpu.SMEM((BANDS,), jnp.float32),
            pltpu.VMEM(coeff_table.shape[::-1], jnp.float32),
            pltpu.VMEM((1, tile_count), jnp.bfloat16),
            pltpu.VMEM((basis, taps), jnp.bfloat16),
            pltpu.VMEM((basis, taps), jnp.bfloat16),
            pltpu.VMEM((tile_count, rows, width), jnp.bfloat16),
            pltpu.VMEM((tile_count * VECTORS, width), jnp.float32),
            pltpu.VMEM((tile_count, width), jnp.float32),
            pltpu.VMEM((per_visit, 2, 4 * FINE_ROWS, 2 * width), jnp.bfloat16),
            pltpu.VMEM((per_visit, 2, COARSE * BLOCK, 2 * width), jnp.bfloat16),
            pltpu.VMEM((per_visit, rows, width), jnp.float32),
            pltpu.VMEM((SPREAD, rows, PW), jnp.float32),
            pltpu.VMEM((SPREAD, EXTRA, PW), jnp.float32),
            pltpu.SemaphoreType.DMA((visits,)),
            pltpu.SemaphoreType.DMA((9,)),
        ],
        compiler_params=pltpu.CompilerParams(vmem_limit_bytes=62 * 1024 * 1024),
        name="match_and_sum",
    )(
        tile_patch,
        tile_offset,
        coeff_index,
        visit_band,
        band_weight,
        coeff_table.T,
        tile_weight.reshape(1, tile_count),
        row_kernels,
        column_kernels,
        tiles,
    )

    def send(message, goal, turn):
        route = [
            (o * groups + g, goal(o) % patches * groups + (g + turn) % groups)
            for o in range(patches)
            for g in range(groups)
        ]
        return lax.ppermute(message, ("ra", "band"), route)

    def onward(distance):
        return lambda o: o + distance if o % 2 else o - distance

    def local_call(kernel, name, out_shape, *operands, **options):
        return pl.pallas_call(
            kernel,
            in_specs=[vmem] * len(operands),
            out_specs=[vmem] * len(out_shape),
            out_shape=out_shape,
            compiler_params=pltpu.CompilerParams(vmem_limit_bytes=40 * 1024 * 1024),
            name=name,
            **options,
        )(*operands)

    held = [pltpu.VMEM(whole_shape.shape, jnp.float32)]
    cross = send(cross, onward(-1), 0)
    far = send(far, onward(2), 0)
    *kept, detect = local_call(
        functools.partial(keep_kernel, visits, groups),
        "keep",
        [
            jax.ShapeDtypeStruct((2,) + whole_shape.shape, jnp.float32),
            jax.ShapeDtypeStruct((2,) + weight_shape.shape, jnp.float32),
            weight_shape,
        ],
        kept,
    )
    *near, home, home_weight = local_call(
        functools.partial(merge_kernel, visits, groups),
        "merge",
        [band_shape] * groups + [whole_shape, weight_shape],
        *kept,
        cross,
        scratch_shapes=held,
    )
    near = [send(near[turn], onward(1), turn) for turn in range(groups)]
    *others, own, own_weight = local_call(
        functools.partial(home_kernel, visits, groups),
        "home",
        [band_shape] * (groups - 1) + [part_shape, weight_shape],
        home,
        home_weight,
        far,
        scratch_shapes=held,
    )
    others = [send(others[turn - 1], onward(0), turn) for turn in range(1, groups)]
    near = local_call(early_kernel, "combine_early", [part_shape, weight_shape], *near)
    return local_call(
        combine_kernel,
        "combine",
        (
            jax.ShapeDtypeStruct((BANDS, row_share, PW), jnp.float32),
            jax.ShapeDtypeStruct((row_share, PW), jnp.float32),
        ),
        detect,
        own,
        own_weight,
        *near,
        *others,
    )


def solution(mesh):
    return jax.shard_map(
        local,
        mesh=mesh,
        in_specs=(
            P(("ra", "band"), None, None),
            P(("ra", "band")),
            P(("ra", "band")),
            P(("ra", "band")),
            P(("ra", "band")),
            P(("ra", "band")),
            P(),
            P(),
            P(),
            P(),
        ),
        out_specs=(P(None, "band", "ra"), P("band", "ra")),
        check_vma=False,
    )
```

```python
import functools

import jax
import jax.numpy as jnp
from jax import lax
from jax.experimental import pallas as pl
from jax.experimental.pallas import tpu as pltpu
from jax.sharding import PartitionSpec as P

PW = 256
BANDS = 6
REACH = 2
SPREAD = 2 * REACH + 1
EXTRA = 16
DETECT = 10
BLOCK = 32
COARSE = 3
VECTORS = 16
FINE_ROWS = 64
LEAD = 6


def match_kernel(
    patches,
    patch_hbm,
    offset_hbm,
    index_hbm,
    band_hbm,
    detect_hbm,
    table_hbm,
    weight_hbm,
    rowk_hbm,
    colk_hbm,
    tiles_hbm,
    far_hbm,
    cross_hbm,
    kept_hbm,
    far,
    cross,
    kept,
    patch_ref,
    offset_ref,
    index_ref,
    band_ref,
    detect_ref,
    table_ref,
    weight_ref,
    rowk_ref,
    colk_ref,
    tiles_ref,
    kernels,
    weights,
    shifted,
    toeplitz,
    matches,
    sums,
    extra,
    arrival,
    ready,
    leaving,
):
    visits = band_ref.shape[0]
    tile_count, rows, width = tiles_ref.shape
    per_visit = tile_count // visits
    basis, taps = rowk_ref.shape
    half = taps // 2
    owner = lax.axis_index("ra")
    way = 2 * lax.rem(owner, 2) - 1

    small = [
        pltpu.make_async_copy(source, target, ready.at[place])
        for place, (source, target) in enumerate(
            (
                (index_hbm, index_ref),
                (table_hbm, table_ref),
                (weight_hbm, weight_ref),
                (rowk_hbm, rowk_ref),
                (colk_hbm, colk_ref),
                (patch_hbm, patch_ref),
                (offset_hbm, offset_ref),
                (band_hbm, band_ref),
                (detect_hbm, detect_ref),
            )
        )
    ]
    for copy in small:
        copy.start()

    def fetch(visit):
        held = pl.ds(visit * per_visit, per_visit)
        return pltpu.make_async_copy(tiles_hbm.at[held], tiles_ref.at[held], arrival.at[visit])

    for visit in range(visits):
        fetch(visit).start()

    def iota(shape, axis):
        return lax.broadcasted_iota(jnp.int32, shape, axis)

    def across(left, right, **options):
        return lax.dot_general(
            left,
            right,
            (((1,), (1,)), ((), ())),
            preferred_element_type=jnp.float32,
            **options,
        )

    extra[...] = jnp.zeros_like(extra)
    for place in range(per_visit):
        for side in range(2):
            for fine in range(4):
                top = fine * FINE_ROWS
                shifted[place, side, top : top + 16, :width] = jnp.zeros(
                    (16, width), jnp.bfloat16
                )
                shifted[place, side, top + 48 : top + 64, width:] = jnp.zeros(
                    (16, width), jnp.bfloat16
                )
    eye = (iota((tile_count, tile_count), 0) == iota((tile_count, tile_count), 1)).astype(
        jnp.bfloat16
    )
    for copy in small:
        copy.wait()
    weights[...] = across(eye, jnp.broadcast_to(weight_ref[...], (width, tile_count)))
    entry = iota((1, table_ref.shape[1]), 1)
    chosen = jnp.concatenate(
        [(entry == index_ref[j]).astype(jnp.float32) for j in range(tile_count)], axis=0
    ).astype(jnp.bfloat16)
    rest_of = table_ref[...]
    coeffs = jnp.zeros((tile_count, basis), jnp.float32)
    for _ in range(3):
        piece = rest_of.astype(jnp.bfloat16)
        rest_of = rest_of - piece.astype(jnp.float32)
        coeffs += across(chosen, piece)

    line = iota((2 * VECTORS, taps), 0)
    column = iota((2 * VECTORS, taps), 1)
    block = lax.rem(line, VECTORS) // 2
    step = 4 * lax.rem(block, COARSE) + 2 * lax.rem(line, 2) + line // VECTORS
    wanted = jnp.where(block < COARSE, half + step, half - 1 - step)
    wanted = jnp.where(lax.rem(line, VECTORS) < 4 * COARSE, wanted, -1)
    col_taps = across((wanted == column).astype(jnp.bfloat16), colk_ref[...])
    tap = iota((taps, width), 0)
    lane = iota((taps, width), 1)
    total = None
    for side in range(2):
        place = (lane == tap + LEAD + side * FINE_ROWS).astype(jnp.bfloat16)
        row_taps = jnp.dot(
            rowk_ref[...], place, preferred_element_type=jnp.float32
        ).astype(jnp.bfloat16)
        part = col_taps[side * VECTORS : (side + 1) * VECTORS]
        mix = jnp.concatenate([part * coeffs[j : j + 1] for j in range(tile_count)], axis=0)
        high = mix.astype(jnp.bfloat16)
        low = (mix - high.astype(jnp.float32)).astype(jnp.bfloat16)
        term = jnp.dot(high, row_taps, preferred_element_type=jnp.float32) + jnp.dot(
            low, row_taps, preferred_element_type=jnp.float32
        )
        total = term if total is None else total + term
    kernels[...] = total

    lane = iota((rows, width), 1)
    column = iota((1, width), 1)

    def edge(distance):
        here = iota((16, width), 1) + distance
        return ((here >= 0) & (here < width)).astype(jnp.float32).astype(jnp.bfloat16)

    edges = {distance: edge(distance) for distance in range(-4, 4) if distance != 0}

    def moved_tile(value, distance):
        if distance == 0:
            return value
        turned = pltpu.roll(value, -distance % width, 1).reshape(rows // 16, 16, width)
        return (turned * edges[distance][None]).reshape(rows, width)

    def moved(value, distance):
        if distance == 0:
            return value
        turned = pltpu.roll(value, -distance % width, 1)
        here = lane[: value.shape[0]] + distance
        return jnp.where((here >= 0) & (here < width), turned, jnp.zeros_like(turned))

    def deliver(part, held):
        return [
            pltpu.make_async_copy(far.at[held], far_hbm.at[held], leaving.at[part, 0]),
            pltpu.make_async_copy(cross.at[:, held], cross_hbm.at[:, held], leaving.at[part, 1]),
            pltpu.make_async_copy(kept.at[:, held], kept_hbm.at[:, held], leaving.at[part, 2]),
        ]

    def one_visit(visit, unused):
        fetch(visit).wait()
        sums[...] = jnp.zeros_like(sums)
        first = visit * per_visit
        for place in range(per_visit):
            tile = first + place
            pixels = tiles_ref[tile]
            for side in range(2):
                for fine in range(4):
                    part = moved_tile(pixels, -1 - fine if side else fine)
                    top = fine * FINE_ROWS
                    shifted[place, side, top + 16 : top + 64, :width] = part[:48]
                    shifted[place, side, top : top + 48, width:] = part[16:]
        for place in range(per_visit):
            tile = first + place
            for side in range(2):
                for coarse in range(COARSE):
                    for pair in range(2):
                        vector = pl.ds(
                            tile * VECTORS + (side * COARSE + coarse) * 2 + pair, 1
                        )
                        spread = jnp.broadcast_to(kernels[vector, :], (BLOCK, width))
                        turned = pltpu.roll(spread, 0, 1, stride=1, stride_axis=0)
                        toeplitz[
                            place,
                            side,
                            coarse * BLOCK : (coarse + 1) * BLOCK,
                            pair * width : (pair + 1) * width,
                        ] = turned.astype(jnp.bfloat16)
        for place in range(per_visit):
            matched = [jnp.zeros((BLOCK, width), jnp.float32) for _ in range(2)]
            for side in range(2):
                passed = jnp.dot(
                    toeplitz[place, side],
                    shifted[place, side],
                    preferred_element_type=jnp.float32,
                )
                for part in range(2):
                    for coarse in range(COARSE):
                        matched[part] += moved(
                            passed[
                                coarse * BLOCK : (coarse + 1) * BLOCK,
                                part * width : (part + 1) * width,
                            ],
                            -4 * coarse if side else 4 * coarse,
                        )
            matches[place] = jnp.concatenate(matched, axis=0)
        for place in range(per_visit):
            tile = first + place
            matches[place] = pltpu.roll(
                matches[place] * weights[pl.ds(tile, 1), :], lax.rem(offset_ref[tile], width), 1
            )
        for place in range(per_visit):
            tile = first + place
            offset = offset_ref[tile]
            bucket = lax.rem(patch_ref[tile] - owner + REACH + patches, patches)
            weight = weights[pl.ds(tile, 1), :]
            turned = matches[place]
            sums[bucket, :, :width] += jnp.where(lane >= offset, turned, 0.0)
            sums[bucket, :, width:] += jnp.where(lane < offset, turned, 0.0)
            extra[bucket, pl.ds(visit, 1), :] += jnp.concatenate(
                [
                    jnp.where(column >= offset, weight, 0.0),
                    jnp.where(column < offset, weight, 0.0),
                ],
                axis=1,
            )

        held = pl.ds(pl.multiple_of(visit * rows, rows), rows)
        far[held, :] = sums[REACH + 2 * way].astype(jnp.bfloat16)
        cross[0, held, :] = sums[REACH - 2 * way].astype(jnp.bfloat16)
        cross[1, held, :] = sums[REACH - way].astype(jnp.bfloat16)
        kept[0, held, :] = sums[REACH + way].astype(jnp.bfloat16)
        kept[1, held, :] = sums[REACH].astype(jnp.bfloat16)
        for copy in deliver(visit, held):
            copy.start()
        return unused

    lax.fori_loop(0, visits, one_visit, 0)

    row = iota((EXTRA, PW), 0)
    lane = iota((1, PW), 1)

    def spread_bands(visit_of, limit):
        line = jnp.full((1, PW), -1.0, jnp.float32)
        for visit in range(visits):
            line = jnp.where(
                (lane < limit) & (visit_of == visit), band_ref[visit].astype(jnp.float32), line
            )
        return line

    by_row = spread_bands(lane // rows, visits * rows)
    by_weight = spread_bands(lax.rem(lane, visits), 2 * visits)
    detect = jnp.zeros((1, PW), jnp.float32)
    for b in range(BANDS):
        detect = jnp.where(lane == b, detect_ref[b], detect)

    def footer(bucket):
        held = extra[bucket]
        high = held.astype(jnp.bfloat16).astype(jnp.float32)
        low = jnp.concatenate([held[-visits:], (held - high)[:-visits]], axis=0)
        mixed = jnp.where((row >= visits) & (row < 2 * visits), low, high)
        mixed = jnp.where(row == 2 * visits, by_row, mixed)
        mixed = jnp.where(row == 2 * visits + 1, by_weight, mixed)
        rest = detect
        for place in range(DETECT, DETECT + 3):
            piece = rest.astype(jnp.bfloat16).astype(jnp.float32)
            rest = rest - piece
            mixed = jnp.where(row == place, piece, mixed)
        return mixed.astype(jnp.bfloat16)

    far[rows * visits :, :] = footer(REACH + 2 * way)
    cross[0, rows * visits :, :] = footer(REACH - 2 * way)
    cross[1, rows * visits :, :] = footer(REACH - way)
    kept[0, rows * visits :, :] = footer(REACH + way)
    kept[1, rows * visits :, :] = footer(REACH)
    for copy in deliver(visits, pl.ds(rows * visits, EXTRA)):
        copy.start()
    for visit in range(visits):
        for copy in deliver(visit, pl.ds(rows * visit, rows)):
            copy.wait()
    for copy in deliver(visits, pl.ds(rows * visits, EXTRA)):
        copy.wait()


def add_message(count, groups, message):
    depth = message.shape[0] - EXTRA
    span = depth // count
    row_share = span // groups
    line = lax.broadcasted_iota(jnp.int32, (row_share, depth), 0)
    lane = lax.rem(lax.broadcasted_iota(jnp.int32, (row_share, depth), 1), span)
    band_line = lax.broadcasted_iota(jnp.int32, (8, EXTRA), 0).astype(jnp.float32)
    extra = message[depth:, :]
    bands = extra[2 * count : 2 * count + 2].astype(jnp.float32)
    pick = jnp.concatenate(
        [
            jnp.where(
                (lane == line + part * row_share) & (bands[:1, :depth] == float(b)), 1.0, 0.0
            )
            for part in range(groups)
            for b in range(BANDS)
        ],
        axis=0,
    ).astype(jnp.bfloat16)
    totals = jnp.dot(pick, message[:depth, :], preferred_element_type=jnp.float32)
    pick = (bands[1:, :EXTRA] == band_line).astype(jnp.bfloat16)
    return totals, jnp.dot(pick, extra, preferred_element_type=jnp.float32)


def add_banded(totals, weights, messages):
    depth = totals.shape[0]
    for message in messages:
        totals += message[:depth, :].astype(jnp.float32)
        footer = message[depth:, :].astype(jnp.float32)
        weights += footer[:8] + footer[8:]
    return totals, weights


def write_banded(message, totals, weights):
    depth = totals.shape[0]
    high = weights.astype(jnp.bfloat16).astype(jnp.float32)
    message[:depth, :] = totals.astype(jnp.bfloat16)
    message[depth:, :] = jnp.concatenate([high, weights - high], axis=0).astype(jnp.bfloat16)


def part_of(held, turn, groups):
    depth = held.shape[0] // groups
    part = lax.rem(lax.axis_index("band") + turn, groups)
    return held[pl.ds(pl.multiple_of(part * depth, depth), depth), :]


def keep_kernel(count, groups, kept_ref, totals_ref, weights_ref, detect_ref):
    for place in range(2):
        totals_ref[place], weights_ref[place] = add_message(count, groups, kept_ref.at[place])
    extra = kept_ref[0, kept_ref.shape[1] - EXTRA :, :].astype(jnp.float32)
    detect = extra[DETECT : DETECT + 1] + extra[DETECT + 1 : DETECT + 2]
    detect += extra[DETECT + 2 : DETECT + 3]
    line = lax.broadcasted_iota(jnp.int32, (8, PW), 0)
    lane = lax.broadcasted_iota(jnp.int32, (8, PW), 1)
    chosen = jnp.sum(jnp.where(line == lane, detect, 0.0), axis=1, keepdims=True)
    detect_ref[...] = jnp.broadcast_to(chosen, (8, PW))


def merge_kernel(count, groups, totals_ref, weights_ref, cross_ref, *refs):
    messages = refs[:groups]
    home_ref, home_weight_ref, held = refs[groups:]
    totals, weights = add_message(count, groups, cross_ref.at[0])
    held[...] = totals + totals_ref[0]
    weights += weights_ref[0]
    for turn, message in enumerate(messages):
        write_banded(message, part_of(held, turn, groups), weights)
    totals, weights = add_message(count, groups, cross_ref.at[1])
    home_ref[...] = totals + totals_ref[1]
    home_weight_ref[...] = weights + weights_ref[1]


def home_kernel(count, groups, home_ref, home_weight_ref, far_ref, *refs):
    messages = refs[: groups - 1]
    own_ref, own_weight_ref, held = refs[groups - 1 :]
    totals, weights = add_message(count, groups, far_ref)
    held[...] = totals + home_ref[...]
    weights += home_weight_ref[...]
    for turn, message in enumerate(messages, 1):
        write_banded(message, part_of(held, turn, groups), weights)
    own_ref[...] = part_of(held, 0, groups)
    own_weight_ref[...] = weights


def early_kernel(*refs):
    messages = refs[:-2]
    totals_ref, weights_ref = refs[-2:]
    depth = totals_ref.shape[0]
    totals_ref[...], weights_ref[...] = add_banded(
        jnp.zeros((depth, PW), jnp.float32), jnp.zeros((8, PW), jnp.float32), messages
    )


def combine_kernel(
    detect_ref, own_ref, own_weight_ref, near_ref, near_weight_ref, *refs
):
    coadd_ref, detection_ref = refs[-2:]
    row_share = coadd_ref.shape[1]
    totals, weights = add_banded(
        own_ref[...] + near_ref[...], own_weight_ref[...] + near_weight_ref[...], refs[:-2]
    )
    weights = jnp.maximum(weights, 1.0)
    detection = jnp.zeros((row_share, PW), jnp.float32)
    for b in range(BANDS):
        coadd = totals[b * row_share : (b + 1) * row_share] / weights[b : b + 1]
        coadd_ref[b] = coadd
        detection += detect_ref[b : b + 1] * coadd
    detection_ref[...] = detection


def local(
    tiles,
    tile_patch,
    tile_offset,
    tile_weight,
    visit_band,
    coeff_index,
    coeff_table,
    row_kernels,
    column_kernels,
    band_weight,
):
    tile_count, rows, width = tiles.shape
    visits = visit_band.shape[0]
    per_visit = tile_count // visits
    basis, taps = row_kernels.shape
    patches = lax.axis_size("ra")
    groups = lax.axis_size("band")
    row_share = rows // groups
    length = visits * rows + EXTRA
    message_shape = jax.ShapeDtypeStruct((length, PW), jnp.bfloat16)
    pair_shape = jax.ShapeDtypeStruct((2, length, PW), jnp.bfloat16)
    band_shape = jax.ShapeDtypeStruct((BANDS * row_share + EXTRA, PW), jnp.bfloat16)
    part_shape = jax.ShapeDtypeStruct((BANDS * row_share, PW), jnp.float32)
    whole_shape = jax.ShapeDtypeStruct((BANDS * rows, PW), jnp.float32)
    weight_shape = jax.ShapeDtypeStruct((8, PW), jnp.float32)

    vmem = pl.BlockSpec(memory_space=pltpu.VMEM)
    anywhere = pl.BlockSpec(memory_space=pl.ANY)
    far, cross, kept = pl.pallas_call(
        functools.partial(match_kernel, patches),
        in_specs=[anywhere] * 10,
        out_specs=[anywhere] * 3,
        out_shape=[message_shape, pair_shape, pair_shape],
        scratch_shapes=[
            pltpu.VMEM(message_shape.shape, jnp.bfloat16),
            pltpu.VMEM(pair_shape.shape, jnp.bfloat16),
            pltpu.VMEM(pair_shape.shape, jnp.bfloat16),
            pltpu.SMEM((tile_count,), jnp.int32),
            pltpu.SMEM((tile_count,), jnp.int32),
            pltpu.SMEM((tile_count,), jnp.int32),
            pltpu.SMEM((visits,), jnp.int32),
            pltpu.SMEM((BANDS,), jnp.float32),
            pltpu.VMEM(coeff_table.shape[::-1], jnp.float32),
            pltpu.VMEM((1, tile_count), jnp.bfloat16),
            pltpu.VMEM((basis, taps), jnp.bfloat16),
            pltpu.VMEM((basis, taps), jnp.bfloat16),
            pltpu.VMEM((tile_count, rows, width), jnp.bfloat16),
            pltpu.VMEM((tile_count * VECTORS, width), jnp.float32),
            pltpu.VMEM((tile_count, width), jnp.float32),
            pltpu.VMEM((per_visit, 2, 4 * FINE_ROWS, 2 * width), jnp.bfloat16),
            pltpu.VMEM((per_visit, 2, COARSE * BLOCK, 2 * width), jnp.bfloat16),
            pltpu.VMEM((per_visit, rows, width), jnp.float32),
            pltpu.VMEM((SPREAD, rows, PW), jnp.float32),
            pltpu.VMEM((SPREAD, EXTRA, PW), jnp.float32),
            pltpu.SemaphoreType.DMA((visits,)),
            pltpu.SemaphoreType.DMA((9,)),
            pltpu.SemaphoreType.DMA((visits + 1, 3)),
        ],
        compiler_params=pltpu.CompilerParams(vmem_limit_bytes=62 * 1024 * 1024),
        name="match_and_sum",
    )(
        tile_patch,
        tile_offset,
        coeff_index,
        visit_band,
        band_weight,
        coeff_table.T,
        tile_weight.reshape(1, tile_count),
        row_kernels,
        column_kernels,
        tiles,
    )

    def send(message, goal, turn):
        route = [
            (o * groups + g, goal(o) % patches * groups + (g + turn) % groups)
            for o in range(patches)
            for g in range(groups)
        ]
        return lax.ppermute(message, ("ra", "band"), route)

    def onward(distance):
        return lambda o: o + distance if o % 2 else o - distance

    def local_call(kernel, name, out_shape, *operands, **options):
        return pl.pallas_call(
            kernel,
            in_specs=[vmem] * len(operands),
            out_specs=[vmem] * len(out_shape),
            out_shape=out_shape,
            compiler_params=pltpu.CompilerParams(vmem_limit_bytes=40 * 1024 * 1024),
            name=name,
            **options,
        )(*operands)

    held = [pltpu.VMEM(whole_shape.shape, jnp.float32)]
    cross = send(cross, onward(-1), 0)
    far = send(far, onward(2), 0)
    *kept, detect = local_call(
        functools.partial(keep_kernel, visits, groups),
        "keep",
        [
            jax.ShapeDtypeStruct((2,) + whole_shape.shape, jnp.float32),
            jax.ShapeDtypeStruct((2,) + weight_shape.shape, jnp.float32),
            weight_shape,
        ],
        kept,
    )
    *near, home, home_weight = local_call(
        functools.partial(merge_kernel, visits, groups),
        "merge",
        [band_shape] * groups + [whole_shape, weight_shape],
        *kept,
        cross,
        scratch_shapes=held,
    )
    near = [send(near[turn], onward(1), turn) for turn in range(groups)]
    *others, own, own_weight = local_call(
        functools.partial(home_kernel, visits, groups),
        "home",
        [band_shape] * (groups - 1) + [part_shape, weight_shape],
        home,
        home_weight,
        far,
        scratch_shapes=held,
    )
    others = [send(others[turn - 1], onward(0), turn) for turn in range(1, groups)]
    near = local_call(early_kernel, "combine_early", [part_shape, weight_shape], *near)
    return local_call(
        combine_kernel,
        "combine",
        (
            jax.ShapeDtypeStruct((BANDS, row_share, PW), jnp.float32),
            jax.ShapeDtypeStruct((row_share, PW), jnp.float32),
        ),
        detect,
        own,
        own_weight,
        *near,
        *others,
    )


def solution(mesh):
    return jax.shard_map(
        local,
        mesh=mesh,
        in_specs=(
            P(("ra", "band"), None, None),
            P(("ra", "band")),
            P(("ra", "band")),
            P(("ra", "band")),
            P(("ra", "band")),
            P(("ra", "band")),
            P(),
            P(),
            P(),
            P(),
        ),
        out_specs=(P(None, "band", "ra"), P("band", "ra")),
        check_vma=False,
    )
```

```python
import functools

import jax
import jax.numpy as jnp
from jax import lax
from jax.experimental import pallas as pl
from jax.experimental.pallas import tpu as pltpu
from jax.sharding import PartitionSpec as P

PW = 256
BANDS = 6
REACH = 2
SPREAD = 2 * REACH + 1
EXTRA = 16
DETECT = 10
BLOCK = 32
COARSE = 3
VECTORS = 16
FINE_ROWS = 64
LEAD = 6


def match_kernel(
    patches,
    patch_hbm,
    offset_hbm,
    index_hbm,
    band_hbm,
    detect_hbm,
    table_hbm,
    weight_hbm,
    rowk_hbm,
    colk_hbm,
    tiles_hbm,
    cross,
    kept,
    patch_ref,
    offset_ref,
    index_ref,
    band_ref,
    detect_ref,
    table_ref,
    weight_ref,
    rowk_ref,
    colk_ref,
    tiles_ref,
    kernels,
    weights,
    shifted,
    toeplitz,
    matches,
    sums,
    extra,
    arrival,
    ready,
):
    visits = band_ref.shape[0]
    tile_count, rows, width = tiles_ref.shape
    per_visit = tile_count // visits
    basis, taps = rowk_ref.shape
    half = taps // 2
    owner = lax.axis_index("ra")
    way = 2 * lax.rem(owner, 2) - 1

    small = [
        pltpu.make_async_copy(source, target, ready.at[place])
        for place, (source, target) in enumerate(
            (
                (index_hbm, index_ref),
                (table_hbm, table_ref),
                (weight_hbm, weight_ref),
                (rowk_hbm, rowk_ref),
                (colk_hbm, colk_ref),
                (patch_hbm, patch_ref),
                (offset_hbm, offset_ref),
                (band_hbm, band_ref),
                (detect_hbm, detect_ref),
            )
        )
    ]
    for copy in small:
        copy.start()

    def fetch(visit):
        held = pl.ds(visit * per_visit, per_visit)
        return pltpu.make_async_copy(tiles_hbm.at[held], tiles_ref.at[held], arrival.at[visit])

    for visit in range(visits):
        fetch(visit).start()

    def iota(shape, axis):
        return lax.broadcasted_iota(jnp.int32, shape, axis)

    def across(left, right, **options):
        return lax.dot_general(
            left,
            right,
            (((1,), (1,)), ((), ())),
            preferred_element_type=jnp.float32,
            **options,
        )

    extra[...] = jnp.zeros_like(extra)
    for place in range(per_visit):
        for side in range(2):
            for fine in range(4):
                top = fine * FINE_ROWS
                shifted[place, side, top : top + 16, :width] = jnp.zeros(
                    (16, width), jnp.bfloat16
                )
                shifted[place, side, top + 48 : top + 64, width:] = jnp.zeros(
                    (16, width), jnp.bfloat16
                )
    eye = (iota((tile_count, tile_count), 0) == iota((tile_count, tile_count), 1)).astype(
        jnp.bfloat16
    )
    for copy in small:
        copy.wait()
    weights[...] = across(eye, jnp.broadcast_to(weight_ref[...], (width, tile_count)))
    entry = iota((1, table_ref.shape[1]), 1)
    chosen = jnp.concatenate(
        [(entry == index_ref[j]).astype(jnp.float32) for j in range(tile_count)], axis=0
    ).astype(jnp.bfloat16)
    rest_of = table_ref[...]
    coeffs = jnp.zeros((tile_count, basis), jnp.float32)
    for _ in range(3):
        piece = rest_of.astype(jnp.bfloat16)
        rest_of = rest_of - piece.astype(jnp.float32)
        coeffs += across(chosen, piece)

    line = iota((2 * VECTORS, taps), 0)
    column = iota((2 * VECTORS, taps), 1)
    block = lax.rem(line, VECTORS) // 2
    step = 4 * lax.rem(block, COARSE) + 2 * lax.rem(line, 2) + line // VECTORS
    wanted = jnp.where(block < COARSE, half + step, half - 1 - step)
    wanted = jnp.where(lax.rem(line, VECTORS) < 4 * COARSE, wanted, -1)
    col_taps = across((wanted == column).astype(jnp.bfloat16), colk_ref[...])
    tap = iota((taps, width), 0)
    lane = iota((taps, width), 1)
    total = None
    for side in range(2):
        place = (lane == tap + LEAD + side * FINE_ROWS).astype(jnp.bfloat16)
        row_taps = jnp.dot(
            rowk_ref[...], place, preferred_element_type=jnp.float32
        ).astype(jnp.bfloat16)
        part = col_taps[side * VECTORS : (side + 1) * VECTORS]
        mix = jnp.concatenate([part * coeffs[j : j + 1] for j in range(tile_count)], axis=0)
        high = mix.astype(jnp.bfloat16)
        low = (mix - high.astype(jnp.float32)).astype(jnp.bfloat16)
        term = jnp.dot(high, row_taps, preferred_element_type=jnp.float32) + jnp.dot(
            low, row_taps, preferred_element_type=jnp.float32
        )
        total = term if total is None else total + term
    kernels[...] = total

    lane = iota((rows, width), 1)
    column = iota((1, width), 1)

    def edge(distance):
        here = iota((16, width), 1) + distance
        return ((here >= 0) & (here < width)).astype(jnp.float32).astype(jnp.bfloat16)

    edges = {distance: edge(distance) for distance in range(-4, 4) if distance != 0}

    def moved_tile(value, distance):
        if distance == 0:
            return value
        turned = pltpu.roll(value, -distance % width, 1).reshape(rows // 16, 16, width)
        return (turned * edges[distance][None]).reshape(rows, width)

    def moved(value, distance):
        if distance == 0:
            return value
        turned = pltpu.roll(value, -distance % width, 1)
        here = lane[: value.shape[0]] + distance
        return jnp.where((here >= 0) & (here < width), turned, jnp.zeros_like(turned))

    def one_visit(visit, unused):
        fetch(visit).wait()
        sums[...] = jnp.zeros_like(sums)
        first = visit * per_visit
        for place in range(per_visit):
            tile = first + place
            pixels = tiles_ref[tile]
            for side in range(2):
                for fine in range(4):
                    part = moved_tile(pixels, -1 - fine if side else fine)
                    top = fine * FINE_ROWS
                    shifted[place, side, top + 16 : top + 64, :width] = part[:48]
                    shifted[place, side, top : top + 48, width:] = part[16:]
        for place in range(per_visit):
            tile = first + place
            for side in range(2):
                for coarse in range(COARSE):
                    for pair in range(2):
                        vector = pl.ds(
                            tile * VECTORS + (side * COARSE + coarse) * 2 + pair, 1
                        )
                        spread = jnp.broadcast_to(kernels[vector, :], (BLOCK, width))
                        turned = pltpu.roll(spread, 0, 1, stride=1, stride_axis=0)
                        toeplitz[
                            place,
                            side,
                            coarse * BLOCK : (coarse + 1) * BLOCK,
                            pair * width : (pair + 1) * width,
                        ] = turned.astype(jnp.bfloat16)
        for place in range(per_visit):
            matched = [jnp.zeros((BLOCK, width), jnp.float32) for _ in range(2)]
            for side in range(2):
                passed = jnp.dot(
                    toeplitz[place, side],
                    shifted[place, side],
                    preferred_element_type=jnp.float32,
                )
                for part in range(2):
                    for coarse in range(COARSE):
                        matched[part] += moved(
                            passed[
                                coarse * BLOCK : (coarse + 1) * BLOCK,
                                part * width : (part + 1) * width,
                            ],
                            -4 * coarse if side else 4 * coarse,
                        )
            matches[place] = jnp.concatenate(matched, axis=0)
        for place in range(per_visit):
            tile = first + place
            matches[place] = pltpu.roll(
                matches[place] * weights[pl.ds(tile, 1), :], lax.rem(offset_ref[tile], width), 1
            )
        for place in range(per_visit):
            tile = first + place
            offset = offset_ref[tile]
            bucket = lax.rem(patch_ref[tile] - owner + REACH + patches, patches)
            weight = weights[pl.ds(tile, 1), :]
            turned = matches[place]
            sums[bucket, :, :width] += jnp.where(lane >= offset, turned, 0.0)
            sums[bucket, :, width:] += jnp.where(lane < offset, turned, 0.0)
            extra[bucket, pl.ds(visit, 1), :] += jnp.concatenate(
                [
                    jnp.where(column >= offset, weight, 0.0),
                    jnp.where(column < offset, weight, 0.0),
                ],
                axis=1,
            )

        held = pl.ds(pl.multiple_of(visit * rows, rows), rows)
        kept[2, held, :] = sums[REACH + 2 * way].astype(jnp.bfloat16)
        cross[0, held, :] = sums[REACH - 2 * way].astype(jnp.bfloat16)
        cross[1, held, :] = sums[REACH - way].astype(jnp.bfloat16)
        kept[0, held, :] = sums[REACH + way].astype(jnp.bfloat16)
        kept[1, held, :] = sums[REACH].astype(jnp.bfloat16)
        return unused

    lax.fori_loop(0, visits, one_visit, 0)

    row = iota((EXTRA, PW), 0)
    lane = iota((1, PW), 1)

    def spread_bands(visit_of, limit):
        line = jnp.full((1, PW), -1.0, jnp.float32)
        for visit in range(visits):
            line = jnp.where(
                (lane < limit) & (visit_of == visit), band_ref[visit].astype(jnp.float32), line
            )
        return line

    by_row = spread_bands(lane // rows, visits * rows)
    by_weight = spread_bands(lax.rem(lane, visits), 2 * visits)
    detect = jnp.zeros((1, PW), jnp.float32)
    for b in range(BANDS):
        detect = jnp.where(lane == b, detect_ref[b], detect)

    def footer(bucket):
        held = extra[bucket]
        high = held.astype(jnp.bfloat16).astype(jnp.float32)
        low = jnp.concatenate([held[-visits:], (held - high)[:-visits]], axis=0)
        mixed = jnp.where((row >= visits) & (row < 2 * visits), low, high)
        mixed = jnp.where(row == 2 * visits, by_row, mixed)
        mixed = jnp.where(row == 2 * visits + 1, by_weight, mixed)
        rest = detect
        for place in range(DETECT, DETECT + 3):
            piece = rest.astype(jnp.bfloat16).astype(jnp.float32)
            rest = rest - piece
            mixed = jnp.where(row == place, piece, mixed)
        return mixed.astype(jnp.bfloat16)

    kept[2, rows * visits :, :] = footer(REACH + 2 * way)
    cross[0, rows * visits :, :] = footer(REACH - 2 * way)
    cross[1, rows * visits :, :] = footer(REACH - way)
    kept[0, rows * visits :, :] = footer(REACH + way)
    kept[1, rows * visits :, :] = footer(REACH)


def add_message(count, groups, message):
    depth = message.shape[0] - EXTRA
    span = depth // count
    row_share = span // groups
    line = lax.broadcasted_iota(jnp.int32, (row_share, depth), 0)
    lane = lax.rem(lax.broadcasted_iota(jnp.int32, (row_share, depth), 1), span)
    band_line = lax.broadcasted_iota(jnp.int32, (8, EXTRA), 0).astype(jnp.float32)
    extra = message[depth:, :]
    bands = extra[2 * count : 2 * count + 2].astype(jnp.float32)
    pick = jnp.concatenate(
        [
            jnp.where(
                (lane == line + part * row_share) & (bands[:1, :depth] == float(b)), 1.0, 0.0
            )
            for part in range(groups)
            for b in range(BANDS)
        ],
        axis=0,
    ).astype(jnp.bfloat16)
    totals = jnp.dot(pick, message[:depth, :], preferred_element_type=jnp.float32)
    pick = (bands[1:, :EXTRA] == band_line).astype(jnp.bfloat16)
    return totals, jnp.dot(pick, extra, preferred_element_type=jnp.float32)


def add_banded(totals, weights, messages):
    depth = totals.shape[0]
    for message in messages:
        totals += message[:depth, :].astype(jnp.float32)
        footer = message[depth:, :].astype(jnp.float32)
        weights += footer[:8] + footer[8:]
    return totals, weights


def write_banded(message, totals, weights):
    depth = totals.shape[0]
    high = weights.astype(jnp.bfloat16).astype(jnp.float32)
    message[:depth, :] = totals.astype(jnp.bfloat16)
    message[depth:, :] = jnp.concatenate([high, weights - high], axis=0).astype(jnp.bfloat16)


def part_of(held, turn, groups):
    depth = held.shape[0] // groups
    part = lax.rem(lax.axis_index("band") + turn, groups)
    return held[pl.ds(pl.multiple_of(part * depth, depth), depth), :]


def keep_kernel(count, groups, kept_ref, totals_ref, weights_ref, detect_ref, far_ref):
    far_ref[...] = kept_ref[2]
    for place in range(2):
        totals_ref[place], weights_ref[place] = add_message(count, groups, kept_ref.at[place])
    extra = kept_ref[0, kept_ref.shape[1] - EXTRA :, :].astype(jnp.float32)
    detect = extra[DETECT : DETECT + 1] + extra[DETECT + 1 : DETECT + 2]
    detect += extra[DETECT + 2 : DETECT + 3]
    line = lax.broadcasted_iota(jnp.int32, (8, PW), 0)
    lane = lax.broadcasted_iota(jnp.int32, (8, PW), 1)
    chosen = jnp.sum(jnp.where(line == lane, detect, 0.0), axis=1, keepdims=True)
    detect_ref[...] = jnp.broadcast_to(chosen, (8, PW))


def near_kernel(count, groups, totals_ref, weights_ref, cross_ref, *refs):
    messages = refs[:groups]
    after_ref, held = refs[groups:]
    totals, weights = add_message(count, groups, cross_ref.at[0])
    held[...] = totals + totals_ref[0]
    weights += weights_ref[0]
    for turn, message in enumerate(messages):
        write_banded(message, part_of(held, turn, groups), weights)
    after_ref[...] = weights


def merge_kernel(
    count,
    groups,
    after_ref,
    totals_ref,
    weights_ref,
    far_in_ref,
    cross_ref,
    home_ref,
    home_weight_ref,
    far_ref,
    rest_ref,
):
    far_ref[...] = far_in_ref[: far_ref.shape[0]]
    rest_ref[...] = far_in_ref[far_ref.shape[0] :]
    totals, weights = add_message(count, groups, cross_ref.at[1])
    home_ref[...] = totals + totals_ref[1]
    home_weight_ref[...] = weights + weights_ref[1]


def home_kernel(count, groups, after_ref, home_ref, home_weight_ref, top_ref, rest_ref, *refs):
    messages = refs[: groups - 1]
    own_ref, own_weight_ref, held, far_ref = refs[groups - 1 :]
    far_ref[: top_ref.shape[0]] = top_ref[...]
    far_ref[top_ref.shape[0] :] = rest_ref[...]
    totals, weights = add_message(count, groups, far_ref)
    held[...] = totals + home_ref[...]
    weights += home_weight_ref[...]
    for turn, message in enumerate(messages, 1):
        write_banded(message, part_of(held, turn, groups), weights)
    own_ref[...] = part_of(held, 0, groups)
    own_weight_ref[...] = weights


def early_kernel(*refs):
    messages = refs[:-2]
    totals_ref, weights_ref = refs[-2:]
    depth = totals_ref.shape[0]
    totals_ref[...], weights_ref[...] = add_banded(
        jnp.zeros((depth, PW), jnp.float32), jnp.zeros((8, PW), jnp.float32), messages
    )


def combine_kernel(
    detect_ref, own_ref, own_weight_ref, near_ref, near_weight_ref, *refs
):
    coadd_ref, detection_ref = refs[-2:]
    row_share = coadd_ref.shape[1]
    totals, weights = add_banded(
        own_ref[...] + near_ref[...], own_weight_ref[...] + near_weight_ref[...], refs[:-2]
    )
    weights = jnp.maximum(weights, 1.0)
    detection = jnp.zeros((row_share, PW), jnp.float32)
    for b in range(BANDS):
        coadd = totals[b * row_share : (b + 1) * row_share] / weights[b : b + 1]
        coadd_ref[b] = coadd
        detection += detect_ref[b : b + 1] * coadd
    detection_ref[...] = detection


def local(
    tiles,
    tile_patch,
    tile_offset,
    tile_weight,
    visit_band,
    coeff_index,
    coeff_table,
    row_kernels,
    column_kernels,
    band_weight,
):
    tile_count, rows, width = tiles.shape
    visits = visit_band.shape[0]
    per_visit = tile_count // visits
    basis, taps = row_kernels.shape
    patches = lax.axis_size("ra")
    groups = lax.axis_size("band")
    row_share = rows // groups
    length = visits * rows + EXTRA
    message_shape = jax.ShapeDtypeStruct((length, PW), jnp.bfloat16)
    pair_shape = jax.ShapeDtypeStruct((2, length, PW), jnp.bfloat16)
    band_shape = jax.ShapeDtypeStruct((BANDS * row_share + EXTRA, PW), jnp.bfloat16)
    part_shape = jax.ShapeDtypeStruct((BANDS * row_share, PW), jnp.float32)
    whole_shape = jax.ShapeDtypeStruct((BANDS * rows, PW), jnp.float32)
    weight_shape = jax.ShapeDtypeStruct((8, PW), jnp.float32)

    vmem = pl.BlockSpec(memory_space=pltpu.VMEM)
    anywhere = pl.BlockSpec(memory_space=pl.ANY)
    cross, kept = pl.pallas_call(
        functools.partial(match_kernel, patches),
        in_specs=[anywhere] * 10,
        out_specs=[vmem] * 2,
        out_shape=[pair_shape, jax.ShapeDtypeStruct((3, length, PW), jnp.bfloat16)],
        scratch_shapes=[
            pltpu.SMEM((tile_count,), jnp.int32),
            pltpu.SMEM((tile_count,), jnp.int32),
            pltpu.SMEM((tile_count,), jnp.int32),
            pltpu.SMEM((visits,), jnp.int32),
            pltpu.SMEM((BANDS,), jnp.float32),
            pltpu.VMEM(coeff_table.shape[::-1], jnp.float32),
            pltpu.VMEM((1, tile_count), jnp.bfloat16),
            pltpu.VMEM((basis, taps), jnp.bfloat16),
            pltpu.VMEM((basis, taps), jnp.bfloat16),
            pltpu.VMEM((tile_count, rows, width), jnp.bfloat16),
            pltpu.VMEM((tile_count * VECTORS, width), jnp.float32),
            pltpu.VMEM((tile_count, width), jnp.float32),
            pltpu.VMEM((per_visit, 2, 4 * FINE_ROWS, 2 * width), jnp.bfloat16),
            pltpu.VMEM((per_visit, 2, COARSE * BLOCK, 2 * width), jnp.bfloat16),
            pltpu.VMEM((per_visit, rows, width), jnp.float32),
            pltpu.VMEM((SPREAD, rows, PW), jnp.float32),
            pltpu.VMEM((SPREAD, EXTRA, PW), jnp.float32),
            pltpu.SemaphoreType.DMA((visits,)),
            pltpu.SemaphoreType.DMA((9,)),
        ],
        compiler_params=pltpu.CompilerParams(vmem_limit_bytes=62 * 1024 * 1024),
        name="match_and_sum",
    )(
        tile_patch,
        tile_offset,
        coeff_index,
        visit_band,
        band_weight,
        coeff_table.T,
        tile_weight.reshape(1, tile_count),
        row_kernels,
        column_kernels,
        tiles,
    )

    def send(message, goal, turn):
        route = [
            (o * groups + g, goal(o) % patches * groups + (g + turn) % groups)
            for o in range(patches)
            for g in range(groups)
        ]
        return lax.ppermute(message, ("ra", "band"), route)

    def onward(distance):
        return lambda o: o + distance if o % 2 else o - distance

    def local_call(kernel, name, out_shape, *operands, **options):
        return pl.pallas_call(
            kernel,
            in_specs=[vmem] * len(operands),
            out_specs=[vmem] * len(out_shape),
            out_shape=out_shape,
            compiler_params=pltpu.CompilerParams(vmem_limit_bytes=40 * 1024 * 1024),
            name=name,
            **options,
        )(*operands)

    held = [pltpu.VMEM(whole_shape.shape, jnp.float32)]
    cross = send(cross, onward(-1), 0)
    *kept, detect, far = local_call(
        functools.partial(keep_kernel, visits, groups),
        "keep",
        [
            jax.ShapeDtypeStruct((2,) + whole_shape.shape, jnp.float32),
            jax.ShapeDtypeStruct((2,) + weight_shape.shape, jnp.float32),
            weight_shape,
            message_shape,
        ],
        kept,
    )
    *near, after = local_call(
        functools.partial(near_kernel, visits, groups),
        "near",
        [band_shape] * groups + [weight_shape],
        *kept,
        cross,
        scratch_shapes=held,
    )
    home, home_weight, *far = local_call(
        functools.partial(merge_kernel, visits, groups),
        "merge",
        [
            whole_shape,
            weight_shape,
            jax.ShapeDtypeStruct((length // 32 * 16 + EXTRA, PW), jnp.bfloat16),
            jax.ShapeDtypeStruct((length - length // 32 * 16 - EXTRA, PW), jnp.bfloat16),
        ],
        after,
        *kept,
        far,
        cross,
    )
    far = [send(piece, onward(2), 0) for piece in far]
    near = [send(near[turn], onward(1), turn) for turn in range(groups)]
    last = near[1:]
    near = local_call(early_kernel, "combine_early", [part_shape, weight_shape], near[0])
    *others, own, own_weight = local_call(
        functools.partial(home_kernel, visits, groups),
        "home",
        [band_shape] * (groups - 1) + [part_shape, weight_shape],
        near[1],
        home,
        home_weight,
        *far,
        scratch_shapes=held + [pltpu.VMEM(message_shape.shape, jnp.bfloat16)],
    )
    others = [send(others[turn - 1], onward(0), turn) for turn in range(1, groups)]
    return local_call(
        combine_kernel,
        "combine",
        (
            jax.ShapeDtypeStruct((BANDS, row_share, PW), jnp.float32),
            jax.ShapeDtypeStruct((row_share, PW), jnp.float32),
        ),
        detect,
        own,
        own_weight,
        *near,
        *others,
        *last,
    )


def solution(mesh):
    return jax.shard_map(
        local,
        mesh=mesh,
        in_specs=(
            P(("ra", "band"), None, None),
            P(("ra", "band")),
            P(("ra", "band")),
            P(("ra", "band")),
            P(("ra", "band")),
            P(("ra", "band")),
            P(),
            P(),
            P(),
            P(),
        ),
        out_specs=(P(None, "band", "ra"), P("band", "ra")),
        check_vma=False,
    )
```

```python
import functools

import jax
import jax.numpy as jnp
from jax import lax
from jax.experimental import pallas as pl
from jax.experimental.pallas import tpu as pltpu
from jax.sharding import PartitionSpec as P

PW = 256
BANDS = 6
REACH = 2
SPREAD = 2 * REACH + 1
EXTRA = 16
DETECT = 10
BLOCK = 32
COARSE = 3
VECTORS = 16
FINE_ROWS = 64
LEAD = 6


def match_kernel(
    patches,
    patch_hbm,
    offset_hbm,
    index_hbm,
    band_hbm,
    detect_hbm,
    table_hbm,
    weight_hbm,
    rowk_hbm,
    colk_hbm,
    tiles_hbm,
    far,
    cross,
    kept,
    patch_ref,
    offset_ref,
    index_ref,
    band_ref,
    detect_ref,
    table_ref,
    weight_ref,
    rowk_ref,
    colk_ref,
    tiles_ref,
    kernels,
    weights,
    shifted,
    toeplitz,
    matches,
    sums,
    extra,
    arrival,
    ready,
):
    visits = band_ref.shape[0]
    tile_count, rows, width = tiles_ref.shape
    per_visit = tile_count // visits
    basis, taps = rowk_ref.shape
    half = taps // 2
    owner = lax.axis_index("ra")
    way = 2 * lax.rem(owner, 2) - 1

    small = [
        pltpu.make_async_copy(source, target, ready.at[place])
        for place, (source, target) in enumerate(
            (
                (index_hbm, index_ref),
                (table_hbm, table_ref),
                (weight_hbm, weight_ref),
                (rowk_hbm, rowk_ref),
                (colk_hbm, colk_ref),
                (patch_hbm, patch_ref),
                (offset_hbm, offset_ref),
                (band_hbm, band_ref),
                (detect_hbm, detect_ref),
            )
        )
    ]
    for copy in small:
        copy.start()

    def fetch(visit):
        held = pl.ds(visit * per_visit, per_visit)
        return pltpu.make_async_copy(tiles_hbm.at[held], tiles_ref.at[held], arrival.at[visit])

    for visit in range(visits):
        fetch(visit).start()

    def iota(shape, axis):
        return lax.broadcasted_iota(jnp.int32, shape, axis)

    def across(left, right, **options):
        return lax.dot_general(
            left,
            right,
            (((1,), (1,)), ((), ())),
            preferred_element_type=jnp.float32,
            **options,
        )

    extra[...] = jnp.zeros_like(extra)
    for place in range(per_visit):
        for side in range(2):
            for fine in range(4):
                top = fine * FINE_ROWS
                shifted[place, side, top : top + 16, :width] = jnp.zeros(
                    (16, width), jnp.bfloat16
                )
                shifted[place, side, top + 48 : top + 64, width:] = jnp.zeros(
                    (16, width), jnp.bfloat16
                )
    eye = (iota((tile_count, tile_count), 0) == iota((tile_count, tile_count), 1)).astype(
        jnp.bfloat16
    )
    for copy in small:
        copy.wait()
    weights[...] = across(eye, jnp.broadcast_to(weight_ref[...], (width, tile_count)))
    entry = iota((1, table_ref.shape[1]), 1)
    chosen = jnp.concatenate(
        [(entry == index_ref[j]).astype(jnp.float32) for j in range(tile_count)], axis=0
    ).astype(jnp.bfloat16)
    rest_of = table_ref[...]
    coeffs = jnp.zeros((tile_count, basis), jnp.float32)
    for _ in range(3):
        piece = rest_of.astype(jnp.bfloat16)
        rest_of = rest_of - piece.astype(jnp.float32)
        coeffs += across(chosen, piece)

    line = iota((2 * VECTORS, taps), 0)
    column = iota((2 * VECTORS, taps), 1)
    block = lax.rem(line, VECTORS) // 2
    step = 4 * lax.rem(block, COARSE) + 2 * lax.rem(line, 2) + line // VECTORS
    wanted = jnp.where(block < COARSE, half + step, half - 1 - step)
    wanted = jnp.where(lax.rem(line, VECTORS) < 4 * COARSE, wanted, -1)
    col_taps = across((wanted == column).astype(jnp.bfloat16), colk_ref[...])
    tap = iota((taps, width), 0)
    lane = iota((taps, width), 1)
    total = None
    for side in range(2):
        place = (lane == tap + LEAD + side * FINE_ROWS).astype(jnp.bfloat16)
        row_taps = jnp.dot(
            rowk_ref[...], place, preferred_element_type=jnp.float32
        ).astype(jnp.bfloat16)
        part = col_taps[side * VECTORS : (side + 1) * VECTORS]
        mix = jnp.concatenate([part * coeffs[j : j + 1] for j in range(tile_count)], axis=0)
        high = mix.astype(jnp.bfloat16)
        low = (mix - high.astype(jnp.float32)).astype(jnp.bfloat16)
        term = jnp.dot(high, row_taps, preferred_element_type=jnp.float32) + jnp.dot(
            low, row_taps, preferred_element_type=jnp.float32
        )
        total = term if total is None else total + term
    kernels[...] = total

    lane = iota((rows, width), 1)
    column = iota((1, width), 1)

    def edge(distance):
        here = iota((16, width), 1) + distance
        return ((here >= 0) & (here < width)).astype(jnp.float32).astype(jnp.bfloat16)

    edges = {distance: edge(distance) for distance in range(-4, 4) if distance != 0}

    def moved_tile(value, distance):
        if distance == 0:
            return value
        turned = pltpu.roll(value, -distance % width, 1).reshape(rows // 16, 16, width)
        return (turned * edges[distance][None]).reshape(rows, width)

    def moved(value, distance):
        if distance == 0:
            return value
        turned = pltpu.roll(value, -distance % width, 1)
        here = lane[: value.shape[0]] + distance
        return jnp.where((here >= 0) & (here < width), turned, jnp.zeros_like(turned))

    def one_visit(visit, unused):
        fetch(visit).wait()
        sums[...] = jnp.zeros_like(sums)
        first = visit * per_visit
        for place in range(per_visit):
            tile = first + place
            pixels = tiles_ref[tile]
            for side in range(2):
                for fine in range(4):
                    part = moved_tile(pixels, -1 - fine if side else fine)
                    top = fine * FINE_ROWS
                    shifted[place, side, top + 16 : top + 64, :width] = part[:48]
                    shifted[place, side, top : top + 48, width:] = part[16:]
        for place in range(per_visit):
            tile = first + place
            for side in range(2):
                for coarse in range(COARSE):
                    for pair in range(2):
                        vector = pl.ds(
                            tile * VECTORS + (side * COARSE + coarse) * 2 + pair, 1
                        )
                        spread = jnp.broadcast_to(kernels[vector, :], (BLOCK, width))
                        turned = pltpu.roll(spread, 0, 1, stride=1, stride_axis=0)
                        toeplitz[
                            place,
                            side,
                            coarse * BLOCK : (coarse + 1) * BLOCK,
                            pair * width : (pair + 1) * width,
                        ] = turned.astype(jnp.bfloat16)
        for place in range(per_visit):
            matched = [jnp.zeros((BLOCK, width), jnp.float32) for _ in range(2)]
            for side in range(2):
                passed = jnp.dot(
                    toeplitz[place, side],
                    shifted[place, side],
                    preferred_element_type=jnp.float32,
                )
                for part in range(2):
                    for coarse in range(COARSE):
                        matched[part] += moved(
                            passed[
                                coarse * BLOCK : (coarse + 1) * BLOCK,
                                part * width : (part + 1) * width,
                            ],
                            -4 * coarse if side else 4 * coarse,
                        )
            matches[place] = jnp.concatenate(matched, axis=0)
        for place in range(per_visit):
            tile = first + place
            matches[place] = pltpu.roll(
                matches[place] * weights[pl.ds(tile, 1), :], lax.rem(offset_ref[tile], width), 1
            )
        for place in range(per_visit):
            tile = first + place
            offset = offset_ref[tile]
            bucket = lax.rem(patch_ref[tile] - owner + REACH + patches, patches)
            weight = weights[pl.ds(tile, 1), :]
            turned = matches[place]
            sums[bucket, :, :width] += jnp.where(lane >= offset, turned, 0.0)
            sums[bucket, :, width:] += jnp.where(lane < offset, turned, 0.0)
            extra[bucket, pl.ds(visit, 1), :] += jnp.concatenate(
                [
                    jnp.where(column >= offset, weight, 0.0),
                    jnp.where(column < offset, weight, 0.0),
                ],
                axis=1,
            )

        held = pl.ds(pl.multiple_of(visit * rows, rows), rows)
        far[held, :] = sums[REACH + 2 * way].astype(jnp.bfloat16)
        cross[0, held, :] = sums[REACH - 2 * way].astype(jnp.bfloat16)
        cross[1, held, :] = sums[REACH - way].astype(jnp.bfloat16)
        kept[0, held, :] = sums[REACH + way].astype(jnp.bfloat16)
        kept[1, held, :] = sums[REACH].astype(jnp.bfloat16)
        return unused

    lax.fori_loop(0, visits, one_visit, 0)

    row = iota((EXTRA, PW), 0)
    lane = iota((1, PW), 1)

    def spread_bands(visit_of, limit):
        line = jnp.full((1, PW), -1.0, jnp.float32)
        for visit in range(visits):
            line = jnp.where(
                (lane < limit) & (visit_of == visit), band_ref[visit].astype(jnp.float32), line
            )
        return line

    by_row = spread_bands(lane // rows, visits * rows)
    by_weight = spread_bands(lax.rem(lane, visits), 2 * visits)
    detect = jnp.zeros((1, PW), jnp.float32)
    for b in range(BANDS):
        detect = jnp.where(lane == b, detect_ref[b], detect)

    def footer(bucket):
        held = extra[bucket]
        high = held.astype(jnp.bfloat16).astype(jnp.float32)
        low = jnp.concatenate([held[-visits:], (held - high)[:-visits]], axis=0)
        mixed = jnp.where((row >= visits) & (row < 2 * visits), low, high)
        mixed = jnp.where(row == 2 * visits, by_row, mixed)
        mixed = jnp.where(row == 2 * visits + 1, by_weight, mixed)
        rest = detect
        for place in range(DETECT, DETECT + 3):
            piece = rest.astype(jnp.bfloat16).astype(jnp.float32)
            rest = rest - piece
            mixed = jnp.where(row == place, piece, mixed)
        return mixed.astype(jnp.bfloat16)

    far[rows * visits :, :] = footer(REACH + 2 * way)
    cross[0, rows * visits :, :] = footer(REACH - 2 * way)
    cross[1, rows * visits :, :] = footer(REACH - way)
    kept[0, rows * visits :, :] = footer(REACH + way)
    kept[1, rows * visits :, :] = footer(REACH)


def add_message(count, groups, message):
    depth = message.shape[0] - EXTRA
    span = depth // count
    row_share = span // groups
    line = lax.broadcasted_iota(jnp.int32, (row_share, depth), 0)
    lane = lax.rem(lax.broadcasted_iota(jnp.int32, (row_share, depth), 1), span)
    band_line = lax.broadcasted_iota(jnp.int32, (8, EXTRA), 0).astype(jnp.float32)
    extra = message[depth:, :]
    bands = extra[2 * count : 2 * count + 2].astype(jnp.float32)
    pick = jnp.concatenate(
        [
            jnp.where(
                (lane == line + part * row_share) & (bands[:1, :depth] == float(b)), 1.0, 0.0
            )
            for part in range(groups)
            for b in range(BANDS)
        ],
        axis=0,
    ).astype(jnp.bfloat16)
    totals = jnp.dot(pick, message[:depth, :], preferred_element_type=jnp.float32)
    pick = (bands[1:, :EXTRA] == band_line).astype(jnp.bfloat16)
    return totals, jnp.dot(pick, extra, preferred_element_type=jnp.float32)


def add_banded(totals, weights, messages):
    depth = totals.shape[0]
    for message in messages:
        totals += message[:depth, :].astype(jnp.float32)
        footer = message[depth:, :].astype(jnp.float32)
        weights += footer[:8] + footer[8:]
    return totals, weights


def write_banded(message, totals, weights):
    depth = totals.shape[0]
    high = weights.astype(jnp.bfloat16).astype(jnp.float32)
    message[:depth, :] = totals.astype(jnp.bfloat16)
    message[depth:, :] = jnp.concatenate([high, weights - high], axis=0).astype(jnp.bfloat16)


def part_of(held, turn, groups):
    depth = held.shape[0] // groups
    part = lax.rem(lax.axis_index("band") + turn, groups)
    return held[pl.ds(pl.multiple_of(part * depth, depth), depth), :]


def keep_kernel(count, groups, kept_ref, totals_ref, weights_ref, detect_ref):
    for place in range(2):
        totals_ref[place], weights_ref[place] = add_message(count, groups, kept_ref.at[place])
    extra = kept_ref[0, kept_ref.shape[1] - EXTRA :, :].astype(jnp.float32)
    detect = extra[DETECT : DETECT + 1] + extra[DETECT + 1 : DETECT + 2]
    detect += extra[DETECT + 2 : DETECT + 3]
    line = lax.broadcasted_iota(jnp.int32, (8, PW), 0)
    lane = lax.broadcasted_iota(jnp.int32, (8, PW), 1)
    chosen = jnp.sum(jnp.where(line == lane, detect, 0.0), axis=1, keepdims=True)
    detect_ref[...] = jnp.broadcast_to(chosen, (8, PW))


def merge_kernel(count, groups, totals_ref, weights_ref, cross_ref, *refs):
    messages = refs[:groups]
    home_ref, home_weight_ref, held = refs[groups:]
    totals, weights = add_message(count, groups, cross_ref.at[0])
    held[...] = totals + totals_ref[0]
    weights += weights_ref[0]
    for turn, message in enumerate(messages):
        write_banded(message, part_of(held, turn, groups), weights)
    totals, weights = add_message(count, groups, cross_ref.at[1])
    home_ref[...] = totals + totals_ref[1]
    home_weight_ref[...] = weights + weights_ref[1]


def home_kernel(count, groups, home_ref, home_weight_ref, far_ref, *refs):
    messages = refs[: groups - 1]
    own_ref, own_weight_ref, held = refs[groups - 1 :]
    totals, weights = add_message(count, groups, far_ref)
    held[...] = totals + home_ref[...]
    weights += home_weight_ref[...]
    for turn, message in enumerate(messages, 1):
        write_banded(message, part_of(held, turn, groups), weights)
    own_ref[...] = part_of(held, 0, groups)
    own_weight_ref[...] = weights


def early_kernel(*refs):
    messages = refs[:-2]
    totals_ref, weights_ref = refs[-2:]
    depth = totals_ref.shape[0]
    totals_ref[...], weights_ref[...] = add_banded(
        jnp.zeros((depth, PW), jnp.float32), jnp.zeros((8, PW), jnp.float32), messages
    )


def combine_kernel(
    detect_ref, own_ref, own_weight_ref, near_ref, near_weight_ref, *refs
):
    coadd_ref, detection_ref = refs[-2:]
    row_share = coadd_ref.shape[1]
    totals, weights = add_banded(
        own_ref[...] + near_ref[...], own_weight_ref[...] + near_weight_ref[...], refs[:-2]
    )
    weights = jnp.maximum(weights, 1.0)
    detection = jnp.zeros((row_share, PW), jnp.float32)
    for b in range(BANDS):
        coadd = totals[b * row_share : (b + 1) * row_share] / weights[b : b + 1]
        coadd_ref[b] = coadd
        detection += detect_ref[b : b + 1] * coadd
    detection_ref[...] = detection


def local(
    tiles,
    tile_patch,
    tile_offset,
    tile_weight,
    visit_band,
    coeff_index,
    coeff_table,
    row_kernels,
    column_kernels,
    band_weight,
):
    tile_count, rows, width = tiles.shape
    visits = visit_band.shape[0]
    per_visit = tile_count // visits
    basis, taps = row_kernels.shape
    patches = lax.axis_size("ra")
    groups = lax.axis_size("band")
    row_share = rows // groups
    length = visits * rows + EXTRA
    message_shape = jax.ShapeDtypeStruct((length, PW), jnp.bfloat16)
    pair_shape = jax.ShapeDtypeStruct((2, length, PW), jnp.bfloat16)
    band_shape = jax.ShapeDtypeStruct((BANDS * row_share + EXTRA, PW), jnp.bfloat16)
    part_shape = jax.ShapeDtypeStruct((BANDS * row_share, PW), jnp.float32)
    whole_shape = jax.ShapeDtypeStruct((BANDS * rows, PW), jnp.float32)
    weight_shape = jax.ShapeDtypeStruct((8, PW), jnp.float32)

    vmem = pl.BlockSpec(memory_space=pltpu.VMEM)
    anywhere = pl.BlockSpec(memory_space=pl.ANY)
    far, cross, kept = pl.pallas_call(
        functools.partial(match_kernel, patches),
        in_specs=[anywhere] * 10,
        out_specs=[vmem] * 3,
        out_shape=[message_shape, pair_shape, pair_shape],
        scratch_shapes=[
            pltpu.SMEM((tile_count,), jnp.int32),
            pltpu.SMEM((tile_count,), jnp.int32),
            pltpu.SMEM((tile_count,), jnp.int32),
            pltpu.SMEM((visits,), jnp.int32),
            pltpu.SMEM((BANDS,), jnp.float32),
            pltpu.VMEM(coeff_table.shape[::-1], jnp.float32),
            pltpu.VMEM((1, tile_count), jnp.bfloat16),
            pltpu.VMEM((basis, taps), jnp.bfloat16),
            pltpu.VMEM((basis, taps), jnp.bfloat16),
            pltpu.VMEM((tile_count, rows, width), jnp.bfloat16),
            pltpu.VMEM((tile_count * VECTORS, width), jnp.float32),
            pltpu.VMEM((tile_count, width), jnp.float32),
            pltpu.VMEM((per_visit, 2, 4 * FINE_ROWS, 2 * width), jnp.bfloat16),
            pltpu.VMEM((per_visit, 2, COARSE * BLOCK, 2 * width), jnp.bfloat16),
            pltpu.VMEM((per_visit, rows, width), jnp.float32),
            pltpu.VMEM((SPREAD, rows, PW), jnp.float32),
            pltpu.VMEM((SPREAD, EXTRA, PW), jnp.float32),
            pltpu.SemaphoreType.DMA((visits,)),
            pltpu.SemaphoreType.DMA((9,)),
        ],
        compiler_params=pltpu.CompilerParams(vmem_limit_bytes=62 * 1024 * 1024),
        name="match_and_sum",
    )(
        tile_patch,
        tile_offset,
        coeff_index,
        visit_band,
        band_weight,
        coeff_table.T,
        tile_weight.reshape(1, tile_count),
        row_kernels,
        column_kernels,
        tiles,
    )

    def send(message, goal, turn):
        route = [
            (o * groups + g, goal(o) % patches * groups + (g + turn) % groups)
            for o in range(patches)
            for g in range(groups)
        ]
        return lax.ppermute(message, ("ra", "band"), route)

    def onward(distance):
        return lambda o: o + distance if o % 2 else o - distance

    def local_call(kernel, name, out_shape, *operands, **options):
        return pl.pallas_call(
            kernel,
            in_specs=[vmem] * len(operands),
            out_specs=[vmem] * len(out_shape),
            out_shape=out_shape,
            compiler_params=pltpu.CompilerParams(vmem_limit_bytes=40 * 1024 * 1024),
            name=name,
            **options,
        )(*operands)

    held = [pltpu.VMEM(whole_shape.shape, jnp.float32)]
    cross = send(cross, onward(-1), 0)
    far = send(far, onward(2), 0)
    *kept, detect = local_call(
        functools.partial(keep_kernel, visits, groups),
        "keep",
        [
            jax.ShapeDtypeStruct((2,) + whole_shape.shape, jnp.float32),
            jax.ShapeDtypeStruct((2,) + weight_shape.shape, jnp.float32),
            weight_shape,
        ],
        kept,
    )
    *near, home, home_weight = local_call(
        functools.partial(merge_kernel, visits, groups),
        "merge",
        [band_shape] * groups + [whole_shape, weight_shape],
        *kept,
        cross,
        scratch_shapes=held,
    )
    near = [send(near[turn], onward(1), turn) for turn in reversed(range(groups))]
    *others, own, own_weight = local_call(
        functools.partial(home_kernel, visits, groups),
        "home",
        [band_shape] * (groups - 1) + [part_shape, weight_shape],
        home,
        home_weight,
        far,
        scratch_shapes=held,
    )
    others = [send(others[turn - 1], onward(0), turn) for turn in range(1, groups)]
    near = local_call(early_kernel, "combine_early", [part_shape, weight_shape], *near)
    return local_call(
        combine_kernel,
        "combine",
        (
            jax.ShapeDtypeStruct((BANDS, row_share, PW), jnp.float32),
            jax.ShapeDtypeStruct((row_share, PW), jnp.float32),
        ),
        detect,
        own,
        own_weight,
        *near,
        *others,
    )


def solution(mesh):
    return jax.shard_map(
        local,
        mesh=mesh,
        in_specs=(
            P(("ra", "band"), None, None),
            P(("ra", "band")),
            P(("ra", "band")),
            P(("ra", "band")),
            P(("ra", "band")),
            P(("ra", "band")),
            P(),
            P(),
            P(),
            P(),
        ),
        out_specs=(P(None, "band", "ra"), P("band", "ra")),
        check_vma=False,
    )
```

```python
import functools

import jax
import jax.numpy as jnp
from jax import lax
from jax.experimental import pallas as pl
from jax.experimental.pallas import tpu as pltpu
from jax.sharding import PartitionSpec as P

PW = 256
BANDS = 6
REACH = 2
SPREAD = 2 * REACH + 1
EXTRA = 16
DETECT = 10
BLOCK = 32
COARSE = 3
VECTORS = 16
FINE_ROWS = 64
LEAD = 6


def match_kernel(
    patches,
    patch_hbm,
    offset_hbm,
    index_hbm,
    band_hbm,
    detect_hbm,
    table_hbm,
    weight_hbm,
    rowk_hbm,
    colk_hbm,
    tiles_hbm,
    far,
    cross,
    kept,
    patch_ref,
    offset_ref,
    index_ref,
    band_ref,
    detect_ref,
    table_ref,
    weight_ref,
    rowk_ref,
    colk_ref,
    tiles_ref,
    kernels,
    weights,
    shifted,
    toeplitz,
    matches,
    sums,
    extra,
    arrival,
    ready,
):
    visits = band_ref.shape[0]
    tile_count, rows, width = tiles_ref.shape
    per_visit = tile_count // visits
    basis, taps = rowk_ref.shape
    half = taps // 2
    owner = lax.axis_index("ra")
    way = 2 * lax.rem(owner, 2) - 1

    small = [
        pltpu.make_async_copy(source, target, ready.at[place])
        for place, (source, target) in enumerate(
            (
                (index_hbm, index_ref),
                (table_hbm, table_ref),
                (weight_hbm, weight_ref),
                (rowk_hbm, rowk_ref),
                (colk_hbm, colk_ref),
                (patch_hbm, patch_ref),
                (offset_hbm, offset_ref),
                (band_hbm, band_ref),
                (detect_hbm, detect_ref),
            )
        )
    ]
    for copy in small:
        copy.start()

    def fetch(visit):
        held = pl.ds(visit * per_visit, per_visit)
        return pltpu.make_async_copy(tiles_hbm.at[held], tiles_ref.at[held], arrival.at[visit])

    for visit in range(visits):
        fetch(visit).start()

    def iota(shape, axis):
        return lax.broadcasted_iota(jnp.int32, shape, axis)

    def across(left, right, **options):
        return lax.dot_general(
            left,
            right,
            (((1,), (1,)), ((), ())),
            preferred_element_type=jnp.float32,
            **options,
        )

    extra[...] = jnp.zeros_like(extra)
    for place in range(per_visit):
        for side in range(2):
            for fine in range(4):
                top = fine * FINE_ROWS
                shifted[place, side, top : top + 16, :width] = jnp.zeros(
                    (16, width), jnp.bfloat16
                )
                shifted[place, side, top + 48 : top + 64, width:] = jnp.zeros(
                    (16, width), jnp.bfloat16
                )
    eye = (iota((tile_count, tile_count), 0) == iota((tile_count, tile_count), 1)).astype(
        jnp.bfloat16
    )
    for copy in small:
        copy.wait()
    weights[...] = across(eye, jnp.broadcast_to(weight_ref[...], (width, tile_count)))
    entry = iota((1, table_ref.shape[1]), 1)
    chosen = jnp.concatenate(
        [(entry == index_ref[j]).astype(jnp.float32) for j in range(tile_count)], axis=0
    ).astype(jnp.bfloat16)
    rest_of = table_ref[...]
    coeffs = jnp.zeros((tile_count, basis), jnp.float32)
    for _ in range(3):
        piece = rest_of.astype(jnp.bfloat16)
        rest_of = rest_of - piece.astype(jnp.float32)
        coeffs += across(chosen, piece)

    line = iota((2 * VECTORS, taps), 0)
    column = iota((2 * VECTORS, taps), 1)
    block = lax.rem(line, VECTORS) // 2
    step = 4 * lax.rem(block, COARSE) + 2 * lax.rem(line, 2) + line // VECTORS
    wanted = jnp.where(block < COARSE, half + step, half - 1 - step)
    wanted = jnp.where(lax.rem(line, VECTORS) < 4 * COARSE, wanted, -1)
    col_taps = across((wanted == column).astype(jnp.bfloat16), colk_ref[...])
    tap = iota((taps, width), 0)
    lane = iota((taps, width), 1)
    total = None
    for side in range(2):
        place = (lane == tap + LEAD + side * FINE_ROWS).astype(jnp.bfloat16)
        row_taps = jnp.dot(
            rowk_ref[...], place, preferred_element_type=jnp.float32
        ).astype(jnp.bfloat16)
        part = col_taps[side * VECTORS : (side + 1) * VECTORS]
        mix = jnp.concatenate([part * coeffs[j : j + 1] for j in range(tile_count)], axis=0)
        high = mix.astype(jnp.bfloat16)
        term = jnp.dot(high, row_taps, preferred_element_type=jnp.float32)
        total = term if total is None else total + term
    kernels[...] = total

    lane = iota((rows, width), 1)
    column = iota((1, width), 1)

    def edge(distance):
        here = iota((16, width), 1) + distance
        return ((here >= 0) & (here < width)).astype(jnp.float32).astype(jnp.bfloat16)

    edges = {distance: edge(distance) for distance in range(-4, 4) if distance != 0}

    def moved_tile(value, distance):
        if distance == 0:
            return value
        turned = pltpu.roll(value, -distance % width, 1).reshape(rows // 16, 16, width)
        return (turned * edges[distance][None]).reshape(rows, width)

    def moved(value, distance):
        if distance == 0:
            return value
        turned = pltpu.roll(value, -distance % width, 1)
        here = lane[: value.shape[0]] + distance
        return jnp.where((here >= 0) & (here < width), turned, jnp.zeros_like(turned))

    def one_visit(visit, unused):
        fetch(visit).wait()
        sums[...] = jnp.zeros_like(sums)
        first = visit * per_visit
        for place in range(per_visit):
            tile = first + place
            pixels = tiles_ref[tile]
            for side in range(2):
                for fine in range(4):
                    part = moved_tile(pixels, -1 - fine if side else fine)
                    top = fine * FINE_ROWS
                    shifted[place, side, top + 16 : top + 64, :width] = part[:48]
                    shifted[place, side, top : top + 48, width:] = part[16:]
        for place in range(per_visit):
            tile = first + place
            for side in range(2):
                for coarse in range(COARSE):
                    for pair in range(2):
                        vector = pl.ds(
                            tile * VECTORS + (side * COARSE + coarse) * 2 + pair, 1
                        )
                        spread = jnp.broadcast_to(kernels[vector, :], (BLOCK, width))
                        turned = pltpu.roll(spread, 0, 1, stride=1, stride_axis=0)
                        toeplitz[
                            place,
                            side,
                            coarse * BLOCK : (coarse + 1) * BLOCK,
                            pair * width : (pair + 1) * width,
                        ] = turned.astype(jnp.bfloat16)
        for place in range(per_visit):
            matched = [jnp.zeros((BLOCK, width), jnp.float32) for _ in range(2)]
            for side in range(2):
                passed = jnp.dot(
                    toeplitz[place, side],
                    shifted[place, side],
                    preferred_element_type=jnp.float32,
                )
                for part in range(2):
                    for coarse in range(COARSE):
                        matched[part] += moved(
                            passed[
                                coarse * BLOCK : (coarse + 1) * BLOCK,
                                part * width : (part + 1) * width,
                            ],
                            -4 * coarse if side else 4 * coarse,
                        )
            matches[place] = jnp.concatenate(matched, axis=0)
        for place in range(per_visit):
            tile = first + place
            matches[place] = pltpu.roll(
                matches[place] * weights[pl.ds(tile, 1), :], lax.rem(offset_ref[tile], width), 1
            )
        for place in range(per_visit):
            tile = first + place
            offset = offset_ref[tile]
            bucket = lax.rem(patch_ref[tile] - owner + REACH + patches, patches)
            weight = weights[pl.ds(tile, 1), :]
            turned = matches[place]
            sums[bucket, :, :width] += jnp.where(lane >= offset, turned, 0.0)
            sums[bucket, :, width:] += jnp.where(lane < offset, turned, 0.0)
            extra[bucket, pl.ds(visit, 1), :] += jnp.concatenate(
                [
                    jnp.where(column >= offset, weight, 0.0),
                    jnp.where(column < offset, weight, 0.0),
                ],
                axis=1,
            )

        held = pl.ds(pl.multiple_of(visit * rows, rows), rows)
        far[held, :] = sums[REACH + 2 * way].astype(jnp.bfloat16)
        cross[0, held, :] = sums[REACH - 2 * way].astype(jnp.bfloat16)
        cross[1, held, :] = sums[REACH - way].astype(jnp.bfloat16)
        kept[0, held, :] = sums[REACH + way].astype(jnp.bfloat16)
        kept[1, held, :] = sums[REACH].astype(jnp.bfloat16)
        return unused

    lax.fori_loop(0, visits, one_visit, 0)

    row = iota((EXTRA, PW), 0)
    lane = iota((1, PW), 1)

    def spread_bands(visit_of, limit):
        line = jnp.full((1, PW), -1.0, jnp.float32)
        for visit in range(visits):
            line = jnp.where(
                (lane < limit) & (visit_of == visit), band_ref[visit].astype(jnp.float32), line
            )
        return line

    by_row = spread_bands(lane // rows, visits * rows)
    by_weight = spread_bands(lax.rem(lane, visits), 2 * visits)
    detect = jnp.zeros((1, PW), jnp.float32)
    for b in range(BANDS):
        detect = jnp.where(lane == b, detect_ref[b], detect)

    def footer(bucket):
        held = extra[bucket]
        high = held.astype(jnp.bfloat16).astype(jnp.float32)
        low = jnp.concatenate([held[-visits:], (held - high)[:-visits]], axis=0)
        mixed = jnp.where((row >= visits) & (row < 2 * visits), low, high)
        mixed = jnp.where(row == 2 * visits, by_row, mixed)
        mixed = jnp.where(row == 2 * visits + 1, by_weight, mixed)
        rest = detect
        for place in range(DETECT, DETECT + 3):
            piece = rest.astype(jnp.bfloat16).astype(jnp.float32)
            rest = rest - piece
            mixed = jnp.where(row == place, piece, mixed)
        return mixed.astype(jnp.bfloat16)

    far[rows * visits :, :] = footer(REACH + 2 * way)
    cross[0, rows * visits :, :] = footer(REACH - 2 * way)
    cross[1, rows * visits :, :] = footer(REACH - way)
    kept[0, rows * visits :, :] = footer(REACH + way)
    kept[1, rows * visits :, :] = footer(REACH)


def add_message(count, groups, message):
    depth = message.shape[0] - EXTRA
    span = depth // count
    row_share = span // groups
    line = lax.broadcasted_iota(jnp.int32, (row_share, depth), 0)
    lane = lax.rem(lax.broadcasted_iota(jnp.int32, (row_share, depth), 1), span)
    band_line = lax.broadcasted_iota(jnp.int32, (8, EXTRA), 0).astype(jnp.float32)
    extra = message[depth:, :]
    bands = extra[2 * count : 2 * count + 2].astype(jnp.float32)
    pick = jnp.concatenate(
        [
            jnp.where(
                (lane == line + part * row_share) & (bands[:1, :depth] == float(b)), 1.0, 0.0
            )
            for part in range(groups)
            for b in range(BANDS)
        ],
        axis=0,
    ).astype(jnp.bfloat16)
    totals = jnp.dot(pick, message[:depth, :], preferred_element_type=jnp.float32)
    pick = (bands[1:, :EXTRA] == band_line).astype(jnp.bfloat16)
    return totals, jnp.dot(pick, extra, preferred_element_type=jnp.float32)


def add_banded(totals, weights, messages):
    depth = totals.shape[0]
    for message in messages:
        totals += message[:depth, :].astype(jnp.float32)
        footer = message[depth:, :].astype(jnp.float32)
        weights += footer[:8] + footer[8:]
    return totals, weights


def write_banded(message, totals, weights):
    depth = totals.shape[0]
    high = weights.astype(jnp.bfloat16).astype(jnp.float32)
    message[:depth, :] = totals.astype(jnp.bfloat16)
    message[depth:, :] = jnp.concatenate([high, weights - high], axis=0).astype(jnp.bfloat16)


def part_of(held, turn, groups):
    depth = held.shape[0] // groups
    part = lax.rem(lax.axis_index("band") + turn, groups)
    return held[pl.ds(pl.multiple_of(part * depth, depth), depth), :]


def keep_kernel(count, groups, kept_ref, totals_ref, weights_ref, detect_ref):
    for place in range(2):
        totals_ref[place], weights_ref[place] = add_message(count, groups, kept_ref.at[place])
    extra = kept_ref[0, kept_ref.shape[1] - EXTRA :, :].astype(jnp.float32)
    detect = extra[DETECT : DETECT + 1] + extra[DETECT + 1 : DETECT + 2]
    detect += extra[DETECT + 2 : DETECT + 3]
    line = lax.broadcasted_iota(jnp.int32, (8, PW), 0)
    lane = lax.broadcasted_iota(jnp.int32, (8, PW), 1)
    chosen = jnp.sum(jnp.where(line == lane, detect, 0.0), axis=1, keepdims=True)
    detect_ref[...] = jnp.broadcast_to(chosen, (8, PW))


def merge_kernel(count, groups, totals_ref, weights_ref, cross_ref, *refs):
    messages = refs[:groups]
    home_ref, home_weight_ref, held = refs[groups:]
    totals, weights = add_message(count, groups, cross_ref.at[0])
    held[...] = totals + totals_ref[0]
    weights += weights_ref[0]
    for turn, message in enumerate(messages):
        write_banded(message, part_of(held, turn, groups), weights)
    totals, weights = add_message(count, groups, cross_ref.at[1])
    home_ref[...] = totals + totals_ref[1]
    home_weight_ref[...] = weights + weights_ref[1]


def home_kernel(count, groups, home_ref, home_weight_ref, far_ref, *refs):
    messages = refs[: groups - 1]
    own_ref, own_weight_ref, held = refs[groups - 1 :]
    totals, weights = add_message(count, groups, far_ref)
    held[...] = totals + home_ref[...]
    weights += home_weight_ref[...]
    for turn, message in enumerate(messages, 1):
        write_banded(message, part_of(held, turn, groups), weights)
    own_ref[...] = part_of(held, 0, groups)
    own_weight_ref[...] = weights


def early_kernel(*refs):
    messages = refs[:-2]
    totals_ref, weights_ref = refs[-2:]
    depth = totals_ref.shape[0]
    totals_ref[...], weights_ref[...] = add_banded(
        jnp.zeros((depth, PW), jnp.float32), jnp.zeros((8, PW), jnp.float32), messages
    )


def combine_kernel(
    detect_ref, own_ref, own_weight_ref, near_ref, near_weight_ref, *refs
):
    coadd_ref, detection_ref = refs[-2:]
    row_share = coadd_ref.shape[1]
    totals, weights = add_banded(
        own_ref[...] + near_ref[...], own_weight_ref[...] + near_weight_ref[...], refs[:-2]
    )
    weights = jnp.maximum(weights, 1.0)
    detection = jnp.zeros((row_share, PW), jnp.float32)
    for b in range(BANDS):
        coadd = totals[b * row_share : (b + 1) * row_share] / weights[b : b + 1]
        coadd_ref[b] = coadd
        detection += detect_ref[b : b + 1] * coadd
    detection_ref[...] = detection


def local(
    tiles,
    tile_patch,
    tile_offset,
    tile_weight,
    visit_band,
    coeff_index,
    coeff_table,
    row_kernels,
    column_kernels,
    band_weight,
):
    tile_count, rows, width = tiles.shape
    visits = visit_band.shape[0]
    per_visit = tile_count // visits
    basis, taps = row_kernels.shape
    patches = lax.axis_size("ra")
    groups = lax.axis_size("band")
    row_share = rows // groups
    length = visits * rows + EXTRA
    message_shape = jax.ShapeDtypeStruct((length, PW), jnp.bfloat16)
    pair_shape = jax.ShapeDtypeStruct((2, length, PW), jnp.bfloat16)
    band_shape = jax.ShapeDtypeStruct((BANDS * row_share + EXTRA, PW), jnp.bfloat16)
    part_shape = jax.ShapeDtypeStruct((BANDS * row_share, PW), jnp.float32)
    whole_shape = jax.ShapeDtypeStruct((BANDS * rows, PW), jnp.float32)
    weight_shape = jax.ShapeDtypeStruct((8, PW), jnp.float32)

    vmem = pl.BlockSpec(memory_space=pltpu.VMEM)
    anywhere = pl.BlockSpec(memory_space=pl.ANY)
    far, cross, kept = pl.pallas_call(
        functools.partial(match_kernel, patches),
        in_specs=[anywhere] * 10,
        out_specs=[vmem] * 3,
        out_shape=[message_shape, pair_shape, pair_shape],
        scratch_shapes=[
            pltpu.SMEM((tile_count,), jnp.int32),
            pltpu.SMEM((tile_count,), jnp.int32),
            pltpu.SMEM((tile_count,), jnp.int32),
            pltpu.SMEM((visits,), jnp.int32),
            pltpu.SMEM((BANDS,), jnp.float32),
            pltpu.VMEM(coeff_table.shape[::-1], jnp.float32),
            pltpu.VMEM((1, tile_count), jnp.bfloat16),
            pltpu.VMEM((basis, taps), jnp.bfloat16),
            pltpu.VMEM((basis, taps), jnp.bfloat16),
            pltpu.VMEM((tile_count, rows, width), jnp.bfloat16),
            pltpu.VMEM((tile_count * VECTORS, width), jnp.float32),
            pltpu.VMEM((tile_count, width), jnp.float32),
            pltpu.VMEM((per_visit, 2, 4 * FINE_ROWS, 2 * width), jnp.bfloat16),
            pltpu.VMEM((per_visit, 2, COARSE * BLOCK, 2 * width), jnp.bfloat16),
            pltpu.VMEM((per_visit, rows, width), jnp.float32),
            pltpu.VMEM((SPREAD, rows, PW), jnp.float32),
            pltpu.VMEM((SPREAD, EXTRA, PW), jnp.float32),
            pltpu.SemaphoreType.DMA((visits,)),
            pltpu.SemaphoreType.DMA((9,)),
        ],
        compiler_params=pltpu.CompilerParams(vmem_limit_bytes=62 * 1024 * 1024),
        name="match_and_sum",
    )(
        tile_patch,
        tile_offset,
        coeff_index,
        visit_band,
        band_weight,
        coeff_table.T,
        tile_weight.reshape(1, tile_count),
        row_kernels,
        column_kernels,
        tiles,
    )

    def send(message, goal, turn):
        route = [
            (o * groups + g, goal(o) % patches * groups + (g + turn) % groups)
            for o in range(patches)
            for g in range(groups)
        ]
        return lax.ppermute(message, ("ra", "band"), route)

    def onward(distance):
        return lambda o: o + distance if o % 2 else o - distance

    def local_call(kernel, name, out_shape, *operands, **options):
        return pl.pallas_call(
            kernel,
            in_specs=[vmem] * len(operands),
            out_specs=[vmem] * len(out_shape),
            out_shape=out_shape,
            compiler_params=pltpu.CompilerParams(vmem_limit_bytes=40 * 1024 * 1024),
            name=name,
            **options,
        )(*operands)

    held = [pltpu.VMEM(whole_shape.shape, jnp.float32)]
    cross = send(cross, onward(-1), 0)
    far = send(far, onward(2), 0)
    *kept, detect = local_call(
        functools.partial(keep_kernel, visits, groups),
        "keep",
        [
            jax.ShapeDtypeStruct((2,) + whole_shape.shape, jnp.float32),
            jax.ShapeDtypeStruct((2,) + weight_shape.shape, jnp.float32),
            weight_shape,
        ],
        kept,
    )
    *near, home, home_weight = local_call(
        functools.partial(merge_kernel, visits, groups),
        "merge",
        [band_shape] * groups + [whole_shape, weight_shape],
        *kept,
        cross,
        scratch_shapes=held,
    )
    near = [send(near[turn], onward(1), turn) for turn in range(groups)]
    *others, own, own_weight = local_call(
        functools.partial(home_kernel, visits, groups),
        "home",
        [band_shape] * (groups - 1) + [part_shape, weight_shape],
        home,
        home_weight,
        far,
        scratch_shapes=held,
    )
    others = [send(others[turn - 1], onward(0), turn) for turn in range(1, groups)]
    near = local_call(early_kernel, "combine_early", [part_shape, weight_shape], *near)
    return local_call(
        combine_kernel,
        "combine",
        (
            jax.ShapeDtypeStruct((BANDS, row_share, PW), jnp.float32),
            jax.ShapeDtypeStruct((row_share, PW), jnp.float32),
        ),
        detect,
        own,
        own_weight,
        *near,
        *others,
    )


def solution(mesh):
    return jax.shard_map(
        local,
        mesh=mesh,
        in_specs=(
            P(("ra", "band"), None, None),
            P(("ra", "band")),
            P(("ra", "band")),
            P(("ra", "band")),
            P(("ra", "band")),
            P(("ra", "band")),
            P(),
            P(),
            P(),
            P(),
        ),
        out_specs=(P(None, "band", "ra"), P("band", "ra")),
        check_vma=False,
    )
```
